32 devices in a mesh: head: 4 (over y, x), blk: 8 (over z, core).
Axes of the slice: x: 2, y: 2, z: 4, core: 2. Of those that a mesh axis runs over, the one named last changes fastest.
Arguments:
- tokens: bfloat16 [4096, 1024], P(('head', 'blk')), may hold values from -6 to 6
- attn_gain: bfloat16 [1024], P(('head', 'blk')), may hold values from 0.25 to 1.75
- w_qkv: bfloat16 [1024, 3072], P(('head', 'blk')), may hold values from -0.1875 to 0.1875
- w_attn_out: bfloat16 [1024, 1024], P(('head', 'blk')), may hold values from -4 to 4
- mlp_gain: bfloat16 [1024], P(('head', 'blk')), may hold values from 0.25 to 1.75
- w_in: bfloat16 [1024, 5248], P(('head', 'blk')), may hold values from -0.1875 to 0.1875
- w_mlp_out: bfloat16 [2624, 1024], P(None, ('head', 'blk')), may hold values from -0.125 to 0.125
- doc_lengths: int32 [32], replicated, may hold values from 1 to 1024, 4096 in all
- cotangent: bfloat16 [4096, 1024], P(('head', 'blk')), may hold values from -6 to 6
Outputs:
- output: bfloat16 [4096, 1024], P(('head', 'blk'))
- input_grad: float32 [4096, 1024], P(('head', 'blk'))
- attn_gain_grad: float32 [1024], P(('head', 'blk'))
- w_qkv_grad: float32 [1024, 3072], P(('head', 'blk'))
- w_attn_out_grad: float32 [1024, 1024], P(('head', 'blk'))
- mlp_gain_grad: float32 [1024], P(('head', 'blk'))
- w_in_grad: float32 [1024, 5248], P(('head', 'blk'))
- w_mlp_out_grad: float32 [2624, 1024], P(None, ('head', 'blk'))
The draws below stay inside these ranges and needn't reach their ends.
Inputs may be any that keep to these rules, and one draw needn't show every extreme that they name: `doc_lengths`: document lengths in stream order; they sum to 4096, and the longest is exactly 1024.
All inputs are finite; a program needn't handle non-finite values.
Results may differ from the reference program's by a relative error of at most 0.023.
Values may be sent and summed in bfloat16 or wider, within the bound.
A program may use at most 192 MiB of HBM per device.

```python
import math
import jax
import jax.numpy as jnp
import numpy as np
from jax import lax

D = 1024
HEADS = 16
HEAD_DIM = 64
FF = 2624
TOKENS = 4096
DOC_MOST = 1024
DOCS = 32


def block_scale(key, dims, shards, smallest, high):
    level, own = 1.0, jax.random.fold_in(key, 6)
    for axis_at, blocks in shards:
        heights = jnp.exp(jax.random.uniform(jax.random.fold_in(own, axis_at), (blocks,), jnp.float32, smallest / len(shards), high / len(shards)))
        level = level * jnp.repeat(heights, dims[axis_at] // blocks).reshape([-1 if axis == axis_at else 1 for axis in range(len(dims))])
    return level


def split_up(amount, total, limit, skew):
    portions = [(1 << 20) // math.isqrt(grade ** skew) + 1 for grade in range(2, amount + 1)]
    surplus, holding = total - limit - (amount - 1), [1] * (amount - 1)
    while surplus > 0:
        movable = [i for i in range(amount - 1) if holding[i] < limit]
        whole, left = sum([portions[i] for i in movable]), surplus
        for i in movable:
            extra = min(limit - holding[i], max(1, left * portions[i] // whole), surplus)
            holding[i] = holding[i] + extra
            surplus = surplus - extra
    return np.array([limit] + holding)


def ragged(rng, number_of, total, bound, skew):
    if number_of == 2:
        one = jax.random.randint(rng, (), max(1, total - bound), min(bound, total - 1) + 1)
        return jnp.stack([one, total - one])
    sizes = jnp.asarray(split_up(number_of, total, bound, skew), jnp.int32)
    pairs = (number_of - 1) // 2
    source_of, receiver = sizes[1:1 + 2 * pairs:2], sizes[2:2 + 2 * pairs:2]
    room = jnp.minimum(source_of - 1, bound - receiver)
    moved = jax.random.randint(jax.random.fold_in(rng, 1), (pairs,), 0, 1 << 20) % (room + 1)
    sizes = sizes.at[1:1 + 2 * pairs:2].set(source_of - moved).at[2:2 + 2 * pairs:2].set(receiver + moved)
    return sizes[jax.random.permutation(jax.random.fold_in(rng, 2), number_of)]


def scatter_about(stream_key, shape, width, most, shards=(), held_as=jnp.bfloat16):
    factor_of = block_scale(stream_key, shape, shards, -0.22, 0.18) if shards else 1.0
    entries = jax.random.normal(stream_key, shape, jnp.float32) * width * factor_of
    return jnp.minimum(jnp.maximum(entries, -most), most).astype(held_as)


def setup_inputs(seed: int = 0) -> dict:
    key_of = jax.random.split(jax.random.key(seed), 10)
    return {
        "tokens": scatter_about(key_of[0], (TOKENS, D), 1.0, 6.0, ((0, 32),)),
        "attn_gain": jnp.clip(1.0 + 0.15 * jax.random.normal(key_of[1], (D,), jnp.float32), 0.25, 1.75).astype(jnp.bfloat16),
        "w_qkv": scatter_about(key_of[2], (D, 3 * D), D ** -0.5, 0.1875, ((0, 32),)),
        "w_attn_out": scatter_about(key_of[3], (D, D), 2 ** -0.5, 4.0, ((0, 32),)),
        "mlp_gain": jnp.clip(1.0 + 0.15 * jax.random.normal(key_of[4], (D,), jnp.float32), 0.25, 1.75).astype(jnp.bfloat16),
        "w_in": scatter_about(key_of[5], (D, 2 * FF), D ** -0.5, 0.1875, ((0, 32),)),
        "w_mlp_out": scatter_about(key_of[6], (FF, D), FF ** -0.5, 0.125, ((1, 32),)),
        "doc_lengths": ragged(key_of[7], DOCS, TOKENS, DOC_MOST, 2).astype(jnp.int32),
        "cotangent": scatter_about(key_of[8], (TOKENS, D), 1.0, 6.0, ((0, 32),)),
    }


norm_eps = 1e-05
rope_base = 160000.0

@jax.custom_vjp
def low(v):
    return lax.optimization_barrier(v.astype(jnp.bfloat16)).astype(jnp.float32)

@jax.custom_vjp
def low_back(v):
    return v

def low_keep(v):
    return (low(v), None)

def low_pass(kept, grad):
    return (grad,)

def back_keep(v):
    return (v, None)

def back_low(kept, grad):
    return (low(grad),)
low.defvjp(low_keep, low_pass)
low_back.defvjp(back_keep, back_low)

def layer_norm(values, gain):
    center = values - lax.optimization_barrier(jnp.mean(values, axis=-1, keepdims=True))
    spread = lax.optimization_barrier(jnp.mean(center * center, axis=-1, keepdims=True))
    return center * lax.rsqrt(spread + norm_eps) * gain

def rope_tables(places, head_size):
    half = head_size // 2
    freqs = rope_base ** (-(jnp.arange(half, dtype=jnp.float32) * 2.0) / head_size)
    angles = places.astype(jnp.float32)[:, None] * freqs[None, :]
    angles = jnp.concatenate([angles, angles], axis=1)
    return (jnp.cos(angles), jnp.sin(angles))

def rotate(values, cosine, sine):
    count = values.shape[0]
    head_size = cosine.shape[1]
    half = head_size // 2
    split = values.reshape(count, -1, head_size)
    turned = jnp.concatenate([-split[..., half:], split[..., :half]], axis=-1)
    return (split * cosine[:, None, :] + turned * sine[:, None, :]).reshape(count, -1)

def doc_numbers(places, ends, lengths):
    passed = places[:, None] >= ends[None, :]
    numbers = lax.optimization_barrier(jnp.sum(passed.astype(jnp.int32), axis=1)).astype(jnp.int32)
    offset = lax.optimization_barrier(jnp.sum(jnp.where(passed, lengths[None, :], 0), axis=1)).astype(jnp.int32)
    return (numbers, (places - offset).astype(jnp.int32))

def product(left, right):
    return jnp.dot(left, right, precision=lax.Precision.HIGHEST)

def gelu_gate(lifted):
    half = lifted.shape[1] // 2
    return jax.nn.gelu(lifted[:, :half], approximate=False) * lifted[:, half:]

def attention(query, keys, values, docs):
    total = query.shape[0]
    block_size = min(512, total)
    query_split = query.reshape(total // block_size, block_size, HEADS, HEAD_DIM)
    key_split = keys.reshape(total, HEADS, HEAD_DIM)
    value_split = values.reshape(total, HEADS, HEAD_DIM)

    def one_block(pair):
        query_block, block_docs = pair
        scores = jnp.einsum('qhd,khd->hqk', query_block, key_split, precision=lax.Precision.HIGHEST) * HEAD_DIM ** (-0.5)
        scores = low_back(scores)
        same = (block_docs[:, None] == docs[None, :])[None]
        scores = jnp.where(same, scores, -jnp.inf)
        weights = low(jax.nn.softmax(scores, axis=-1))
        return jnp.einsum('hqk,khd->qhd', weights, value_split, precision=lax.Precision.HIGHEST)
    mixed = lax.map(jax.checkpoint(one_block), (query_split, docs.reshape(total // block_size, block_size)))
    return mixed.reshape(total, HEADS * HEAD_DIM)

def reference(tokens, attn_gain, w_qkv, w_attn_out, mlp_gain, w_in, w_mlp_out, doc_lengths, cotangent):
    doc_ends = jnp.cumsum(doc_lengths).astype(jnp.int32)
    places = jnp.arange(TOKENS, dtype=jnp.int32)
    docs, positions = doc_numbers(places, doc_ends, doc_lengths)
    cosine, sine = rope_tables(positions, HEAD_DIM)

    def forward(inputs, gain_one, weight_qkv, weight_out, gain_two, weight_in, weight_down):
        normed_one = low(layer_norm(inputs, gain_one))
        projected = low_back(product(normed_one, weight_qkv))
        query = low_back(low(rotate(projected[:, :D], cosine, sine)))
        keys = low_back(low(rotate(projected[:, D:2 * D], cosine, sine)))
        values = low_back(low(projected[:, 2 * D:]))
        mixed = low_back(low(attention(query, keys, values, docs)))
        middle = inputs + low_back(product(mixed, weight_out))
        normed_two = low(layer_norm(middle, gain_two))
        lifted = low_back(product(normed_two, weight_in))
        activated = low(gelu_gate(lifted))
        return middle + product(activated, weight_down)
    result, pull = jax.vjp(forward, tokens.astype(jnp.float32), attn_gain.astype(jnp.float32), w_qkv.astype(jnp.float32), w_attn_out.astype(jnp.float32), mlp_gain.astype(jnp.float32), w_in.astype(jnp.float32), w_mlp_out.astype(jnp.float32))
    grads = pull(cotangent.astype(jnp.float32))
    return (result.astype(jnp.bfloat16), grads[0], grads[1], grads[2], grads[3], grads[4], grads[5], grads[6])
```

```python
from functools import partial

import jax
import jax.numpy as jnp
from jax import lax
from jax.experimental import pallas as pl
from jax.experimental.pallas import tpu as pltpu
from jax.sharding import PartitionSpec as P

HEAD_DIM = 64


norm_eps = 1e-05
rope_base = 160000.0
neg_large = -1e30


def from_behind(value, axis, by):
    devices = lax.axis_size(axis)
    return lax.ppermute(value, axis, [(i, (i + by) % devices) for i in range(devices)])


def layer_norm(values, gain):
    center = values - jnp.mean(values, axis=-1, keepdims=True)
    spread = jnp.mean(center * center, axis=-1, keepdims=True)
    return center * lax.rsqrt(spread + norm_eps) * gain


def rope_tables(places, head_size):
    half = head_size // 2
    freqs = rope_base ** (-(jnp.arange(half, dtype=jnp.float32) * 2.0) / head_size)
    angles = places.astype(jnp.float32)[:, None] * freqs[None, :]
    angles = jnp.concatenate([angles, angles], axis=1)
    return (jnp.cos(angles), jnp.sin(angles))


def rotate(values, cosine, sine):
    count = values.shape[0]
    head_size = cosine.shape[1]
    half = head_size // 2
    split = values.reshape(count, -1, head_size)
    turned = jnp.concatenate([-split[..., half:], split[..., :half]], axis=-1)
    return (split * cosine[:, None, :] + turned * sine[:, None, :]).reshape(count, -1)


def rotate_pair(query, keys, cosine, sine):
    return (rotate(query, cosine, sine), rotate(keys, cosine, sine))


def doc_numbers(places, ends, lengths):
    passed = places[:, None] >= ends[None, :]
    numbers = jnp.sum(passed.astype(jnp.int32), axis=1)
    offset = jnp.sum(jnp.where(passed, lengths[None, :], 0), axis=1)
    return (numbers, places - offset)


def gelu_gate(lifted):
    half = lifted.shape[1] // 2
    return jax.nn.gelu(lifted[:, :half], approximate=False) * lifted[:, half:]


def tile_scores(query, keys):
    heads = query.shape[1] // HEAD_DIM
    query_split = query.reshape(query.shape[0], heads, HEAD_DIM)
    key_split = keys.reshape(keys.shape[0], heads, HEAD_DIM)
    return jnp.einsum(
        "qhd,khd->hqk", query_split, key_split, preferred_element_type=jnp.float32
    ) * HEAD_DIM ** (-0.5)


def unchanged(state):
    return state


def forward_tile(state, query, keys, values, mask):
    top, total, running = state
    count = query.shape[0]
    heads = top.shape[0]
    scores = tile_scores(query, keys)
    filled = jnp.where(mask[None], scores, neg_large)
    new_top = jnp.maximum(top, jnp.max(filled, axis=-1))
    weights = jnp.where(mask[None], jnp.exp(scores - new_top[:, :, None]), 0.0)
    factor = jnp.exp(top - new_top)
    new_total = total * factor + jnp.sum(weights, axis=-1)
    mixed = jnp.einsum(
        "hqk,khd->qhd",
        weights.astype(jnp.bfloat16),
        values.reshape(-1, heads, HEAD_DIM),
        preferred_element_type=jnp.float32,
    )
    new_running = running.reshape(count, heads, HEAD_DIM) * factor.T[:, :, None] + mixed
    return (new_top, new_total, new_running.reshape(count, heads * HEAD_DIM))


def backward_tile(carry, query, keys, values, mask, norm_log, grad_out, delta):
    query_grad, run_grads = carry
    count = query.shape[0]
    columns = keys.shape[0]
    heads = norm_log.shape[0]
    scores = tile_scores(query, keys)
    probs = jnp.where(mask[None], jnp.exp(scores - norm_log[:, :, None]), 0.0)
    grad_split = grad_out.reshape(count, heads, HEAD_DIM)
    value_split = values.reshape(columns, heads, HEAD_DIM)
    grad_values = jnp.einsum(
        "hqk,qhd->khd", probs.astype(jnp.bfloat16), grad_split, preferred_element_type=jnp.float32
    )
    grad_probs = jnp.einsum(
        "qhd,khd->hqk", grad_split, value_split, preferred_element_type=jnp.float32
    )
    grad_scores = (probs * (grad_probs - delta[:, :, None])).astype(jnp.bfloat16)
    grad_query = jnp.einsum(
        "hqk,khd->qhd",
        grad_scores,
        keys.reshape(columns, heads, HEAD_DIM),
        preferred_element_type=jnp.float32,
    ) * HEAD_DIM ** (-0.5)
    grad_keys = jnp.einsum(
        "hqk,qhd->khd",
        grad_scores,
        query.reshape(count, heads, HEAD_DIM),
        preferred_element_type=jnp.float32,
    ) * HEAD_DIM ** (-0.5)
    added = jnp.stack([grad_keys.reshape(columns, -1), grad_values.reshape(columns, -1)])
    return (query_grad + grad_query.reshape(count, -1), run_grads + added)


def per_device_general(
    tokens, attn_gain, w_qkv, w_attn_out, mlp_gain, w_in, w_mlp_out, doc_lengths, cotangent
):
    own_rows = tokens.shape[0]
    width = tokens.shape[1]
    head_count = lax.axis_size("head")
    cycle_count = lax.axis_size("blk")
    head_place = lax.axis_index("head")
    cycle_place = lax.axis_index("blk")
    group_rows = head_count * own_rows
    block_runs = min(head_count, max(1, 512 // own_rows))
    block_count = head_count // block_runs
    block_rows = block_runs * own_rows
    doc_ends = jnp.cumsum(doc_lengths)
    counter = jnp.arange(own_rows, dtype=jnp.int32)
    own_places = (head_place * cycle_count + cycle_place) * own_rows + counter
    unused_docs, own_positions = doc_numbers(own_places, doc_ends, doc_lengths)
    cosine, sine = rope_tables(own_positions, HEAD_DIM)
    run_numbers = jnp.arange(head_count, dtype=jnp.int32)
    query_places = (
        (run_numbers[:, None] * cycle_count + cycle_place) * own_rows + counter[None, :]
    ).reshape(group_rows)
    query_docs, unused_positions = doc_numbers(query_places, doc_ends, doc_lengths)
    params = (
        lax.all_gather(attn_gain, ("head", "blk"), axis=0, tiled=True),
        lax.all_gather(w_qkv, ("head", "blk"), axis=0, tiled=True),
        lax.all_gather(w_attn_out, ("head", "blk"), axis=0, tiled=True),
        lax.all_gather(mlp_gain, ("head", "blk"), axis=0, tiled=True),
        lax.all_gather(w_in, ("head", "blk"), axis=0, tiled=True),
        lax.all_gather(w_mlp_out, ("head", "blk"), axis=1, tiled=True),
    )
    gain_one, full_qkv, full_attn_out, gain_two, full_in, full_mlp_out = params
    inputs = tokens.astype(jnp.float32)
    normed_one, norm_one_pull = jax.vjp(layer_norm, inputs, gain_one.astype(jnp.float32))
    normed_low = normed_one.astype(jnp.bfloat16)
    projected = jnp.dot(normed_low, full_qkv, preferred_element_type=jnp.float32)
    turned, rope_pull = jax.vjp(
        partial(rotate_pair, cosine=cosine, sine=sine),
        projected[:, :width],
        projected[:, width : 2 * width],
    )
    stacked = jnp.stack(
        [
            turned[0].astype(jnp.bfloat16),
            turned[1].astype(jnp.bfloat16),
            projected[:, 2 * width :].astype(jnp.bfloat16),
        ]
    )
    regrouped = lax.all_to_all(stacked, "head", split_axis=2, concat_axis=1, tiled=True)
    query_heads = regrouped[0]
    key_heads = regrouped[1]
    value_heads = regrouped[2]
    head_width = query_heads.shape[1]
    heads_here = head_width // HEAD_DIM

    def key_docs_at(first):
        places = (
            first % group_rows // own_rows * cycle_count + first // group_rows
        ) * own_rows + counter
        found, unused = doc_numbers(places, doc_ends, doc_lengths)
        return found

    def block_live(block, key_docs):
        block_docs = query_docs[block * block_rows : (block + 1) * block_rows]
        live = jnp.maximum(jnp.min(block_docs), jnp.min(key_docs)) <= jnp.minimum(
            jnp.max(block_docs), jnp.max(key_docs)
        )
        return (block_docs[:, None] == key_docs[None, :], live)

    def fold_forward(state, piece):
        key_part, value_part = piece

        def fold_one_run(number, carried):
            first = number * own_rows
            key_docs = key_docs_at(first)
            keys = lax.dynamic_slice_in_dim(key_part, number * own_rows, own_rows, 0)
            values = lax.dynamic_slice_in_dim(value_part, number * own_rows, own_rows, 0)
            updated = []
            for block in range(block_count):
                mask, live = block_live(block, key_docs)
                query = query_heads[block * block_rows : (block + 1) * block_rows]
                advance = partial(forward_tile, query=query, keys=keys, values=values, mask=mask)
                updated.append(lax.cond(live, advance, unchanged, carried[block]))
            return tuple(updated)

        return lax.fori_loop(0, key_part.shape[0] // own_rows, fold_one_run, state)

    def fresh_state():
        return tuple(
            (
                (
                    jnp.full((heads_here, block_rows), neg_large, jnp.float32),
                    jnp.zeros((heads_here, block_rows), jnp.float32),
                    jnp.zeros((block_rows, head_width), jnp.float32),
                )
                for block in range(block_count)
            )
        )

    def finish(state):
        outputs = []
        logs = []
        for top, total, running in state:
            scaled = running.reshape(block_rows, heads_here, HEAD_DIM) / total.T[:, :, None]
            outputs.append(scaled.reshape(block_rows, head_width))
            logs.append(top + jnp.log(total))
        return (
            jnp.concatenate(outputs, axis=0).astype(jnp.bfloat16),
            jnp.concatenate(logs, axis=1),
        )

    state = fold_forward(
        fresh_state(),
        (
            lax.all_gather(key_heads, "blk", axis=0, tiled=True),
            lax.all_gather(value_heads, "blk", axis=0, tiled=True),
        ),
    )
    out_heads, norm_log = finish(state)
    out_tokens = lax.all_to_all(out_heads, "head", split_axis=0, concat_axis=1, tiled=True)
    middle = inputs + jnp.dot(out_tokens, full_attn_out, preferred_element_type=jnp.float32)
    normed_two, norm_two_pull = jax.vjp(layer_norm, middle, gain_two.astype(jnp.float32))
    normed_two_low = normed_two.astype(jnp.bfloat16)
    lifted = jnp.dot(normed_two_low, full_in, preferred_element_type=jnp.float32)
    activated, geglu_pull = jax.vjp(gelu_gate, lifted)
    activated_low = activated.astype(jnp.bfloat16)
    output = (
        middle + jnp.dot(activated_low, full_mlp_out, preferred_element_type=jnp.float32)
    ).astype(jnp.bfloat16)
    params = (
        lax.all_gather(attn_gain, ("head", "blk"), axis=0, tiled=True),
        lax.all_gather(w_qkv, ("head", "blk"), axis=0, tiled=True),
        lax.all_gather(w_attn_out, ("head", "blk"), axis=0, tiled=True),
        lax.all_gather(mlp_gain, ("head", "blk"), axis=0, tiled=True),
        lax.all_gather(w_in, ("head", "blk"), axis=0, tiled=True),
        lax.all_gather(w_mlp_out, ("head", "blk"), axis=1, tiled=True),
    )
    gain_one, full_qkv, full_attn_out, gain_two, full_in, full_mlp_out = params
    grad_act = jnp.einsum("td,fd->tf", cotangent, full_mlp_out, preferred_element_type=jnp.float32)
    grad_lifted = geglu_pull(grad_act)[0].astype(jnp.bfloat16)
    grad_normed_two = jnp.einsum(
        "tf,df->td", grad_lifted, full_in, preferred_element_type=jnp.float32
    )
    grad_middle_part, grad_gain_two = norm_two_pull(grad_normed_two)
    grad_middle = cotangent.astype(jnp.float32) + grad_middle_part
    grad_branch = grad_middle.astype(jnp.bfloat16)
    grad_mixed = jnp.einsum(
        "te,de->td", grad_branch, full_attn_out, preferred_element_type=jnp.float32
    ).astype(jnp.bfloat16)
    grad_heads = lax.all_to_all(grad_mixed, "head", split_axis=1, concat_axis=0, tiled=True)
    state = fold_forward(
        fresh_state(),
        (
            lax.all_gather(key_heads, "blk", axis=0, tiled=True),
            lax.all_gather(value_heads, "blk", axis=0, tiled=True),
        ),
    )
    out_heads, norm_log = finish(state)
    delta = jnp.einsum(
        "qhd,qhd->hq",
        grad_heads.reshape(group_rows, heads_here, HEAD_DIM).astype(jnp.float32),
        out_heads.reshape(group_rows, heads_here, HEAD_DIM).astype(jnp.float32),
    )

    def piece_backward(query_grads, key_part, value_part, start):
        piece_rows = key_part.shape[0]

        def piece_one_run(number, carried):
            query_now, piece_grads = carried
            first = start + number * own_rows
            key_docs = key_docs_at(first)
            keys = lax.dynamic_slice_in_dim(key_part, number * own_rows, own_rows, 0)
            values = lax.dynamic_slice_in_dim(value_part, number * own_rows, own_rows, 0)
            run_grads = jnp.zeros((2, own_rows, head_width), jnp.float32)
            updated = []
            for block in range(block_count):
                mask, live = block_live(block, key_docs)
                lower = block * block_rows
                upper = (block + 1) * block_rows
                advance = partial(
                    backward_tile,
                    query=query_heads[lower:upper],
                    keys=keys,
                    values=values,
                    mask=mask,
                    norm_log=norm_log[:, lower:upper],
                    grad_out=grad_heads[lower:upper],
                    delta=delta[:, lower:upper],
                )
                new_query, run_grads = lax.cond(
                    live, advance, unchanged, (query_now[block], run_grads)
                )
                updated.append(new_query)
            piece_grads = lax.dynamic_update_slice_in_dim(
                piece_grads, run_grads, number * own_rows, 1
            )
            return (tuple(updated), piece_grads)

        return lax.fori_loop(
            0,
            piece_rows // own_rows,
            piece_one_run,
            (query_grads, jnp.zeros((2, piece_rows, head_width), jnp.float32)),
        )

    start_query = tuple(
        (jnp.zeros((block_rows, head_width), jnp.float32) for block in range(block_count))
    )

    def cycle_step(step, carried):
        query_now, blocks, travelling = carried
        owner = (cycle_place - step) % cycle_count
        query_now, piece_grads = piece_backward(query_now, blocks[0], blocks[1], owner * group_rows)
        travelling = travelling + piece_grads
        blocks = from_behind(blocks, "blk", 1)
        travelling = from_behind(travelling.astype(jnp.bfloat16), "blk", 1).astype(travelling.dtype)
        return (query_now, blocks, travelling)

    start_cycle = (
        start_query,
        jnp.stack([key_heads, value_heads]),
        jnp.zeros((2, group_rows, head_width), jnp.float32),
    )
    query_grads, unused_blocks, own_grads = lax.fori_loop(0, cycle_count, cycle_step, start_cycle)
    grad_stack = jnp.stack(
        [
            jnp.concatenate(query_grads, axis=0).astype(jnp.bfloat16),
            own_grads[0].astype(jnp.bfloat16),
            own_grads[1].astype(jnp.bfloat16),
        ]
    )
    back_tokens = lax.all_to_all(grad_stack, "head", split_axis=1, concat_axis=2, tiled=True)
    grad_query, grad_keys = rope_pull(
        (back_tokens[0].astype(jnp.float32), back_tokens[1].astype(jnp.float32))
    )
    grad_projected = jnp.concatenate(
        [grad_query, grad_keys, back_tokens[2].astype(jnp.float32)], axis=1
    ).astype(jnp.bfloat16)
    grad_normed_one = jnp.einsum(
        "te,de->td", grad_projected, full_qkv, preferred_element_type=jnp.float32
    )
    grad_input_part, grad_gain_one = norm_one_pull(grad_normed_one)
    input_grad = grad_middle + grad_input_part

    def columns(source):
        return source

    term_qkv = jnp.einsum(
        "td,te->de", columns(normed_low), grad_projected, preferred_element_type=jnp.float32
    )
    term_out = jnp.einsum(
        "td,te->de", columns(out_tokens), grad_branch, preferred_element_type=jnp.float32
    )
    term_in = jnp.einsum(
        "td,tf->df", columns(normed_two_low), grad_lifted, preferred_element_type=jnp.float32
    )
    term_down = jnp.einsum(
        "td,tf->df", columns(cotangent), activated_low, preferred_element_type=jnp.float32
    )
    sums = lax.psum_scatter(
        jnp.concatenate([term_qkv, term_out, term_in, term_down], axis=1),
        ("head", "blk"),
        scatter_dimension=0,
        tiled=True,
    )
    ff_width = full_mlp_out.shape[0]
    qkv_grad = sums[:, : 3 * width]
    attn_out_grad = sums[:, 3 * width : 4 * width]
    in_grad = sums[:, 4 * width : 4 * width + 2 * ff_width]
    down_grad = sums[:, 4 * width + 2 * ff_width :].T
    gain_sums = lax.psum_scatter(
        jnp.stack([grad_gain_one, grad_gain_two]), ("head", "blk"), scatter_dimension=1, tiled=True
    )
    return (
        output,
        input_grad,
        gain_sums[0],
        qkv_grad,
        attn_out_grad,
        gain_sums[1],
        in_grad,
        down_grad,
    )


KEY_TILE = 256
NN = (((1,), (0,)), ((), ()))
NT = (((1,), (1,)), ((), ()))
TN = (((0,), (0,)), ((), ()))


def mm(left, right, dims=NN):
    return lax.dot_general(left, right, dims, preferred_element_type=jnp.float32)


def halves(packed, side):
    wide = packed.astype(jnp.float32)
    if side:
        wide = pltpu.roll(wide, HEAD_DIM, 1)
    lane = lax.broadcasted_iota(jnp.int32, wide.shape, 1)
    return jnp.where(lane < HEAD_DIM, wide, 0.0)


def attend_kernel(span, qp, kv, qdoc, kdoc, op, lse, s_scr):
    pairs, tall = qp.shape[0] * qp.shape[2], qp.shape[2]
    half_runs = pl.num_programs(0)
    hh, u = pl.program_id(0), pl.program_id(1)
    lane = lax.broadcasted_iota(jnp.int32, (pairs, 2 * HEAD_DIM), 1)
    results = []
    for side in (0, 1):
        tile = (hh + side * half_runs) * pl.num_programs(1) + u
        query = (halves(qp[...].reshape(pairs, 2 * HEAD_DIM), side) * HEAD_DIM**-0.5).astype(
            jnp.bfloat16
        )
        docs = qdoc[tile]
        first, last = span[tile, 0], span[tile, 1]

        def score(kb, top):
            keys = kv[pl.ds(pl.multiple_of(kb * KEY_TILE, KEY_TILE), KEY_TILE), :]
            scores = jnp.where(docs == kdoc[pl.ds(kb, 1), :], mm(query, keys, NT), neg_large)
            s_scr[kb] = scores
            return jnp.maximum(top, jnp.maximum(scores[:, :128], scores[:, 128:]))

        top = lax.fori_loop(first, last, score, jnp.full((pairs, 128), neg_large, jnp.float32))
        top = jnp.max(top, axis=1, keepdims=True)

        def mix(kb, carried):
            total, acc = carried
            keys = kv[pl.ds(pl.multiple_of(kb * KEY_TILE, KEY_TILE), KEY_TILE), :]
            weights = jnp.exp(s_scr[kb] - top)
            total = total + weights[:, :128] + weights[:, 128:]
            return (total, acc + mm(weights.astype(jnp.bfloat16), keys))

        zeros = jnp.zeros((pairs, 128), jnp.float32)
        total, acc = lax.fori_loop(first, last, mix, (zeros, zeros))
        total = jnp.sum(total, axis=1, keepdims=True)
        lse[tile] = top + jnp.log(total)
        results.append(acc / total)
    both = jnp.where(lane < HEAD_DIM, pltpu.roll(results[0], HEAD_DIM, 1), results[1])
    op[...] = both.astype(jnp.bfloat16).reshape(op.shape)


def attend(span, qp, kv, qdoc, kdoc):
    parts, half_runs, rows, lanes = qp.shape
    tiles = qdoc.shape[0]
    piece = pl.BlockSpec((2, 1, rows, lanes), lambda i, j, s: (j, i, 0, 0))
    whole = pl.BlockSpec(memory_space=pltpu.VMEM)
    return pl.pallas_call(
        attend_kernel,
        grid_spec=pltpu.PrefetchScalarGridSpec(
            num_scalar_prefetch=1,
            grid=(half_runs, parts // 2),
            in_specs=[piece, whole, whole, whole],
            out_specs=[piece, whole],
            scratch_shapes=[
                pltpu.VMEM((kv.shape[0] // KEY_TILE, 2 * rows, KEY_TILE), jnp.float32)
            ],
        ),
        out_shape=[
            jax.ShapeDtypeStruct(qp.shape, jnp.bfloat16),
            jax.ShapeDtypeStruct((tiles, 2 * rows, 1), jnp.float32),
        ],
        compiler_params=pltpu.CompilerParams(vmem_limit_bytes=48 * 2**20),
        cost_estimate=pl.CostEstimate(flops=10**9, bytes_accessed=4 * 10**6, transcendentals=10**6),
        name="attend",
    )(span, qp, kv, qdoc, kdoc)


def attend_back_kernel(span, qp, gp, op, lse, kv, qdoc, kdoc, dqp, dkv, acc_scr):
    pairs, tall = qp.shape[0] * qp.shape[2], qp.shape[2]
    half_runs = pl.num_programs(0)
    hh, u = pl.program_id(0), pl.program_id(1)
    lane = lax.broadcasted_iota(jnp.int32, (pairs, 2 * HEAD_DIM), 1)

    @pl.when((hh == 0) & (u == 0))
    def _():
        acc_scr[...] = jnp.zeros_like(acc_scr)

    results = []
    flat = (pairs, 2 * HEAD_DIM)
    both = gp[...].reshape(flat).astype(jnp.float32) * op[...].reshape(flat).astype(jnp.float32)
    for side in (0, 1):
        tile = (hh + side * half_runs) * pl.num_programs(1) + u
        query = (halves(qp[...].reshape(flat), side) * HEAD_DIM**-0.5).astype(jnp.bfloat16)
        grad = gp[...].reshape(flat).astype(jnp.float32)
        if not side:
            grad = pltpu.roll(grad, HEAD_DIM, 1)
        grad = jnp.where(lane < HEAD_DIM, 0.0, grad).astype(jnp.bfloat16)
        here = (lane >= HEAD_DIM) if side else (lane < HEAD_DIM)
        delta = jnp.sum(jnp.where(here, both, 0.0), axis=1, keepdims=True)
        docs = qdoc[tile]
        logs = lse[tile]

        def step(kb, dq):
            keys = kv[pl.ds(pl.multiple_of(kb * KEY_TILE, KEY_TILE), KEY_TILE), :]
            scores = mm(query, keys, NT)
            probs = jnp.where(docs == kdoc[pl.ds(kb, 1), :], jnp.exp(scores - logs), 0.0)
            grad_scores = (probs * (mm(grad, keys, NT) - delta)).astype(jnp.bfloat16)
            acc_scr[kb] += mm(grad_scores, query, TN) + mm(probs.astype(jnp.bfloat16), grad, TN)
            return dq + mm(grad_scores, keys)

        dq = lax.fori_loop(span[tile, 0], span[tile, 1], step, jnp.zeros(flat, jnp.float32))
        results.append(dq * HEAD_DIM**-0.5)
    both = jnp.where(lane < HEAD_DIM, results[0], pltpu.roll(results[1], HEAD_DIM, 1))
    dqp[...] = both.astype(jnp.bfloat16).reshape(dqp.shape)

    @pl.when((hh == half_runs - 1) & (u == pl.num_programs(1) - 1))
    def _():
        dkv[...] = acc_scr[...].reshape(dkv.shape).astype(dkv.dtype)


def attend_back(span, qp, gp, op, lse, kv, qdoc, kdoc):
    parts, half_runs, rows, lanes = qp.shape
    piece = pl.BlockSpec((2, 1, rows, lanes), lambda i, j, s: (j, i, 0, 0))
    whole = pl.BlockSpec(memory_space=pltpu.VMEM)
    return pl.pallas_call(
        attend_back_kernel,
        grid_spec=pltpu.PrefetchScalarGridSpec(
            num_scalar_prefetch=1,
            grid=(half_runs, parts // 2),
            in_specs=[piece, piece, piece, whole, whole, whole, whole],
            out_specs=[piece, whole],
            scratch_shapes=[pltpu.VMEM((kv.shape[0] // KEY_TILE, KEY_TILE, lanes), jnp.float32)],
        ),
        out_shape=[
            jax.ShapeDtypeStruct(qp.shape, jnp.bfloat16),
            jax.ShapeDtypeStruct(kv.shape, jnp.bfloat16),
        ],
        compiler_params=pltpu.CompilerParams(vmem_limit_bytes=48 * 2**20),
        cost_estimate=pl.CostEstimate(flops=3 * 10**9, bytes_accessed=6 * 10**6, transcendentals=10**6),
        name="attend_back",
    )(span, qp, gp, op, lse, kv, qdoc, kdoc)


def pack_pairs(value):
    half = value.shape[1] // 2
    return jnp.concatenate([value[:, :half], value[:, half:]], axis=-1)


def unpack_pairs(value):
    return jnp.concatenate([value[..., :HEAD_DIM], value[..., HEAD_DIM:]], axis=1)


def per_device_split(
    tokens, attn_gain, w_qkv, w_attn_out, mlp_gain, w_in, w_mlp_out, doc_lengths, cotangent
):
    R, W = tokens.shape
    H, B = lax.axis_size("head"), lax.axis_size("blk")
    A = W // HEAD_DIM // H
    G = B // A
    hw = W // H
    D = w_qkv.shape[0]
    F = w_mlp_out.shape[0] // H
    T = H * B * R
    N = H * R
    h, b = lax.axis_index("head"), lax.axis_index("blk")
    f32, bf16 = jnp.float32, jnp.bfloat16
    part_groups = [[a * G + g for a in range(A)] for g in range(G)]
    share_groups = [[a * G + g for g in range(G)] for a in range(A)]

    ends = jnp.cumsum(doc_lengths)
    places = jnp.arange(T, dtype=jnp.int32)
    passed = places[:, None] >= ends[None, :]
    docs = jnp.sum(passed.astype(jnp.int32), axis=1)
    starts = jnp.sum(jnp.where(passed, doc_lengths[None, :], 0), axis=1)
    stops = jnp.min(jnp.where(passed, T, ends[None, :]), axis=1)
    runs = (T // R,)
    run_docs = docs.reshape(H, A, G, R)
    run_lo = starts.reshape(H, A, G, R)[..., 0]
    run_hi = stops.reshape(H, A, G, R)[..., R - 1]
    g = b % G
    pick = lambda v: lax.dynamic_index_in_dim(v, g, 2, keepdims=False)
    qdoc = pick(run_docs).reshape(H * A // 2, 2 * R, 1)
    lo = pick(run_lo).reshape(H * A // 2, 2)[:, 0] // KEY_TILE
    hi = (pick(run_hi).reshape(H * A // 2, 2)[:, 1] + KEY_TILE - 1) // KEY_TILE
    span = jnp.stack([lo, hi], axis=1).astype(jnp.int32)
    kdoc = docs.reshape(T // KEY_TILE, KEY_TILE)
    own = lambda v: lax.dynamic_index_in_dim(v.reshape(H, B, R), b, 1, keepdims=False).reshape(N)
    cosine, sine = rope_tables(own(places - starts), HEAD_DIM)

    tok_all = lax.all_gather(tokens, "head", axis=0, tiled=True)
    gains = jnp.stack([attn_gain, mlp_gain], axis=1)
    wq = w_qkv.reshape(D, 3, H, hw).transpose(2, 0, 1, 3).reshape(H, D, 3 * hw)
    wq = jnp.concatenate(
        [wq, jnp.broadcast_to(jnp.pad(gains, ((0, 0), (0, 126)))[None], (H, D, 128))], axis=2
    )
    wq = lax.all_to_all(wq, "head", 0, 0, tiled=True)
    wq = lax.all_gather(wq, "blk", axis=0, tiled=False).transpose(1, 0, 2, 3).reshape(W, 3 * hw + 128)
    gain_one, gain_two = wq[:, 3 * hw].astype(f32), wq[:, 3 * hw + 1].astype(f32)
    full_out = lax.all_gather(w_attn_out, ("head", "blk"), axis=0, tiled=True)
    wm = jnp.concatenate(
        [
            w_in.reshape(D, 2, H, F).transpose(2, 0, 1, 3).reshape(H, D, 2 * F),
            w_mlp_out.reshape(H, F, D).transpose(0, 2, 1),
        ],
        axis=2,
    )
    wm = lax.all_to_all(wm, "head", 0, 0, tiled=True)
    wm = lax.all_gather(wm, "blk", axis=0, tiled=False).transpose(1, 0, 2, 3).reshape(W, 3 * F)
    cot_all = lax.all_gather(cotangent, "head", axis=0, tiled=True)

    inputs = tok_all.astype(f32)
    normed_one = layer_norm(inputs, gain_one).astype(bf16)
    projected = mm(normed_one, wq[:, : 3 * hw])
    query = rotate(projected[:, :hw], cosine, sine).astype(bf16)
    keys = rotate(projected[:, hw : 2 * hw], cosine, sine).astype(bf16)
    values = projected[:, 2 * hw :].astype(bf16)
    split = lambda v: v.reshape(H, R, A, HEAD_DIM).transpose(2, 0, 1, 3)
    qp = lax.all_to_all(
        pack_pairs(split(query)), "blk", 0, 0, tiled=True, axis_index_groups=part_groups
    )
    kv = lax.all_to_all(
        jnp.concatenate([split(keys), split(values)], axis=-1),
        "blk", 0, 0, tiled=True, axis_index_groups=part_groups,
    )
    kv = lax.all_gather(kv, "blk", axis=0, tiled=False, axis_index_groups=share_groups)
    kv = kv.transpose(2, 1, 0, 3, 4).reshape(T, 2 * HEAD_DIM)
    op, lse = attend(span, qp, kv, qdoc, kdoc)
    back = lax.all_to_all(op, "blk", 0, 0, tiled=True, axis_index_groups=part_groups)
    mixed = unpack_pairs(back).transpose(1, 2, 0, 3).reshape(N, hw)
    mixed_all = lax.all_gather(mixed, "head", axis=1, tiled=True)

    middle = inputs + mm(mixed_all, full_out)
    normed_two, _ = jax.vjp(layer_norm, middle, gain_two)
    normed_two = normed_two.astype(bf16)
    lifted = mm(normed_two, wm[:, : 2 * F])
    activated, geglu_pull = jax.vjp(gelu_gate, lifted)
    activated = activated.astype(bf16)
    out_part = mm(activated, wm[:, 2 * F :], NT).astype(bf16)
    output = lax.psum_scatter(out_part, "head", scatter_dimension=0, tiled=True).astype(f32)
    grad_act = mm(cot_all, wm[:, 2 * F :])
    grad_lifted = geglu_pull(grad_act)[0].astype(bf16)
    grad_two = mm(grad_lifted, wm[:, : 2 * F], NT).astype(bf16)
    grad_two = lax.psum_scatter(grad_two, "head", scatter_dimension=0, tiled=True).astype(f32)
    term_mlp = jnp.concatenate(
        [mm(normed_two, grad_lifted, TN), mm(cot_all, activated, TN)], axis=1
    ).astype(bf16)
    term_mlp = term_mlp.reshape(H, B, D, 3 * F).transpose(1, 0, 2, 3)
    sum_mlp = lax.psum_scatter(term_mlp, "blk", scatter_dimension=0, tiled=False)
    middle_own = lax.dynamic_slice_in_dim(middle, h * R, R, 0)
    output = (middle_own + output).astype(bf16)
    _, norm_two_pull = jax.vjp(layer_norm, middle_own, gain_two)
    grad_middle, grad_gain_two = norm_two_pull(grad_two)
    grad_middle = grad_middle + cotangent.astype(f32)
    grad_branch = grad_middle.astype(bf16)
    grad_mixed = mm(grad_branch, full_out, NT).astype(bf16)
    branch_all = lax.all_gather(grad_branch, "head", axis=0, tiled=True)
    gp = lax.all_to_all(grad_mixed, "head", 1, 0, tiled=True)
    gp = lax.all_to_all(
        pack_pairs(split(gp)), "blk", 0, 0, tiled=True, axis_index_groups=part_groups
    )
    dqp, dkv = attend_back(span, qp, gp, op, lse, kv, qdoc, kdoc)
    dqp = lax.all_to_all(dqp, "blk", 0, 0, tiled=True, axis_index_groups=part_groups)
    dkv = dkv.reshape(H, A, G, R, 2 * HEAD_DIM).transpose(2, 1, 0, 3, 4)
    dkv = lax.psum_scatter(dkv, "blk", scatter_dimension=0, tiled=False, axis_index_groups=share_groups)
    dkv = lax.all_to_all(dkv, "blk", 0, 0, tiled=True, axis_index_groups=part_groups)
    merge = lambda v: v.transpose(1, 2, 0, 3).reshape(N, hw)
    _, rope_pull = jax.vjp(
        partial(rotate_pair, cosine=cosine, sine=sine), projected[:, :hw], projected[:, hw : 2 * hw]
    )
    grad_query, grad_keys = rope_pull(
        (merge(unpack_pairs(dqp)).astype(f32), merge(dkv[..., :HEAD_DIM]).astype(f32))
    )
    grad_projected = jnp.concatenate(
        [grad_query.astype(bf16), grad_keys.astype(bf16), merge(dkv[..., HEAD_DIM:])], axis=1
    )
    grad_one = mm(grad_projected, wq[:, : 3 * hw], NT).astype(bf16)
    grad_one = lax.psum_scatter(grad_one, "head", scatter_dimension=0, tiled=True).astype(f32)
    _, norm_one_pull = jax.vjp(layer_norm, tokens.astype(f32), gain_one)
    grad_input, grad_gain_one = norm_one_pull(grad_one)
    input_grad = grad_middle + grad_input
    term_qkv = mm(normed_one, grad_projected, TN)
    gain_terms = jnp.pad(jnp.stack([grad_gain_one, grad_gain_two], axis=1), ((0, 0), (0, 126)))
    term_qkv = jnp.concatenate([term_qkv, gain_terms], axis=1).astype(bf16)
    term_qkv = term_qkv.reshape(H, B, D, 3 * hw + 128).transpose(1, 0, 2, 3)
    term_out = mm(mixed, branch_all, TN).astype(bf16).reshape(B, D, W)
    sum_qkv = lax.psum_scatter(term_qkv, "blk", scatter_dimension=0, tiled=False)
    sum_out = lax.psum_scatter(term_out, "blk", scatter_dimension=0, tiled=False)
    sum_mlp = lax.all_to_all(sum_mlp, "head", 0, 0, tiled=True).astype(f32)
    sum_qkv = lax.all_to_all(sum_qkv, "head", 0, 0, tiled=True).astype(f32)
    in_grad = sum_mlp[:, :, : 2 * F].reshape(H, D, 2, F).transpose(1, 2, 0, 3).reshape(D, 2 * H * F)
    down_grad = sum_mlp[:, :, 2 * F :].transpose(0, 2, 1).reshape(H * F, D)
    qkv_grad = sum_qkv[:, :, : 3 * hw].reshape(H, D, 3, hw).transpose(1, 2, 0, 3).reshape(D, 3 * W)
    gain_sums = jnp.sum(sum_qkv[:, :, 3 * hw : 3 * hw + 2], axis=0)
    return (
        output,
        input_grad,
        gain_sums[:, 0],
        qkv_grad,
        sum_out.astype(f32),
        gain_sums[:, 1],
        in_grad,
        down_grad,
    )


def per_device(tokens, attn_gain, w_qkv, *rest):
    heads, blocks = lax.axis_size("head"), lax.axis_size("blk")
    parts = tokens.shape[1] // HEAD_DIM // heads
    fits = (
        blocks % parts == 0
        and blocks // parts == 2
        and parts % 2 == 0
        and heads % 2 == 0
        and w_qkv.shape[0] % 16 == 0
        and tokens.shape[0] % 128 == 0
    )
    chosen = per_device_split if fits else per_device_general
    return chosen(tokens, attn_gain, w_qkv, *rest)


def solution(mesh):
    placed = (
        P(("head", "blk"), None),
        P(("head", "blk")),
        P(("head", "blk"), None),
        P(("head", "blk"), None),
        P(("head", "blk")),
        P(("head", "blk"), None),
        P(None, ("head", "blk")),
        P(),
        P(("head", "blk"), None),
    )
    return jax.shard_map(
        per_device,
        mesh=mesh,
        in_specs=placed,
        out_specs=(
            P(("head", "blk"), None),
            P(("head", "blk"), None),
            P(("head", "blk")),
            P(("head", "blk"), None),
            P(("head", "blk"), None),
            P(("head", "blk")),
            P(("head", "blk"), None),
            P(None, ("head", "blk")),
        ),
        check_vma=False,
    )
```

```python
from functools import partial

import jax
import jax.numpy as jnp
import numpy as np
from jax import lax
from jax.experimental import pallas as pl
from jax.experimental.pallas import tpu as pltpu
from jax.sharding import PartitionSpec as P

HEAD_DIM = 64


norm_eps = 1e-05
rope_base = 160000.0
neg_large = -1e30


def from_behind(value, axis, by):
    devices = lax.axis_size(axis)
    return lax.ppermute(value, axis, [(i, (i + by) % devices) for i in range(devices)])


def layer_norm(values, gain):
    center = values - jnp.mean(values, axis=-1, keepdims=True)
    spread = jnp.mean(center * center, axis=-1, keepdims=True)
    return center * lax.rsqrt(spread + norm_eps) * gain


def rope_tables(places, head_size):
    half = head_size // 2
    freqs = rope_base ** (-(jnp.arange(half, dtype=jnp.float32) * 2.0) / head_size)
    angles = places.astype(jnp.float32)[:, None] * freqs[None, :]
    angles = jnp.concatenate([angles, angles], axis=1)
    return (jnp.cos(angles), jnp.sin(angles))


def rotate(values, cosine, sine):
    count = values.shape[0]
    head_size = cosine.shape[1]
    half = head_size // 2
    split = values.reshape(count, -1, head_size)
    turned = jnp.concatenate([-split[..., half:], split[..., :half]], axis=-1)
    return (split * cosine[:, None, :] + turned * sine[:, None, :]).reshape(count, -1)


def rotate_pair(query, keys, cosine, sine):
    return (rotate(query, cosine, sine), rotate(keys, cosine, sine))


def doc_numbers(places, ends, lengths):
    passed = places[:, None] >= ends[None, :]
    numbers = jnp.sum(passed.astype(jnp.int32), axis=1)
    offset = jnp.sum(jnp.where(passed, lengths[None, :], 0), axis=1)
    return (numbers, places - offset)


def gelu_gate(lifted):
    half = lifted.shape[1] // 2
    return jax.nn.gelu(lifted[:, :half], approximate=False) * lifted[:, half:]


def tile_scores(query, keys):
    heads = query.shape[1] // HEAD_DIM
    query_split = query.reshape(query.shape[0], heads, HEAD_DIM)
    key_split = keys.reshape(keys.shape[0], heads, HEAD_DIM)
    return jnp.einsum(
        "qhd,khd->hqk", query_split, key_split, preferred_element_type=jnp.float32
    ) * HEAD_DIM ** (-0.5)


def unchanged(state):
    return state


def forward_tile(state, query, keys, values, mask):
    top, total, running = state
    count = query.shape[0]
    heads = top.shape[0]
    scores = tile_scores(query, keys)
    filled = jnp.where(mask[None], scores, neg_large)
    new_top = jnp.maximum(top, jnp.max(filled, axis=-1))
    weights = jnp.where(mask[None], jnp.exp(scores - new_top[:, :, None]), 0.0)
    factor = jnp.exp(top - new_top)
    new_total = total * factor + jnp.sum(weights, axis=-1)
    mixed = jnp.einsum(
        "hqk,khd->qhd",
        weights.astype(jnp.bfloat16),
        values.reshape(-1, heads, HEAD_DIM),
        preferred_element_type=jnp.float32,
    )
    new_running = running.reshape(count, heads, HEAD_DIM) * factor.T[:, :, None] + mixed
    return (new_top, new_total, new_running.reshape(count, heads * HEAD_DIM))


def backward_tile(carry, query, keys, values, mask, norm_log, grad_out, delta):
    query_grad, run_grads = carry
    count = query.shape[0]
    columns = keys.shape[0]
    heads = norm_log.shape[0]
    scores = tile_scores(query, keys)
    probs = jnp.where(mask[None], jnp.exp(scores - norm_log[:, :, None]), 0.0)
    grad_split = grad_out.reshape(count, heads, HEAD_DIM)
    value_split = values.reshape(columns, heads, HEAD_DIM)
    grad_values = jnp.einsum(
        "hqk,qhd->khd", probs.astype(jnp.bfloat16), grad_split, preferred_element_type=jnp.float32
    )
    grad_probs = jnp.einsum(
        "qhd,khd->hqk", grad_split, value_split, preferred_element_type=jnp.float32
    )
    grad_scores = (probs * (grad_probs - delta[:, :, None])).astype(jnp.bfloat16)
    grad_query = jnp.einsum(
        "hqk,khd->qhd",
        grad_scores,
        keys.reshape(columns, heads, HEAD_DIM),
        preferred_element_type=jnp.float32,
    ) * HEAD_DIM ** (-0.5)
    grad_keys = jnp.einsum(
        "hqk,qhd->khd",
        grad_scores,
        query.reshape(count, heads, HEAD_DIM),
        preferred_element_type=jnp.float32,
    ) * HEAD_DIM ** (-0.5)
    added = jnp.stack([grad_keys.reshape(columns, -1), grad_values.reshape(columns, -1)])
    return (query_grad + grad_query.reshape(count, -1), run_grads + added)


def per_device_general(
    tokens, attn_gain, w_qkv, w_attn_out, mlp_gain, w_in, w_mlp_out, doc_lengths, cotangent
):
    own_rows = tokens.shape[0]
    width = tokens.shape[1]
    head_count = lax.axis_size("head")
    cycle_count = lax.axis_size("blk")
    head_place = lax.axis_index("head")
    cycle_place = lax.axis_index("blk")
    group_rows = head_count * own_rows
    block_runs = min(head_count, max(1, 512 // own_rows))
    block_count = head_count // block_runs
    block_rows = block_runs * own_rows
    doc_ends = jnp.cumsum(doc_lengths)
    counter = jnp.arange(own_rows, dtype=jnp.int32)
    own_places = (head_place * cycle_count + cycle_place) * own_rows + counter
    unused_docs, own_positions = doc_numbers(own_places, doc_ends, doc_lengths)
    cosine, sine = rope_tables(own_positions, HEAD_DIM)
    run_numbers = jnp.arange(head_count, dtype=jnp.int32)
    query_places = (
        (run_numbers[:, None] * cycle_count + cycle_place) * own_rows + counter[None, :]
    ).reshape(group_rows)
    query_docs, unused_positions = doc_numbers(query_places, doc_ends, doc_lengths)
    params = (
        lax.all_gather(attn_gain, ("head", "blk"), axis=0, tiled=True),
        lax.all_gather(w_qkv, ("head", "blk"), axis=0, tiled=True),
        lax.all_gather(w_attn_out, ("head", "blk"), axis=0, tiled=True),
        lax.all_gather(mlp_gain, ("head", "blk"), axis=0, tiled=True),
        lax.all_gather(w_in, ("head", "blk"), axis=0, tiled=True),
        lax.all_gather(w_mlp_out, ("head", "blk"), axis=1, tiled=True),
    )
    gain_one, full_qkv, full_attn_out, gain_two, full_in, full_mlp_out = params
    inputs = tokens.astype(jnp.float32)
    normed_one, norm_one_pull = jax.vjp(layer_norm, inputs, gain_one.astype(jnp.float32))
    normed_low = normed_one.astype(jnp.bfloat16)
    projected = jnp.dot(normed_low, full_qkv, preferred_element_type=jnp.float32)
    turned, rope_pull = jax.vjp(
        partial(rotate_pair, cosine=cosine, sine=sine),
        projected[:, :width],
        projected[:, width : 2 * width],
    )
    stacked = jnp.stack(
        [
            turned[0].astype(jnp.bfloat16),
            turned[1].astype(jnp.bfloat16),
            projected[:, 2 * width :].astype(jnp.bfloat16),
        ]
    )
    regrouped = lax.all_to_all(stacked, "head", split_axis=2, concat_axis=1, tiled=True)
    query_heads = regrouped[0]
    key_heads = regrouped[1]
    value_heads = regrouped[2]
    head_width = query_heads.shape[1]
    heads_here = head_width // HEAD_DIM

    def key_docs_at(first):
        places = (
            first % group_rows // own_rows * cycle_count + first // group_rows
        ) * own_rows + counter
        found, unused = doc_numbers(places, doc_ends, doc_lengths)
        return found

    def block_live(block, key_docs):
        block_docs = query_docs[block * block_rows : (block + 1) * block_rows]
        live = jnp.maximum(jnp.min(block_docs), jnp.min(key_docs)) <= jnp.minimum(
            jnp.max(block_docs), jnp.max(key_docs)
        )
        return (block_docs[:, None] == key_docs[None, :], live)

    def fold_forward(state, piece):
        key_part, value_part = piece

        def fold_one_run(number, carried):
            first = number * own_rows
            key_docs = key_docs_at(first)
            keys = lax.dynamic_slice_in_dim(key_part, number * own_rows, own_rows, 0)
            values = lax.dynamic_slice_in_dim(value_part, number * own_rows, own_rows, 0)
            updated = []
            for block in range(block_count):
                mask, live = block_live(block, key_docs)
                query = query_heads[block * block_rows : (block + 1) * block_rows]
                advance = partial(forward_tile, query=query, keys=keys, values=values, mask=mask)
                updated.append(lax.cond(live, advance, unchanged, carried[block]))
            return tuple(updated)

        return lax.fori_loop(0, key_part.shape[0] // own_rows, fold_one_run, state)

    def fresh_state():
        return tuple(
            (
                (
                    jnp.full((heads_here, block_rows), neg_large, jnp.float32),
                    jnp.zeros((heads_here, block_rows), jnp.float32),
                    jnp.zeros((block_rows, head_width), jnp.float32),
                )
                for block in range(block_count)
            )
        )

    def finish(state):
        outputs = []
        logs = []
        for top, total, running in state:
            scaled = running.reshape(block_rows, heads_here, HEAD_DIM) / total.T[:, :, None]
            outputs.append(scaled.reshape(block_rows, head_width))
            logs.append(top + jnp.log(total))
        return (
            jnp.concatenate(outputs, axis=0).astype(jnp.bfloat16),
            jnp.concatenate(logs, axis=1),
        )

    state = fold_forward(
        fresh_state(),
        (
            lax.all_gather(key_heads, "blk", axis=0, tiled=True),
            lax.all_gather(value_heads, "blk", axis=0, tiled=True),
        ),
    )
    out_heads, norm_log = finish(state)
    out_tokens = lax.all_to_all(out_heads, "head", split_axis=0, concat_axis=1, tiled=True)
    middle = inputs + jnp.dot(out_tokens, full_attn_out, preferred_element_type=jnp.float32)
    normed_two, norm_two_pull = jax.vjp(layer_norm, middle, gain_two.astype(jnp.float32))
    normed_two_low = normed_two.astype(jnp.bfloat16)
    lifted = jnp.dot(normed_two_low, full_in, preferred_element_type=jnp.float32)
    activated, geglu_pull = jax.vjp(gelu_gate, lifted)
    activated_low = activated.astype(jnp.bfloat16)
    output = (
        middle + jnp.dot(activated_low, full_mlp_out, preferred_element_type=jnp.float32)
    ).astype(jnp.bfloat16)
    params = (
        lax.all_gather(attn_gain, ("head", "blk"), axis=0, tiled=True),
        lax.all_gather(w_qkv, ("head", "blk"), axis=0, tiled=True),
        lax.all_gather(w_attn_out, ("head", "blk"), axis=0, tiled=True),
        lax.all_gather(mlp_gain, ("head", "blk"), axis=0, tiled=True),
        lax.all_gather(w_in, ("head", "blk"), axis=0, tiled=True),
        lax.all_gather(w_mlp_out, ("head", "blk"), axis=1, tiled=True),
    )
    gain_one, full_qkv, full_attn_out, gain_two, full_in, full_mlp_out = params
    grad_act = jnp.einsum("td,fd->tf", cotangent, full_mlp_out, preferred_element_type=jnp.float32)
    grad_lifted = geglu_pull(grad_act)[0].astype(jnp.bfloat16)
    grad_normed_two = jnp.einsum(
        "tf,df->td", grad_lifted, full_in, preferred_element_type=jnp.float32
    )
    grad_middle_part, grad_gain_two = norm_two_pull(grad_normed_two)
    grad_middle = cotangent.astype(jnp.float32) + grad_middle_part
    grad_branch = grad_middle.astype(jnp.bfloat16)
    grad_mixed = jnp.einsum(
        "te,de->td", grad_branch, full_attn_out, preferred_element_type=jnp.float32
    ).astype(jnp.bfloat16)
    grad_heads = lax.all_to_all(grad_mixed, "head", split_axis=1, concat_axis=0, tiled=True)
    state = fold_forward(
        fresh_state(),
        (
            lax.all_gather(key_heads, "blk", axis=0, tiled=True),
            lax.all_gather(value_heads, "blk", axis=0, tiled=True),
        ),
    )
    out_heads, norm_log = finish(state)
    delta = jnp.einsum(
        "qhd,qhd->hq",
        grad_heads.reshape(group_rows, heads_here, HEAD_DIM).astype(jnp.float32),
        out_heads.reshape(group_rows, heads_here, HEAD_DIM).astype(jnp.float32),
    )

    def piece_backward(query_grads, key_part, value_part, start):
        piece_rows = key_part.shape[0]

        def piece_one_run(number, carried):
            query_now, piece_grads = carried
            first = start + number * own_rows
            key_docs = key_docs_at(first)
            keys = lax.dynamic_slice_in_dim(key_part, number * own_rows, own_rows, 0)
            values = lax.dynamic_slice_in_dim(value_part, number * own_rows, own_rows, 0)
            run_grads = jnp.zeros((2, own_rows, head_width), jnp.float32)
            updated = []
            for block in range(block_count):
                mask, live = block_live(block, key_docs)
                lower = block * block_rows
                upper = (block + 1) * block_rows
                advance = partial(
                    backward_tile,
                    query=query_heads[lower:upper],
                    keys=keys,
                    values=values,
                    mask=mask,
                    norm_log=norm_log[:, lower:upper],
                    grad_out=grad_heads[lower:upper],
                    delta=delta[:, lower:upper],
                )
                new_query, run_grads = lax.cond(
                    live, advance, unchanged, (query_now[block], run_grads)
                )
                updated.append(new_query)
            piece_grads = lax.dynamic_update_slice_in_dim(
                piece_grads, run_grads, number * own_rows, 1
            )
            return (tuple(updated), piece_grads)

        return lax.fori_loop(
            0,
            piece_rows // own_rows,
            piece_one_run,
            (query_grads, jnp.zeros((2, piece_rows, head_width), jnp.float32)),
        )

    start_query = tuple(
        (jnp.zeros((block_rows, head_width), jnp.float32) for block in range(block_count))
    )

    def cycle_step(step, carried):
        query_now, blocks, travelling = carried
        owner = (cycle_place - step) % cycle_count
        query_now, piece_grads = piece_backward(query_now, blocks[0], blocks[1], owner * group_rows)
        travelling = travelling + piece_grads
        blocks = from_behind(blocks, "blk", 1)
        travelling = from_behind(travelling.astype(jnp.bfloat16), "blk", 1).astype(travelling.dtype)
        return (query_now, blocks, travelling)

    start_cycle = (
        start_query,
        jnp.stack([key_heads, value_heads]),
        jnp.zeros((2, group_rows, head_width), jnp.float32),
    )
    query_grads, unused_blocks, own_grads = lax.fori_loop(0, cycle_count, cycle_step, start_cycle)
    grad_stack = jnp.stack(
        [
            jnp.concatenate(query_grads, axis=0).astype(jnp.bfloat16),
            own_grads[0].astype(jnp.bfloat16),
            own_grads[1].astype(jnp.bfloat16),
        ]
    )
    back_tokens = lax.all_to_all(grad_stack, "head", split_axis=1, concat_axis=2, tiled=True)
    grad_query, grad_keys = rope_pull(
        (back_tokens[0].astype(jnp.float32), back_tokens[1].astype(jnp.float32))
    )
    grad_projected = jnp.concatenate(
        [grad_query, grad_keys, back_tokens[2].astype(jnp.float32)], axis=1
    ).astype(jnp.bfloat16)
    grad_normed_one = jnp.einsum(
        "te,de->td", grad_projected, full_qkv, preferred_element_type=jnp.float32
    )
    grad_input_part, grad_gain_one = norm_one_pull(grad_normed_one)
    input_grad = grad_middle + grad_input_part

    def columns(source):
        return source

    term_qkv = jnp.einsum(
        "td,te->de", columns(normed_low), grad_projected, preferred_element_type=jnp.float32
    )
    term_out = jnp.einsum(
        "td,te->de", columns(out_tokens), grad_branch, preferred_element_type=jnp.float32
    )
    term_in = jnp.einsum(
        "td,tf->df", columns(normed_two_low), grad_lifted, preferred_element_type=jnp.float32
    )
    term_down = jnp.einsum(
        "td,tf->df", columns(cotangent), activated_low, preferred_element_type=jnp.float32
    )
    sums = lax.psum_scatter(
        jnp.concatenate([term_qkv, term_out, term_in, term_down], axis=1),
        ("head", "blk"),
        scatter_dimension=0,
        tiled=True,
    )
    ff_width = full_mlp_out.shape[0]
    qkv_grad = sums[:, : 3 * width]
    attn_out_grad = sums[:, 3 * width : 4 * width]
    in_grad = sums[:, 4 * width : 4 * width + 2 * ff_width]
    down_grad = sums[:, 4 * width + 2 * ff_width :].T
    gain_sums = lax.psum_scatter(
        jnp.stack([grad_gain_one, grad_gain_two]), ("head", "blk"), scatter_dimension=1, tiled=True
    )
    return (
        output,
        input_grad,
        gain_sums[0],
        qkv_grad,
        attn_out_grad,
        gain_sums[1],
        in_grad,
        down_grad,
    )


KEY_TILE = 256
NN = (((1,), (0,)), ((), ()))
NT = (((1,), (1,)), ((), ()))
TN = (((0,), (0,)), ((), ()))


def mm(left, right, dims=NN):
    return lax.dot_general(left, right, dims, preferred_element_type=jnp.float32)


def halves(packed, side):
    wide = packed.astype(jnp.float32)
    if side:
        wide = pltpu.roll(wide, HEAD_DIM, 1)
    lane = lax.broadcasted_iota(jnp.int32, wide.shape, 1)
    return jnp.where(lane < HEAD_DIM, wide, 0.0)


def attend_kernel(span, qp, kv, qdoc, kdoc, op, lse, s_scr):
    pairs, tall = qp.shape[0] * qp.shape[2], qp.shape[2]
    half_runs = pl.num_programs(0)
    hh, u = pl.program_id(0), pl.program_id(1)
    lane = lax.broadcasted_iota(jnp.int32, (pairs, 2 * HEAD_DIM), 1)
    results = []
    for side in (0, 1):
        tile = (hh + side * half_runs) * pl.num_programs(1) + u
        query = (halves(qp[...].reshape(pairs, 2 * HEAD_DIM), side) * HEAD_DIM**-0.5).astype(
            jnp.bfloat16
        )
        docs = qdoc[tile]
        first, last = span[tile, 0], span[tile, 1]

        def score(kb, top):
            keys = kv[pl.ds(pl.multiple_of(kb * KEY_TILE, KEY_TILE), KEY_TILE), :]
            scores = jnp.where(docs == kdoc[pl.ds(kb, 1), :], mm(query, keys, NT), neg_large)
            s_scr[kb] = scores
            return jnp.maximum(top, jnp.maximum(scores[:, :128], scores[:, 128:]))

        top = lax.fori_loop(first, last, score, jnp.full((pairs, 128), neg_large, jnp.float32))
        top = jnp.max(top, axis=1, keepdims=True)

        def mix(kb, carried):
            total, acc = carried
            keys = kv[pl.ds(pl.multiple_of(kb * KEY_TILE, KEY_TILE), KEY_TILE), :]
            weights = jnp.exp(s_scr[kb] - top)
            total = total + weights[:, :128] + weights[:, 128:]
            return (total, acc + mm(weights.astype(jnp.bfloat16), keys))

        zeros = jnp.zeros((pairs, 128), jnp.float32)
        total, acc = lax.fori_loop(first, last, mix, (zeros, zeros))
        total = jnp.sum(total, axis=1, keepdims=True)
        lse[tile] = top + jnp.log(total)
        results.append(acc / total)
    both = jnp.where(lane < HEAD_DIM, pltpu.roll(results[0], HEAD_DIM, 1), results[1])
    op[...] = both.astype(jnp.bfloat16).reshape(op.shape)


def attend(span, qp, kv, qdoc, kdoc):
    parts, half_runs, rows, lanes = qp.shape
    tiles = qdoc.shape[0]
    piece = pl.BlockSpec((2, 1, rows, lanes), lambda i, j, s: (j, i, 0, 0))
    whole = pl.BlockSpec(memory_space=pltpu.VMEM)
    return pl.pallas_call(
        attend_kernel,
        grid_spec=pltpu.PrefetchScalarGridSpec(
            num_scalar_prefetch=1,
            grid=(half_runs, parts // 2),
            in_specs=[piece, whole, whole, whole],
            out_specs=[piece, whole],
            scratch_shapes=[
                pltpu.VMEM((kv.shape[0] // KEY_TILE, 2 * rows, KEY_TILE), jnp.float32)
            ],
        ),
        out_shape=[
            jax.ShapeDtypeStruct(qp.shape, jnp.bfloat16),
            jax.ShapeDtypeStruct((tiles, 2 * rows, 1), jnp.float32),
        ],
        compiler_params=pltpu.CompilerParams(vmem_limit_bytes=48 * 2**20),
        cost_estimate=pl.CostEstimate(flops=10**9, bytes_accessed=4 * 10**6, transcendentals=10**6),
        name="attend",
    )(span, qp, kv, qdoc, kdoc)


def attend_back_kernel(span, qp, gp, op, lse, kv, qdoc, kdoc, dqp, dkv, acc_scr):
    pairs, tall = qp.shape[0] * qp.shape[2], qp.shape[2]
    half_runs = pl.num_programs(0)
    hh, u = pl.program_id(0), pl.program_id(1)
    lane = lax.broadcasted_iota(jnp.int32, (pairs, 2 * HEAD_DIM), 1)

    @pl.when((hh == 0) & (u == 0))
    def _():
        acc_scr[...] = jnp.zeros_like(acc_scr)

    results = []
    flat = (pairs, 2 * HEAD_DIM)
    for side in (0, 1):
        tile = (hh + side * half_runs) * pl.num_programs(1) + u
        query = (halves(qp[...].reshape(flat), side) * HEAD_DIM**-0.5).astype(jnp.bfloat16)
        pieces = []
        for n in range(2):
            piece = gp[n, hh + side * half_runs].astype(jnp.float32)
            pieces += [pltpu.roll(piece, HEAD_DIM, 1), piece]
        grad = jnp.where(lane < HEAD_DIM, 0.0, jnp.concatenate(pieces, axis=0))
        mixed = op[...].reshape(flat).astype(jnp.float32)
        if not side:
            mixed = pltpu.roll(mixed, HEAD_DIM, 1)
        delta = jnp.sum(grad * mixed, axis=1, keepdims=True)
        grad = grad.astype(jnp.bfloat16)
        docs = qdoc[tile]
        logs = lse[tile]

        def step(kb, dq):
            keys = kv[pl.ds(pl.multiple_of(kb * KEY_TILE, KEY_TILE), KEY_TILE), :]
            scores = mm(query, keys, NT)
            probs = jnp.where(docs == kdoc[pl.ds(kb, 1), :], jnp.exp(scores - logs), 0.0)
            grad_scores = (probs * (mm(grad, keys, NT) - delta)).astype(jnp.bfloat16)
            acc_scr[kb] += mm(grad_scores, query, TN) + mm(probs.astype(jnp.bfloat16), grad, TN)
            return dq + mm(grad_scores, keys)

        dq = lax.fori_loop(span[tile, 0], span[tile, 1], step, jnp.zeros(flat, jnp.float32))
        results.append(dq * HEAD_DIM**-0.5)
    both = jnp.where(lane < HEAD_DIM, results[0], pltpu.roll(results[1], HEAD_DIM, 1))
    dqp[...] = both.astype(jnp.bfloat16).reshape(dqp.shape)

    @pl.when((hh == half_runs - 1) & (u == pl.num_programs(1) - 1))
    def _():
        dkv[...] = acc_scr[...].reshape(dkv.shape).astype(dkv.dtype)


def attend_back(span, qp, gp, op, lse, kv, qdoc, kdoc):
    parts, half_runs, rows, lanes = qp.shape
    piece = pl.BlockSpec((2, 1, rows, lanes), lambda i, j, s: (j, i, 0, 0))
    grads = pl.BlockSpec((2, 2 * half_runs, rows // 2, lanes), lambda i, j, s: (j, 0, 0, 0))
    whole = pl.BlockSpec(memory_space=pltpu.VMEM)
    return pl.pallas_call(
        attend_back_kernel,
        grid_spec=pltpu.PrefetchScalarGridSpec(
            num_scalar_prefetch=1,
            grid=(half_runs, parts // 2),
            in_specs=[piece, grads, piece, whole, whole, whole, whole],
            out_specs=[piece, whole],
            scratch_shapes=[pltpu.VMEM((kv.shape[0] // KEY_TILE, KEY_TILE, lanes), jnp.float32)],
        ),
        out_shape=[
            jax.ShapeDtypeStruct(qp.shape, jnp.bfloat16),
            jax.ShapeDtypeStruct(kv.shape, jnp.bfloat16),
        ],
        compiler_params=pltpu.CompilerParams(vmem_limit_bytes=48 * 2**20),
        cost_estimate=pl.CostEstimate(flops=3 * 10**9, bytes_accessed=6 * 10**6, transcendentals=10**6),
        name="attend_back",
    )(span, qp, gp, op, lse, kv, qdoc, kdoc)


def pack_pairs(value):
    half = value.shape[1] // 2
    return jnp.concatenate([value[:, :half], value[:, half:]], axis=-1)


def unpack_pairs(value):
    return jnp.concatenate([value[..., :HEAD_DIM], value[..., HEAD_DIM:]], axis=1)


MESH = pl.DeviceIdType.MESH


def meet(peers):
    barrier = pltpu.get_barrier_semaphore()
    for peer in peers:
        pl.semaphore_signal(barrier, inc=1, device_id=peer, device_id_type=MESH)
    pl.semaphore_wait(barrier, len(peers))


def send(source, target, send_sem, recv_sem, peer):
    copy = pltpu.make_async_remote_copy(
        src_ref=source,
        dst_ref=target,
        send_sem=send_sem,
        recv_sem=recv_sem,
        device_id=peer,
        device_id_type=MESH,
    )
    copy.start()
    return copy


def grid_peers(heads, parts):
    h, b = lax.axis_index("head"), lax.axis_index("blk")
    part, share = b // 2, b % 2
    across = [(lax.rem(h + i, heads), b) for i in range(1, heads)]
    along = [(h, lax.rem(part + i, parts) * 2 + share) for i in range(1, parts)]
    return (h, b, part, share, across, along, (h, part * 2 + 1 - share))


def standardize(values):
    center = values - jnp.mean(values, axis=-1, keepdims=True)
    spread = jnp.mean(center * center, axis=-1, keepdims=True)
    scale = lax.rsqrt(spread + norm_eps)
    return (center * scale, scale)


def turn(values, cosine, sine, back=False):
    lane = lax.broadcasted_iota(jnp.int32, values.shape, 1)
    first = lax.rem(lane, HEAD_DIM) < HEAD_DIM // 2
    source = values * sine if back else values
    ahead = pltpu.roll(source, 128 - HEAD_DIM // 2, 1)
    behind = pltpu.roll(source, HEAD_DIM // 2, 1)
    if back:
        return values * cosine + jnp.where(first, ahead, -behind)
    return values * cosine + jnp.where(first, -ahead, behind) * sine


def join(left, left_side, right, right_side):
    lane = lax.broadcasted_iota(jnp.int32, left.shape, 1)
    left = pltpu.roll(left, HEAD_DIM, 1) if left_side else left
    right = right if right_side else pltpu.roll(right, HEAD_DIM, 1)
    return jnp.where(lane < HEAD_DIM, left, right)


def project_kernel(
    H, A, tok, cot, wq, gains, w_in, w_down, w_out, docs,
    kv_all, q_all, tok_all, cot_all, wq_all, wm_all, wo_all, gain_rows, cos_all, sin_all,
    wq_src, wq_st, wm_src, kv_send, q_send, q_runs, normed,
    tok_s, tok_r, cot_s, cot_r, wq_s, wq_r, wm_s, wm_r, wx_s, wx_r,
    q_s, q_r, kv_s, kv_r, kc_s, kc_r, *line,
):
    f32, bf16 = jnp.float32, jnp.bfloat16
    R, W = tok.shape
    B = 2 * A
    hw = W // H
    D = wq.shape[0]
    F = w_in.shape[1] // 2 // H
    h, b, part, share, across, along, beside = grid_peers(H, A)
    meet([*across, *along, beside])

    tok_copies = []
    for place in range(H):
        for j in range(3):
            wq_src[place, :, j * hw : (j + 1) * hw] = wq[:, j * W + place * hw : j * W + (place + 1) * hw]
        wq_src[place, :, 3 * hw :] = gains[...]
    wq_copies = [
        send(wq_src.at[peer[0]], wq_st.at[h], wq_s.at[i], wq_r.at[i], peer)
        for i, peer in enumerate(across)
    ]
    tok_copies = [
        send(tok, tok_all.at[h], tok_s.at[i], tok_r.at[i], peer) for i, peer in enumerate(across)
    ]
    wq_st[h] = wq_src[h]
    tok_all[h] = tok[...]
    cot_all[h] = cot[...]
    unit = (
        lax.broadcasted_iota(jnp.int32, (D, D), 0) == lax.broadcasted_iota(jnp.int32, (D, D), 1)
    ).astype(bf16)
    down = mm(unit, w_down[...], NT).astype(bf16)
    for place in range(H):
        wm_src[place, :, :F] = w_in[:, place * F : (place + 1) * F]
        wm_src[place, :, F : 2 * F] = w_in[:, (H + place) * F : (H + place + 1) * F]
        wm_src[place, :, 2 * F :] = down[:, place * F : (place + 1) * F]
    wm_all[h] = wm_src[h]
    wm_copies = [
        send(wm_src.at[peer[0]], wm_all.at[h], wm_s.at[i], wm_r.at[i], peer)
        for i, peer in enumerate(across)
    ]
    cot_copies = [
        send(cot, cot_all.at[h], cot_s.at[i], cot_r.at[i], peer) for i, peer in enumerate(across)
    ]

    for copy in wq_copies:
        copy.wait_recv()
    wq_line = LineGather(
        lambda block, side: wq_all.at[:, block * 2 + side], wq_st, h, part, share, A, line[:5]
    )
    wq_line.start()
    wq_all[:, b] = wq_st[...]
    wo_line = LineGather(
        lambda block, side: wo_all.at[h, block, side], w_out, h, part, share, A, line[5:]
    )
    wo_all[h, part, share] = w_out[...]
    wo_line.start()

    lane = lax.broadcasted_iota(jnp.int32, (R, 128), 1)
    freqs = jnp.exp(
        lax.rem(lane, HEAD_DIM // 2).astype(f32) * (-2.0 / HEAD_DIM * float(np.log(rope_base)))
    )
    for run in range(H):
        place = (run * B + b) * R + lax.broadcasted_iota(jnp.int32, (R, 128), 0)
        begin = jnp.zeros((R, 1), jnp.int32)
        passed = place[:, : docs.shape[1]] >= docs[0:1, :]
        begin = jnp.sum(jnp.where(passed, docs[1:2, :], 0), axis=1, keepdims=True)
        angles = (place - begin).astype(f32) * freqs
        cos_all[run] = jnp.cos(angles)
        sin_all[run] = jnp.sin(angles)

    for copy in tok_copies:
        copy.wait_recv()
    for k in range(1, A):
        wq_line.step(k)
        wo_line.step(k)
    wq_line.arrive()
    wo_line.arrive()
    spread_out = wo_all.at[h, :, share]
    wx_copies = [
        send(spread_out, spread_out, wx_s.at[i], wx_r.at[i], peer) for i, peer in enumerate(across)
    ]

    pick = (
        lax.broadcasted_iota(jnp.int32, (8, 128), 0) == lax.broadcasted_iota(jnp.int32, (8, 128), 1)
    ).astype(bf16)
    for chunk in range(H):
        block = wq_all[chunk].reshape(B * D, 3 * hw + 128)
        gain_rows[:, chunk * hw : (chunk + 1) * hw] = mm(pick, block[:, 3 * hw :], NT)

    kv_copies = []
    for run in range(H):
        hat, unused = standardize(tok_all[run].astype(f32))
        low = (hat * gain_rows[0:1, :]).astype(bf16)
        projected = jnp.zeros((R, 3 * hw), f32)
        for chunk in range(H):
            block = wq_all[chunk].reshape(B * D, 3 * hw + 128)
            projected += mm(low[:, chunk * hw : (chunk + 1) * hw], block[:, : 3 * hw])
        cosine, sine = cos_all[run], sin_all[run]
        for slab in range(hw // 128):
            at = slab * 128
            q_runs[run, :, at : at + 128] = turn(projected[:, at : at + 128], cosine, sine)
            key = turn(projected[:, hw + at : hw + at + 128], cosine, sine)
            value = projected[:, 2 * hw + at : 2 * hw + at + 128]
            kv_send[2 * slab, run] = join(key, 0, value, 0).astype(bf16)
            kv_send[2 * slab + 1, run] = join(key, 1, value, 1).astype(bf16)
    for i, peer in enumerate(along):
        there = peer[1] // 2
        kv_copies.append(
            send(kv_send.at[there], kv_all.at[:, b], kv_s.at[i], kv_r.at[i], peer)
        )
    kv_all[:, b] = kv_send[part]
    kc_copies = [send(kv_send.at[part], kv_all.at[:, b], kc_s.at[0], kc_r.at[0], beside)]
    for run in range(H // 2):
        for a in range(A):
            at = a // 2 * 128
            q_send[a, run] = join(
                q_runs[run, :, at : at + 128], a % 2, q_runs[run + H // 2, :, at : at + 128], a % 2
            ).astype(bf16)
    q_copies = [
        send(q_send.at[peer[1] // 2], q_all.at[part], q_s.at[i], q_r.at[i], peer)
        for i, peer in enumerate(along)
    ]
    q_all[part] = q_send[part]
    for i, copy in enumerate(kv_copies):
        copy.wait_recv()
        there = kv_all.at[:, lax.rem(part + A - 1 - i, A) * 2 + share]
        kc_copies.append(send(there, there, kc_s.at[i + 1], kc_r.at[i + 1], beside))
    for i, copy in enumerate(wx_copies):
        copy.wait_recv()
        there = wo_all.at[lax.rem(h + H - 1 - i, H), :, share]
        n = H - 1 + i
        kc_copies.append(send(there, there, wx_s.at[n], wx_r.at[n], beside))
    for copy in [*kc_copies, *q_copies, *wm_copies, *cot_copies]:
        copy.wait_recv()
    for copy in [
        *kc_copies, *q_copies, *wm_copies, *cot_copies, *wq_copies, *tok_copies, *wx_copies, *kv_copies
    ]:
        copy.wait_send()
    wq_line.finish()
    wo_line.finish()


def project(tokens, cotangent, w_qkv, gains, w_in, w_down, w_out, docs):
    R, W = tokens.shape
    H, B = lax.axis_size("head"), lax.axis_size("blk")
    A = B // 2
    hw = W // H
    D = w_qkv.shape[0]
    F = w_down.shape[0] // H
    f32, bf16 = jnp.float32, jnp.bfloat16
    shape = jax.ShapeDtypeStruct
    dma = lambda count: pltpu.SemaphoreType.DMA((count,))
    vmem = pl.BlockSpec(memory_space=pltpu.VMEM)
    return pl.pallas_call(
        partial(project_kernel, H, A),
        in_specs=[vmem] * 8,
        out_specs=[vmem] * 10,
        out_shape=[
            shape((H, B, R, 128), bf16),
            shape((A, H // 2, R, 128), bf16),
            shape((H, R, W), bf16),
            shape((H, R, W), bf16),
            shape((H, B, D, 3 * hw + 128), bf16),
            shape((H, D, 3 * F), bf16),
            shape((H, A, 2, D, W), bf16),
            shape((8, W), f32),
            shape((H, R, 128), f32),
            shape((H, R, 128), f32),
        ],
        scratch_shapes=[
            pltpu.VMEM((H, D, 3 * hw + 128), bf16),
            pltpu.VMEM((H, D, 3 * hw + 128), bf16),
            pltpu.VMEM((H, D, 3 * F), bf16),
            pltpu.VMEM((A, H, R, 128), bf16),
            pltpu.VMEM((A, H // 2, R, 128), bf16),
            pltpu.VMEM((H, R, hw), f32),
            pltpu.VMEM((H, R, W), bf16),
            *[dma(H - 1)] * 8,
            *[dma(2 * H - 2)] * 2,
            *[dma(A - 1)] * 4,
            *[dma(A)] * 2,
            *line_sems(A),
            *line_sems(A),
        ],
        compiler_params=pltpu.CompilerParams(
            collective_id=0, has_side_effects=True, vmem_limit_bytes=48 * 2**20
        ),
        cost_estimate=pl.CostEstimate(flops=10**9, bytes_accessed=10**7, transcendentals=10**6),
        name="project",
    )(tokens, cotangent, w_qkv, gains, w_in, w_down, w_out, docs)


class LineGather:
    def __init__(self, view, own, h, part, share, parts, sems):
        self.view, self.own, self.h, self.part, self.share, self.parts = view, own, h, part, share, parts
        self.right_s, self.left_s, self.line_r, self.core_s, self.core_r = sems

    def _copy(self, source, block, side):
        if side == 0:
            sems, peer = (self.core_s, self.core_r), (self.h, self.part * 2 + 1 - self.share)
            target = self.view(block, self.share)
        else:
            sems = (self.right_s if side > 0 else self.left_s, self.line_r)
            peer = (self.h, (self.part + side) * 2 + self.share)
            target = self.view(block, self.share)
        return pltpu.make_async_remote_copy(
            src_ref=source,
            dst_ref=target,
            send_sem=sems[0].at[block],
            recv_sem=sems[1].at[block],
            device_id=peer,
            device_id_type=MESH,
        )

    def _can(self, side):
        return self.part < self.parts - 1 if side > 0 else self.part > 0

    def start(self):
        for side in (1, -1):

            @pl.when(self._can(side))
            def _():
                self._copy(self.own, self.part, side).start()

        self._copy(self.own, self.part, 0).start()

    def step(self, k):
        for side in (1, -1):
            block = self.part - side * k

            @pl.when((block >= 0) & (block < self.parts))
            def _():
                there = self.view(block, self.share)
                self._copy(there, block, side).wait_recv()

                @pl.when(self._can(side))
                def _():
                    self._copy(there, block, side).start()

                self._copy(there, block, 0).start()

    def arrive(self):
        for block in range(self.parts):
            self._copy(self.own, block, 0).wait_recv()

    def finish(self):
        for side in (1, -1):
            for block in range(self.parts):
                sent = block <= self.part if side > 0 else block >= self.part

                @pl.when(sent & self._can(side))
                def _():
                    self._copy(self.own, block, side).wait_send()

        for block in range(self.parts):
            self._copy(self.own, block, 0).wait_send()


def line_sems(parts):
    return [pltpu.SemaphoreType.DMA((parts,))] * 5


def norm_back(grad, hat, scale, gain):
    inner = grad * gain
    return scale * (
        inner
        - jnp.mean(inner, axis=-1, keepdims=True)
        - hat * jnp.mean(inner * hat, axis=-1, keepdims=True)
    )


def feed_kernel(
    H, A, op, tok_all, cot_all, wo, wm_own, gain_rows,
    output, grad_middle, go, term, mixed_own, gain_part,
    mx_in, mixed_all, wm_all, middle, normed, act, lift, g2_send, g2_in, g2_own, o_send, o_in, o_own, gm_send,
    mx_s, mx_r, ma_s, ma_r, g2_s, g2_r, o_s, o_r, gm_s, gm_r, *line,
):
    f32, bf16 = jnp.float32, jnp.bfloat16
    R, W = tok_all.shape[1:]
    B = 2 * A
    hw = W // H
    D = wm_own.shape[1]
    F = wm_own.shape[2] // 3
    h, b, part, share, across, along, beside = grid_peers(H, A)
    others = [
        (lax.rem(h + i, H), lax.rem(part + j, A) * 2 + share)
        for i in range(H)
        for j in range(A)
        if i or j
    ]
    meet([*others, beside])

    mx_copies = [
        send(op.at[peer[1] // 2], mx_in.at[part], mx_s.at[i], mx_r.at[i], peer)
        for i, peer in enumerate(along)
    ]
    gather = LineGather(
        lambda block, side: wm_all.at[:, block * 2 + side], wm_own, h, part, share, A, line
    )
    gather.start()
    wm_all[:, b] = wm_own[...]
    mx_in[part] = op[part]
    for copy in mx_copies:
        copy.wait_recv()
    for run in range(H):
        side, at = run // (H // 2), run % (H // 2)
        for slab in range(hw // 128):
            left, right = mx_in[2 * slab, at].astype(f32), mx_in[2 * slab + 1, at].astype(f32)
            mixed_own[run, :, slab * 128 : (slab + 1) * 128] = join(left, side, right, side).astype(bf16)
    mixed_all[h] = mixed_own[...]
    ma_copies = [
        send(mixed_own, mixed_all.at[h], ma_s.at[i], ma_r.at[i], peer) for i, peer in enumerate(across)
    ]

    def project_out(source, first):
        def one(run, carried):
            before = tok_all[run].astype(f32) if first else middle[run]
            middle[run] = before + mm(mixed_all[source, run], wo[source])
            return carried

        lax.fori_loop(0, H, one, 0)

    project_out(h, True)
    gather.step(1)
    for i, copy in enumerate(ma_copies):
        copy.wait_recv()
        project_out(lax.rem(h + H - 1 - i, H), False)

    def norm_run(run, carried):
        hat, unused = standardize(middle[run])
        normed[run] = (hat * gain_rows[1:2, :]).astype(bf16)
        return carried

    lax.fori_loop(0, H, norm_run, 0)
    for k in range(2, A):
        gather.step(k)
    gather.arrive()

    def block(chunk):
        return wm_all[chunk].reshape(B * D, 3 * F)

    def feed_run(i, carried):
        run = lax.rem(h + 1 + i, H)
        lifted = jnp.zeros((R, 2 * F), f32)
        grad_act = jnp.zeros((R, F), f32)
        for chunk in range(H):
            lanes = slice(chunk * hw, (chunk + 1) * hw)
            weights = block(chunk)
            lifted += mm(normed[run, :, lanes], weights[:, : 2 * F])
            grad_act += mm(cot_all[run, :, lanes], weights[:, 2 * F :])
        gate, up = lifted[:, :F], lifted[:, F:]
        below = 0.5 + 0.5 * lax.erf(gate * (0.5**0.5))
        slope = below + gate * jnp.exp(-0.5 * gate * gate) * ((2.0 * np.pi) ** -0.5)
        act[run] = (gate * below * up).astype(bf16)
        lift[run, :, :F] = (grad_act * up * slope).astype(bf16)
        lift[run, :, F:] = (grad_act * gate * below).astype(bf16)

        for chunk in range(H):
            lanes = slice(chunk * hw, (chunk + 1) * hw)
            g2_own[:, lanes] = mm(lift[run], block(chunk)[:, : 2 * F], NT)

        @pl.when(i < H - 1)
        def _():
            g2_send[i] = g2_own[...].astype(bf16)
            pltpu.make_async_remote_copy(
                g2_send.at[i], g2_in.at[i], g2_s.at[i], g2_r.at[i], device_id=(run, b), device_id_type=MESH
            ).start()

        return carried

    lax.fori_loop(0, H, feed_run, 0)

    def out_run(i, carried):
        run = lax.rem(h + 1 + i, H)
        for chunk in range(H):
            lanes = slice(chunk * hw, (chunk + 1) * hw)
            o_own[:, lanes] = mm(act[run], block(chunk)[:, 2 * F :], NT)

        @pl.when(i < H - 1)
        def _():
            o_send[i] = o_own[...].astype(bf16)
            pltpu.make_async_remote_copy(
                o_send.at[i], o_in.at[i], o_s.at[i], o_r.at[i], device_id=(run, b), device_id_type=MESH
            ).start()

        return carried

    lax.fori_loop(0, H, out_run, 0)

    def rest(sent, landed, send_sem, recv_sem, i):
        return pltpu.make_async_remote_copy(
            sent.at[i], landed.at[i], send_sem.at[i], recv_sem.at[i], device_id=across[i], device_id_type=MESH
        )

    grad = g2_own[...]
    for i in range(H - 1):
        rest(g2_send, g2_in, g2_s, g2_r, i).wait_recv()
        grad += g2_in[i].astype(f32)
    hat, scale = standardize(middle[h])
    gain_part[...] = jnp.broadcast_to(jnp.sum(grad * hat, axis=0, keepdims=True), gain_part.shape)
    total = cot_all[h].astype(f32) + norm_back(grad, hat, scale, gain_rows[1:2, :])
    grad_middle[...] = total
    branch = total.astype(bf16)
    gm_copies = []
    for i in range(H):
        place = lax.rem(h + i, H)
        mixed_grad = mm(branch, wo[place], NT)
        for a in range(A):
            slab = mixed_grad[:, a // 2 * 128 : a // 2 * 128 + 128]
            gm_send[i, a] = join(slab[: R // 2], a % 2, slab[R // 2 :], a % 2).astype(bf16)
        for j in range(A):
            there = lax.rem(part + j, A)
            if i or j:
                n = i * A + j
                gm_copies.append(
                    send(gm_send.at[i, there], go.at[part, h], gm_s.at[n], gm_r.at[n], (place, there * 2 + share))
                )
            else:
                go[part, h] = gm_send[0, part]

    def term_chunk(chunk, carried):
        lanes = pl.ds(pl.multiple_of(chunk * hw, hw), hw)
        left = normed[:, :, lanes].reshape(H * R, hw)
        grads = mm(left, lift[...].reshape(H * R, 2 * F), TN).astype(bf16)
        term[:, chunk, :, : 2 * F] = grads.reshape(B, D, 2 * F)
        left = cot_all[:, :, lanes].reshape(H * R, hw)
        grads = mm(left, act[...].reshape(H * R, F), TN).astype(bf16)
        term[:, chunk, :, 2 * F :] = grads.reshape(B, D, F)
        return carried

    lax.fori_loop(0, H, term_chunk, 0)
    result = middle[h] + o_own[...]
    for i in range(H - 1):
        rest(o_send, o_in, o_s, o_r, i).wait_recv()
        result += o_in[i].astype(f32)
    output[...] = result.astype(bf16)
    for copy in gm_copies:
        copy.wait_recv()
    for copy in [*mx_copies, *ma_copies, *gm_copies]:
        copy.wait_send()
    for i in range(H - 1):
        rest(g2_send, g2_in, g2_s, g2_r, i).wait_send()
        rest(o_send, o_in, o_s, o_r, i).wait_send()
    gather.finish()


def feed(op, tok_all, cot_all, wo, wm_own, gain_rows):
    A, half, R, lanes = op.shape
    H = 2 * half
    W = tok_all.shape[-1]
    B = 2 * A
    hw = W // H
    D = wm_own.shape[1]
    F = wm_own.shape[2] // 3
    f32, bf16 = jnp.float32, jnp.bfloat16
    shape = jax.ShapeDtypeStruct
    dma = lambda count: pltpu.SemaphoreType.DMA((count,))
    vmem = pl.BlockSpec(memory_space=pltpu.VMEM)
    return pl.pallas_call(
        partial(feed_kernel, H, A),
        in_specs=[vmem] * 6,
        out_specs=[vmem] * 6,
        out_shape=[
            shape((R, W), bf16),
            shape((R, W), f32),
            shape((A, H, R // 2, 128), bf16),
            shape((B, H, D, 3 * F), bf16),
            shape((H, R, hw), bf16),
            shape((8, W), f32),
        ],
        scratch_shapes=[
            pltpu.VMEM((A, half, R, 128), bf16),
            pltpu.VMEM((H, H, R, hw), bf16),
            pltpu.VMEM((H, B, D, 3 * F), bf16),
            pltpu.VMEM((H, R, W), f32),
            pltpu.VMEM((H, R, W), bf16),
            pltpu.VMEM((H, R, F), bf16),
            pltpu.VMEM((H, R, 2 * F), bf16),
            *[pltpu.VMEM((H - 1, R, W), bf16), pltpu.VMEM((H - 1, R, W), bf16), pltpu.VMEM((R, W), f32)] * 2,
            pltpu.VMEM((H, A, R // 2, 128), bf16),
            *[dma(A - 1)] * 2,
            *[dma(H - 1)] * 6,
            *[dma(H * A)] * 2,
            *line_sems(A),
        ],
        compiler_params=pltpu.CompilerParams(
            collective_id=1, has_side_effects=True, vmem_limit_bytes=56 * 2**20
        ),
        cost_estimate=pl.CostEstimate(flops=6 * 10**9, bytes_accessed=10**7, transcendentals=10**6),
        name="feed",
    )(op, tok_all, cot_all, wo, wm_own, gain_rows)


def per_device_split(
    tokens, attn_gain, w_qkv, w_attn_out, mlp_gain, w_in, w_mlp_out, doc_lengths, cotangent
):
    R, W = tokens.shape
    H, B = lax.axis_size("head"), lax.axis_size("blk")
    A = W // HEAD_DIM // H
    G = B // A
    hw = W // H
    D = w_qkv.shape[0]
    F = w_mlp_out.shape[0] // H
    T = H * B * R
    N = H * R
    h, b = lax.axis_index("head"), lax.axis_index("blk")
    f32, bf16 = jnp.float32, jnp.bfloat16
    part_groups = [[a * G + g for a in range(A)] for g in range(G)]
    share_groups = [[a * G + g for g in range(G)] for a in range(A)]

    ends = jnp.cumsum(doc_lengths)
    places = jnp.arange(T, dtype=jnp.int32)
    passed = places[:, None] >= ends[None, :]
    docs = jnp.sum(passed.astype(jnp.int32), axis=1)
    starts = jnp.sum(jnp.where(passed, doc_lengths[None, :], 0), axis=1)
    stops = jnp.min(jnp.where(passed, T, ends[None, :]), axis=1)
    runs = (T // R,)
    run_docs = docs.reshape(H, A, G, R)
    run_lo = starts.reshape(H, A, G, R)[..., 0]
    run_hi = stops.reshape(H, A, G, R)[..., R - 1]
    g = b % G
    pick = lambda v: lax.dynamic_index_in_dim(v, g, 2, keepdims=False)
    qdoc = pick(run_docs).reshape(H * A // 2, 2 * R, 1)
    lo = pick(run_lo).reshape(H * A // 2, 2)[:, 0] // KEY_TILE
    hi = (pick(run_hi).reshape(H * A // 2, 2)[:, 1] + KEY_TILE - 1) // KEY_TILE
    span = jnp.stack([lo, hi], axis=1).astype(jnp.int32)
    kdoc = docs.reshape(T // KEY_TILE, KEY_TILE)
    own = lambda v: lax.dynamic_index_in_dim(v.reshape(H, B, R), b, 1, keepdims=False).reshape(N)
    gains = jnp.pad(jnp.stack([attn_gain, mlp_gain], axis=1), ((0, 0), (0, 126)))
    kv, qp, tok_all, cot_all, wq, wm, wo, gain_rows, cos_all, sin_all = project(
        tokens, cotangent, w_qkv, gains, w_in, w_mlp_out, w_attn_out, jnp.stack([ends, doc_lengths])
    )
    cosine, sine = cos_all.reshape(N, 128)[:, :HEAD_DIM], sin_all.reshape(N, 128)[:, :HEAD_DIM]
    kv = kv.reshape(T, 2 * HEAD_DIM)
    op, lse = attend(span, qp, kv, qdoc, kdoc)
    output, grad_middle, gp, term_mlp, mixed, gain_part = feed(
        op, tok_all, cot_all, wo.reshape(H, hw, W), wm, gain_rows
    )
    sum_mlp = lax.psum_scatter(
        term_mlp.reshape(B * H * D, 3 * F), "blk", scatter_dimension=0, tiled=True
    ).reshape(H, D, 3 * F)
    dqp, dkv = attend_back(span, qp, gp, op, lse, kv, qdoc, kdoc)
    wq = wq.reshape(W, 3 * hw + 128)
    gain_one = gain_rows[0]
    normed_one = layer_norm(tok_all.reshape(N, W).astype(f32), gain_one).astype(bf16)
    branch_all = lax.all_gather(grad_middle.astype(bf16), "head", axis=0, tiled=True)
    grad_gain_two = gain_part[0]
    mixed = mixed.reshape(N, hw)
    dqp = lax.all_to_all(dqp, "blk", 0, 0, tiled=True, axis_index_groups=part_groups)
    dkv = dkv.reshape(H, A, G, R, 2 * HEAD_DIM).transpose(2, 1, 0, 3, 4)
    dkv = lax.psum_scatter(dkv, "blk", scatter_dimension=0, tiled=False, axis_index_groups=share_groups)
    dkv = lax.all_to_all(dkv, "blk", 0, 0, tiled=True, axis_index_groups=part_groups)
    merge = lambda v: v.transpose(1, 2, 0, 3).reshape(N, hw)
    _, rope_pull = jax.vjp(
        partial(rotate_pair, cosine=cosine, sine=sine),
        jnp.zeros((N, hw), f32),
        jnp.zeros((N, hw), f32),
    )
    grad_query, grad_keys = rope_pull(
        (merge(unpack_pairs(dqp)).astype(f32), merge(dkv[..., :HEAD_DIM]).astype(f32))
    )
    grad_projected = jnp.concatenate(
        [grad_query.astype(bf16), grad_keys.astype(bf16), merge(dkv[..., HEAD_DIM:])], axis=1
    )
    grad_one = mm(grad_projected, wq[:, : 3 * hw], NT).astype(bf16)
    grad_one = lax.psum_scatter(grad_one, "head", scatter_dimension=0, tiled=True).astype(f32)
    _, norm_one_pull = jax.vjp(layer_norm, tokens.astype(f32), gain_one)
    grad_input, grad_gain_one = norm_one_pull(grad_one)
    input_grad = grad_middle + grad_input
    term_qkv = mm(normed_one, grad_projected, TN)
    gain_terms = jnp.pad(jnp.stack([grad_gain_one, grad_gain_two], axis=1), ((0, 0), (0, 126)))
    term_qkv = jnp.concatenate([term_qkv, gain_terms], axis=1).astype(bf16)
    term_qkv = term_qkv.reshape(H, B, D, 3 * hw + 128).transpose(1, 0, 2, 3)
    term_out = mm(mixed, branch_all, TN).astype(bf16).reshape(B, D, W)
    sum_qkv = lax.psum_scatter(term_qkv, "blk", scatter_dimension=0, tiled=False)
    sum_out = lax.psum_scatter(term_out, "blk", scatter_dimension=0, tiled=False)
    sum_mlp = lax.all_to_all(sum_mlp, "head", 0, 0, tiled=True).astype(f32)
    sum_qkv = lax.all_to_all(sum_qkv, "head", 0, 0, tiled=True).astype(f32)
    in_grad = sum_mlp[:, :, : 2 * F].reshape(H, D, 2, F).transpose(1, 2, 0, 3).reshape(D, 2 * H * F)
    down_grad = sum_mlp[:, :, 2 * F :].transpose(0, 2, 1).reshape(H * F, D)
    qkv_grad = sum_qkv[:, :, : 3 * hw].reshape(H, D, 3, hw).transpose(1, 2, 0, 3).reshape(D, 3 * W)
    gain_sums = jnp.sum(sum_qkv[:, :, 3 * hw : 3 * hw + 2], axis=0)
    return (
        output,
        input_grad,
        gain_sums[:, 0],
        qkv_grad,
        sum_out.astype(f32),
        gain_sums[:, 1],
        in_grad,
        down_grad,
    )


def per_device(tokens, attn_gain, w_qkv, *rest):
    heads, blocks = lax.axis_size("head"), lax.axis_size("blk")
    parts = tokens.shape[1] // HEAD_DIM // heads
    fits = (
        blocks % parts == 0
        and blocks // parts == 2
        and parts % 2 == 0
        and heads % 2 == 0
        and w_qkv.shape[0] % 16 == 0
        and tokens.shape[0] % 128 == 0
    )
    chosen = per_device_split if fits else per_device_general
    return chosen(tokens, attn_gain, w_qkv, *rest)


def solution(mesh):
    placed = (
        P(("head", "blk"), None),
        P(("head", "blk")),
        P(("head", "blk"), None),
        P(("head", "blk"), None),
        P(("head", "blk")),
        P(("head", "blk"), None),
        P(None, ("head", "blk")),
        P(),
        P(("head", "blk"), None),
    )
    return jax.shard_map(
        per_device,
        mesh=mesh,
        in_specs=placed,
        out_specs=(
            P(("head", "blk"), None),
            P(("head", "blk"), None),
            P(("head", "blk")),
            P(("head", "blk"), None),
            P(("head", "blk"), None),
            P(("head", "blk")),
            P(("head", "blk"), None),
            P(None, ("head", "blk")),
        ),
        check_vma=False,
    )
```

```python
from functools import partial

import jax
import jax.numpy as jnp
import numpy as np
from jax import lax
from jax.experimental import pallas as pl
from jax.experimental.pallas import tpu as pltpu
from jax.sharding import PartitionSpec as P

HEAD_DIM = 64


norm_eps = 1e-05
rope_base = 160000.0
neg_large = -1e30


def from_behind(value, axis, by):
    devices = lax.axis_size(axis)
    return lax.ppermute(value, axis, [(i, (i + by) % devices) for i in range(devices)])


def layer_norm(values, gain):
    center = values - jnp.mean(values, axis=-1, keepdims=True)
    spread = jnp.mean(center * center, axis=-1, keepdims=True)
    return center * lax.rsqrt(spread + norm_eps) * gain


def rope_tables(places, head_size):
    half = head_size // 2
    freqs = rope_base ** (-(jnp.arange(half, dtype=jnp.float32) * 2.0) / head_size)
    angles = places.astype(jnp.float32)[:, None] * freqs[None, :]
    angles = jnp.concatenate([angles, angles], axis=1)
    return (jnp.cos(angles), jnp.sin(angles))


def rotate(values, cosine, sine):
    count = values.shape[0]
    head_size = cosine.shape[1]
    half = head_size // 2
    split = values.reshape(count, -1, head_size)
    turned = jnp.concatenate([-split[..., half:], split[..., :half]], axis=-1)
    return (split * cosine[:, None, :] + turned * sine[:, None, :]).reshape(count, -1)


def rotate_pair(query, keys, cosine, sine):
    return (rotate(query, cosine, sine), rotate(keys, cosine, sine))


def doc_numbers(places, ends, lengths):
    passed = places[:, None] >= ends[None, :]
    numbers = jnp.sum(passed.astype(jnp.int32), axis=1)
    offset = jnp.sum(jnp.where(passed, lengths[None, :], 0), axis=1)
    return (numbers, places - offset)


def gelu_gate(lifted):
    half = lifted.shape[1] // 2
    return jax.nn.gelu(lifted[:, :half], approximate=False) * lifted[:, half:]


def tile_scores(query, keys):
    heads = query.shape[1] // HEAD_DIM
    query_split = query.reshape(query.shape[0], heads, HEAD_DIM)
    key_split = keys.reshape(keys.shape[0], heads, HEAD_DIM)
    return jnp.einsum(
        "qhd,khd->hqk", query_split, key_split, preferred_element_type=jnp.float32
    ) * HEAD_DIM ** (-0.5)


def unchanged(state):
    return state


def forward_tile(state, query, keys, values, mask):
    top, total, running = state
    count = query.shape[0]
    heads = top.shape[0]
    scores = tile_scores(query, keys)
    filled = jnp.where(mask[None], scores, neg_large)
    new_top = jnp.maximum(top, jnp.max(filled, axis=-1))
    weights = jnp.where(mask[None], jnp.exp(scores - new_top[:, :, None]), 0.0)
    factor = jnp.exp(top - new_top)
    new_total = total * factor + jnp.sum(weights, axis=-1)
    mixed = jnp.einsum(
        "hqk,khd->qhd",
        weights.astype(jnp.bfloat16),
        values.reshape(-1, heads, HEAD_DIM),
        preferred_element_type=jnp.float32,
    )
    new_running = running.reshape(count, heads, HEAD_DIM) * factor.T[:, :, None] + mixed
    return (new_top, new_total, new_running.reshape(count, heads * HEAD_DIM))


def backward_tile(carry, query, keys, values, mask, norm_log, grad_out, delta):
    query_grad, run_grads = carry
    count = query.shape[0]
    columns = keys.shape[0]
    heads = norm_log.shape[0]
    scores = tile_scores(query, keys)
    probs = jnp.where(mask[None], jnp.exp(scores - norm_log[:, :, None]), 0.0)
    grad_split = grad_out.reshape(count, heads, HEAD_DIM)
    value_split = values.reshape(columns, heads, HEAD_DIM)
    grad_values = jnp.einsum(
        "hqk,qhd->khd", probs.astype(jnp.bfloat16), grad_split, preferred_element_type=jnp.float32
    )
    grad_probs = jnp.einsum(
        "qhd,khd->hqk", grad_split, value_split, preferred_element_type=jnp.float32
    )
    grad_scores = (probs * (grad_probs - delta[:, :, None])).astype(jnp.bfloat16)
    grad_query = jnp.einsum(
        "hqk,khd->qhd",
        grad_scores,
        keys.reshape(columns, heads, HEAD_DIM),
        preferred_element_type=jnp.float32,
    ) * HEAD_DIM ** (-0.5)
    grad_keys = jnp.einsum(
        "hqk,qhd->khd",
        grad_scores,
        query.reshape(count, heads, HEAD_DIM),
        preferred_element_type=jnp.float32,
    ) * HEAD_DIM ** (-0.5)
    added = jnp.stack([grad_keys.reshape(columns, -1), grad_values.reshape(columns, -1)])
    return (query_grad + grad_query.reshape(count, -1), run_grads + added)


def per_device_general(
    tokens, attn_gain, w_qkv, w_attn_out, mlp_gain, w_in, w_mlp_out, doc_lengths, cotangent
):
    own_rows = tokens.shape[0]
    width = tokens.shape[1]
    head_count = lax.axis_size("head")
    cycle_count = lax.axis_size("blk")
    head_place = lax.axis_index("head")
    cycle_place = lax.axis_index("blk")
    group_rows = head_count * own_rows
    block_runs = min(head_count, max(1, 512 // own_rows))
    block_count = head_count // block_runs
    block_rows = block_runs * own_rows
    doc_ends = jnp.cumsum(doc_lengths)
    counter = jnp.arange(own_rows, dtype=jnp.int32)
    own_places = (head_place * cycle_count + cycle_place) * own_rows + counter
    unused_docs, own_positions = doc_numbers(own_places, doc_ends, doc_lengths)
    cosine, sine = rope_tables(own_positions, HEAD_DIM)
    run_numbers = jnp.arange(head_count, dtype=jnp.int32)
    query_places = (
        (run_numbers[:, None] * cycle_count + cycle_place) * own_rows + counter[None, :]
    ).reshape(group_rows)
    query_docs, unused_positions = doc_numbers(query_places, doc_ends, doc_lengths)
    params = (
        lax.all_gather(attn_gain, ("head", "blk"), axis=0, tiled=True),
        lax.all_gather(w_qkv, ("head", "blk"), axis=0, tiled=True),
        lax.all_gather(w_attn_out, ("head", "blk"), axis=0, tiled=True),
        lax.all_gather(mlp_gain, ("head", "blk"), axis=0, tiled=True),
        lax.all_gather(w_in, ("head", "blk"), axis=0, tiled=True),
        lax.all_gather(w_mlp_out, ("head", "blk"), axis=1, tiled=True),
    )
    gain_one, full_qkv, full_attn_out, gain_two, full_in, full_mlp_out = params
    inputs = tokens.astype(jnp.float32)
    normed_one, norm_one_pull = jax.vjp(layer_norm, inputs, gain_one.astype(jnp.float32))
    normed_low = normed_one.astype(jnp.bfloat16)
    projected = jnp.dot(normed_low, full_qkv, preferred_element_type=jnp.float32)
    turned, rope_pull = jax.vjp(
        partial(rotate_pair, cosine=cosine, sine=sine),
        projected[:, :width],
        projected[:, width : 2 * width],
    )
    stacked = jnp.stack(
        [
            turned[0].astype(jnp.bfloat16),
            turned[1].astype(jnp.bfloat16),
            projected[:, 2 * width :].astype(jnp.bfloat16),
        ]
    )
    regrouped = lax.all_to_all(stacked, "head", split_axis=2, concat_axis=1, tiled=True)
    query_heads = regrouped[0]
    key_heads = regrouped[1]
    value_heads = regrouped[2]
    head_width = query_heads.shape[1]
    heads_here = head_width // HEAD_DIM

    def key_docs_at(first):
        places = (
            first % group_rows // own_rows * cycle_count + first // group_rows
        ) * own_rows + counter
        found, unused = doc_numbers(places, doc_ends, doc_lengths)
        return found

    def block_live(block, key_docs):
        block_docs = query_docs[block * block_rows : (block + 1) * block_rows]
        live = jnp.maximum(jnp.min(block_docs), jnp.min(key_docs)) <= jnp.minimum(
            jnp.max(block_docs), jnp.max(key_docs)
        )
        return (block_docs[:, None] == key_docs[None, :], live)

    def fold_forward(state, piece):
        key_part, value_part = piece

        def fold_one_run(number, carried):
            first = number * own_rows
            key_docs = key_docs_at(first)
            keys = lax.dynamic_slice_in_dim(key_part, number * own_rows, own_rows, 0)
            values = lax.dynamic_slice_in_dim(value_part, number * own_rows, own_rows, 0)
            updated = []
            for block in range(block_count):
                mask, live = block_live(block, key_docs)
                query = query_heads[block * block_rows : (block + 1) * block_rows]
                advance = partial(forward_tile, query=query, keys=keys, values=values, mask=mask)
                updated.append(lax.cond(live, advance, unchanged, carried[block]))
            return tuple(updated)

        return lax.fori_loop(0, key_part.shape[0] // own_rows, fold_one_run, state)

    def fresh_state():
        return tuple(
            (
                (
                    jnp.full((heads_here, block_rows), neg_large, jnp.float32),
                    jnp.zeros((heads_here, block_rows), jnp.float32),
                    jnp.zeros((block_rows, head_width), jnp.float32),
                )
                for block in range(block_count)
            )
        )

    def finish(state):
        outputs = []
        logs = []
        for top, total, running in state:
            scaled = running.reshape(block_rows, heads_here, HEAD_DIM) / total.T[:, :, None]
            outputs.append(scaled.reshape(block_rows, head_width))
            logs.append(top + jnp.log(total))
        return (
            jnp.concatenate(outputs, axis=0).astype(jnp.bfloat16),
            jnp.concatenate(logs, axis=1),
        )

    state = fold_forward(
        fresh_state(),
        (
            lax.all_gather(key_heads, "blk", axis=0, tiled=True),
            lax.all_gather(value_heads, "blk", axis=0, tiled=True),
        ),
    )
    out_heads, norm_log = finish(state)
    out_tokens = lax.all_to_all(out_heads, "head", split_axis=0, concat_axis=1, tiled=True)
    middle = inputs + jnp.dot(out_tokens, full_attn_out, preferred_element_type=jnp.float32)
    normed_two, norm_two_pull = jax.vjp(layer_norm, middle, gain_two.astype(jnp.float32))
    normed_two_low = normed_two.astype(jnp.bfloat16)
    lifted = jnp.dot(normed_two_low, full_in, preferred_element_type=jnp.float32)
    activated, geglu_pull = jax.vjp(gelu_gate, lifted)
    activated_low = activated.astype(jnp.bfloat16)
    output = (
        middle + jnp.dot(activated_low, full_mlp_out, preferred_element_type=jnp.float32)
    ).astype(jnp.bfloat16)
    params = (
        lax.all_gather(attn_gain, ("head", "blk"), axis=0, tiled=True),
        lax.all_gather(w_qkv, ("head", "blk"), axis=0, tiled=True),
        lax.all_gather(w_attn_out, ("head", "blk"), axis=0, tiled=True),
        lax.all_gather(mlp_gain, ("head", "blk"), axis=0, tiled=True),
        lax.all_gather(w_in, ("head", "blk"), axis=0, tiled=True),
        lax.all_gather(w_mlp_out, ("head", "blk"), axis=1, tiled=True),
    )
    gain_one, full_qkv, full_attn_out, gain_two, full_in, full_mlp_out = params
    grad_act = jnp.einsum("td,fd->tf", cotangent, full_mlp_out, preferred_element_type=jnp.float32)
    grad_lifted = geglu_pull(grad_act)[0].astype(jnp.bfloat16)
    grad_normed_two = jnp.einsum(
        "tf,df->td", grad_lifted, full_in, preferred_element_type=jnp.float32
    )
    grad_middle_part, grad_gain_two = norm_two_pull(grad_normed_two)
    grad_middle = cotangent.astype(jnp.float32) + grad_middle_part
    grad_branch = grad_middle.astype(jnp.bfloat16)
    grad_mixed = jnp.einsum(
        "te,de->td", grad_branch, full_attn_out, preferred_element_type=jnp.float32
    ).astype(jnp.bfloat16)
    grad_heads = lax.all_to_all(grad_mixed, "head", split_axis=1, concat_axis=0, tiled=True)
    state = fold_forward(
        fresh_state(),
        (
            lax.all_gather(key_heads, "blk", axis=0, tiled=True),
            lax.all_gather(value_heads, "blk", axis=0, tiled=True),
        ),
    )
    out_heads, norm_log = finish(state)
    delta = jnp.einsum(
        "qhd,qhd->hq",
        grad_heads.reshape(group_rows, heads_here, HEAD_DIM).astype(jnp.float32),
        out_heads.reshape(group_rows, heads_here, HEAD_DIM).astype(jnp.float32),
    )

    def piece_backward(query_grads, key_part, value_part, start):
        piece_rows = key_part.shape[0]

        def piece_one_run(number, carried):
            query_now, piece_grads = carried
            first = start + number * own_rows
            key_docs = key_docs_at(first)
            keys = lax.dynamic_slice_in_dim(key_part, number * own_rows, own_rows, 0)
            values = lax.dynamic_slice_in_dim(value_part, number * own_rows, own_rows, 0)
            run_grads = jnp.zeros((2, own_rows, head_width), jnp.float32)
            updated = []
            for block in range(block_count):
                mask, live = block_live(block, key_docs)
                lower = block * block_rows
                upper = (block + 1) * block_rows
                advance = partial(
                    backward_tile,
                    query=query_heads[lower:upper],
                    keys=keys,
                    values=values,
                    mask=mask,
                    norm_log=norm_log[:, lower:upper],
                    grad_out=grad_heads[lower:upper],
                    delta=delta[:, lower:upper],
                )
                new_query, run_grads = lax.cond(
                    live, advance, unchanged, (query_now[block], run_grads)
                )
                updated.append(new_query)
            piece_grads = lax.dynamic_update_slice_in_dim(
                piece_grads, run_grads, number * own_rows, 1
            )
            return (tuple(updated), piece_grads)

        return lax.fori_loop(
            0,
            piece_rows // own_rows,
            piece_one_run,
            (query_grads, jnp.zeros((2, piece_rows, head_width), jnp.float32)),
        )

    start_query = tuple(
        (jnp.zeros((block_rows, head_width), jnp.float32) for block in range(block_count))
    )

    def cycle_step(step, carried):
        query_now, blocks, travelling = carried
        owner = (cycle_place - step) % cycle_count
        query_now, piece_grads = piece_backward(query_now, blocks[0], blocks[1], owner * group_rows)
        travelling = travelling + piece_grads
        blocks = from_behind(blocks, "blk", 1)
        travelling = from_behind(travelling.astype(jnp.bfloat16), "blk", 1).astype(travelling.dtype)
        return (query_now, blocks, travelling)

    start_cycle = (
        start_query,
        jnp.stack([key_heads, value_heads]),
        jnp.zeros((2, group_rows, head_width), jnp.float32),
    )
    query_grads, unused_blocks, own_grads = lax.fori_loop(0, cycle_count, cycle_step, start_cycle)
    grad_stack = jnp.stack(
        [
            jnp.concatenate(query_grads, axis=0).astype(jnp.bfloat16),
            own_grads[0].astype(jnp.bfloat16),
            own_grads[1].astype(jnp.bfloat16),
        ]
    )
    back_tokens = lax.all_to_all(grad_stack, "head", split_axis=1, concat_axis=2, tiled=True)
    grad_query, grad_keys = rope_pull(
        (back_tokens[0].astype(jnp.float32), back_tokens[1].astype(jnp.float32))
    )
    grad_projected = jnp.concatenate(
        [grad_query, grad_keys, back_tokens[2].astype(jnp.float32)], axis=1
    ).astype(jnp.bfloat16)
    grad_normed_one = jnp.einsum(
        "te,de->td", grad_projected, full_qkv, preferred_element_type=jnp.float32
    )
    grad_input_part, grad_gain_one = norm_one_pull(grad_normed_one)
    input_grad = grad_middle + grad_input_part

    def columns(source):
        return source

    term_qkv = jnp.einsum(
        "td,te->de", columns(normed_low), grad_projected, preferred_element_type=jnp.float32
    )
    term_out = jnp.einsum(
        "td,te->de", columns(out_tokens), grad_branch, preferred_element_type=jnp.float32
    )
    term_in = jnp.einsum(
        "td,tf->df", columns(normed_two_low), grad_lifted, preferred_element_type=jnp.float32
    )
    term_down = jnp.einsum(
        "td,tf->df", columns(cotangent), activated_low, preferred_element_type=jnp.float32
    )
    sums = lax.psum_scatter(
        jnp.concatenate([term_qkv, term_out, term_in, term_down], axis=1),
        ("head", "blk"),
        scatter_dimension=0,
        tiled=True,
    )
    ff_width = full_mlp_out.shape[0]
    qkv_grad = sums[:, : 3 * width]
    attn_out_grad = sums[:, 3 * width : 4 * width]
    in_grad = sums[:, 4 * width : 4 * width + 2 * ff_width]
    down_grad = sums[:, 4 * width + 2 * ff_width :].T
    gain_sums = lax.psum_scatter(
        jnp.stack([grad_gain_one, grad_gain_two]), ("head", "blk"), scatter_dimension=1, tiled=True
    )
    return (
        output,
        input_grad,
        gain_sums[0],
        qkv_grad,
        attn_out_grad,
        gain_sums[1],
        in_grad,
        down_grad,
    )


KEY_TILE = 256
NN = (((1,), (0,)), ((), ()))
NT = (((1,), (1,)), ((), ()))
TN = (((0,), (0,)), ((), ()))


def mm(left, right, dims=NN):
    return lax.dot_general(left, right, dims, preferred_element_type=jnp.float32)


def halves(packed, side):
    wide = packed.astype(jnp.float32)
    if side:
        wide = pltpu.roll(wide, HEAD_DIM, 1)
    lane = lax.broadcasted_iota(jnp.int32, wide.shape, 1)
    return jnp.where(lane < HEAD_DIM, wide, 0.0)


def attend_kernel(span, qp, kv, qdoc, kdoc, op, lse, s_scr):
    pairs, tall = qp.shape[0] * qp.shape[2], qp.shape[2]
    half_runs = pl.num_programs(0)
    hh, u = pl.program_id(0), pl.program_id(1)
    lane = lax.broadcasted_iota(jnp.int32, (pairs, 2 * HEAD_DIM), 1)
    results = []
    for side in (0, 1):
        tile = (hh + side * half_runs) * pl.num_programs(1) + u
        query = (halves(qp[...].reshape(pairs, 2 * HEAD_DIM), side) * HEAD_DIM**-0.5).astype(
            jnp.bfloat16
        )
        docs = qdoc[tile]
        first, last = span[tile, 0], span[tile, 1]

        def score(kb, top):
            keys = kv[pl.ds(pl.multiple_of(kb * KEY_TILE, KEY_TILE), KEY_TILE), :]
            scores = jnp.where(docs == kdoc[pl.ds(kb, 1), :], mm(query, keys, NT), neg_large)
            s_scr[kb] = scores
            return jnp.maximum(top, jnp.maximum(scores[:, :128], scores[:, 128:]))

        top = lax.fori_loop(first, last, score, jnp.full((pairs, 128), neg_large, jnp.float32))
        top = jnp.max(top, axis=1, keepdims=True)

        def mix(kb, carried):
            total, acc = carried
            keys = kv[pl.ds(pl.multiple_of(kb * KEY_TILE, KEY_TILE), KEY_TILE), :]
            weights = jnp.exp(s_scr[kb] - top)
            total = total + weights[:, :128] + weights[:, 128:]
            return (total, acc + mm(weights.astype(jnp.bfloat16), keys))

        zeros = jnp.zeros((pairs, 128), jnp.float32)
        total, acc = lax.fori_loop(first, last, mix, (zeros, zeros))
        total = jnp.sum(total, axis=1, keepdims=True)
        lse[tile] = top + jnp.log(total)
        results.append(acc / total)
    both = jnp.where(lane < HEAD_DIM, pltpu.roll(results[0], HEAD_DIM, 1), results[1])
    op[...] = both.astype(jnp.bfloat16).reshape(op.shape)


def attend(span, qp, kv, qdoc, kdoc):
    parts, half_runs, rows, lanes = qp.shape
    tiles = qdoc.shape[0]
    piece = pl.BlockSpec((2, 1, rows, lanes), lambda i, j, s: (j, i, 0, 0))
    whole = pl.BlockSpec(memory_space=pltpu.VMEM)
    return pl.pallas_call(
        attend_kernel,
        grid_spec=pltpu.PrefetchScalarGridSpec(
            num_scalar_prefetch=1,
            grid=(half_runs, parts // 2),
            in_specs=[piece, whole, whole, whole],
            out_specs=[piece, whole],
            scratch_shapes=[
                pltpu.VMEM((kv.shape[0] // KEY_TILE, 2 * rows, KEY_TILE), jnp.float32)
            ],
        ),
        out_shape=[
            jax.ShapeDtypeStruct(qp.shape, jnp.bfloat16),
            jax.ShapeDtypeStruct((tiles, 2 * rows, 1), jnp.float32),
        ],
        compiler_params=pltpu.CompilerParams(vmem_limit_bytes=48 * 2**20),
        cost_estimate=pl.CostEstimate(flops=10**9, bytes_accessed=4 * 10**6, transcendentals=10**6),
        name="attend",
    )(span, qp, kv, qdoc, kdoc)


def attend_back_kernel(span, qp, gp, op, lse, kv, qdoc, kdoc, dqp, dkv, acc_scr):
    pairs, tall = qp.shape[0] * qp.shape[2], qp.shape[2]
    half_runs = pl.num_programs(0)
    hh, u = pl.program_id(0), pl.program_id(1)
    lane = lax.broadcasted_iota(jnp.int32, (pairs, 2 * HEAD_DIM), 1)

    @pl.when((hh == 0) & (u == 0))
    def _():
        acc_scr[...] = jnp.zeros_like(acc_scr)

    results = []
    flat = (pairs, 2 * HEAD_DIM)
    for side in (0, 1):
        tile = (hh + side * half_runs) * pl.num_programs(1) + u
        query = (halves(qp[...].reshape(flat), side) * HEAD_DIM**-0.5).astype(jnp.bfloat16)
        pieces = []
        for n in range(2):
            piece = gp[n, hh + side * half_runs].astype(jnp.float32)
            pieces += [pltpu.roll(piece, HEAD_DIM, 1), piece]
        grad = jnp.where(lane < HEAD_DIM, 0.0, jnp.concatenate(pieces, axis=0))
        mixed = op[...].reshape(flat).astype(jnp.float32)
        if not side:
            mixed = pltpu.roll(mixed, HEAD_DIM, 1)
        delta = jnp.sum(grad * mixed, axis=1, keepdims=True)
        grad = grad.astype(jnp.bfloat16)
        docs = qdoc[tile]
        logs = lse[tile]

        def step(kb, dq):
            keys = kv[pl.ds(pl.multiple_of(kb * KEY_TILE, KEY_TILE), KEY_TILE), :]
            scores = mm(query, keys, NT)
            probs = jnp.where(docs == kdoc[pl.ds(kb, 1), :], jnp.exp(scores - logs), 0.0)
            grad_scores = (probs * (mm(grad, keys, NT) - delta)).astype(jnp.bfloat16)
            acc_scr[kb] += mm(grad_scores, query, TN) + mm(probs.astype(jnp.bfloat16), grad, TN)
            return dq + mm(grad_scores, keys)

        dq = lax.fori_loop(span[tile, 0], span[tile, 1], step, jnp.zeros(flat, jnp.float32))
        results.append(dq * HEAD_DIM**-0.5)
    both = jnp.where(lane < HEAD_DIM, results[0], pltpu.roll(results[1], HEAD_DIM, 1))
    dqp[...] = both.astype(jnp.bfloat16).reshape(dqp.shape)

    @pl.when((hh == half_runs - 1) & (u == pl.num_programs(1) - 1))
    def _():
        dkv[...] = acc_scr[...].reshape(dkv.shape).astype(dkv.dtype)


def attend_back(span, qp, gp, op, lse, kv, qdoc, kdoc):
    parts, half_runs, rows, lanes = qp.shape
    piece = pl.BlockSpec((2, 1, rows, lanes), lambda i, j, s: (j, i, 0, 0))
    grads = pl.BlockSpec((2, 2 * half_runs, rows // 2, lanes), lambda i, j, s: (j, 0, 0, 0))
    whole = pl.BlockSpec(memory_space=pltpu.VMEM)
    return pl.pallas_call(
        attend_back_kernel,
        grid_spec=pltpu.PrefetchScalarGridSpec(
            num_scalar_prefetch=1,
            grid=(half_runs, parts // 2),
            in_specs=[piece, grads, piece, whole, whole, whole, whole],
            out_specs=[piece, whole],
            scratch_shapes=[pltpu.VMEM((kv.shape[0] // KEY_TILE, KEY_TILE, lanes), jnp.float32)],
        ),
        out_shape=[
            jax.ShapeDtypeStruct(qp.shape, jnp.bfloat16),
            jax.ShapeDtypeStruct(kv.shape, jnp.bfloat16),
        ],
        compiler_params=pltpu.CompilerParams(vmem_limit_bytes=48 * 2**20),
        cost_estimate=pl.CostEstimate(flops=3 * 10**9, bytes_accessed=6 * 10**6, transcendentals=10**6),
        name="attend_back",
    )(span, qp, gp, op, lse, kv, qdoc, kdoc)


def pack_pairs(value):
    half = value.shape[1] // 2
    return jnp.concatenate([value[:, :half], value[:, half:]], axis=-1)


def unpack_pairs(value):
    return jnp.concatenate([value[..., :HEAD_DIM], value[..., HEAD_DIM:]], axis=1)


MESH = pl.DeviceIdType.MESH


def meet(peers):
    barrier = pltpu.get_barrier_semaphore()
    for peer in peers:
        pl.semaphore_signal(barrier, inc=1, device_id=peer, device_id_type=MESH)
    pl.semaphore_wait(barrier, len(peers))


def send(source, target, send_sem, recv_sem, peer):
    copy = pltpu.make_async_remote_copy(
        src_ref=source,
        dst_ref=target,
        send_sem=send_sem,
        recv_sem=recv_sem,
        device_id=peer,
        device_id_type=MESH,
    )
    copy.start()
    return copy


def grid_peers(heads, parts):
    h, b = lax.axis_index("head"), lax.axis_index("blk")
    part, share = b // 2, b % 2
    across = [(lax.rem(h + i, heads), b) for i in range(1, heads)]
    along = [(h, lax.rem(part + i, parts) * 2 + share) for i in range(1, parts)]
    return (h, b, part, share, across, along, (h, part * 2 + 1 - share))


def standardize(values):
    center = values - jnp.mean(values, axis=-1, keepdims=True)
    spread = jnp.mean(center * center, axis=-1, keepdims=True)
    scale = lax.rsqrt(spread + norm_eps)
    return (center * scale, scale)


def turn(values, cosine, sine, back=False):
    lane = lax.broadcasted_iota(jnp.int32, values.shape, 1)
    first = lax.rem(lane, HEAD_DIM) < HEAD_DIM // 2
    source = values * sine if back else values
    ahead = pltpu.roll(source, 128 - HEAD_DIM // 2, 1)
    behind = pltpu.roll(source, HEAD_DIM // 2, 1)
    if back:
        return values * cosine + jnp.where(first, ahead, -behind)
    return values * cosine + jnp.where(first, -ahead, behind) * sine


def join(left, left_side, right, right_side):
    lane = lax.broadcasted_iota(jnp.int32, left.shape, 1)
    left = pltpu.roll(left, HEAD_DIM, 1) if left_side else left
    right = right if right_side else pltpu.roll(right, HEAD_DIM, 1)
    return jnp.where(lane < HEAD_DIM, left, right)


def project_kernel(
    H, A, tok, cot, wq, gains, w_in, w_down, w_out, docs,
    kv_all, q_all, tok_all, cot_all, wq_all, wm_all, wo_all, gain_rows, cos_all, sin_all,
    wq_src, wq_st, wm_src, kv_send, q_send, q_runs, normed,
    tok_s, tok_r, cot_s, cot_r, wq_s, wq_r, wm_s, wm_r, wx_s, wx_r,
    q_s, q_r, kv_s, kv_r, kc_s, kc_r, *line,
):
    f32, bf16 = jnp.float32, jnp.bfloat16
    R, W = tok.shape
    B = 2 * A
    hw = W // H
    D = wq.shape[0]
    F = w_in.shape[1] // 2 // H
    h, b, part, share, across, along, beside = grid_peers(H, A)
    meet([*across, *along, beside])

    tok_copies = []
    for place in range(H):
        for j in range(3):
            wq_src[place, :, j * hw : (j + 1) * hw] = wq[:, j * W + place * hw : j * W + (place + 1) * hw]
        wq_src[place, :, 3 * hw :] = gains[...]
    wq_copies = [
        send(wq_src.at[peer[0]], wq_st.at[h], wq_s.at[i], wq_r.at[i], peer)
        for i, peer in enumerate(across)
    ]
    tok_copies = [
        send(tok, tok_all.at[h], tok_s.at[i], tok_r.at[i], peer) for i, peer in enumerate(across)
    ]
    wq_st[h] = wq_src[h]
    tok_all[h] = tok[...]
    cot_all[h] = cot[...]
    unit = (
        lax.broadcasted_iota(jnp.int32, (D, D), 0) == lax.broadcasted_iota(jnp.int32, (D, D), 1)
    ).astype(bf16)
    down = mm(unit, w_down[...], NT).astype(bf16)
    for place in range(H):
        wm_src[place, :, :F] = w_in[:, place * F : (place + 1) * F]
        wm_src[place, :, F : 2 * F] = w_in[:, (H + place) * F : (H + place + 1) * F]
        wm_src[place, :, 2 * F :] = down[:, place * F : (place + 1) * F]
    wm_all[h] = wm_src[h]
    wm_copies = [
        send(wm_src.at[peer[0]], wm_all.at[h], wm_s.at[i], wm_r.at[i], peer)
        for i, peer in enumerate(across)
    ]
    cot_copies = [
        send(cot, cot_all.at[h], cot_s.at[i], cot_r.at[i], peer) for i, peer in enumerate(across)
    ]

    for copy in wq_copies:
        copy.wait_recv()
    wq_line = LineGather(
        lambda block, side: wq_all.at[:, block * 2 + side], wq_st, h, part, share, A, line[:5]
    )
    wq_line.start()
    wq_all[:, b] = wq_st[...]
    wo_line = LineGather(
        lambda block, side: wo_all.at[h, block, side], w_out, h, part, share, A, line[5:]
    )
    wo_all[h, part, share] = w_out[...]
    wo_line.start()

    lane = lax.broadcasted_iota(jnp.int32, (R, 128), 1)
    freqs = jnp.exp(
        lax.rem(lane, HEAD_DIM // 2).astype(f32) * (-2.0 / HEAD_DIM * float(np.log(rope_base)))
    )
    for run in range(H):
        place = (run * B + b) * R + lax.broadcasted_iota(jnp.int32, (R, 128), 0)
        begin = jnp.zeros((R, 1), jnp.int32)
        passed = place[:, : docs.shape[1]] >= docs[0:1, :]
        begin = jnp.sum(jnp.where(passed, docs[1:2, :], 0), axis=1, keepdims=True)
        angles = (place - begin).astype(f32) * freqs
        cos_all[run] = jnp.cos(angles)
        sin_all[run] = jnp.sin(angles)

    for copy in tok_copies:
        copy.wait_recv()
    for k in range(1, A):
        wq_line.step(k)
        wo_line.step(k)
    wq_line.arrive()
    wo_line.arrive()
    spread_out = wo_all.at[h, :, share]
    wx_copies = [
        send(spread_out, spread_out, wx_s.at[i], wx_r.at[i], peer) for i, peer in enumerate(across)
    ]

    pick = (
        lax.broadcasted_iota(jnp.int32, (8, 128), 0) == lax.broadcasted_iota(jnp.int32, (8, 128), 1)
    ).astype(bf16)
    for chunk in range(H):
        block = wq_all[chunk].reshape(B * D, 3 * hw + 128)
        gain_rows[:, chunk * hw : (chunk + 1) * hw] = mm(pick, block[:, 3 * hw :], NT)

    kv_copies = []
    for run in range(H):
        hat, unused = standardize(tok_all[run].astype(f32))
        low = (hat * gain_rows[0:1, :]).astype(bf16)
        projected = jnp.zeros((R, 3 * hw), f32)
        for chunk in range(H):
            block = wq_all[chunk].reshape(B * D, 3 * hw + 128)
            projected += mm(low[:, chunk * hw : (chunk + 1) * hw], block[:, : 3 * hw])
        cosine, sine = cos_all[run], sin_all[run]
        for slab in range(hw // 128):
            at = slab * 128
            q_runs[run, :, at : at + 128] = turn(projected[:, at : at + 128], cosine, sine)
            key = turn(projected[:, hw + at : hw + at + 128], cosine, sine)
            value = projected[:, 2 * hw + at : 2 * hw + at + 128]
            kv_send[2 * slab, run] = join(key, 0, value, 0).astype(bf16)
            kv_send[2 * slab + 1, run] = join(key, 1, value, 1).astype(bf16)
    for i, peer in enumerate(along):
        there = peer[1] // 2
        kv_copies.append(
            send(kv_send.at[there], kv_all.at[:, b], kv_s.at[i], kv_r.at[i], peer)
        )
    kv_all[:, b] = kv_send[part]
    kc_copies = [send(kv_send.at[part], kv_all.at[:, b], kc_s.at[0], kc_r.at[0], beside)]
    for run in range(H // 2):
        for a in range(A):
            at = a // 2 * 128
            q_send[a, run] = join(
                q_runs[run, :, at : at + 128], a % 2, q_runs[run + H // 2, :, at : at + 128], a % 2
            ).astype(bf16)
    q_copies = [
        send(q_send.at[peer[1] // 2], q_all.at[part], q_s.at[i], q_r.at[i], peer)
        for i, peer in enumerate(along)
    ]
    q_all[part] = q_send[part]
    for i, copy in enumerate(kv_copies):
        copy.wait_recv()
        there = kv_all.at[:, lax.rem(part + A - 1 - i, A) * 2 + share]
        kc_copies.append(send(there, there, kc_s.at[i + 1], kc_r.at[i + 1], beside))
    for i, copy in enumerate(wx_copies):
        copy.wait_recv()
        there = wo_all.at[lax.rem(h + H - 1 - i, H), :, share]
        n = H - 1 + i
        kc_copies.append(send(there, there, wx_s.at[n], wx_r.at[n], beside))
    for copy in [*kc_copies, *q_copies, *wm_copies, *cot_copies]:
        copy.wait_recv()
    for copy in [
        *kc_copies, *q_copies, *wm_copies, *cot_copies, *wq_copies, *tok_copies, *wx_copies, *kv_copies
    ]:
        copy.wait_send()
    wq_line.finish()
    wo_line.finish()


def project(tokens, cotangent, w_qkv, gains, w_in, w_down, w_out, docs):
    R, W = tokens.shape
    H, B = lax.axis_size("head"), lax.axis_size("blk")
    A = B // 2
    hw = W // H
    D = w_qkv.shape[0]
    F = w_down.shape[0] // H
    f32, bf16 = jnp.float32, jnp.bfloat16
    shape = jax.ShapeDtypeStruct
    dma = lambda count: pltpu.SemaphoreType.DMA((count,))
    vmem = pl.BlockSpec(memory_space=pltpu.VMEM)
    return pl.pallas_call(
        partial(project_kernel, H, A),
        in_specs=[vmem] * 8,
        out_specs=[vmem] * 10,
        out_shape=[
            shape((H, B, R, 128), bf16),
            shape((A, H // 2, R, 128), bf16),
            shape((H, R, W), bf16),
            shape((H, R, W), bf16),
            shape((H, B, D, 3 * hw + 128), bf16),
            shape((H, D, 3 * F), bf16),
            shape((H, A, 2, D, W), bf16),
            shape((8, W), f32),
            shape((H, R, 128), f32),
            shape((H, R, 128), f32),
        ],
        scratch_shapes=[
            pltpu.VMEM((H, D, 3 * hw + 128), bf16),
            pltpu.VMEM((H, D, 3 * hw + 128), bf16),
            pltpu.VMEM((H, D, 3 * F), bf16),
            pltpu.VMEM((A, H, R, 128), bf16),
            pltpu.VMEM((A, H // 2, R, 128), bf16),
            pltpu.VMEM((H, R, hw), f32),
            pltpu.VMEM((H, R, W), bf16),
            *[dma(H - 1)] * 8,
            *[dma(2 * H - 2)] * 2,
            *[dma(A - 1)] * 4,
            *[dma(A)] * 2,
            *line_sems(A),
            *line_sems(A),
        ],
        compiler_params=pltpu.CompilerParams(
            collective_id=0, has_side_effects=True, vmem_limit_bytes=48 * 2**20
        ),
        cost_estimate=pl.CostEstimate(flops=10**9, bytes_accessed=10**7, transcendentals=10**6),
        name="project",
    )(tokens, cotangent, w_qkv, gains, w_in, w_down, w_out, docs)


class LineGather:
    def __init__(self, view, own, h, part, share, parts, sems):
        self.view, self.own, self.h, self.part, self.share, self.parts = view, own, h, part, share, parts
        self.right_s, self.left_s, self.line_r, self.core_s, self.core_r = sems

    def _copy(self, source, block, side):
        if side == 0:
            sems, peer = (self.core_s, self.core_r), (self.h, self.part * 2 + 1 - self.share)
            target = self.view(block, self.share)
        else:
            sems = (self.right_s if side > 0 else self.left_s, self.line_r)
            peer = (self.h, (self.part + side) * 2 + self.share)
            target = self.view(block, self.share)
        return pltpu.make_async_remote_copy(
            src_ref=source,
            dst_ref=target,
            send_sem=sems[0].at[block],
            recv_sem=sems[1].at[block],
            device_id=peer,
            device_id_type=MESH,
        )

    def _can(self, side):
        return self.part < self.parts - 1 if side > 0 else self.part > 0

    def start(self):
        for side in (1, -1):

            @pl.when(self._can(side))
            def _():
                self._copy(self.own, self.part, side).start()

        self._copy(self.own, self.part, 0).start()

    def step(self, k):
        for side in (1, -1):
            block = self.part - side * k

            @pl.when((block >= 0) & (block < self.parts))
            def _():
                there = self.view(block, self.share)
                self._copy(there, block, side).wait_recv()

                @pl.when(self._can(side))
                def _():
                    self._copy(there, block, side).start()

                self._copy(there, block, 0).start()

    def arrive(self):
        for block in range(self.parts):
            self._copy(self.own, block, 0).wait_recv()

    def finish(self):
        for side in (1, -1):
            for block in range(self.parts):
                sent = block <= self.part if side > 0 else block >= self.part

                @pl.when(sent & self._can(side))
                def _():
                    self._copy(self.own, block, side).wait_send()

        for block in range(self.parts):
            self._copy(self.own, block, 0).wait_send()


def line_sems(parts):
    return [pltpu.SemaphoreType.DMA((parts,))] * 5


def norm_back(grad, hat, scale, gain):
    inner = grad * gain
    return scale * (
        inner
        - jnp.mean(inner, axis=-1, keepdims=True)
        - hat * jnp.mean(inner * hat, axis=-1, keepdims=True)
    )


class Reduce:
    def __init__(self, term, core_in, line_out, line_in, h, part, share, parts, sems):
        self.term, self.core_in, self.line_out, self.line_in = term, core_in, line_out, line_in
        self.h, self.part, self.share, self.parts = h, part, share, parts
        self.core_s, self.core_r, self.line_s, self.line_r = sems

    def _core(self):
        return pltpu.make_async_remote_copy(
            self.term.at[:, 1 - self.share],
            self.core_in,
            self.core_s.at[0],
            self.core_r.at[0],
            device_id=(self.h, self.part * 2 + 1 - self.share),
            device_id_type=MESH,
        )

    def _line(self, i):
        there = lax.rem(self.part + i, self.parts)
        return pltpu.make_async_remote_copy(
            self.line_out.at[i - 1],
            self.line_in.at[i - 1],
            self.line_s.at[i - 1],
            self.line_r.at[i - 1],
            device_id=(self.h, there * 2 + self.share),
            device_id_type=MESH,
        )

    def _sum(self, i):
        there = lax.rem(self.part + i, self.parts)
        return self.term[there, self.share].astype(jnp.float32) + self.core_in[there].astype(
            jnp.float32
        )

    def start(self):
        self._core().start()

    def middle(self):
        self._core().wait_recv()
        for i in range(1, self.parts):
            self.line_out[i - 1] = self._sum(i).astype(jnp.bfloat16)
            self._line(i).start()

    def close(self):
        total = self._sum(0)
        for i in range(1, self.parts):
            self._line(i).wait_recv()
            total += self.line_in[i - 1].astype(jnp.float32)
        return total

    def finish(self):
        self._core().wait_send()
        for i in range(1, self.parts):
            self._line(i).wait_send()


def reduce_scratch(parts, shape):
    return [
        pltpu.VMEM((parts, *shape), jnp.bfloat16),
        pltpu.VMEM((parts - 1, *shape), jnp.bfloat16),
        pltpu.VMEM((parts - 1, *shape), jnp.bfloat16),
        pltpu.SemaphoreType.DMA((1,)),
        pltpu.SemaphoreType.DMA((1,)),
        pltpu.SemaphoreType.DMA((parts - 1,)),
        pltpu.SemaphoreType.DMA((parts - 1,)),
    ]


class Swap:
    def __init__(self, out, landed, h, across, sems):
        self.out, self.landed, self.h, self.across = out, landed, h, across
        self.send_s, self.recv_s = sems

    def start(self, value):
        self.out[...] = value.astype(jnp.bfloat16)
        self.landed[self.h] = self.out[self.h]
        self.copies = [
            send(self.out.at[peer[0]], self.landed.at[self.h], self.send_s.at[i], self.recv_s.at[i], peer)
            for i, peer in enumerate(self.across)
        ]

    def arrive(self):
        for copy in self.copies:
            copy.wait_recv()

    def finish(self):
        for copy in self.copies:
            copy.wait_send()


def swap_scratch(heads, shape):
    return [
        pltpu.VMEM((heads, *shape), jnp.bfloat16),
        pltpu.VMEM((heads, *shape), jnp.bfloat16),
        pltpu.SemaphoreType.DMA((heads - 1,)),
        pltpu.SemaphoreType.DMA((heads - 1,)),
    ]


def feed_kernel(
    H, A, op, tok_all, cot_all, wo, wm_own, gain_rows,
    output, grad_middle, go, term, down_grad, mixed_own, gain_part,
    mx_in, mixed_all, wm_all, middle, normed, act, lift, g2_send, g2_in, g2_own, o_send, o_in, o_own, gm_send, term_down,
    mx_s, mx_r, ma_s, ma_r, g2_s, g2_r, o_s, o_r, gm_s, gm_r, *more,
):
    f32, bf16 = jnp.float32, jnp.bfloat16
    R, W = tok_all.shape[1:]
    B = 2 * A
    hw = W // H
    D = wm_own.shape[1]
    F = wm_own.shape[2] // 3
    h, b, part, share, across, along, beside = grid_peers(H, A)
    others = [
        (lax.rem(h + i, H), lax.rem(part + j, A) * 2 + share)
        for i in range(H)
        for j in range(A)
        if i or j
    ]
    meet([*others, beside])

    mx_copies = [
        send(op.at[peer[1] // 2], mx_in.at[part], mx_s.at[i], mx_r.at[i], peer)
        for i, peer in enumerate(along)
    ]
    gather = LineGather(
        lambda block, side: wm_all.at[:, block * 2 + side], wm_own, h, part, share, A, more[:5]
    )
    down_sum = Reduce(term_down, *more[5:8], h, part, share, A, more[8:12])
    down_swap = Swap(*more[12:14], h, across, more[14:16])
    gather.start()
    wm_all[:, b] = wm_own[...]
    mx_in[part] = op[part]
    for copy in mx_copies:
        copy.wait_recv()
    for run in range(H):
        side, at = run // (H // 2), run % (H // 2)
        for slab in range(hw // 128):
            left, right = mx_in[2 * slab, at].astype(f32), mx_in[2 * slab + 1, at].astype(f32)
            mixed_own[run, :, slab * 128 : (slab + 1) * 128] = join(left, side, right, side).astype(bf16)
    mixed_all[h] = mixed_own[...]
    ma_copies = [
        send(mixed_own, mixed_all.at[h], ma_s.at[i], ma_r.at[i], peer) for i, peer in enumerate(across)
    ]

    def project_out(source, first):
        def one(run, carried):
            before = tok_all[run].astype(f32) if first else middle[run]
            middle[run] = before + mm(mixed_all[source, run], wo[source])
            return carried

        lax.fori_loop(0, H, one, 0)

    project_out(h, True)
    gather.step(1)
    for i, copy in enumerate(ma_copies):
        copy.wait_recv()
        project_out(lax.rem(h + H - 1 - i, H), False)

    def norm_run(run, carried):
        hat, unused = standardize(middle[run])
        normed[run] = (hat * gain_rows[1:2, :]).astype(bf16)
        return carried

    lax.fori_loop(0, H, norm_run, 0)
    for k in range(2, A):
        gather.step(k)
    gather.arrive()

    def block(chunk):
        return wm_all[chunk].reshape(B * D, 3 * F)

    def feed_run(i, carried):
        run = lax.rem(h + 1 + i, H)
        lifted = jnp.zeros((R, 2 * F), f32)
        grad_act = jnp.zeros((R, F), f32)
        for chunk in range(H):
            lanes = slice(chunk * hw, (chunk + 1) * hw)
            weights = block(chunk)
            lifted += mm(normed[run, :, lanes], weights[:, : 2 * F])
            grad_act += mm(cot_all[run, :, lanes], weights[:, 2 * F :])
        gate, up = lifted[:, :F], lifted[:, F:]
        below = 0.5 + 0.5 * lax.erf(gate * (0.5**0.5))
        slope = below + gate * jnp.exp(-0.5 * gate * gate) * ((2.0 * np.pi) ** -0.5)
        act[run] = (gate * below * up).astype(bf16)
        lift[run, :, :F] = (grad_act * up * slope).astype(bf16)
        lift[run, :, F:] = (grad_act * gate * below).astype(bf16)

        for chunk in range(H):
            lanes = slice(chunk * hw, (chunk + 1) * hw)
            g2_own[:, lanes] = mm(lift[run], block(chunk)[:, : 2 * F], NT)

        @pl.when(i < H - 1)
        def _():
            g2_send[i] = g2_own[...].astype(bf16)
            pltpu.make_async_remote_copy(
                g2_send.at[i], g2_in.at[i], g2_s.at[i], g2_r.at[i], device_id=(run, b), device_id_type=MESH
            ).start()

        return carried

    lax.fori_loop(0, H, feed_run, 0)

    def down_chunk(chunk, carried):
        lanes = pl.ds(pl.multiple_of(chunk * hw, hw), hw)
        left = cot_all[:, :, lanes].reshape(H * R, hw)
        grads = mm(left, act[...].reshape(H * R, F), TN).astype(bf16)
        term_down[:, :, chunk] = grads.reshape(A, 2, D, F)
        return carried

    lax.fori_loop(0, H, down_chunk, 0)
    down_sum.start()

    def out_run(i, carried):
        run = lax.rem(h + 1 + i, H)
        for chunk in range(H):
            lanes = slice(chunk * hw, (chunk + 1) * hw)
            o_own[:, lanes] = mm(act[run], block(chunk)[:, 2 * F :], NT)

        @pl.when(i < H - 1)
        def _():
            o_send[i] = o_own[...].astype(bf16)
            pltpu.make_async_remote_copy(
                o_send.at[i], o_in.at[i], o_s.at[i], o_r.at[i], device_id=(run, b), device_id_type=MESH
            ).start()

        return carried

    lax.fori_loop(0, H, out_run, 0)

    down_sum.middle()

    def rest(sent, landed, send_sem, recv_sem, i):
        return pltpu.make_async_remote_copy(
            sent.at[i], landed.at[i], send_sem.at[i], recv_sem.at[i], device_id=across[i], device_id_type=MESH
        )

    grad = g2_own[...]
    for i in range(H - 1):
        rest(g2_send, g2_in, g2_s, g2_r, i).wait_recv()
        grad += g2_in[i].astype(f32)
    hat, scale = standardize(middle[h])
    gain_part[...] = jnp.broadcast_to(jnp.sum(grad * hat, axis=0, keepdims=True), gain_part.shape)
    total = cot_all[h].astype(f32) + norm_back(grad, hat, scale, gain_rows[1:2, :])
    grad_middle[...] = total
    branch = total.astype(bf16)
    gm_copies = []
    for i in range(H):
        place = lax.rem(h + i, H)
        mixed_grad = mm(branch, wo[place], NT)
        for a in range(A):
            slab = mixed_grad[:, a // 2 * 128 : a // 2 * 128 + 128]
            gm_send[i, a] = join(slab[: R // 2], a % 2, slab[R // 2 :], a % 2).astype(bf16)
        for j in range(A):
            there = lax.rem(part + j, A)
            if i or j:
                n = i * A + j
                gm_copies.append(
                    send(gm_send.at[i, there], go.at[part, h], gm_s.at[n], gm_r.at[n], (place, there * 2 + share))
                )
            else:
                go[part, h] = gm_send[0, part]

    def term_chunk(chunk, carried):
        lanes = pl.ds(pl.multiple_of(chunk * hw, hw), hw)
        left = normed[:, :, lanes].reshape(H * R, hw)
        grads = mm(left, lift[...].reshape(H * R, 2 * F), TN).astype(bf16)
        term[:, :, chunk] = grads.reshape(A, 2, D, 2 * F)
        return carried

    lax.fori_loop(0, H, term_chunk, 0)
    down_swap.start(down_sum.close())
    result = middle[h] + o_own[...]
    for i in range(H - 1):
        rest(o_send, o_in, o_s, o_r, i).wait_recv()
        result += o_in[i].astype(f32)
    output[...] = result.astype(bf16)
    for copy in gm_copies:
        copy.wait_recv()
    down_swap.arrive()
    unit = (
        lax.broadcasted_iota(jnp.int32, (D, D), 0) == lax.broadcasted_iota(jnp.int32, (D, D), 1)
    ).astype(bf16)
    for place in range(H):
        down_grad[place * F : (place + 1) * F, :] = mm(down_swap.landed[place], unit, TN)
    for copy in [*mx_copies, *ma_copies, *gm_copies]:
        copy.wait_send()
    for i in range(H - 1):
        rest(g2_send, g2_in, g2_s, g2_r, i).wait_send()
        rest(o_send, o_in, o_s, o_r, i).wait_send()
    gather.finish()
    down_sum.finish()
    down_swap.finish()


def feed(op, tok_all, cot_all, wo, wm_own, gain_rows):
    A, half, R, lanes = op.shape
    H = 2 * half
    W = tok_all.shape[-1]
    B = 2 * A
    hw = W // H
    D = wm_own.shape[1]
    F = wm_own.shape[2] // 3
    f32, bf16 = jnp.float32, jnp.bfloat16
    shape = jax.ShapeDtypeStruct
    dma = lambda count: pltpu.SemaphoreType.DMA((count,))
    vmem = pl.BlockSpec(memory_space=pltpu.VMEM)
    return pl.pallas_call(
        partial(feed_kernel, H, A),
        in_specs=[vmem] * 6,
        out_specs=[vmem] * 7,
        out_shape=[
            shape((R, W), bf16),
            shape((R, W), f32),
            shape((A, H, R // 2, 128), bf16),
            shape((A, 2, H, D, 2 * F), bf16),
            shape((H * F, D), f32),
            shape((H, R, hw), bf16),
            shape((8, W), f32),
        ],
        scratch_shapes=[
            pltpu.VMEM((A, half, R, 128), bf16),
            pltpu.VMEM((H, H, R, hw), bf16),
            pltpu.VMEM((H, B, D, 3 * F), bf16),
            pltpu.VMEM((H, R, W), f32),
            pltpu.VMEM((H, R, W), bf16),
            pltpu.VMEM((H, R, F), bf16),
            pltpu.VMEM((H, R, 2 * F), bf16),
            *[pltpu.VMEM((H - 1, R, W), bf16), pltpu.VMEM((H - 1, R, W), bf16), pltpu.VMEM((R, W), f32)] * 2,
            pltpu.VMEM((H, A, R // 2, 128), bf16),
            pltpu.VMEM((A, 2, H, D, F), bf16),
            *[dma(A - 1)] * 2,
            *[dma(H - 1)] * 6,
            *[dma(H * A)] * 2,
            *line_sems(A),
            *reduce_scratch(A, (H, D, F)),
            *swap_scratch(H, (D, F)),
        ],
        compiler_params=pltpu.CompilerParams(
            collective_id=1, has_side_effects=True, vmem_limit_bytes=56 * 2**20
        ),
        cost_estimate=pl.CostEstimate(flops=6 * 10**9, bytes_accessed=10**7, transcendentals=10**6),
        name="feed",
    )(op, tok_all, cot_all, wo, wm_own, gain_rows)


def finish_kernel(
    H, A, dqp, dkv, tok_all, wq_all, cos_all, sin_all, gain_rows, mixed_own, grad_middle, gain_part, term_in,
    input_grad, qkv_grad, out_grad, in_grad, gain_grads,
    dk_in, dkv_send, dkv_in, dq_in, branch, branch_all, gp, normed, g1_send, g1_in, g1_own, term_out, term_qkv, term_gain,
    dk_s, dk_r, dz_s, dz_r, dq_s, dq_r, br_s, br_r, g1_s, g1_r, *rest,
):
    f32, bf16 = jnp.float32, jnp.bfloat16
    R, W = tok_all.shape[1:]
    B = 2 * A
    hw = W // H
    D = term_in.shape[3]
    F = term_in.shape[4] // 2
    h, b, part, share, across, along, beside = grid_peers(H, A)

    def reducer(n, term):
        scratch = rest[7 * n : 7 * n + 7]
        return Reduce(term, *scratch[:3], h, part, share, A, scratch[3:])

    def swapper(n):
        scratch = rest[28 + 4 * n : 32 + 4 * n]
        return Swap(*scratch[:2], h, across, scratch[2:])

    in_sum, out_sum = reducer(0, term_in), reducer(1, term_out)
    qkv_sum, gain_sum = reducer(2, term_qkv), reducer(3, term_gain)
    in_swap, qkv_swap, gain_swap = swapper(0), swapper(1), swapper(2)
    meet([*across, *along, beside])

    order = [*[lax.rem(part + i, A) for i in range(1, A)], part]
    dk_copies = [
        send(dkv.at[:, there * 2 + 1 - share], dk_in.at[i], dk_s.at[i], dk_r.at[i], beside)
        for i, there in enumerate(order)
    ]
    dq_copies = [
        send(dqp.at[peer[1] // 2], dq_in.at[part], dq_s.at[i], dq_r.at[i], peer)
        for i, peer in enumerate(along)
    ]
    dq_in[part] = dqp[part]
    branch[...] = grad_middle[...].astype(bf16)
    br_copies = [
        send(branch, branch_all.at[h], br_s.at[i], br_r.at[i], peer) for i, peer in enumerate(across)
    ]
    branch_all[h] = branch[...]
    in_sum.start()
    dz_copies = []
    for i, there in enumerate(order):
        dk_copies[i].wait_recv()
        summed = dkv[:, there * 2 + share].astype(f32) + dk_in[i].astype(f32)
        if i < A - 1:
            dkv_send[i] = summed.astype(bf16)
            dz_copies.append(
                send(dkv_send.at[i], dkv_in.at[part], dz_s.at[i], dz_r.at[i], along[i])
            )
        else:
            dkv_in[part] = summed.astype(bf16)
    in_sum.middle()

    def norm_run(run, carried):
        hat, unused = standardize(tok_all[run].astype(f32))
        normed[run] = (hat * gain_rows[0:1, :]).astype(bf16)
        return carried

    lax.fori_loop(0, H, norm_run, 0)
    for copy in br_copies:
        copy.wait_recv()

    def out_tile(n, carried):
        lanes = pl.ds(pl.multiple_of(n * hw, hw), hw)
        grads = mm(mixed_own[...].reshape(H * R, hw), branch_all[:, :, lanes].reshape(H * R, hw), TN)
        term_out[:, :, :, lanes] = grads.astype(bf16).reshape(A, 2, D, hw)
        return carried

    lax.fori_loop(0, W // hw, out_tile, 0)
    out_sum.start()
    for copy in [*dq_copies, *dz_copies]:
        copy.wait_recv()
    for run in range(H):
        side, at = run // (H // 2), run % (H // 2)
        cosine, sine = cos_all[run], sin_all[run]
        for slab in range(hw // 128):
            lanes = slab * 128
            left, right = dq_in[2 * slab, at].astype(f32), dq_in[2 * slab + 1, at].astype(f32)
            gp[run, :, lanes : lanes + 128] = turn(
                join(left, side, right, side), cosine, sine, True
            ).astype(bf16)
            left, right = dkv_in[2 * slab, run].astype(f32), dkv_in[2 * slab + 1, run].astype(f32)
            gp[run, :, hw + lanes : hw + lanes + 128] = turn(
                join(left, 0, right, 0), cosine, sine, True
            ).astype(bf16)
            gp[run, :, 2 * hw + lanes : 2 * hw + lanes + 128] = join(left, 1, right, 1).astype(bf16)

    def block(chunk):
        return wq_all[chunk].reshape(B * D, 3 * hw + 128)

    def term_chunk(chunk, carried):
        lanes = pl.ds(pl.multiple_of(chunk * hw, hw), hw)
        left = normed[:, :, lanes].reshape(H * R, hw)
        grads = mm(left, gp[...].reshape(H * R, 3 * hw), TN).astype(bf16)
        term_qkv[:, :, chunk] = grads.reshape(A, 2, D, 3 * hw)
        return carried

    lax.fori_loop(0, H, term_chunk, 0)
    qkv_sum.start()

    def one_run(i, carried):
        run = lax.rem(h + 1 + i, H)
        for chunk in range(H):
            lanes = slice(chunk * hw, (chunk + 1) * hw)
            g1_own[:, lanes] = mm(gp[run], block(chunk)[:, : 3 * hw], NT)

        @pl.when(i < H - 1)
        def _():
            g1_send[i] = g1_own[...].astype(bf16)
            pltpu.make_async_remote_copy(
                g1_send.at[i], g1_in.at[i], g1_s.at[i], g1_r.at[i], device_id=(run, b), device_id_type=MESH
            ).start()

        return carried

    lax.fori_loop(0, H, one_run, 0)
    qkv_sum.middle()
    out_sum.middle()

    g1_copies = [
        pltpu.make_async_remote_copy(
            g1_send.at[i], g1_in.at[i], g1_s.at[i], g1_r.at[i], device_id=across[i], device_id_type=MESH
        )
        for i in range(H - 1)
    ]
    grad = g1_own[...]
    for i in range(H - 1):
        g1_copies[i].wait_recv()
        grad += g1_in[i].astype(f32)
    hat, scale = standardize(tok_all[h].astype(f32))
    gain_part_one = jnp.sum(grad * hat, axis=0, keepdims=True)
    input_grad[...] = grad_middle[...] + norm_back(grad, hat, scale, gain_rows[0:1, :])
    row = lax.broadcasted_iota(jnp.int32, (8, W), 0)
    rows = jnp.where(row == 0, gain_part_one, jnp.where(row == 1, gain_part[...], 0.0))
    pick = (
        lax.broadcasted_iota(jnp.int32, (8, 128), 0) == lax.broadcasted_iota(jnp.int32, (8, 128), 1)
    ).astype(bf16)
    for chunk in range(H):
        gain_columns = mm(rows[:, chunk * hw : (chunk + 1) * hw].astype(bf16), pick, TN)
        term_gain[:, :, chunk] = gain_columns.astype(bf16).reshape(A, 2, D, 128)
    gain_sum.start()
    in_swap.start(in_sum.close())
    gain_sum.middle()
    out_grad[...] = out_sum.close()
    qkv_swap.start(qkv_sum.close())
    gain_swap.start(gain_sum.close())
    in_swap.arrive()
    for place in range(H):
        in_grad[:, place * F : (place + 1) * F] = in_swap.landed[place, :, :F].astype(f32)
        in_grad[:, (H + place) * F : (H + place + 1) * F] = in_swap.landed[place, :, F:].astype(f32)
    qkv_swap.arrive()
    for place in range(H):
        for j in range(3):
            qkv_grad[:, j * W + place * hw : j * W + (place + 1) * hw] = qkv_swap.landed[
                place, :, j * hw : (j + 1) * hw
            ].astype(f32)
    gain_swap.arrive()
    total = gain_swap.landed[0].astype(f32)
    for place in range(1, H):
        total += gain_swap.landed[place].astype(f32)
    gain_grads[...] = total
    for copy in [*dk_copies, *dq_copies, *br_copies, *dz_copies, *g1_copies]:
        copy.wait_send()
    for part_of in (in_sum, out_sum, qkv_sum, gain_sum, in_swap, qkv_swap, gain_swap):
        part_of.finish()


def finish(dqp, dkv, tok_all, wq_all, cos_all, sin_all, gain_rows, mixed, grad_middle, gain_part, term_in):
    A, half, R, lanes = dqp.shape
    H = 2 * half
    W = tok_all.shape[-1]
    B = 2 * A
    hw = W // H
    D = term_in.shape[3]
    F = term_in.shape[4] // 2
    f32, bf16 = jnp.float32, jnp.bfloat16
    shape = jax.ShapeDtypeStruct
    dma = lambda count: pltpu.SemaphoreType.DMA((count,))
    vmem = pl.BlockSpec(memory_space=pltpu.VMEM)
    buffer = lambda *sizes: pltpu.VMEM(sizes, bf16)
    return pl.pallas_call(
        partial(finish_kernel, H, A),
        in_specs=[vmem] * 11,
        out_specs=[vmem] * 5,
        out_shape=[
            shape((R, W), f32),
            shape((D, 3 * W), f32),
            shape((D, W), f32),
            shape((D, 2 * H * F), f32),
            shape((D, 128), f32),
        ],
        scratch_shapes=[
            buffer(A, H, R, 128),
            buffer(A - 1, H, R, 128),
            buffer(A, H, R, 128),
            buffer(A, half, R, 128),
            buffer(R, W),
            buffer(H, R, W),
            buffer(H, R, 3 * hw),
            buffer(H, R, W),
            buffer(H - 1, R, W),
            buffer(H - 1, R, W),
            pltpu.VMEM((R, W), f32),
            buffer(A, 2, D, W),
            buffer(A, 2, H, D, 3 * hw),
            buffer(A, 2, H, D, 128),
            *[dma(A)] * 2,
            *[dma(A - 1)] * 4,
            *[dma(H - 1)] * 4,
            *reduce_scratch(A, (H, D, 2 * F)),
            *reduce_scratch(A, (D, W)),
            *reduce_scratch(A, (H, D, 3 * hw)),
            *reduce_scratch(A, (H, D, 128)),
            *swap_scratch(H, (D, 2 * F)),
            *swap_scratch(H, (D, 3 * hw)),
            *swap_scratch(H, (D, 128)),
        ],
        compiler_params=pltpu.CompilerParams(
            collective_id=2, has_side_effects=True, vmem_limit_bytes=56 * 2**20
        ),
        cost_estimate=pl.CostEstimate(flops=2 * 10**9, bytes_accessed=10**7, transcendentals=10**5),
        name="finish",
    )(dqp, dkv, tok_all, wq_all, cos_all, sin_all, gain_rows, mixed, grad_middle, gain_part, term_in)


def per_device_split(
    tokens, attn_gain, w_qkv, w_attn_out, mlp_gain, w_in, w_mlp_out, doc_lengths, cotangent
):
    R, W = tokens.shape
    H, B = lax.axis_size("head"), lax.axis_size("blk")
    A = W // HEAD_DIM // H
    G = B // A
    hw = W // H
    D = w_qkv.shape[0]
    F = w_mlp_out.shape[0] // H
    T = H * B * R
    N = H * R
    h, b = lax.axis_index("head"), lax.axis_index("blk")
    f32, bf16 = jnp.float32, jnp.bfloat16
    part_groups = [[a * G + g for a in range(A)] for g in range(G)]
    share_groups = [[a * G + g for g in range(G)] for a in range(A)]

    ends = jnp.cumsum(doc_lengths)
    places = jnp.arange(T, dtype=jnp.int32)
    passed = places[:, None] >= ends[None, :]
    docs = jnp.sum(passed.astype(jnp.int32), axis=1)
    starts = jnp.sum(jnp.where(passed, doc_lengths[None, :], 0), axis=1)
    stops = jnp.min(jnp.where(passed, T, ends[None, :]), axis=1)
    runs = (T // R,)
    run_docs = docs.reshape(H, A, G, R)
    run_lo = starts.reshape(H, A, G, R)[..., 0]
    run_hi = stops.reshape(H, A, G, R)[..., R - 1]
    g = b % G
    pick = lambda v: lax.dynamic_index_in_dim(v, g, 2, keepdims=False)
    qdoc = pick(run_docs).reshape(H * A // 2, 2 * R, 1)
    lo = pick(run_lo).reshape(H * A // 2, 2)[:, 0] // KEY_TILE
    hi = (pick(run_hi).reshape(H * A // 2, 2)[:, 1] + KEY_TILE - 1) // KEY_TILE
    span = jnp.stack([lo, hi], axis=1).astype(jnp.int32)
    kdoc = docs.reshape(T // KEY_TILE, KEY_TILE)
    own = lambda v: lax.dynamic_index_in_dim(v.reshape(H, B, R), b, 1, keepdims=False).reshape(N)
    gains = jnp.pad(jnp.stack([attn_gain, mlp_gain], axis=1), ((0, 0), (0, 126)))
    kv, qp, tok_all, cot_all, wq, wm, wo, gain_rows, cos_all, sin_all = project(
        tokens, cotangent, w_qkv, gains, w_in, w_mlp_out, w_attn_out, jnp.stack([ends, doc_lengths])
    )
    kv = kv.reshape(T, 2 * HEAD_DIM)
    op, lse = attend(span, qp, kv, qdoc, kdoc)
    output, grad_middle, gp, term_in, down_grad, mixed, gain_part = feed(
        op, tok_all, cot_all, wo.reshape(H, hw, W), wm, gain_rows
    )
    dqp, dkv = attend_back(span, qp, gp, op, lse, kv, qdoc, kdoc)
    input_grad, qkv_grad, out_grad, in_grad, gain_grads = finish(
        dqp, dkv.reshape(H, B, R, 128), tok_all, wq, cos_all, sin_all, gain_rows, mixed, grad_middle, gain_part, term_in
    )
    return (
        output,
        input_grad,
        gain_grads[:, 0],
        qkv_grad,
        out_grad,
        gain_grads[:, 1],
        in_grad,
        down_grad,
    )


def per_device(tokens, attn_gain, w_qkv, *rest):
    heads, blocks = lax.axis_size("head"), lax.axis_size("blk")
    parts = tokens.shape[1] // HEAD_DIM // heads
    fits = (
        blocks % parts == 0
        and blocks // parts == 2
        and parts % 2 == 0
        and heads % 2 == 0
        and w_qkv.shape[0] % 16 == 0
        and tokens.shape[0] % 128 == 0
    )
    chosen = per_device_split if fits else per_device_general
    return chosen(tokens, attn_gain, w_qkv, *rest)


def solution(mesh):
    placed = (
        P(("head", "blk"), None),
        P(("head", "blk")),
        P(("head", "blk"), None),
        P(("head", "blk"), None),
        P(("head", "blk")),
        P(("head", "blk"), None),
        P(None, ("head", "blk")),
        P(),
        P(("head", "blk"), None),
    )
    return jax.shard_map(
        per_device,
        mesh=mesh,
        in_specs=placed,
        out_specs=(
            P(("head", "blk"), None),
            P(("head", "blk"), None),
            P(("head", "blk")),
            P(("head", "blk"), None),
            P(("head", "blk"), None),
            P(("head", "blk")),
            P(("head", "blk"), None),
            P(None, ("head", "blk")),
        ),
        check_vma=False,
    )
```

```python
from functools import partial

import jax
import jax.numpy as jnp
import numpy as np
from jax import lax
from jax.experimental import pallas as pl
from jax.experimental.pallas import tpu as pltpu
from jax.sharding import PartitionSpec as P

HEAD_DIM = 64


norm_eps = 1e-05
rope_base = 160000.0
neg_large = -1e30


def from_behind(value, axis, by):
    devices = lax.axis_size(axis)
    return lax.ppermute(value, axis, [(i, (i + by) % devices) for i in range(devices)])


def layer_norm(values, gain):
    center = values - jnp.mean(values, axis=-1, keepdims=True)
    spread = jnp.mean(center * center, axis=-1, keepdims=True)
    return center * lax.rsqrt(spread + norm_eps) * gain


def rope_tables(places, head_size):
    half = head_size // 2
    freqs = rope_base ** (-(jnp.arange(half, dtype=jnp.float32) * 2.0) / head_size)
    angles = places.astype(jnp.float32)[:, None] * freqs[None, :]
    angles = jnp.concatenate([angles, angles], axis=1)
    return (jnp.cos(angles), jnp.sin(angles))


def rotate(values, cosine, sine):
    count = values.shape[0]
    head_size = cosine.shape[1]
    half = head_size // 2
    split = values.reshape(count, -1, head_size)
    turned = jnp.concatenate([-split[..., half:], split[..., :half]], axis=-1)
    return (split * cosine[:, None, :] + turned * sine[:, None, :]).reshape(count, -1)


def rotate_pair(query, keys, cosine, sine):
    return (rotate(query, cosine, sine), rotate(keys, cosine, sine))


def doc_numbers(places, ends, lengths):
    passed = places[:, None] >= ends[None, :]
    numbers = jnp.sum(passed.astype(jnp.int32), axis=1)
    offset = jnp.sum(jnp.where(passed, lengths[None, :], 0), axis=1)
    return (numbers, places - offset)


def gelu_gate(lifted):
    half = lifted.shape[1] // 2
    return jax.nn.gelu(lifted[:, :half], approximate=False) * lifted[:, half:]


def tile_scores(query, keys):
    heads = query.shape[1] // HEAD_DIM
    query_split = query.reshape(query.shape[0], heads, HEAD_DIM)
    key_split = keys.reshape(keys.shape[0], heads, HEAD_DIM)
    return jnp.einsum(
        "qhd,khd->hqk", query_split, key_split, preferred_element_type=jnp.float32
    ) * HEAD_DIM ** (-0.5)


def unchanged(state):
    return state


def forward_tile(state, query, keys, values, mask):
    top, total, running = state
    count = query.shape[0]
    heads = top.shape[0]
    scores = tile_scores(query, keys)
    filled = jnp.where(mask[None], scores, neg_large)
    new_top = jnp.maximum(top, jnp.max(filled, axis=-1))
    weights = jnp.where(mask[None], jnp.exp(scores - new_top[:, :, None]), 0.0)
    factor = jnp.exp(top - new_top)
    new_total = total * factor + jnp.sum(weights, axis=-1)
    mixed = jnp.einsum(
        "hqk,khd->qhd",
        weights.astype(jnp.bfloat16),
        values.reshape(-1, heads, HEAD_DIM),
        preferred_element_type=jnp.float32,
    )
    new_running = running.reshape(count, heads, HEAD_DIM) * factor.T[:, :, None] + mixed
    return (new_top, new_total, new_running.reshape(count, heads * HEAD_DIM))


def backward_tile(carry, query, keys, values, mask, norm_log, grad_out, delta):
    query_grad, run_grads = carry
    count = query.shape[0]
    columns = keys.shape[0]
    heads = norm_log.shape[0]
    scores = tile_scores(query, keys)
    probs = jnp.where(mask[None], jnp.exp(scores - norm_log[:, :, None]), 0.0)
    grad_split = grad_out.reshape(count, heads, HEAD_DIM)
    value_split = values.reshape(columns, heads, HEAD_DIM)
    grad_values = jnp.einsum(
        "hqk,qhd->khd", probs.astype(jnp.bfloat16), grad_split, preferred_element_type=jnp.float32
    )
    grad_probs = jnp.einsum(
        "qhd,khd->hqk", grad_split, value_split, preferred_element_type=jnp.float32
    )
    grad_scores = (probs * (grad_probs - delta[:, :, None])).astype(jnp.bfloat16)
    grad_query = jnp.einsum(
        "hqk,khd->qhd",
        grad_scores,
        keys.reshape(columns, heads, HEAD_DIM),
        preferred_element_type=jnp.float32,
    ) * HEAD_DIM ** (-0.5)
    grad_keys = jnp.einsum(
        "hqk,qhd->khd",
        grad_scores,
        query.reshape(count, heads, HEAD_DIM),
        preferred_element_type=jnp.float32,
    ) * HEAD_DIM ** (-0.5)
    added = jnp.stack([grad_keys.reshape(columns, -1), grad_values.reshape(columns, -1)])
    return (query_grad + grad_query.reshape(count, -1), run_grads + added)


def per_device_general(
    tokens, attn_gain, w_qkv, w_attn_out, mlp_gain, w_in, w_mlp_out, doc_lengths, cotangent
):
    own_rows = tokens.shape[0]
    width = tokens.shape[1]
    head_count = lax.axis_size("head")
    cycle_count = lax.axis_size("blk")
    head_place = lax.axis_index("head")
    cycle_place = lax.axis_index("blk")
    group_rows = head_count * own_rows
    block_runs = min(head_count, max(1, 512 // own_rows))
    block_count = head_count // block_runs
    block_rows = block_runs * own_rows
    doc_ends = jnp.cumsum(doc_lengths)
    counter = jnp.arange(own_rows, dtype=jnp.int32)
    own_places = (head_place * cycle_count + cycle_place) * own_rows + counter
    unused_docs, own_positions = doc_numbers(own_places, doc_ends, doc_lengths)
    cosine, sine = rope_tables(own_positions, HEAD_DIM)
    run_numbers = jnp.arange(head_count, dtype=jnp.int32)
    query_places = (
        (run_numbers[:, None] * cycle_count + cycle_place) * own_rows + counter[None, :]
    ).reshape(group_rows)
    query_docs, unused_positions = doc_numbers(query_places, doc_ends, doc_lengths)
    params = (
        lax.all_gather(attn_gain, ("head", "blk"), axis=0, tiled=True),
        lax.all_gather(w_qkv, ("head", "blk"), axis=0, tiled=True),
        lax.all_gather(w_attn_out, ("head", "blk"), axis=0, tiled=True),
        lax.all_gather(mlp_gain, ("head", "blk"), axis=0, tiled=True),
        lax.all_gather(w_in, ("head", "blk"), axis=0, tiled=True),
        lax.all_gather(w_mlp_out, ("head", "blk"), axis=1, tiled=True),
    )
    gain_one, full_qkv, full_attn_out, gain_two, full_in, full_mlp_out = params
    inputs = tokens.astype(jnp.float32)
    normed_one, norm_one_pull = jax.vjp(layer_norm, inputs, gain_one.astype(jnp.float32))
    normed_low = normed_one.astype(jnp.bfloat16)
    projected = jnp.dot(normed_low, full_qkv, preferred_element_type=jnp.float32)
    turned, rope_pull = jax.vjp(
        partial(rotate_pair, cosine=cosine, sine=sine),
        projected[:, :width],
        projected[:, width : 2 * width],
    )
    stacked = jnp.stack(
        [
            turned[0].astype(jnp.bfloat16),
            turned[1].astype(jnp.bfloat16),
            projected[:, 2 * width :].astype(jnp.bfloat16),
        ]
    )
    regrouped = lax.all_to_all(stacked, "head", split_axis=2, concat_axis=1, tiled=True)
    query_heads = regrouped[0]
    key_heads = regrouped[1]
    value_heads = regrouped[2]
    head_width = query_heads.shape[1]
    heads_here = head_width // HEAD_DIM

    def key_docs_at(first):
        places = (
            first % group_rows // own_rows * cycle_count + first // group_rows
        ) * own_rows + counter
        found, unused = doc_numbers(places, doc_ends, doc_lengths)
        return found

    def block_live(block, key_docs):
        block_docs = query_docs[block * block_rows : (block + 1) * block_rows]
        live = jnp.maximum(jnp.min(block_docs), jnp.min(key_docs)) <= jnp.minimum(
            jnp.max(block_docs), jnp.max(key_docs)
        )
        return (block_docs[:, None] == key_docs[None, :], live)

    def fold_forward(state, piece):
        key_part, value_part = piece

        def fold_one_run(number, carried):
            first = number * own_rows
            key_docs = key_docs_at(first)
            keys = lax.dynamic_slice_in_dim(key_part, number * own_rows, own_rows, 0)
            values = lax.dynamic_slice_in_dim(value_part, number * own_rows, own_rows, 0)
            updated = []
            for block in range(block_count):
                mask, live = block_live(block, key_docs)
                query = query_heads[block * block_rows : (block + 1) * block_rows]
                advance = partial(forward_tile, query=query, keys=keys, values=values, mask=mask)
                updated.append(lax.cond(live, advance, unchanged, carried[block]))
            return tuple(updated)

        return lax.fori_loop(0, key_part.shape[0] // own_rows, fold_one_run, state)

    def fresh_state():
        return tuple(
            (
                (
                    jnp.full((heads_here, block_rows), neg_large, jnp.float32),
                    jnp.zeros((heads_here, block_rows), jnp.float32),
                    jnp.zeros((block_rows, head_width), jnp.float32),
                )
                for block in range(block_count)
            )
        )

    def finish(state):
        outputs = []
        logs = []
        for top, total, running in state:
            scaled = running.reshape(block_rows, heads_here, HEAD_DIM) / total.T[:, :, None]
            outputs.append(scaled.reshape(block_rows, head_width))
            logs.append(top + jnp.log(total))
        return (
            jnp.concatenate(outputs, axis=0).astype(jnp.bfloat16),
            jnp.concatenate(logs, axis=1),
        )

    state = fold_forward(
        fresh_state(),
        (
            lax.all_gather(key_heads, "blk", axis=0, tiled=True),
            lax.all_gather(value_heads, "blk", axis=0, tiled=True),
        ),
    )
    out_heads, norm_log = finish(state)
    out_tokens = lax.all_to_all(out_heads, "head", split_axis=0, concat_axis=1, tiled=True)
    middle = inputs + jnp.dot(out_tokens, full_attn_out, preferred_element_type=jnp.float32)
    normed_two, norm_two_pull = jax.vjp(layer_norm, middle, gain_two.astype(jnp.float32))
    normed_two_low = normed_two.astype(jnp.bfloat16)
    lifted = jnp.dot(normed_two_low, full_in, preferred_element_type=jnp.float32)
    activated, geglu_pull = jax.vjp(gelu_gate, lifted)
    activated_low = activated.astype(jnp.bfloat16)
    output = (
        middle + jnp.dot(activated_low, full_mlp_out, preferred_element_type=jnp.float32)
    ).astype(jnp.bfloat16)
    params = (
        lax.all_gather(attn_gain, ("head", "blk"), axis=0, tiled=True),
        lax.all_gather(w_qkv, ("head", "blk"), axis=0, tiled=True),
        lax.all_gather(w_attn_out, ("head", "blk"), axis=0, tiled=True),
        lax.all_gather(mlp_gain, ("head", "blk"), axis=0, tiled=True),
        lax.all_gather(w_in, ("head", "blk"), axis=0, tiled=True),
        lax.all_gather(w_mlp_out, ("head", "blk"), axis=1, tiled=True),
    )
    gain_one, full_qkv, full_attn_out, gain_two, full_in, full_mlp_out = params
    grad_act = jnp.einsum("td,fd->tf", cotangent, full_mlp_out, preferred_element_type=jnp.float32)
    grad_lifted = geglu_pull(grad_act)[0].astype(jnp.bfloat16)
    grad_normed_two = jnp.einsum(
        "tf,df->td", grad_lifted, full_in, preferred_element_type=jnp.float32
    )
    grad_middle_part, grad_gain_two = norm_two_pull(grad_normed_two)
    grad_middle = cotangent.astype(jnp.float32) + grad_middle_part
    grad_branch = grad_middle.astype(jnp.bfloat16)
    grad_mixed = jnp.einsum(
        "te,de->td", grad_branch, full_attn_out, preferred_element_type=jnp.float32
    ).astype(jnp.bfloat16)
    grad_heads = lax.all_to_all(grad_mixed, "head", split_axis=1, concat_axis=0, tiled=True)
    state = fold_forward(
        fresh_state(),
        (
            lax.all_gather(key_heads, "blk", axis=0, tiled=True),
            lax.all_gather(value_heads, "blk", axis=0, tiled=True),
        ),
    )
    out_heads, norm_log = finish(state)
    delta = jnp.einsum(
        "qhd,qhd->hq",
        grad_heads.reshape(group_rows, heads_here, HEAD_DIM).astype(jnp.float32),
        out_heads.reshape(group_rows, heads_here, HEAD_DIM).astype(jnp.float32),
    )

    def piece_backward(query_grads, key_part, value_part, start):
        piece_rows = key_part.shape[0]

        def piece_one_run(number, carried):
            query_now, piece_grads = carried
            first = start + number * own_rows
            key_docs = key_docs_at(first)
            keys = lax.dynamic_slice_in_dim(key_part, number * own_rows, own_rows, 0)
            values = lax.dynamic_slice_in_dim(value_part, number * own_rows, own_rows, 0)
            run_grads = jnp.zeros((2, own_rows, head_width), jnp.float32)
            updated = []
            for block in range(block_count):
                mask, live = block_live(block, key_docs)
                lower = block * block_rows
                upper = (block + 1) * block_rows
                advance = partial(
                    backward_tile,
                    query=query_heads[lower:upper],
                    keys=keys,
                    values=values,
                    mask=mask,
                    norm_log=norm_log[:, lower:upper],
                    grad_out=grad_heads[lower:upper],
                    delta=delta[:, lower:upper],
                )
                new_query, run_grads = lax.cond(
                    live, advance, unchanged, (query_now[block], run_grads)
                )
                updated.append(new_query)
            piece_grads = lax.dynamic_update_slice_in_dim(
                piece_grads, run_grads, number * own_rows, 1
            )
            return (tuple(updated), piece_grads)

        return lax.fori_loop(
            0,
            piece_rows // own_rows,
            piece_one_run,
            (query_grads, jnp.zeros((2, piece_rows, head_width), jnp.float32)),
        )

    start_query = tuple(
        (jnp.zeros((block_rows, head_width), jnp.float32) for block in range(block_count))
    )

    def cycle_step(step, carried):
        query_now, blocks, travelling = carried
        owner = (cycle_place - step) % cycle_count
        query_now, piece_grads = piece_backward(query_now, blocks[0], blocks[1], owner * group_rows)
        travelling = travelling + piece_grads
        blocks = from_behind(blocks, "blk", 1)
        travelling = from_behind(travelling.astype(jnp.bfloat16), "blk", 1).astype(travelling.dtype)
        return (query_now, blocks, travelling)

    start_cycle = (
        start_query,
        jnp.stack([key_heads, value_heads]),
        jnp.zeros((2, group_rows, head_width), jnp.float32),
    )
    query_grads, unused_blocks, own_grads = lax.fori_loop(0, cycle_count, cycle_step, start_cycle)
    grad_stack = jnp.stack(
        [
            jnp.concatenate(query_grads, axis=0).astype(jnp.bfloat16),
            own_grads[0].astype(jnp.bfloat16),
            own_grads[1].astype(jnp.bfloat16),
        ]
    )
    back_tokens = lax.all_to_all(grad_stack, "head", split_axis=1, concat_axis=2, tiled=True)
    grad_query, grad_keys = rope_pull(
        (back_tokens[0].astype(jnp.float32), back_tokens[1].astype(jnp.float32))
    )
    grad_projected = jnp.concatenate(
        [grad_query, grad_keys, back_tokens[2].astype(jnp.float32)], axis=1
    ).astype(jnp.bfloat16)
    grad_normed_one = jnp.einsum(
        "te,de->td", grad_projected, full_qkv, preferred_element_type=jnp.float32
    )
    grad_input_part, grad_gain_one = norm_one_pull(grad_normed_one)
    input_grad = grad_middle + grad_input_part

    def columns(source):
        return source

    term_qkv = jnp.einsum(
        "td,te->de", columns(normed_low), grad_projected, preferred_element_type=jnp.float32
    )
    term_out = jnp.einsum(
        "td,te->de", columns(out_tokens), grad_branch, preferred_element_type=jnp.float32
    )
    term_in = jnp.einsum(
        "td,tf->df", columns(normed_two_low), grad_lifted, preferred_element_type=jnp.float32
    )
    term_down = jnp.einsum(
        "td,tf->df", columns(cotangent), activated_low, preferred_element_type=jnp.float32
    )
    sums = lax.psum_scatter(
        jnp.concatenate([term_qkv, term_out, term_in, term_down], axis=1),
        ("head", "blk"),
        scatter_dimension=0,
        tiled=True,
    )
    ff_width = full_mlp_out.shape[0]
    qkv_grad = sums[:, : 3 * width]
    attn_out_grad = sums[:, 3 * width : 4 * width]
    in_grad = sums[:, 4 * width : 4 * width + 2 * ff_width]
    down_grad = sums[:, 4 * width + 2 * ff_width :].T
    gain_sums = lax.psum_scatter(
        jnp.stack([grad_gain_one, grad_gain_two]), ("head", "blk"), scatter_dimension=1, tiled=True
    )
    return (
        output,
        input_grad,
        gain_sums[0],
        qkv_grad,
        attn_out_grad,
        gain_sums[1],
        in_grad,
        down_grad,
    )


VMEM = 62 * 2**20
MESH = pl.DeviceIdType.MESH
KEY_STEP = 512
KEY_ALIGN = 256
NN = (((1,), (0,)), ((), ()))
NT = (((1,), (1,)), ((), ()))
TN = (((0,), (0,)), ((), ()))


def mm(left, right, dims=NN):
    return lax.dot_general(left, right, dims, preferred_element_type=jnp.float32)


def params(collective_id=None):
    if collective_id is None:
        return pltpu.CompilerParams(vmem_limit_bytes=VMEM)
    return pltpu.CompilerParams(
        collective_id=collective_id, has_side_effects=True, vmem_limit_bytes=VMEM
    )


def in_vmem():
    return pl.BlockSpec(memory_space=pltpu.VMEM)


def anywhere():
    return pl.BlockSpec(memory_space=pl.ANY)


def in_smem():
    return pl.BlockSpec(memory_space=pltpu.SMEM)


def dma(*counts):
    return pltpu.SemaphoreType.DMA(counts)


def halves(packed, side):
    wide = packed.astype(jnp.float32)
    if side:
        wide = pltpu.roll(wide, HEAD_DIM, 1)
    lane = lax.broadcasted_iota(jnp.int32, wide.shape, 1)
    return jnp.where(lane < HEAD_DIM, wide, 0.0)


def tile_span(lengths, side, R, T):
    hh, u = pl.program_id(0), pl.program_id(1)
    runs, parts = 2 * pl.num_programs(0), 2 * pl.num_programs(1)
    share = lax.rem(lax.axis_index("blk"), 2)
    first = (((hh + side * (runs // 2)) * parts + 2 * u) * 2 + share) * R
    last = first + 3 * R - 1
    lane = lax.broadcasted_iota(jnp.int32, (1, 2 * R), 1)
    place = first + lane + jnp.where(lane < R, 0, R)

    def one(d, carried):
        low, begin, stop, start, end = carried
        high = low + lengths[d]
        inside = (place >= low) & (place < high)
        return (
            high,
            jnp.where(inside, low, begin),
            jnp.where(inside, high, stop),
            jnp.where((first >= low) & (first < high), low, start),
            jnp.where((last >= low) & (last < high), high, end),
        )

    zero = jnp.int32(0)
    unused, begin, stop, start, end = lax.fori_loop(
        0,
        lengths.shape[0],
        one,
        (zero, jnp.zeros_like(place), jnp.zeros_like(place), zero, zero),
        unroll=True,
    )
    start = start // KEY_ALIGN
    steps = (end - start * KEY_ALIGN + KEY_STEP - 1) // KEY_STEP
    start = jnp.minimum(start, T // KEY_ALIGN - steps * (KEY_STEP // KEY_ALIGN))
    return (begin, stop, start, steps)


def attend_kernel(lengths, qp, kv, op, lse, s_scr):
    pairs = qp.shape[0] * qp.shape[2]
    T = kv.shape[0]
    half_runs = pl.num_programs(0)
    hh, u = pl.program_id(0), pl.program_id(1)
    at = lax.broadcasted_iota(jnp.int32, (KEY_STEP, pairs), 0)
    results = []
    for side in (0, 1):
        tile = (hh + side * half_runs) * pl.num_programs(1) + u
        begin, stop, start, steps = tile_span(lengths, side, pairs // 2, T)
        query = (halves(qp[...].reshape(pairs, 2 * HEAD_DIM), side) * HEAD_DIM**-0.5).astype(
            jnp.bfloat16
        )

        def keys_at(n):
            first = pl.multiple_of(start * KEY_ALIGN + n * KEY_STEP, KEY_ALIGN)
            return (first, kv[pl.ds(first, KEY_STEP), :])

        def score(n, top):
            first, keys = keys_at(n)
            same = (at >= begin - first) & (at < stop - first)
            scores = jnp.where(same, mm(keys, query, NT), neg_large)
            s_scr[n] = scores
            return jnp.maximum(top, jnp.max(scores, axis=0, keepdims=True))

        top = lax.fori_loop(0, steps, score, jnp.full((1, pairs), neg_large, jnp.float32))

        def mix(n, carried):
            total, acc = carried
            unused, keys = keys_at(n)
            weights = jnp.exp(s_scr[n] - top)
            total = total + jnp.sum(weights, axis=0, keepdims=True)
            return (total, acc + mm(keys, weights.astype(jnp.bfloat16), TN))

        total, acc = lax.fori_loop(
            0,
            steps,
            mix,
            (jnp.zeros((1, pairs), jnp.float32), jnp.zeros((2 * HEAD_DIM, pairs), jnp.float32)),
        )
        lse[tile] = top + jnp.log(total)
        results.append(acc[HEAD_DIM:] / total)
    both = jnp.concatenate(results, axis=0).T
    op[...] = both.astype(jnp.bfloat16).reshape(op.shape)


def attend(lengths, qp, kv):
    parts, half_runs, rows, lanes = qp.shape
    tiles = half_runs * parts
    piece = pl.BlockSpec((2, 1, rows, lanes), lambda i, j, s: (j, i, 0, 0))
    return pl.pallas_call(
        attend_kernel,
        grid_spec=pltpu.PrefetchScalarGridSpec(
            num_scalar_prefetch=1,
            grid=(half_runs, parts // 2),
            in_specs=[piece, in_vmem()],
            out_specs=[piece, in_vmem()],
            scratch_shapes=[pltpu.VMEM((kv.shape[0] // KEY_STEP, KEY_STEP, 2 * rows), jnp.float32)],
        ),
        out_shape=[
            jax.ShapeDtypeStruct(qp.shape, jnp.bfloat16),
            jax.ShapeDtypeStruct((tiles, 1, 2 * rows), jnp.float32),
        ],
        compiler_params=params(),
        cost_estimate=pl.CostEstimate(
            flops=10**9, bytes_accessed=50 * 10**6, transcendentals=10**6
        ),
        name="attend",
    )(lengths, qp, kv)


def attend_back_kernel(
    lengths, qp, gp, op, lse, kv, output, down, dqp, dkv, output_to, down_to, acc_scr
):
    pairs = qp.shape[0] * qp.shape[2]
    T = kv.shape[0]
    half_runs = pl.num_programs(0)
    hh, u = pl.program_id(0), pl.program_id(1)
    begins = (hh == 0) & (u == 0)
    ends = (hh == half_runs - 1) & (u == pl.num_programs(1) - 1)
    @pl.when(begins)
    def _():
        output_to[...] = output[...]
        down_to[...] = down[...]
        acc_scr[...] = jnp.zeros_like(acc_scr)

    at = lax.broadcasted_iota(jnp.int32, (KEY_STEP, pairs), 0)
    lane = lax.broadcasted_iota(jnp.int32, (pairs, 2 * HEAD_DIM), 1)
    flat = (pairs, 2 * HEAD_DIM)
    results = []
    for side in (0, 1):
        tile = (hh + side * half_runs) * pl.num_programs(1) + u
        begin, stop, start, steps = tile_span(lengths, side, pairs // 2, T)
        query = (halves(qp[...].reshape(flat), side) * HEAD_DIM**-0.5).astype(jnp.bfloat16)
        pieces = []
        for n in range(2):
            piece = gp[n, hh + side * half_runs].astype(jnp.float32)
            pieces += [pltpu.roll(piece, HEAD_DIM, 1), piece]
        grad = jnp.where(lane < HEAD_DIM, 0.0, jnp.concatenate(pieces, axis=0))
        mixed = op[...].reshape(flat).astype(jnp.float32)
        if not side:
            mixed = pltpu.roll(mixed, HEAD_DIM, 1)
        delta = jnp.sum((grad * mixed).T, axis=0, keepdims=True)
        both = jnp.concatenate([query, grad.astype(jnp.bfloat16)], axis=0)
        logs = lse[tile]

        def step(n, dq):
            first = pl.multiple_of(start * KEY_ALIGN + n * KEY_STEP, KEY_ALIGN)
            rows = pl.ds(first, KEY_STEP)
            keys = kv[rows, :]
            same = (at >= begin - first) & (at < stop - first)
            products = mm(keys, both, NT)
            probs = jnp.where(same, jnp.exp(products[:, :pairs] - logs), 0.0)
            grad_scores = (probs * (products[:, pairs:] - delta)).astype(jnp.bfloat16)
            left = jnp.concatenate([grad_scores, probs.astype(jnp.bfloat16)], axis=1)
            acc_scr[rows, :] += mm(left, both)
            return dq + mm(keys, grad_scores, TN)

        dq = lax.fori_loop(0, steps, step, jnp.zeros((2 * HEAD_DIM, pairs), jnp.float32))
        results.append(dq[:HEAD_DIM] * HEAD_DIM**-0.5)
    dqp[...] = jnp.concatenate(results, axis=0).T.astype(jnp.bfloat16).reshape(dqp.shape)

    @pl.when(ends)
    def _():
        dkv[...] = acc_scr[...].astype(dkv.dtype)


def attend_back(lengths, qp, gp, op, lse, kv, output, down):
    parts, half_runs, rows, lanes = qp.shape
    piece = pl.BlockSpec((2, 1, rows, lanes), lambda i, j, s: (j, i, 0, 0))
    grads = pl.BlockSpec((2, 2 * half_runs, rows // 2, lanes), lambda i, j, s: (j, 0, 0, 0))
    return pl.pallas_call(
        attend_back_kernel,
        grid_spec=pltpu.PrefetchScalarGridSpec(
            num_scalar_prefetch=1,
            grid=(half_runs, parts // 2),
            in_specs=[piece, grads, piece, *[in_vmem()] * 4],
            out_specs=[piece, *[in_vmem()] * 3],
            scratch_shapes=[pltpu.VMEM(kv.shape, jnp.float32)],
        ),
        out_shape=[
            jax.ShapeDtypeStruct(qp.shape, jnp.bfloat16),
            jax.ShapeDtypeStruct(kv.shape, jnp.bfloat16),
            jax.ShapeDtypeStruct(output.shape, output.dtype),
            jax.ShapeDtypeStruct(down.shape, down.dtype),
        ],
        compiler_params=params(),
        cost_estimate=pl.CostEstimate(
            flops=3 * 10**9, bytes_accessed=60 * 10**6, transcendentals=10**6
        ),
        name="attend_back",
    )(lengths, qp, gp, op, lse, kv, output, down)


def deliver_kernel(*refs):
    count = len(refs) // 2
    for source, target in zip(refs[:count], refs[count:]):
        target[...] = source[...]


def deliver(*arrays):
    return pl.pallas_call(
        deliver_kernel,
        in_specs=[in_vmem()] * len(arrays),
        out_specs=[in_vmem()] * len(arrays),
        out_shape=[jax.ShapeDtypeStruct(a.shape, a.dtype) for a in arrays],
        compiler_params=params(),
        name="deliver",
    )(*arrays)


def meet(peers):
    barrier = pltpu.get_barrier_semaphore()
    for peer in peers:
        pl.semaphore_signal(barrier, inc=1, device_id=peer, device_id_type=MESH)
    pl.semaphore_wait(barrier, len(peers))


def remote(source, target, send_sem, recv_sem, peer):
    return pltpu.make_async_remote_copy(
        src_ref=source,
        dst_ref=target,
        send_sem=send_sem,
        recv_sem=recv_sem,
        device_id=peer,
        device_id_type=MESH,
    )


def send(source, target, send_sem, recv_sem, peer):
    copy = remote(source, target, send_sem, recv_sem, peer)
    copy.start()
    return copy


class Place:
    def __init__(self, parts):
        h, b = lax.axis_index("head"), lax.axis_index("blk")
        self.h, self.b, self.parts = h, b, parts
        self.part, self.share = b // 2, lax.rem(b, 2)
        x, y = lax.rem(h, 2), h // 2
        self.places = [(1 - y) * 2 + 1 - x, y * 2 + 1 - x, (1 - y) * 2 + x]
        self.across = [(place, b) for place in self.places]
        self.there = [lax.rem(self.part + i, parts) for i in range(1, parts)]
        self.back = [lax.rem(self.part + parts - i, parts) for i in range(1, parts)]
        self.along = [(h, part * 2 + self.share) for part in self.there]
        self.beside = (h, self.part * 2 + 1 - self.share)
        self.askew = [(h, part * 2 + 1 - self.share) for part in self.there]


class LineGather:
    def __init__(self, view, own, here, sems):
        self.view, self.own, self.here, self.parts = view, own, here, here.parts
        self.right_s, self.left_s, self.line_r, self.core_s, self.core_r = sems
        self.first = 0

    def _copy(self, source, block, side):
        here = self.here
        if side == 0:
            sems, peer = (self.core_s, self.core_r), here.beside
        else:
            sems = (self.right_s if side > 0 else self.left_s, self.line_r)
            peer = (here.h, (here.part + side) * 2 + here.share)
        return remote(
            source, self.view(block, here.share), sems[0].at[block], sems[1].at[block], peer
        )

    def _can(self, side):
        return self.here.part < self.parts - 1 if side > 0 else self.here.part > 0

    def start(self):
        for side in (1, -1):

            @pl.when(self._can(side))
            def _():
                self._copy(self.own, self.here.part, side).start()

        self._copy(self.own, self.here.part, 0).start()

    def start_from(self, near):
        self.first = 1
        for side in (1, -1):
            block = self.here.part - side

            @pl.when((block >= 0) & (block < self.parts) & self._can(side))
            def _():
                self._copy(near[side], block, side).start()

        self._copy(self.own, self.here.part, 0).start()
        for side in (1, -1):
            block = self.here.part - side

            @pl.when((block >= 0) & (block < self.parts))
            def _():
                self._copy(near[side], block, 0).start()

    def step(self, k):
        for side in (1, -1):
            block = self.here.part - side * k

            @pl.when((block >= 0) & (block < self.parts))
            def _():
                there = self.view(block, self.here.share)
                self._copy(there, block, side).wait_recv()

                @pl.when(self._can(side))
                def _():
                    self._copy(there, block, side).start()

                self._copy(there, block, 0).start()

    def arrive(self):
        for block in range(self.parts):
            self._copy(self.own, block, 0).wait_recv()

    def finish(self):
        for side in (1, -1):
            for block in range(self.parts):
                first = self.here.part - side * self.first
                sent = block <= first if side > 0 else block >= first

                @pl.when(sent & self._can(side))
                def _():
                    self._copy(self.own, block, side).wait_send()

        for block in range(self.parts):
            self._copy(self.own, block, 0).wait_send()


def line_sems(parts):
    return [dma(parts)] * 5


def standardize(values):
    center = values - jnp.mean(values, axis=-1, keepdims=True)
    spread = jnp.mean(center * center, axis=-1, keepdims=True)
    scale = lax.rsqrt(spread + norm_eps)
    return (center * scale, scale)


def norm_back(grad, hat, scale, gain):
    inner = grad * gain
    return scale * (
        inner
        - jnp.mean(inner, axis=-1, keepdims=True)
        - hat * jnp.mean(inner * hat, axis=-1, keepdims=True)
    )


def turn(values, cosine, sine, back=False):
    lane = lax.broadcasted_iota(jnp.int32, values.shape, 1)
    first = lax.rem(lane, HEAD_DIM) < HEAD_DIM // 2
    source = values * sine if back else values
    ahead = pltpu.roll(source, 128 - HEAD_DIM // 2, 1)
    behind = pltpu.roll(source, HEAD_DIM // 2, 1)
    if back:
        return values * cosine + jnp.where(first, ahead, -behind)
    return values * cosine + jnp.where(first, -ahead, behind) * sine


def join(left, left_side, right, right_side):
    lane = lax.broadcasted_iota(jnp.int32, left.shape, 1)
    left = pltpu.roll(left, HEAD_DIM, 1) if left_side else left
    right = right if right_side else pltpu.roll(right, HEAD_DIM, 1)
    return jnp.where(lane < HEAD_DIM, left, right)


def project_kernel(
    H, A, tok, cot, wq, gain_one, gain_two, w_in, w_down, w_out, lengths,
    kv_all, q_all, tok_all, cot_all, wq_all, wm_all, wo_all, gain_rows, cos_all, sin_all,
    wq_src, wq_st, wm_src, kv_send, q_send, q_runs, hats, gain_src, gain_st, gain_tile, gain_all,
    tok_s, tok_r, cot_s, cot_r, wq_s, wq_r, wm_s, wm_r, ga_s, ga_r, gb_s, gb_r, wx_s, wx_r,
    q_s, q_r, kv_s, kv_r, kc_s, kc_r, *line,
):
    f32, bf16 = jnp.float32, jnp.bfloat16
    R, W = tok.shape
    B = 2 * A
    hw = W // H
    D = wq.shape[0]
    F = w_in.shape[1] // 2 // H
    here = Place(A)
    h, b, part, share = here.h, here.b, here.part, here.share
    across, along, beside = here.across, here.along, here.beside

    for place in range(H):
        for j in range(3):
            wq_src[place, :, j * hw : (j + 1) * hw] = wq[:, j * W + place * hw : j * W + (place + 1) * hw]
    row = lax.broadcasted_iota(jnp.int32, (8, 128), 0)
    lane = lax.broadcasted_iota(jnp.int32, (8, 128), 1)
    gain_src[...] = jnp.zeros((8, 128), f32)
    gain_src[0:1, :D] = gain_one[...].astype(f32)
    gain_src[1:2, :D] = gain_two[...].astype(f32)
    gain_src[...] = pltpu.roll(gain_src[...], h * D, 1)
    meet([*across, *along, beside, *here.askew])

    wq_copies = [
        send(wq_src.at[peer[0]], wq_st.at[h], wq_s.at[i], wq_r.at[i], peer)
        for i, peer in enumerate(across)
    ]
    gain_copies = [
        send(gain_src, gain_st.at[i], ga_s.at[i], ga_r.at[i], peer) for i, peer in enumerate(across)
    ]
    wo_line = LineGather(lambda block, side: wo_all.at[h, block, side], w_out, here, line[5:])
    wo_line.start()
    wo_all[h, part, share] = w_out[...]
    wq_st[h] = wq_src[h]
    tok_all[h] = tok[...]
    cot_all[h] = cot[...]
    for place in range(H):
        wm_src[place, :, :F] = w_in[:, place * F : (place + 1) * F]
        wm_src[place, :, F : 2 * F] = w_in[:, (H + place) * F : (H + place + 1) * F]
        wm_src[place, :, 2 * F :] = w_down[:, place * F : (place + 1) * F]
    wm_all[h] = wm_src[h]
    wo_line.step(1)

    for copy in wq_copies:
        copy.wait_recv()
    wq_line = LineGather(lambda block, side: wq_all.at[:, block * 2 + side], wq_st, here, line[:5])
    wq_line.start()
    tok_copies = [
        send(tok, tok_all.at[h], tok_s.at[i], tok_r.at[i], peer) for i, peer in enumerate(across)
    ]
    wq_all[:, b] = wq_st[...]
    tile = gain_src[...]
    for i, copy in enumerate(gain_copies):
        copy.wait_recv()
        tile += gain_st[i]
    gain_tile[...] = tile
    gain_all[b] = tile
    gain_copies += [
        send(gain_tile, gain_all.at[b], gb_s.at[i], gb_r.at[i], peer)
        for i, peer in enumerate([*along, *here.askew, beside])
    ]
    wo_line.step(2)

    wide = lax.broadcasted_iota(jnp.int32, (R, 128), 1)
    freqs = jnp.exp(
        lax.rem(wide, HEAD_DIM // 2).astype(f32) * (-2.0 / HEAD_DIM * float(np.log(rope_base)))
    )
    for run in range(H):
        place = (run * B + b) * R + lax.broadcasted_iota(jnp.int32, (R, 128), 0)

        def one(d, carried, place=place):
            low, begin = carried
            return (low + lengths[d], jnp.where(place >= low, low, begin))

        unused, begin = lax.fori_loop(
            0, lengths.shape[0], one, (jnp.int32(0), jnp.zeros((R, 128), jnp.int32))
        )
        angles = (place - begin).astype(f32) * freqs
        cos_all[run] = jnp.cos(angles)
        sin_all[run] = jnp.sin(angles)

    wq_line.step(1)
    wm_copies = [
        send(wm_src.at[peer[0]], wm_all.at[h], wm_s.at[i], wm_r.at[i], peer)
        for i, peer in enumerate(across)
    ]
    cot_copies = [
        send(cot, cot_all.at[h], cot_s.at[i], cot_r.at[i], peer) for i, peer in enumerate(across)
    ]
    wo_line.step(3)
    for copy in tok_copies:
        copy.wait_recv()

    def norm_run(run, carried):
        hat, unused = standardize(tok_all[run].astype(f32))
        hats[run] = hat
        return carried

    lax.fori_loop(0, H // 2, norm_run, 0)
    wq_line.step(2)
    lax.fori_loop(H // 2, H, norm_run, 0)
    for copy in gain_copies[len(across) :]:
        copy.wait_recv()
    for slab in range(W // 128):
        place, first = slab // (hw // 128), slab % (hw // 128) * (128 // D)
        piece = jnp.zeros((8, 128), f32)
        for j in range(128 // D):
            moved = gain_all[first + j]
            if j != place:
                moved = pltpu.roll(moved, (j - place) * D % 128, 1)
            piece = jnp.where(lane // D == j, moved, piece)
        gain_rows[:, slab * 128 : (slab + 1) * 128] = piece
    wq_line.step(3)
    wo_line.arrive()
    spread_out = wo_all.at[h, :, share]
    wx_copies = [
        send(spread_out, spread_out, wx_s.at[i], wx_r.at[i], peer) for i, peer in enumerate(across)
    ]
    wq_line.arrive()

    q_copies = []
    for run in [run for low in range(H // 2) for run in (low, low + H // 2)]:
        normed = (hats[run] * gain_rows[0:1, :]).astype(bf16)
        projected = jnp.zeros((R, 3 * hw), f32)
        for chunk in range(H):
            block = wq_all[chunk].reshape(B * D, 3 * hw)
            projected += mm(normed[:, chunk * hw : (chunk + 1) * hw], block)
        cosine, sine = cos_all[run], sin_all[run]
        for slab in range(hw // 128):
            at = slab * 128
            q_runs[run, :, at : at + 128] = turn(projected[:, at : at + 128], cosine, sine)
            key = turn(projected[:, hw + at : hw + at + 128], cosine, sine)
            value = projected[:, 2 * hw + at : 2 * hw + at + 128]
            kv_send[2 * slab, run] = join(key, 0, value, 0).astype(bf16)
            kv_send[2 * slab + 1, run] = join(key, 1, value, 1).astype(bf16)
        for i, peer in enumerate(along):
            send(kv_send.at[here.there[i], run], kv_all.at[run, b], kv_s.at[i], kv_r.at[i], peer)
        kv_all[run, b] = kv_send[part, run]
        send(kv_send.at[part, run], kv_all.at[run, b], kc_s.at[0], kc_r.at[0], beside)
        if run >= H // 2:
            low = run - H // 2
            for a in range(A):
                at = a // 2 * 128
                q_send[a, low] = join(
                    q_runs[low, :, at : at + 128], a % 2, q_runs[run, :, at : at + 128], a % 2
                ).astype(bf16)
            for i, peer in enumerate(along):
                send(q_send.at[here.there[i], low], q_all.at[part, low], q_s.at[i], q_r.at[i], peer)
            q_all[part, low] = q_send[part, low]

    kv_copies = [
        remote(kv_send.at[here.there[i]], kv_all.at[:, b], kv_s.at[i], kv_r.at[i], peer)
        for i, peer in enumerate(along)
    ]
    kc_copies = [remote(kv_send.at[part], kv_all.at[:, b], kc_s.at[0], kc_r.at[0], beside)]
    q_copies = [
        remote(q_send.at[here.there[i]], q_all.at[part], q_s.at[i], q_r.at[i], peer)
        for i, peer in enumerate(along)
    ]
    for i, copy in enumerate(wx_copies):
        copy.wait_recv()
        there = wo_all.at[here.places[i], :, share]
        n = H - 1 + i
        kc_copies.append(send(there, there, wx_s.at[n], wx_r.at[n], beside))
    for i, copy in enumerate(kv_copies):
        copy.wait_recv()
        there = kv_all.at[:, here.back[i] * 2 + share]
        kc_copies.append(send(there, there, kc_s.at[i + 1], kc_r.at[i + 1], beside))
    for copy in [*kc_copies, *q_copies, *wm_copies, *cot_copies]:
        copy.wait_recv()
    for copy in [
        *kc_copies, *q_copies, *wm_copies, *cot_copies, *wq_copies, *gain_copies, *tok_copies, *wx_copies, *kv_copies
    ]:
        copy.wait_send()
    wq_line.finish()
    wo_line.finish()


def project(tokens, cotangent, w_qkv, gain_one, gain_two, w_in, w_down, w_out, lengths):
    R, W = tokens.shape
    H, B = lax.axis_size("head"), lax.axis_size("blk")
    A = B // 2
    hw = W // H
    D = w_qkv.shape[0]
    F = w_down.shape[1] // H
    f32, bf16 = jnp.float32, jnp.bfloat16
    shape = jax.ShapeDtypeStruct
    return pl.pallas_call(
        partial(project_kernel, H, A),
        in_specs=[*[in_vmem()] * 8, in_smem()],
        out_specs=[in_vmem()] * 10,
        out_shape=[
            shape((H, B, R, 128), bf16),
            shape((A, H // 2, R, 128), bf16),
            shape((H, R, W), bf16),
            shape((H, R, W), bf16),
            shape((H, B, D, 3 * hw), bf16),
            shape((H, D, 3 * F), bf16),
            shape((H, A, 2, D, W), bf16),
            shape((8, W), f32),
            shape((H, R, 128), f32),
            shape((H, R, 128), f32),
        ],
        scratch_shapes=[
            pltpu.VMEM((H, D, 3 * hw), bf16),
            pltpu.VMEM((H, D, 3 * hw), bf16),
            pltpu.VMEM((H, D, 3 * F), bf16),
            pltpu.VMEM((A, H, R, 128), bf16),
            pltpu.VMEM((A, H // 2, R, 128), bf16),
            pltpu.VMEM((H, R, hw), f32),
            pltpu.VMEM((H, R, W), f32),
            pltpu.VMEM((8, 128), f32),
            pltpu.VMEM((H - 1, 8, 128), f32),
            pltpu.VMEM((8, 128), f32),
            pltpu.VMEM((B, 8, 128), f32),
            *[dma(H - 1)] * 10,
            *[dma(B - 1)] * 2,
            *[dma(2 * H - 2)] * 2,
            *[dma(A - 1)] * 4,
            *[dma(A)] * 2,
            *line_sems(A),
            *line_sems(A),
        ],
        compiler_params=params(0),
        cost_estimate=pl.CostEstimate(flops=10**9, bytes_accessed=10**7, transcendentals=10**6),
        name="project",
    )(tokens, cotangent, w_qkv, gain_one, gain_two, w_in, w_down, w_out, lengths)


class Reduce:
    def __init__(self, term, core_in, line_out, line_in, here, sems):
        self.term, self.core_in, self.line_out, self.line_in = term, core_in, line_out, line_in
        self.here, self.parts = here, here.parts
        self.core_s, self.core_r, self.line_s, self.line_r = sems

    def _core(self):
        return remote(
            self.term.at[:, 1 - self.here.share],
            self.core_in,
            self.core_s.at[0],
            self.core_r.at[0],
            self.here.beside,
        )

    def _line(self, i):
        return remote(
            self.line_out[i],
            self.line_in.at[i],
            self.line_s.at[i],
            self.line_r.at[i],
            self.here.along[i],
        )

    def _sum(self, there):
        own = self.term[there, self.here.share].astype(jnp.float32)
        return own + self.core_in[there].astype(jnp.float32)

    def start(self):
        self._core().start()

    def gather(self):
        self._core().wait_recv()
        for i, there in enumerate(self.here.there):
            self.line_out[i][...] = self._sum(there).astype(jnp.bfloat16)
        return self._sum(self.here.part)

    def middle(self):
        self._core().wait_recv()
        for i, there in enumerate(self.here.there):
            self.line_out[i][...] = self._sum(there).astype(jnp.bfloat16)
            self._line(i).start()

    def close(self):
        total = self._sum(self.here.part)
        for i in range(self.parts - 1):
            self._line(i).wait_recv()
            total += self.line_in[i].astype(jnp.float32)
        return total

    def core_finish(self):
        self._core().wait_send()

    def finish(self):
        self.core_finish()
        for i in range(self.parts - 1):
            self._line(i).wait_send()


def reduce_scratch(parts, shape):
    return [
        pltpu.VMEM((parts, 2, *shape), jnp.bfloat16),
        pltpu.VMEM((parts, *shape), jnp.bfloat16),
        pltpu.VMEM((parts - 1, *shape), jnp.bfloat16),
        pltpu.VMEM((parts - 1, *shape), jnp.bfloat16),
        dma(1),
        dma(1),
        dma(parts - 1),
        dma(parts - 1),
    ]


def reducer(scratch, here):
    term, core_in, line_out, line_in, *sems = scratch
    outs = [line_out.at[i] for i in range(here.parts - 1)]
    return (term, Reduce(term, core_in, outs, line_in, here, sems))


class Swap:
    def __init__(self, out, landed, send_s, recv_s, here):
        self.out, self.landed, self.here = out, landed, here
        self.send_s, self.recv_s = send_s, recv_s

    def start(self, value):
        here = self.here
        self.out[...] = value.astype(jnp.bfloat16)
        self.copies = [
            send(self.out.at[peer[0]], self.landed.at[here.h], self.send_s.at[i], self.recv_s.at[i], peer)
            for i, peer in enumerate(here.across)
        ]
        self.landed[here.h] = self.out[here.h]

    def arrive(self):
        for copy in self.copies:
            copy.wait_recv()

    def finish(self):
        for copy in self.copies:
            copy.wait_send()


def swap_scratch(heads, shape):
    return [
        pltpu.VMEM((heads, *shape), jnp.bfloat16),
        pltpu.VMEM((heads, *shape), jnp.bfloat16),
        dma(heads - 1),
        dma(heads - 1),
    ]


def run_of(here, i):
    x, y = lax.rem(here.h, 2), here.h // 2
    x = x + (1 - i // 2) * (1 - 2 * x)
    y = y + (1 - i % 2) * (1 - 2 * y)
    return y * 2 + x


def load(pairs, sems):
    copies = [pltpu.make_async_copy(*pair, sems.at[i]) for i, pair in enumerate(pairs)]
    for copy in copies:
        copy.start()
    return copies


def feed_kernel(
    H, A, op, tok_in, cot_in, wo_in, wm_own, wm_before, wm_after, gain_rows,
    output, grad_middle, go, in_own, down_grad, mixed_own, gain_part, *rest,
):
    in_out, rest = rest[: A - 1], rest[A - 1 :]
    (
        tok_all, cot_all, wo, mx_in, mixed_all, wm_all, middle, normed, act, lift,
        g2_send, g2_in, g2_own, o_send, o_in, o_own, gm_send, in_term, in_core, in_core_s, in_core_r,
        load_s, mx_s, mx_r, ma_s, ma_r, g2_s, g2_r, o_s, o_r, gm_s, gm_r, *more,
    ) = rest
    f32, bf16 = jnp.float32, jnp.bfloat16
    R, W = tok_all.shape[1:]
    B = 2 * A
    hw = W // H
    D = wm_own.shape[1]
    F = wm_own.shape[2] // 3
    here = Place(A)
    h, b, part, share = here.h, here.b, here.part, here.share
    across, along = here.across, here.along
    line, down_scratch, swap = more[:5], more[5:13], more[13:17]
    down_term, down_sum = reducer(down_scratch, here)
    down_swap = Swap(*swap, here)
    in_sum = Reduce(in_term, in_core, in_out, None, here, [in_core_s, in_core_r, None, None])
    slot = lambda block: wm_all.at[:, block * 2 + share]
    own_loads = load(
        [(wm_own, slot(part)), (tok_in, tok_all), (wo_in, wo), (cot_in, cot_all)], load_s
    )
    near_loads = [
        pltpu.make_async_copy(wm_before, slot(part - 1), load_s.at[4]),
        pltpu.make_async_copy(wm_after, slot(part + 1), load_s.at[5]),
    ]

    @pl.when(part > 0)
    def _():
        near_loads[0].start()

    @pl.when(part < A - 1)
    def _():
        near_loads[1].start()

    others = [
        (run_of(here, i), lax.rem(part + j, A) * 2 + share)
        for i in range(H)
        for j in range(A)
        if i < H - 1 or j
    ]
    meet([*others, here.beside])

    mx_copies = [
        send(op.at[here.there[i]], mx_in.at[part], mx_s.at[i], mx_r.at[i], peer)
        for i, peer in enumerate(along)
    ]
    gather = LineGather(lambda block, side: wm_all.at[:, block * 2 + side], wm_own, here, line)
    gather.start_from({1: wm_before, -1: wm_after})
    mx_in[part] = op[part]
    for copy in own_loads[:3]:
        copy.wait()
    for copy in mx_copies:
        copy.wait_recv()
    for run in range(H):
        side, at = run // (H // 2), run % (H // 2)
        for slab in range(hw // 128):
            left, right = mx_in[2 * slab, at].astype(f32), mx_in[2 * slab + 1, at].astype(f32)
            mixed_own[run, :, slab * 128 : (slab + 1) * 128] = join(left, side, right, side).astype(bf16)
    ma_copies = [
        send(mixed_own, mixed_all.at[h], ma_s.at[i], ma_r.at[i], peer) for i, peer in enumerate(across)
    ]
    mixed_all[h] = mixed_own[...]

    def project_out(source, first):
        def one(run, carried):
            before = tok_all[run].astype(f32) if first else middle[run]
            middle[run] = before + mm(mixed_all[source, run], wo[source])
            return carried

        lax.fori_loop(0, H, one, 0)

    project_out(h, True)
    gather.step(2)
    for i in (1, 2, 0):
        ma_copies[i].wait_recv()
        project_out(here.places[i], False)

    def norm_run(run, carried):
        hat, unused = standardize(middle[run])
        normed[run] = (hat * gain_rows[1:2, :]).astype(bf16)
        return carried

    lax.fori_loop(0, H, norm_run, 0)
    own_loads[3].wait()

    @pl.when(part > 0)
    def _():
        near_loads[0].wait()

    @pl.when(part < A - 1)
    def _():
        near_loads[1].wait()

    gather.step(3)
    gather.arrive()

    def block(chunk):
        return wm_all[chunk].reshape(B * D, 3 * F)

    def part_of(run, i):
        return remote(g2_send.at[i], g2_in.at[i], g2_s.at[i], g2_r.at[i], (run, b))

    def part_out(run, i):
        return remote(o_send.at[i], o_in.at[i], o_s.at[i], o_r.at[i], (run, b))

    def feed_run(i, carried):
        run = run_of(here, i)
        lifted = jnp.zeros((R, 2 * F), f32)
        grad_act = jnp.zeros((R, F), f32)
        for chunk in range(H):
            lanes = slice(chunk * hw, (chunk + 1) * hw)
            weights = block(chunk)
            lifted += mm(normed[run, :, lanes], weights[:, : 2 * F])
            grad_act += mm(cot_all[run, :, lanes], weights[:, 2 * F :])
        gate, up = lifted[:, :F], lifted[:, F:]
        below = 0.5 + 0.5 * lax.erf(gate * (0.5**0.5))
        slope = below + gate * jnp.exp(-0.5 * gate * gate) * ((2.0 * np.pi) ** -0.5)
        act[run] = (gate * below * up).astype(bf16)
        lift[run, :, :F] = (grad_act * up * slope).astype(bf16)
        lift[run, :, F:] = (grad_act * gate * below).astype(bf16)

        for chunk in range(H):
            lanes = slice(chunk * hw, (chunk + 1) * hw)
            g2_own[:, lanes] = mm(lift[run], block(chunk)[:, : 2 * F], NT)

        @pl.when(i < H - 1)
        def _():
            g2_send[i] = g2_own[...].astype(bf16)
            part_of(run, i).start()

        return carried

    lax.fori_loop(0, H, feed_run, 0)

    def down_chunk(chunk, carried):
        lanes = pl.ds(pl.multiple_of(chunk * hw, hw), hw)
        left = cot_all[:, :, lanes].reshape(H * R, hw)
        grads = mm(left, act[...].reshape(H * R, F), TN).astype(bf16)
        down_term[:, :, chunk] = grads.reshape(A, 2, D, F)
        return carried

    lax.fori_loop(0, H, down_chunk, 0)
    down_sum.start()

    def out_run(i, carried):
        run = run_of(here, i)
        for chunk in range(H):
            lanes = slice(chunk * hw, (chunk + 1) * hw)
            o_own[:, lanes] = mm(act[run], block(chunk)[:, 2 * F :], NT)

        @pl.when(i < H - 1)
        def _():
            o_send[i] = o_own[...].astype(bf16)
            part_out(run, i).start()

        return carried

    lax.fori_loop(0, H, out_run, 0)
    down_sum.middle()

    hat, scale = standardize(middle[h])
    grad = g2_own[...]
    for i in (1, 2, 0):
        part_of(here.places[i], i).wait_recv()
        grad += g2_in[i].astype(f32)
    gain_part[...] = jnp.broadcast_to(jnp.sum(grad * hat, axis=0, keepdims=True), gain_part.shape)
    total = cot_all[h].astype(f32) + norm_back(grad, hat, scale, gain_rows[1:2, :])
    grad_middle[...] = total
    branch = total.astype(bf16)
    gm_copies = []
    for i in range(H):
        place = run_of(here, i)
        mixed_grad = mm(branch, wo[place], NT)
        for a in range(A):
            slab = mixed_grad[:, a // 2 * 128 : a // 2 * 128 + 128]
            gm_send[i, a] = join(slab[: R // 2], a % 2, slab[R // 2 :], a % 2).astype(bf16)
        for j in range(A):
            there = lax.rem(part + j, A)
            if i < H - 1 or j:
                n = i * A + j
                gm_copies.append(
                    send(gm_send.at[i, there], go.at[part, h], gm_s.at[n], gm_r.at[n], (place, there * 2 + share))
                )
            else:
                go[part, h] = gm_send[i, part]

    def in_chunk(chunk, carried):
        lanes = pl.ds(pl.multiple_of(chunk * hw, hw), hw)
        left = normed[:, :, lanes].reshape(H * R, hw)
        grads = mm(left, lift[...].reshape(H * R, 2 * F), TN).astype(bf16)
        in_term[:, :, chunk] = grads.reshape(A, 2, D, 2 * F)
        return carried

    lax.fori_loop(0, H, in_chunk, 0)
    in_sum.start()
    down_swap.start(down_sum.close())
    result = middle[h] + o_own[...]
    for i in range(H - 1):
        part_out(here.places[i], i).wait_recv()
        result += o_in[i].astype(f32)
    output[...] = result.astype(bf16)
    in_own[...] = in_sum.gather()
    down_swap.arrive()
    for place in range(H):
        down_grad[:, place * F : (place + 1) * F] = down_swap.landed[place].astype(f32)
    for copy in gm_copies:
        copy.wait_recv()
    for copy in [*mx_copies, *ma_copies, *gm_copies]:
        copy.wait_send()
    for i in range(H - 1):
        part_of(here.places[i], i).wait_send()
        part_out(here.places[i], i).wait_send()
    gather.finish()
    in_sum.core_finish()
    down_sum.finish()
    down_swap.finish()


def feed(op, tok_all, cot_all, wo, wm_own, wm_before, wm_after, gain_rows):
    A, half, R, lanes = op.shape
    H = 2 * half
    W = tok_all.shape[-1]
    B = 2 * A
    hw = W // H
    D = wm_own.shape[1]
    F = wm_own.shape[2] // 3
    f32, bf16 = jnp.float32, jnp.bfloat16
    shape = jax.ShapeDtypeStruct
    return pl.pallas_call(
        partial(feed_kernel, H, A),
        in_specs=[in_vmem(), *[anywhere()] * 6, in_vmem()],
        out_specs=[in_vmem()] * (6 + A),
        out_shape=[
            shape((R, W), bf16),
            shape((R, W), f32),
            shape((A, H, R // 2, 128), bf16),
            shape((H, D, 2 * F), f32),
            shape((D, H * F), f32),
            shape((H, R, hw), bf16),
            shape((8, W), f32),
            *[shape((H, D, 2 * F), bf16)] * (A - 1),
        ],
        scratch_shapes=[
            pltpu.VMEM((H, R, W), bf16),
            pltpu.VMEM((H, R, W), bf16),
            pltpu.VMEM((H, hw, W), bf16),
            pltpu.VMEM((A, half, R, 128), bf16),
            pltpu.VMEM((H, H, R, hw), bf16),
            pltpu.VMEM((H, B, D, 3 * F), bf16),
            pltpu.VMEM((H, R, W), f32),
            pltpu.VMEM((H, R, W), bf16),
            pltpu.VMEM((H, R, F), bf16),
            pltpu.VMEM((H, R, 2 * F), bf16),
            *[pltpu.VMEM((H - 1, R, W), bf16), pltpu.VMEM((H - 1, R, W), bf16), pltpu.VMEM((R, W), f32)] * 2,
            pltpu.VMEM((H, A, R // 2, 128), bf16),
            pltpu.VMEM((A, 2, H, D, 2 * F), bf16),
            pltpu.VMEM((A, H, D, 2 * F), bf16),
            *[dma(1)] * 2,
            dma(6),
            *[dma(A - 1)] * 2,
            *[dma(H - 1)] * 6,
            *[dma(H * A)] * 2,
            *line_sems(A),
            *reduce_scratch(A, (H, D, F)),
            *swap_scratch(H, (D, F)),
        ],
        compiler_params=params(1),
        cost_estimate=pl.CostEstimate(flops=6 * 10**9, bytes_accessed=10**7, transcendentals=10**6),
        name="feed",
    )(op, tok_all, cot_all, wo, wm_own, wm_before, wm_after, gain_rows)


def finish_kernel(
    H, A, dqp, dkv, tok_in, wq_in, cos_in, sin_in, gain_rows, mixed_in, middle_in, gain_part, own_in, near_in, send_in, far_in,
    input_grad, qkv_grad, out_grad, in_grad, gain_one, gain_two,
    dkv_own, tok_all, wq_all, cos_all, sin_all, mixed_own, grad_middle, in_own, in_near, in_far, in_mid,
    dk_in, dkv_send, dkv_in, dq_in, branch, branch_all, gp, normed, g1_send, g1_in, g1_own,
    load_s, in_s, in_r, dk_s, dk_r, dz_s, dz_r, dq_s, dq_r, br_s, br_r, g1_s, g1_r, *rest,
):
    f32, bf16 = jnp.float32, jnp.bfloat16
    R, W = tok_all.shape[1:]
    B = 2 * A
    hw = W // H
    D = own_in.shape[1]
    F = own_in.shape[2] // 2
    here = Place(A)
    h, b, part, share = here.h, here.b, here.part, here.share
    across, along, beside = here.across, here.along, here.beside
    term_out, out_sum = reducer(rest[:8], here)
    term_qkv, qkv_sum = reducer(rest[8:16], here)
    term_gain, gain_sum = reducer(rest[16:24], here)
    in_swap, qkv_swap, gain_swap = (Swap(*rest[24 + 4 * n : 28 + 4 * n], here) for n in range(3))
    loads = load(
        [
            (dkv, dkv_own), (middle_in, grad_middle), (tok_in, tok_all), (mixed_in, mixed_own), (cos_in, cos_all),
            (sin_in, sin_all), (wq_in, wq_all), (own_in, in_own), (near_in, in_near), (far_in, in_far),
        ],
        load_s,
    )
    meet([*across, *along, beside])

    order = [*here.there, part]
    dk_copies = [
        send(dkv.at[:, there * 2 + 1 - share], dk_in.at[i], dk_s.at[i], dk_r.at[i], beside)
        for i, there in enumerate(order)
    ]
    dq_copies = [
        send(dqp.at[here.there[i]], dq_in.at[part], dq_s.at[i], dq_r.at[i], peer)
        for i, peer in enumerate(along)
    ]
    loads[0].wait()
    dz_copies = []
    for i, there in enumerate(order):
        dk_copies[i].wait_recv()
        summed = dkv_own[:, there * 2 + share].astype(f32) + dk_in[i].astype(f32)
        if i < A - 1:
            dkv_send[i] = summed.astype(bf16)
            dz_copies.append(
                send(dkv_send.at[i], dkv_in.at[part], dz_s.at[i], dz_r.at[i], along[i])
            )
        else:
            dkv_in[part] = summed.astype(bf16)
    dq_in[part] = dqp[part]
    loads[1].wait()
    branch[...] = grad_middle[...].astype(bf16)
    br_copies = [
        send(branch, branch_all.at[h], br_s.at[i], br_r.at[i], peer) for i, peer in enumerate(across)
    ]
    branch_all[h] = branch[...]
    for copy in loads[2:]:
        copy.wait()

    def norm_run(run, carried):
        hat, unused = standardize(tok_all[run].astype(f32))
        normed[run] = (hat * gain_rows[0:1, :]).astype(bf16)
        return carried

    lax.fori_loop(0, H, norm_run, 0)
    for copy in br_copies:
        copy.wait_recv()

    def out_tile(n, carried):
        lanes = pl.ds(pl.multiple_of(n * hw, hw), hw)
        grads = mm(mixed_own[...].reshape(H * R, hw), branch_all[:, :, lanes].reshape(H * R, hw), TN)
        term_out[:, :, :, lanes] = grads.astype(bf16).reshape(A, 2, D, hw)
        return carried

    lax.fori_loop(0, W // hw, out_tile, 0)
    out_sum.start()
    for copy in [*dq_copies, *dz_copies]:
        copy.wait_recv()
    in_copy = send(send_in, in_mid, in_s.at[0], in_r.at[0], along[1])
    for run in range(H):
        side, at = run // (H // 2), run % (H // 2)
        cosine, sine = cos_all[run], sin_all[run]
        for slab in range(hw // 128):
            lanes = slab * 128
            left, right = dq_in[2 * slab, at].astype(f32), dq_in[2 * slab + 1, at].astype(f32)
            gp[run, :, lanes : lanes + 128] = turn(
                join(left, side, right, side), cosine, sine, True
            ).astype(bf16)
            left, right = dkv_in[2 * slab, run].astype(f32), dkv_in[2 * slab + 1, run].astype(f32)
            gp[run, :, hw + lanes : hw + lanes + 128] = turn(
                join(left, 0, right, 0), cosine, sine, True
            ).astype(bf16)
            gp[run, :, 2 * hw + lanes : 2 * hw + lanes + 128] = join(left, 1, right, 1).astype(bf16)

    def block(chunk):
        return wq_all[chunk].reshape(B * D, 3 * hw)

    def term_chunk(chunk, carried):
        lanes = pl.ds(pl.multiple_of(chunk * hw, hw), hw)
        left = normed[:, :, lanes].reshape(H * R, hw)
        grads = mm(left, gp[...].reshape(H * R, 3 * hw), TN).astype(bf16)
        term_qkv[:, :, chunk] = grads.reshape(A, 2, D, 3 * hw)
        return carried

    lax.fori_loop(0, H, term_chunk, 0)
    qkv_sum.start()

    def part_of(run, i):
        return remote(g1_send.at[i], g1_in.at[i], g1_s.at[i], g1_r.at[i], (run, b))

    def one_run(i, carried):
        run = run_of(here, i)
        for chunk in range(H):
            lanes = slice(chunk * hw, (chunk + 1) * hw)
            g1_own[:, lanes] = mm(gp[run], block(chunk), NT)

        @pl.when(i < H - 1)
        def _():
            g1_send[i] = g1_own[...].astype(bf16)
            part_of(run, i).start()

        return carried

    lax.fori_loop(0, 1, one_run, 0)
    qkv_sum.middle()
    lax.fori_loop(1, H, one_run, 0)
    out_sum.middle()
    in_copy.wait_recv()
    total = in_own[...]
    for term in (in_near, in_mid, in_far):
        total += term[...].astype(f32)
    in_swap.start(total)

    grad = g1_own[...]
    hat, scale = standardize(tok_all[h].astype(f32))
    for i in (1, 2, 0):
        part_of(here.places[i], i).wait_recv()
        grad += g1_in[i].astype(f32)
    row = lax.broadcasted_iota(jnp.int32, (8, W), 0)
    rows = jnp.where(
        row == 0,
        jnp.sum(grad * hat, axis=0, keepdims=True),
        jnp.where(row == 1, gain_part[...], 0.0),
    )
    pick = (
        lax.broadcasted_iota(jnp.int32, (8, 128), 0) == lax.broadcasted_iota(jnp.int32, (8, 128), 1)
    ).astype(bf16)
    for chunk in range(H):
        gain_columns = mm(rows[:, chunk * hw : (chunk + 1) * hw].astype(bf16), pick, TN)
        term_gain[:, :, chunk] = gain_columns.astype(bf16).reshape(A, 2, D, 128)
    gain_sum.start()
    input_grad[...] = grad_middle[...] + norm_back(grad, hat, scale, gain_rows[0:1, :])
    gain_sum.middle()
    in_swap.arrive()
    for place in range(H):
        in_grad[:, place * F : (place + 1) * F] = in_swap.landed[place, :, :F].astype(f32)
        in_grad[:, (H + place) * F : (H + place + 1) * F] = in_swap.landed[place, :, F:].astype(f32)
    qkv_swap.start(qkv_sum.close())
    gain_swap.start(gain_sum.close())
    out_grad[...] = out_sum.close()
    qkv_swap.arrive()
    for place in range(H):
        for j in range(3):
            qkv_grad[:, j * W + place * hw : j * W + (place + 1) * hw] = qkv_swap.landed[
                place, :, j * hw : (j + 1) * hw
            ].astype(f32)
    gain_swap.arrive()
    total = gain_swap.landed[0].astype(f32)
    for place in range(1, H):
        total += gain_swap.landed[place].astype(f32)
    rows = total.T
    gain_one[...] = rows[0:1, :]
    gain_two[...] = rows[1:2, :]
    for copy in [*dk_copies, *dq_copies, *br_copies, *dz_copies, in_copy]:
        copy.wait_send()
    for i in range(H - 1):
        part_of(here.places[i], i).wait_send()
    for item in (out_sum, qkv_sum, gain_sum, in_swap, qkv_swap, gain_swap):
        item.finish()


def finish(dqp, dkv, tok_all, wq_all, cos_all, sin_all, gain_rows, mixed, grad_middle, gain_part, in_own, *in_terms):
    A, half, R, lanes = dqp.shape
    H = 2 * half
    W = tok_all.shape[-1]
    B = 2 * A
    hw = W // H
    D = in_own.shape[1]
    F = in_own.shape[2] // 2
    f32, bf16 = jnp.float32, jnp.bfloat16
    shape = jax.ShapeDtypeStruct
    buffer = lambda *sizes: pltpu.VMEM(sizes, bf16)
    arrays = [
        dqp, dkv, tok_all, wq_all, cos_all, sin_all, gain_rows, mixed, grad_middle, gain_part, in_own, *in_terms
    ]
    return pl.pallas_call(
        partial(finish_kernel, H, A),
        in_specs=[in_vmem() if n in (0, 6, 9) else anywhere() for n in range(len(arrays))],
        out_specs=[in_vmem()] * 6,
        out_shape=[
            shape((R, W), f32),
            shape((D, 3 * W), f32),
            shape((D, W), f32),
            shape((D, 2 * H * F), f32),
            shape((1, D), f32),
            shape((1, D), f32),
        ],
        scratch_shapes=[
            buffer(*dkv.shape),
            buffer(*tok_all.shape),
            buffer(*wq_all.shape),
            pltpu.VMEM(cos_all.shape, f32),
            pltpu.VMEM(sin_all.shape, f32),
            buffer(*mixed.shape),
            pltpu.VMEM(grad_middle.shape, f32),
            pltpu.VMEM(in_own.shape, f32),
            *[buffer(H, D, 2 * F)] * 3,
            buffer(A, H, R, 128),
            buffer(A - 1, H, R, 128),
            buffer(A, H, R, 128),
            buffer(A, half, R, 128),
            buffer(R, W),
            buffer(H, R, W),
            buffer(H, R, 3 * hw),
            buffer(H, R, W),
            buffer(H - 1, R, W),
            buffer(H - 1, R, W),
            pltpu.VMEM((R, W), f32),
            dma(10),
            *[dma(1)] * 2,
            *[dma(A)] * 2,
            *[dma(A - 1)] * 4,
            *[dma(H - 1)] * 4,
            *reduce_scratch(A, (D, W)),
            *reduce_scratch(A, (H, D, 3 * hw)),
            *reduce_scratch(A, (H, D, 128)),
            *swap_scratch(H, (D, 2 * F)),
            *swap_scratch(H, (D, 3 * hw)),
            *swap_scratch(H, (D, 128)),
        ],
        compiler_params=params(2),
        cost_estimate=pl.CostEstimate(flops=2 * 10**9, bytes_accessed=10**7, transcendentals=10**5),
        name="finish",
    )(*arrays)


def per_device_split(
    tokens, attn_gain, w_qkv, w_attn_out, mlp_gain, w_in, w_mlp_out, doc_lengths, cotangent
):
    R, W = tokens.shape
    H, B = lax.axis_size("head"), lax.axis_size("blk")
    A = B // 2
    hw = W // H
    T = H * B * R
    kv, qp, tok_all, cot_all, wq, wm, wo, gain_rows, cos_all, sin_all = project(
        tokens, cotangent, w_qkv, attn_gain[None], mlp_gain[None], w_in, w_mlp_out.T, w_attn_out, doc_lengths
    )
    kv = kv.reshape(T, 2 * HEAD_DIM)
    wm_before = lax.ppermute(wm, "blk", [(i, i + 2) for i in range(B - 2)])
    wm_after = lax.ppermute(wm, "blk", [(i + 2, i) for i in range(B - 2)])
    op, lse = attend(doc_lengths, qp, kv)
    output, grad_middle, gp, in_own, down_grad, mixed, gain_part, *in_out = feed(
        op, tok_all, cot_all, wo.reshape(H, hw, W), wm, wm_before, wm_after, gain_rows
    )
    shifted = lambda i: lax.ppermute(in_out[i - 1], "blk", [(p, (p + i * 2) % B) for p in range(B)])
    in_near, in_far = shifted(1), shifted(3)
    dqp, dkv, output, down_grad = attend_back(doc_lengths, qp, gp, op, lse, kv, output, down_grad)
    input_grad, qkv_grad, out_grad, in_grad, gain_one, gain_two = deliver(
        *finish(
            dqp, dkv.reshape(H, B, R, 128), tok_all, wq, cos_all, sin_all, gain_rows, mixed, grad_middle, gain_part,
            in_own, in_near, in_out[1], in_far,
        )
    )
    return (
        output,
        input_grad,
        gain_one[0],
        qkv_grad,
        out_grad,
        gain_two[0],
        in_grad,
        down_grad.T,
    )


def per_device(tokens, attn_gain, w_qkv, *rest):
    heads, blocks = lax.axis_size("head"), lax.axis_size("blk")
    fits = (
        heads == 4
        and blocks == 2 * (tokens.shape[1] // HEAD_DIM // heads) == 8
        and w_qkv.shape[0] * heads == 128
        and tokens.shape[0] == 128
    )
    chosen = per_device_split if fits else per_device_general
    return chosen(tokens, attn_gain, w_qkv, *rest)


def solution(mesh):
    placed = (
        P(("head", "blk"), None),
        P(("head", "blk")),
        P(("head", "blk"), None),
        P(("head", "blk"), None),
        P(("head", "blk")),
        P(("head", "blk"), None),
        P(None, ("head", "blk")),
        P(),
        P(("head", "blk"), None),
    )
    return jax.shard_map(
        per_device,
        mesh=mesh,
        in_specs=placed,
        out_specs=(
            P(("head", "blk"), None),
            P(("head", "blk"), None),
            P(("head", "blk")),
            P(("head", "blk"), None),
            P(("head", "blk"), None),
            P(("head", "blk")),
            P(("head", "blk"), None),
            P(None, ("head", "blk")),
        ),
        check_vma=False,
    )
```

```python
from functools import partial

import jax
import jax.numpy as jnp
import numpy as np
from jax import lax
from jax.experimental import pallas as pl
from jax.experimental.pallas import tpu as pltpu
from jax.sharding import PartitionSpec as P

HEAD_DIM = 64


norm_eps = 1e-05
rope_base = 160000.0
neg_large = -1e30


def from_behind(value, axis, by):
    devices = lax.axis_size(axis)
    return lax.ppermute(value, axis, [(i, (i + by) % devices) for i in range(devices)])


def layer_norm(values, gain):
    center = values - jnp.mean(values, axis=-1, keepdims=True)
    spread = jnp.mean(center * center, axis=-1, keepdims=True)
    return center * lax.rsqrt(spread + norm_eps) * gain


def rope_tables(places, head_size):
    half = head_size // 2
    freqs = rope_base ** (-(jnp.arange(half, dtype=jnp.float32) * 2.0) / head_size)
    angles = places.astype(jnp.float32)[:, None] * freqs[None, :]
    angles = jnp.concatenate([angles, angles], axis=1)
    return (jnp.cos(angles), jnp.sin(angles))


def rotate(values, cosine, sine):
    count = values.shape[0]
    head_size = cosine.shape[1]
    half = head_size // 2
    split = values.reshape(count, -1, head_size)
    turned = jnp.concatenate([-split[..., half:], split[..., :half]], axis=-1)
    return (split * cosine[:, None, :] + turned * sine[:, None, :]).reshape(count, -1)


def rotate_pair(query, keys, cosine, sine):
    return (rotate(query, cosine, sine), rotate(keys, cosine, sine))


def doc_numbers(places, ends, lengths):
    passed = places[:, None] >= ends[None, :]
    numbers = jnp.sum(passed.astype(jnp.int32), axis=1)
    offset = jnp.sum(jnp.where(passed, lengths[None, :], 0), axis=1)
    return (numbers, places - offset)


def gelu_gate(lifted):
    half = lifted.shape[1] // 2
    return jax.nn.gelu(lifted[:, :half], approximate=False) * lifted[:, half:]


def tile_scores(query, keys):
    heads = query.shape[1] // HEAD_DIM
    query_split = query.reshape(query.shape[0], heads, HEAD_DIM)
    key_split = keys.reshape(keys.shape[0], heads, HEAD_DIM)
    return jnp.einsum(
        "qhd,khd->hqk", query_split, key_split, preferred_element_type=jnp.float32
    ) * HEAD_DIM ** (-0.5)


def unchanged(state):
    return state


def forward_tile(state, query, keys, values, mask):
    top, total, running = state
    count = query.shape[0]
    heads = top.shape[0]
    scores = tile_scores(query, keys)
    filled = jnp.where(mask[None], scores, neg_large)
    new_top = jnp.maximum(top, jnp.max(filled, axis=-1))
    weights = jnp.where(mask[None], jnp.exp(scores - new_top[:, :, None]), 0.0)
    factor = jnp.exp(top - new_top)
    new_total = total * factor + jnp.sum(weights, axis=-1)
    mixed = jnp.einsum(
        "hqk,khd->qhd",
        weights.astype(jnp.bfloat16),
        values.reshape(-1, heads, HEAD_DIM),
        preferred_element_type=jnp.float32,
    )
    new_running = running.reshape(count, heads, HEAD_DIM) * factor.T[:, :, None] + mixed
    return (new_top, new_total, new_running.reshape(count, heads * HEAD_DIM))


def backward_tile(carry, query, keys, values, mask, norm_log, grad_out, delta):
    query_grad, run_grads = carry
    count = query.shape[0]
    columns = keys.shape[0]
    heads = norm_log.shape[0]
    scores = tile_scores(query, keys)
    probs = jnp.where(mask[None], jnp.exp(scores - norm_log[:, :, None]), 0.0)
    grad_split = grad_out.reshape(count, heads, HEAD_DIM)
    value_split = values.reshape(columns, heads, HEAD_DIM)
    grad_values = jnp.einsum(
        "hqk,qhd->khd", probs.astype(jnp.bfloat16), grad_split, preferred_element_type=jnp.float32
    )
    grad_probs = jnp.einsum(
        "qhd,khd->hqk", grad_split, value_split, preferred_element_type=jnp.float32
    )
    grad_scores = (probs * (grad_probs - delta[:, :, None])).astype(jnp.bfloat16)
    grad_query = jnp.einsum(
        "hqk,khd->qhd",
        grad_scores,
        keys.reshape(columns, heads, HEAD_DIM),
        preferred_element_type=jnp.float32,
    ) * HEAD_DIM ** (-0.5)
    grad_keys = jnp.einsum(
        "hqk,qhd->khd",
        grad_scores,
        query.reshape(count, heads, HEAD_DIM),
        preferred_element_type=jnp.float32,
    ) * HEAD_DIM ** (-0.5)
    added = jnp.stack([grad_keys.reshape(columns, -1), grad_values.reshape(columns, -1)])
    return (query_grad + grad_query.reshape(count, -1), run_grads + added)


def per_device_general(
    tokens, attn_gain, w_qkv, w_attn_out, mlp_gain, w_in, w_mlp_out, doc_lengths, cotangent
):
    own_rows = tokens.shape[0]
    width = tokens.shape[1]
    head_count = lax.axis_size("head")
    cycle_count = lax.axis_size("blk")
    head_place = lax.axis_index("head")
    cycle_place = lax.axis_index("blk")
    group_rows = head_count * own_rows
    block_runs = min(head_count, max(1, 512 // own_rows))
    block_count = head_count // block_runs
    block_rows = block_runs * own_rows
    doc_ends = jnp.cumsum(doc_lengths)
    counter = jnp.arange(own_rows, dtype=jnp.int32)
    own_places = (head_place * cycle_count + cycle_place) * own_rows + counter
    unused_docs, own_positions = doc_numbers(own_places, doc_ends, doc_lengths)
    cosine, sine = rope_tables(own_positions, HEAD_DIM)
    run_numbers = jnp.arange(head_count, dtype=jnp.int32)
    query_places = (
        (run_numbers[:, None] * cycle_count + cycle_place) * own_rows + counter[None, :]
    ).reshape(group_rows)
    query_docs, unused_positions = doc_numbers(query_places, doc_ends, doc_lengths)
    params = (
        lax.all_gather(attn_gain, ("head", "blk"), axis=0, tiled=True),
        lax.all_gather(w_qkv, ("head", "blk"), axis=0, tiled=True),
        lax.all_gather(w_attn_out, ("head", "blk"), axis=0, tiled=True),
        lax.all_gather(mlp_gain, ("head", "blk"), axis=0, tiled=True),
        lax.all_gather(w_in, ("head", "blk"), axis=0, tiled=True),
        lax.all_gather(w_mlp_out, ("head", "blk"), axis=1, tiled=True),
    )
    gain_one, full_qkv, full_attn_out, gain_two, full_in, full_mlp_out = params
    inputs = tokens.astype(jnp.float32)
    normed_one, norm_one_pull = jax.vjp(layer_norm, inputs, gain_one.astype(jnp.float32))
    normed_low = normed_one.astype(jnp.bfloat16)
    projected = jnp.dot(normed_low, full_qkv, preferred_element_type=jnp.float32)
    turned, rope_pull = jax.vjp(
        partial(rotate_pair, cosine=cosine, sine=sine),
        projected[:, :width],
        projected[:, width : 2 * width],
    )
    stacked = jnp.stack(
        [
            turned[0].astype(jnp.bfloat16),
            turned[1].astype(jnp.bfloat16),
            projected[:, 2 * width :].astype(jnp.bfloat16),
        ]
    )
    regrouped = lax.all_to_all(stacked, "head", split_axis=2, concat_axis=1, tiled=True)
    query_heads = regrouped[0]
    key_heads = regrouped[1]
    value_heads = regrouped[2]
    head_width = query_heads.shape[1]
    heads_here = head_width // HEAD_DIM

    def key_docs_at(first):
        places = (
            first % group_rows // own_rows * cycle_count + first // group_rows
        ) * own_rows + counter
        found, unused = doc_numbers(places, doc_ends, doc_lengths)
        return found

    def block_live(block, key_docs):
        block_docs = query_docs[block * block_rows : (block + 1) * block_rows]
        live = jnp.maximum(jnp.min(block_docs), jnp.min(key_docs)) <= jnp.minimum(
            jnp.max(block_docs), jnp.max(key_docs)
        )
        return (block_docs[:, None] == key_docs[None, :], live)

    def fold_forward(state, piece):
        key_part, value_part = piece

        def fold_one_run(number, carried):
            first = number * own_rows
            key_docs = key_docs_at(first)
            keys = lax.dynamic_slice_in_dim(key_part, number * own_rows, own_rows, 0)
            values = lax.dynamic_slice_in_dim(value_part, number * own_rows, own_rows, 0)
            updated = []
            for block in range(block_count):
                mask, live = block_live(block, key_docs)
                query = query_heads[block * block_rows : (block + 1) * block_rows]
                advance = partial(forward_tile, query=query, keys=keys, values=values, mask=mask)
                updated.append(lax.cond(live, advance, unchanged, carried[block]))
            return tuple(updated)

        return lax.fori_loop(0, key_part.shape[0] // own_rows, fold_one_run, state)

    def fresh_state():
        return tuple(
            (
                (
                    jnp.full((heads_here, block_rows), neg_large, jnp.float32),
                    jnp.zeros((heads_here, block_rows), jnp.float32),
                    jnp.zeros((block_rows, head_width), jnp.float32),
                )
                for block in range(block_count)
            )
        )

    def finish(state):
        outputs = []
        logs = []
        for top, total, running in state:
            scaled = running.reshape(block_rows, heads_here, HEAD_DIM) / total.T[:, :, None]
            outputs.append(scaled.reshape(block_rows, head_width))
            logs.append(top + jnp.log(total))
        return (
            jnp.concatenate(outputs, axis=0).astype(jnp.bfloat16),
            jnp.concatenate(logs, axis=1),
        )

    state = fold_forward(
        fresh_state(),
        (
            lax.all_gather(key_heads, "blk", axis=0, tiled=True),
            lax.all_gather(value_heads, "blk", axis=0, tiled=True),
        ),
    )
    out_heads, norm_log = finish(state)
    out_tokens = lax.all_to_all(out_heads, "head", split_axis=0, concat_axis=1, tiled=True)
    middle = inputs + jnp.dot(out_tokens, full_attn_out, preferred_element_type=jnp.float32)
    normed_two, norm_two_pull = jax.vjp(layer_norm, middle, gain_two.astype(jnp.float32))
    normed_two_low = normed_two.astype(jnp.bfloat16)
    lifted = jnp.dot(normed_two_low, full_in, preferred_element_type=jnp.float32)
    activated, geglu_pull = jax.vjp(gelu_gate, lifted)
    activated_low = activated.astype(jnp.bfloat16)
    output = (
        middle + jnp.dot(activated_low, full_mlp_out, preferred_element_type=jnp.float32)
    ).astype(jnp.bfloat16)
    params = (
        lax.all_gather(attn_gain, ("head", "blk"), axis=0, tiled=True),
        lax.all_gather(w_qkv, ("head", "blk"), axis=0, tiled=True),
        lax.all_gather(w_attn_out, ("head", "blk"), axis=0, tiled=True),
        lax.all_gather(mlp_gain, ("head", "blk"), axis=0, tiled=True),
        lax.all_gather(w_in, ("head", "blk"), axis=0, tiled=True),
        lax.all_gather(w_mlp_out, ("head", "blk"), axis=1, tiled=True),
    )
    gain_one, full_qkv, full_attn_out, gain_two, full_in, full_mlp_out = params
    grad_act = jnp.einsum("td,fd->tf", cotangent, full_mlp_out, preferred_element_type=jnp.float32)
    grad_lifted = geglu_pull(grad_act)[0].astype(jnp.bfloat16)
    grad_normed_two = jnp.einsum(
        "tf,df->td", grad_lifted, full_in, preferred_element_type=jnp.float32
    )
    grad_middle_part, grad_gain_two = norm_two_pull(grad_normed_two)
    grad_middle = cotangent.astype(jnp.float32) + grad_middle_part
    grad_branch = grad_middle.astype(jnp.bfloat16)
    grad_mixed = jnp.einsum(
        "te,de->td", grad_branch, full_attn_out, preferred_element_type=jnp.float32
    ).astype(jnp.bfloat16)
    grad_heads = lax.all_to_all(grad_mixed, "head", split_axis=1, concat_axis=0, tiled=True)
    state = fold_forward(
        fresh_state(),
        (
            lax.all_gather(key_heads, "blk", axis=0, tiled=True),
            lax.all_gather(value_heads, "blk", axis=0, tiled=True),
        ),
    )
    out_heads, norm_log = finish(state)
    delta = jnp.einsum(
        "qhd,qhd->hq",
        grad_heads.reshape(group_rows, heads_here, HEAD_DIM).astype(jnp.float32),
        out_heads.reshape(group_rows, heads_here, HEAD_DIM).astype(jnp.float32),
    )

    def piece_backward(query_grads, key_part, value_part, start):
        piece_rows = key_part.shape[0]

        def piece_one_run(number, carried):
            query_now, piece_grads = carried
            first = start + number * own_rows
            key_docs = key_docs_at(first)
            keys = lax.dynamic_slice_in_dim(key_part, number * own_rows, own_rows, 0)
            values = lax.dynamic_slice_in_dim(value_part, number * own_rows, own_rows, 0)
            run_grads = jnp.zeros((2, own_rows, head_width), jnp.float32)
            updated = []
            for block in range(block_count):
                mask, live = block_live(block, key_docs)
                lower = block * block_rows
                upper = (block + 1) * block_rows
                advance = partial(
                    backward_tile,
                    query=query_heads[lower:upper],
                    keys=keys,
                    values=values,
                    mask=mask,
                    norm_log=norm_log[:, lower:upper],
                    grad_out=grad_heads[lower:upper],
                    delta=delta[:, lower:upper],
                )
                new_query, run_grads = lax.cond(
                    live, advance, unchanged, (query_now[block], run_grads)
                )
                updated.append(new_query)
            piece_grads = lax.dynamic_update_slice_in_dim(
                piece_grads, run_grads, number * own_rows, 1
            )
            return (tuple(updated), piece_grads)

        return lax.fori_loop(
            0,
            piece_rows // own_rows,
            piece_one_run,
            (query_grads, jnp.zeros((2, piece_rows, head_width), jnp.float32)),
        )

    start_query = tuple(
        (jnp.zeros((block_rows, head_width), jnp.float32) for block in range(block_count))
    )

    def cycle_step(step, carried):
        query_now, blocks, travelling = carried
        owner = (cycle_place - step) % cycle_count
        query_now, piece_grads = piece_backward(query_now, blocks[0], blocks[1], owner * group_rows)
        travelling = travelling + piece_grads
        blocks = from_behind(blocks, "blk", 1)
        travelling = from_behind(travelling.astype(jnp.bfloat16), "blk", 1).astype(travelling.dtype)
        return (query_now, blocks, travelling)

    start_cycle = (
        start_query,
        jnp.stack([key_heads, value_heads]),
        jnp.zeros((2, group_rows, head_width), jnp.float32),
    )
    query_grads, unused_blocks, own_grads = lax.fori_loop(0, cycle_count, cycle_step, start_cycle)
    grad_stack = jnp.stack(
        [
            jnp.concatenate(query_grads, axis=0).astype(jnp.bfloat16),
            own_grads[0].astype(jnp.bfloat16),
            own_grads[1].astype(jnp.bfloat16),
        ]
    )
    back_tokens = lax.all_to_all(grad_stack, "head", split_axis=1, concat_axis=2, tiled=True)
    grad_query, grad_keys = rope_pull(
        (back_tokens[0].astype(jnp.float32), back_tokens[1].astype(jnp.float32))
    )
    grad_projected = jnp.concatenate(
        [grad_query, grad_keys, back_tokens[2].astype(jnp.float32)], axis=1
    ).astype(jnp.bfloat16)
    grad_normed_one = jnp.einsum(
        "te,de->td", grad_projected, full_qkv, preferred_element_type=jnp.float32
    )
    grad_input_part, grad_gain_one = norm_one_pull(grad_normed_one)
    input_grad = grad_middle + grad_input_part

    def columns(source):
        return source

    term_qkv = jnp.einsum(
        "td,te->de", columns(normed_low), grad_projected, preferred_element_type=jnp.float32
    )
    term_out = jnp.einsum(
        "td,te->de", columns(out_tokens), grad_branch, preferred_element_type=jnp.float32
    )
    term_in = jnp.einsum(
        "td,tf->df", columns(normed_two_low), grad_lifted, preferred_element_type=jnp.float32
    )
    term_down = jnp.einsum(
        "td,tf->df", columns(cotangent), activated_low, preferred_element_type=jnp.float32
    )
    sums = lax.psum_scatter(
        jnp.concatenate([term_qkv, term_out, term_in, term_down], axis=1),
        ("head", "blk"),
        scatter_dimension=0,
        tiled=True,
    )
    ff_width = full_mlp_out.shape[0]
    qkv_grad = sums[:, : 3 * width]
    attn_out_grad = sums[:, 3 * width : 4 * width]
    in_grad = sums[:, 4 * width : 4 * width + 2 * ff_width]
    down_grad = sums[:, 4 * width + 2 * ff_width :].T
    gain_sums = lax.psum_scatter(
        jnp.stack([grad_gain_one, grad_gain_two]), ("head", "blk"), scatter_dimension=1, tiled=True
    )
    return (
        output,
        input_grad,
        gain_sums[0],
        qkv_grad,
        attn_out_grad,
        gain_sums[1],
        in_grad,
        down_grad,
    )


VMEM = 62 * 2**20
MESH = pl.DeviceIdType.MESH
KEY_STEP = 512
KEY_ALIGN = 256
NN = (((1,), (0,)), ((), ()))
NT = (((1,), (1,)), ((), ()))
TN = (((0,), (0,)), ((), ()))


def mm(left, right, dims=NN):
    return lax.dot_general(left, right, dims, preferred_element_type=jnp.float32)


def params(collective_id=None):
    if collective_id is None:
        return pltpu.CompilerParams(vmem_limit_bytes=VMEM)
    return pltpu.CompilerParams(
        collective_id=collective_id, has_side_effects=True, vmem_limit_bytes=VMEM
    )


def in_vmem():
    return pl.BlockSpec(memory_space=pltpu.VMEM)


def anywhere():
    return pl.BlockSpec(memory_space=pl.ANY)


def in_smem():
    return pl.BlockSpec(memory_space=pltpu.SMEM)


def dma(*counts):
    return pltpu.SemaphoreType.DMA(counts)


def halves(packed, side):
    wide = packed.astype(jnp.float32)
    if side:
        wide = pltpu.roll(wide, HEAD_DIM, 1)
    lane = lax.broadcasted_iota(jnp.int32, wide.shape, 1)
    return jnp.where(lane < HEAD_DIM, wide, 0.0)


def tile_span(lengths, side, R, T):
    hh, u = pl.program_id(0), pl.program_id(1)
    runs, parts = 2 * pl.num_programs(0), 2 * pl.num_programs(1)
    share = lax.rem(lax.axis_index("blk"), 2)
    first = (((hh + side * (runs // 2)) * parts + 2 * u) * 2 + share) * R
    last = first + 3 * R - 1
    lane = lax.broadcasted_iota(jnp.int32, (1, 2 * R), 1)
    place = first + lane + jnp.where(lane < R, 0, R)

    def one(d, carried):
        low, begin, stop, start, end = carried
        high = low + lengths[d]
        inside = (place >= low) & (place < high)
        return (
            high,
            jnp.where(inside, low, begin),
            jnp.where(inside, high, stop),
            jnp.where((first >= low) & (first < high), low, start),
            jnp.where((last >= low) & (last < high), high, end),
        )

    zero = jnp.int32(0)
    unused, begin, stop, start, end = lax.fori_loop(
        0,
        lengths.shape[0],
        one,
        (zero, jnp.zeros_like(place), jnp.zeros_like(place), zero, zero),
        unroll=True,
    )
    start = start // KEY_ALIGN
    steps = (end - start * KEY_ALIGN + KEY_STEP - 1) // KEY_STEP
    start = jnp.minimum(start, T // KEY_ALIGN - steps * (KEY_STEP // KEY_ALIGN))
    return (begin, stop, start, steps)


def attend_kernel(lengths, qp, kv, op, lse, s_scr):
    pairs = qp.shape[0] * qp.shape[2]
    T = kv.shape[0]
    half_runs = pl.num_programs(0)
    hh, u = pl.program_id(0), pl.program_id(1)
    at = lax.broadcasted_iota(jnp.int32, (KEY_STEP, pairs), 0)
    results = []
    for side in (0, 1):
        tile = (hh + side * half_runs) * pl.num_programs(1) + u
        begin, stop, start, steps = tile_span(lengths, side, pairs // 2, T)
        query = (halves(qp[...].reshape(pairs, 2 * HEAD_DIM), side) * HEAD_DIM**-0.5).astype(
            jnp.bfloat16
        )

        def keys_at(n):
            first = pl.multiple_of(start * KEY_ALIGN + n * KEY_STEP, KEY_ALIGN)
            return (first, kv[pl.ds(first, KEY_STEP), :])

        def score(n, top):
            first, keys = keys_at(n)
            same = (at >= begin - first) & (at < stop - first)
            scores = jnp.where(same, mm(keys, query, NT), neg_large)
            s_scr[n] = scores
            return jnp.maximum(top, jnp.max(scores, axis=0, keepdims=True))

        top = lax.fori_loop(0, steps, score, jnp.full((1, pairs), neg_large, jnp.float32))

        def mix(n, carried):
            total, acc = carried
            unused, keys = keys_at(n)
            weights = jnp.exp(s_scr[n] - top)
            total = total + jnp.sum(weights, axis=0, keepdims=True)
            return (total, acc + mm(keys, weights.astype(jnp.bfloat16), TN))

        total, acc = lax.fori_loop(
            0,
            steps,
            mix,
            (jnp.zeros((1, pairs), jnp.float32), jnp.zeros((2 * HEAD_DIM, pairs), jnp.float32)),
        )
        lse[tile] = top + jnp.log(total)
        results.append(acc[HEAD_DIM:] / total)
    both = jnp.concatenate(results, axis=0).T
    op[...] = both.astype(jnp.bfloat16).reshape(op.shape)


def attend(lengths, qp, kv):
    parts, half_runs, rows, lanes = qp.shape
    tiles = half_runs * parts
    piece = pl.BlockSpec((2, 1, rows, lanes), lambda i, j, s: (j, i, 0, 0))
    return pl.pallas_call(
        attend_kernel,
        grid_spec=pltpu.PrefetchScalarGridSpec(
            num_scalar_prefetch=1,
            grid=(half_runs, parts // 2),
            in_specs=[piece, in_vmem()],
            out_specs=[piece, in_vmem()],
            scratch_shapes=[pltpu.VMEM((kv.shape[0] // KEY_STEP, KEY_STEP, 2 * rows), jnp.float32)],
        ),
        out_shape=[
            jax.ShapeDtypeStruct(qp.shape, jnp.bfloat16),
            jax.ShapeDtypeStruct((tiles, 1, 2 * rows), jnp.float32),
        ],
        compiler_params=params(),
        cost_estimate=pl.CostEstimate(
            flops=10**9, bytes_accessed=50 * 10**6, transcendentals=10**6
        ),
        name="attend",
    )(lengths, qp, kv)


def attend_back_kernel(
    lengths, qp, gp, op, lse, kv, dqp, dkv, acc_scr
):
    pairs = qp.shape[0] * qp.shape[2]
    T = kv.shape[0]
    half_runs = pl.num_programs(0)
    hh, u = pl.program_id(0), pl.program_id(1)
    begins = (hh == 0) & (u == 0)
    ends = (hh == half_runs - 1) & (u == pl.num_programs(1) - 1)
    @pl.when(begins)
    def _():
        acc_scr[...] = jnp.zeros_like(acc_scr)

    at = lax.broadcasted_iota(jnp.int32, (KEY_STEP, pairs), 0)
    lane = lax.broadcasted_iota(jnp.int32, (pairs, 2 * HEAD_DIM), 1)
    flat = (pairs, 2 * HEAD_DIM)
    results = []
    for side in (0, 1):
        tile = (hh + side * half_runs) * pl.num_programs(1) + u
        begin, stop, start, steps = tile_span(lengths, side, pairs // 2, T)
        query = (halves(qp[...].reshape(flat), side) * HEAD_DIM**-0.5).astype(jnp.bfloat16)
        pieces = []
        for n in range(2):
            piece = gp[n, hh + side * half_runs].astype(jnp.float32)
            pieces += [pltpu.roll(piece, HEAD_DIM, 1), piece]
        grad = jnp.where(lane < HEAD_DIM, 0.0, jnp.concatenate(pieces, axis=0))
        mixed = op[...].reshape(flat).astype(jnp.float32)
        if not side:
            mixed = pltpu.roll(mixed, HEAD_DIM, 1)
        delta = jnp.sum((grad * mixed).T, axis=0, keepdims=True)
        both = jnp.concatenate([query, grad.astype(jnp.bfloat16)], axis=0)
        logs = lse[tile]

        def step(n, dq):
            first = pl.multiple_of(start * KEY_ALIGN + n * KEY_STEP, KEY_ALIGN)
            rows = pl.ds(first, KEY_STEP)
            keys = kv[rows, :]
            same = (at >= begin - first) & (at < stop - first)
            products = mm(keys, both, NT)
            probs = jnp.where(same, jnp.exp(products[:, :pairs] - logs), 0.0)
            grad_scores = (probs * (products[:, pairs:] - delta)).astype(jnp.bfloat16)
            left = jnp.concatenate([grad_scores, probs.astype(jnp.bfloat16)], axis=1)
            acc_scr[rows, :] += mm(left, both)
            return dq + mm(keys, grad_scores, TN)

        dq = lax.fori_loop(0, steps, step, jnp.zeros((2 * HEAD_DIM, pairs), jnp.float32))
        results.append(dq[:HEAD_DIM] * HEAD_DIM**-0.5)
    dqp[...] = jnp.concatenate(results, axis=0).T.astype(jnp.bfloat16).reshape(dqp.shape)

    @pl.when(ends)
    def _():
        dkv[...] = acc_scr[...].astype(dkv.dtype)


def attend_back(lengths, qp, gp, op, lse, kv):
    parts, half_runs, rows, lanes = qp.shape
    piece = pl.BlockSpec((2, 1, rows, lanes), lambda i, j, s: (j, i, 0, 0))
    grads = pl.BlockSpec((2, 2 * half_runs, rows // 2, lanes), lambda i, j, s: (j, 0, 0, 0))
    return pl.pallas_call(
        attend_back_kernel,
        grid_spec=pltpu.PrefetchScalarGridSpec(
            num_scalar_prefetch=1,
            grid=(half_runs, parts // 2),
            in_specs=[piece, grads, piece, *[in_vmem()] * 2],
            out_specs=[piece, in_vmem()],
            scratch_shapes=[pltpu.VMEM(kv.shape, jnp.float32)],
        ),
        out_shape=[
            jax.ShapeDtypeStruct(qp.shape, jnp.bfloat16),
            jax.ShapeDtypeStruct(kv.shape, jnp.bfloat16),
        ],
        compiler_params=params(),
        cost_estimate=pl.CostEstimate(
            flops=3 * 10**9, bytes_accessed=60 * 10**6, transcendentals=10**6
        ),
        name="attend_back",
    )(lengths, qp, gp, op, lse, kv)


def deliver_kernel(*refs):
    count = len(refs) // 2
    for source, target in zip(refs[:count], refs[count:]):
        target[...] = source[...]


def deliver(*arrays):
    return pl.pallas_call(
        deliver_kernel,
        in_specs=[in_vmem()] * len(arrays),
        out_specs=[in_vmem()] * len(arrays),
        out_shape=[jax.ShapeDtypeStruct(a.shape, a.dtype) for a in arrays],
        compiler_params=params(),
        name="deliver",
    )(*arrays)


def meet(peers):
    barrier = pltpu.get_barrier_semaphore()
    for peer in peers:
        pl.semaphore_signal(barrier, inc=1, device_id=peer, device_id_type=MESH)
    pl.semaphore_wait(barrier, len(peers))


def remote(source, target, send_sem, recv_sem, peer):
    return pltpu.make_async_remote_copy(
        src_ref=source,
        dst_ref=target,
        send_sem=send_sem,
        recv_sem=recv_sem,
        device_id=peer,
        device_id_type=MESH,
    )


def send(source, target, send_sem, recv_sem, peer):
    copy = remote(source, target, send_sem, recv_sem, peer)
    copy.start()
    return copy


class Place:
    def __init__(self, parts):
        h, b = lax.axis_index("head"), lax.axis_index("blk")
        self.h, self.b, self.parts = h, b, parts
        self.part, self.share = b // 2, lax.rem(b, 2)
        x, y = lax.rem(h, 2), h // 2
        self.places = [(1 - y) * 2 + 1 - x, y * 2 + 1 - x, (1 - y) * 2 + x]
        self.across = [(place, b) for place in self.places]
        self.there = [lax.rem(self.part + i, parts) for i in range(1, parts)]
        self.back = [lax.rem(self.part + parts - i, parts) for i in range(1, parts)]
        self.along = [(h, part * 2 + self.share) for part in self.there]
        self.beside = (h, self.part * 2 + 1 - self.share)
        self.near = self.part + 1 - 2 * lax.rem(self.part, 2)
        self.over = lax.rem(self.part + 2, 4)
        self.far = 3 - self.part
        self.askew = [(h, part * 2 + 1 - self.share) for part in self.there]


class LineGather:
    def __init__(self, view, own, here, sems):
        self.view, self.own, self.here, self.parts = view, own, here, here.parts
        self.right_s, self.left_s, self.line_r, self.core_s, self.core_r = sems
        self.first = 0

    def _copy(self, source, block, side):
        here = self.here
        if side == 0:
            sems, peer = (self.core_s, self.core_r), here.beside
        else:
            sems = (self.right_s if side > 0 else self.left_s, self.line_r)
            peer = (here.h, (here.part + side) * 2 + here.share)
        return remote(
            source, self.view(block, here.share), sems[0].at[block], sems[1].at[block], peer
        )

    def _can(self, side):
        return self.here.part < self.parts - 1 if side > 0 else self.here.part > 0

    def start(self):
        for side in (1, -1):

            @pl.when(self._can(side))
            def _():
                self._copy(self.own, self.here.part, side).start()

        self._copy(self.own, self.here.part, 0).start()

    def start_from(self, near):
        self.first = 1
        for side in (1, -1):
            block = self.here.part - side

            @pl.when((block >= 0) & (block < self.parts) & self._can(side))
            def _():
                self._copy(near[side], block, side).start()

        self._copy(self.own, self.here.part, 0).start()
        for side in (1, -1):
            block = self.here.part - side

            @pl.when((block >= 0) & (block < self.parts))
            def _():
                self._copy(near[side], block, 0).start()

    def step(self, k):
        for side in (1, -1):
            block = self.here.part - side * k

            @pl.when((block >= 0) & (block < self.parts))
            def _():
                there = self.view(block, self.here.share)
                self._copy(there, block, side).wait_recv()

                @pl.when(self._can(side))
                def _():
                    self._copy(there, block, side).start()

                self._copy(there, block, 0).start()

    def arrive(self):
        for block in range(self.parts):
            self._copy(self.own, block, 0).wait_recv()

    def finish(self):
        for side in (1, -1):
            for block in range(self.parts):
                first = self.here.part - side * self.first
                sent = block <= first if side > 0 else block >= first

                @pl.when(sent & self._can(side))
                def _():
                    self._copy(self.own, block, side).wait_send()

        for block in range(self.parts):
            self._copy(self.own, block, 0).wait_send()


class CornerGather:
    def __init__(self, whole, half, own, here, sems):
        self.whole, self.half, self.own, self.here = whole, half, own, here
        self.send_s, self.recv_s = sems

    def _copy(self, n):
        h, (corner, x, y) = self.here.h, self.here.across
        if n < 2:
            source, target, peer = self.own, self.whole(h), (x, y)[n]
        else:
            block = (y, x)[n - 2][0]
            source = target = self.half(block, n - 2)
            peer = (x, y)[n - 2]
        return remote(source, target, self.send_s.at[n], self.recv_s.at[n], peer)

    def start(self):
        for n in range(2):
            self._copy(n).start()

    def forward(self):
        for n in range(2):
            self._copy(n).wait_recv()
        for n in range(2, 4):
            self._copy(n).start()

    def arrive(self):
        for n in range(2, 4):
            self._copy(n).wait_recv()

    def finish(self):
        for n in range(4):
            self._copy(n).wait_send()


def local(source, target, sem):
    copy = pltpu.make_async_copy(source, target, sem)
    copy.start()
    return copy


def line_sems(parts):
    return [dma(parts)] * 5


def standardize(values):
    center = values - jnp.mean(values, axis=-1, keepdims=True)
    spread = jnp.mean(center * center, axis=-1, keepdims=True)
    scale = lax.rsqrt(spread + norm_eps)
    return (center * scale, scale)


def norm_back(grad, hat, scale, gain):
    inner = grad * gain
    return scale * (
        inner
        - jnp.mean(inner, axis=-1, keepdims=True)
        - hat * jnp.mean(inner * hat, axis=-1, keepdims=True)
    )


def turn(values, cosine, sine, back=False):
    lane = lax.broadcasted_iota(jnp.int32, values.shape, 1)
    first = lax.rem(lane, HEAD_DIM) < HEAD_DIM // 2
    source = values * sine if back else values
    ahead = pltpu.roll(source, 128 - HEAD_DIM // 2, 1)
    behind = pltpu.roll(source, HEAD_DIM // 2, 1)
    if back:
        return values * cosine + jnp.where(first, ahead, -behind)
    return values * cosine + jnp.where(first, -ahead, behind) * sine


def join(left, left_side, right, right_side):
    lane = lax.broadcasted_iota(jnp.int32, left.shape, 1)
    left = pltpu.roll(left, HEAD_DIM, 1) if left_side else left
    right = right if right_side else pltpu.roll(right, HEAD_DIM, 1)
    return jnp.where(lane < HEAD_DIM, left, right)


def project_kernel(
    H, A, tok_in, cot_in, wq_in, gain_one, gain_two, w_in_in, w_down_in, w_out_in, lengths,
    kv_all, q_all, tok_out, cot_all, wq_out, wm_all, wo_all, gain_rows, cos_out, sin_out,
    cot, w_in, w_down, w_out, tok_all, wq_all, cos_all, sin_all,
    wq_st, wm_src, kv_send, q_send, q_runs, hats, gain_src, gain_st, gain_tile, gain_all,
    load_s, store_s, own_s, kv_o, q_o,
    tok_s, tok_r, wq_s, wq_r, wm_s, wm_r, ga_s, ga_r, gb_s, gb_r, wx_s, wx_r, wf_s, wf_r, cot_s, cot_r,
    q_s, q_r, kv_s, kv_r, kc_s, kc_r, *line,
):
    f32, bf16 = jnp.float32, jnp.bfloat16
    R, W = tok_all.shape[1:]
    B = 2 * A
    hw = W // H
    D = wq_in.shape[0]
    F = w_in.shape[1] // 2 // H
    here = Place(A)
    h, b, part, share = here.h, here.b, here.part, here.share
    across, along, beside = here.across, here.along, here.beside

    def slices(source, target, place):
        return [
            (
                source.at[:, pl.ds(pl.multiple_of(j * W + place * hw, hw), hw)],
                target.at[h, :, j * hw : (j + 1) * hw],
            )
            for j in range(3)
        ]

    loads = [
        local(source, target, load_s.at[n])
        for n, (source, target) in enumerate(
            [
                (w_out_in, w_out), (w_in_in, w_in), (w_down_in, w_down), (cot_in, cot), (tok_in, tok_all.at[h]),
                *slices(wq_in, wq_st, h),
            ]
        )
    ]
    row = lax.broadcasted_iota(jnp.int32, (8, 128), 0)
    lane = lax.broadcasted_iota(jnp.int32, (8, 128), 1)
    gain_src[...] = jnp.zeros((8, 128), f32)
    gain_src[0:1, :D] = gain_one[...].astype(f32)
    gain_src[1:2, :D] = gain_two[...].astype(f32)
    gain_src[...] = pltpu.roll(gain_src[...], h * D, 1)
    meet([*across, *along, beside, *here.askew])

    for i, peer in enumerate(across):
        for source, target in slices(wq_in, wq_st, peer[0]):
            send(source, target, wq_s.at[i], wq_r.at[i], peer)
    wq_copies = [
        remote(wq_st.at[peer[0]], wq_st.at[h], wq_s.at[i], wq_r.at[i], peer)
        for i, peer in enumerate(across)
    ]
    gain_copies = [
        send(gain_src, gain_st.at[i], ga_s.at[i], ga_r.at[i], peer) for i, peer in enumerate(across)
    ]
    wo_line = LineGather(lambda block, side: wo_all.at[h, block, side], w_out, here, line[:5])
    loads[0].wait()
    wo_line.start()
    stores = [local(w_out, wo_all.at[h, part, share], own_s.at[0])]
    for copy in loads[1:]:
        copy.wait()
    for place in range(H):
        wm_src[place, :, :F] = w_in[:, place * F : (place + 1) * F]
        wm_src[place, :, F : 2 * F] = w_in[:, (H + place) * F : (H + place + 1) * F]
        wm_src[place, :, 2 * F :] = w_down[:, place * F : (place + 1) * F]
    stores += [
        local(wm_src.at[h], wm_all.at[h], own_s.at[1]),
        local(cot, cot_all.at[h], own_s.at[2]),
    ]

    wide = lax.broadcasted_iota(jnp.int32, (R, 128), 1)
    freqs = jnp.exp(
        lax.rem(wide, HEAD_DIM // 2).astype(f32) * (-2.0 / HEAD_DIM * float(np.log(rope_base)))
    )

    def tables(run):
        place = (run * B + b) * R + lax.broadcasted_iota(jnp.int32, (R, 128), 0)

        def one(d, carried):
            low, begin = carried
            return (low + lengths[d], jnp.where(place >= low, low, begin))

        unused, begin = lax.fori_loop(
            0, lengths.shape[0], one, (jnp.int32(0), jnp.zeros((R, 128), jnp.int32))
        )
        angles = (place - begin).astype(f32) * freqs
        cos_all[run] = jnp.cos(angles)
        sin_all[run] = jnp.sin(angles)

    tables(0)
    tables(1)
    wo_line.step(1)
    for copy in wq_copies:
        copy.wait_recv()
    wq_lines = []
    for half in range(2):
        rows = pl.ds(half * (H // 2), H // 2)
        wq_lines.append(
            LineGather(
                lambda block, side, rows=rows: wq_all.at[rows, block * 2 + side],
                wq_st.at[rows],
                here,
                line[5 * half + 5 : 5 * half + 10],
            )
        )
        wq_lines[half].start()
    tok_copies = [
        send(tok_in, tok_all.at[h], tok_s.at[i], tok_r.at[i], peer) for i, peer in enumerate(across)
    ]
    tile = gain_src[...]
    for i, copy in enumerate(gain_copies):
        copy.wait_recv()
        tile += gain_st[i]
    gain_tile[...] = tile
    gain_all[b] = tile
    gain_copies += [
        send(gain_tile, gain_all.at[b], gb_s.at[i], gb_r.at[i], peer)
        for i, peer in enumerate([*along, *here.askew, beside])
    ]
    wo_line.step(2)
    wq_all[:, b] = wq_st[...]
    tables(2)
    wq_lines[0].step(1)
    wo_line.step(3)
    wq_lines[1].step(1)
    wo_line.arrive()
    spread = CornerGather(
        lambda place: wo_all.at[place, :, share],
        lambda place, half: wo_all.at[place, half * (A // 2) : (half + 1) * (A // 2), share],
        wo_all.at[h, :, share],
        here,
        (wx_s, wx_r),
    )
    for copy in stores[:1]:
        copy.wait()
    spread.start()
    wm_copies = [
        send(wm_src.at[peer[0]], wm_all.at[h], wm_s.at[i], wm_r.at[i], peer)
        for i, peer in enumerate(across)
    ]
    cot_gather = CornerGather(
        lambda place: cot_all.at[place],
        lambda place, half: cot_all.at[place, half * (R // 2) : (half + 1) * (R // 2)],
        cot,
        here,
        (cot_s, cot_r),
    )
    cot_gather.start()
    tables(3)
    stores += [local(cos_all, cos_out, store_s.at[0]), local(sin_all, sin_out, store_s.at[1])]
    for copy in tok_copies:
        copy.wait_recv()
    stores.append(local(tok_all, tok_out, store_s.at[2]))

    def norm_run(run, carried):
        hat, unused = standardize(tok_all[run].astype(f32))
        hats[run] = hat
        return carried

    wq_lines[0].step(2)
    lax.fori_loop(0, H // 2, norm_run, 0)
    wq_lines[1].step(2)
    lax.fori_loop(H // 2, H, norm_run, 0)
    for copy in gain_copies[len(across) :]:
        copy.wait_recv()
    for slab in range(W // 128):
        place, first = slab // (hw // 128), slab % (hw // 128) * (128 // D)
        piece = jnp.zeros((8, 128), f32)
        for j in range(128 // D):
            moved = gain_all[first + j]
            if j != place:
                moved = pltpu.roll(moved, (j - place) * D % 128, 1)
            piece = jnp.where(lane // D == j, moved, piece)
        gain_rows[:, slab * 128 : (slab + 1) * 128] = piece
    wq_lines[0].step(3)
    wq_lines[1].step(3)
    wq_lines[0].arrive()
    wq_lines[1].arrive()
    stores.append(local(wq_all, wq_out, store_s.at[3]))

    for run in [run for low in range(H // 2) for run in (low, low + H // 2)]:
        normed = (hats[run] * gain_rows[0:1, :]).astype(bf16)
        projected = jnp.zeros((R, 3 * hw), f32)
        for chunk in range(H):
            block = wq_all[chunk].reshape(B * D, 3 * hw)
            projected += mm(normed[:, chunk * hw : (chunk + 1) * hw], block)
        cosine, sine = cos_all[run], sin_all[run]
        for slab in range(hw // 128):
            at = slab * 128
            q_runs[run, :, at : at + 128] = turn(projected[:, at : at + 128], cosine, sine)
            key = turn(projected[:, hw + at : hw + at + 128], cosine, sine)
            value = projected[:, 2 * hw + at : 2 * hw + at + 128]
            kv_send[2 * slab, run] = join(key, 0, value, 0).astype(bf16)
            kv_send[2 * slab + 1, run] = join(key, 1, value, 1).astype(bf16)
        for i, peer in enumerate(along):
            send(kv_send.at[here.there[i], run], kv_all.at[run, b], kv_s.at[i], kv_r.at[i], peer)
        send(kv_send.at[part, run], kv_all.at[run, b], kc_s.at[0], kc_r.at[0], beside)
        stores.append(local(kv_send.at[part, run], kv_all.at[run, b], kv_o.at[run]))
        if run >= H // 2:
            low = run - H // 2
            for a in range(A):
                at = a // 2 * 128
                q_send[a, low] = join(
                    q_runs[low, :, at : at + 128], a % 2, q_runs[run, :, at : at + 128], a % 2
                ).astype(bf16)
            for i, peer in enumerate(along):
                send(q_send.at[here.there[i], low], q_all.at[part, low], q_s.at[i], q_r.at[i], peer)
            stores.append(local(q_send.at[part, low], q_all.at[part, low], q_o.at[low]))

    kv_copies = [
        remote(kv_send.at[here.there[i]], kv_all.at[:, b], kv_s.at[i], kv_r.at[i], peer)
        for i, peer in enumerate(along)
    ]
    kc_copies = [remote(kv_send.at[part], kv_all.at[:, b], kc_s.at[0], kc_r.at[0], beside)]
    q_copies = [
        remote(q_send.at[here.there[i]], q_all.at[part], q_s.at[i], q_r.at[i], peer)
        for i, peer in enumerate(along)
    ]
    spread.forward()
    cot_gather.forward()

    def pass_on(i):
        there = wo_all.at[here.places[i], :, share]
        kc_copies.append(send(there, there, wf_s.at[i], wf_r.at[i], beside))

    pass_on(1)
    pass_on(2)
    spread.arrive()
    pass_on(0)
    for i, copy in enumerate(kv_copies):
        copy.wait_recv()
        there = kv_all.at[:, here.back[i] * 2 + share]
        kc_copies.append(send(there, there, kc_s.at[i + 1], kc_r.at[i + 1], beside))
    cot_gather.arrive()
    for copy in [*kc_copies, *q_copies, *wm_copies]:
        copy.wait_recv()
    for copy in [*kc_copies, *q_copies, *wm_copies, *wq_copies, *gain_copies, *tok_copies, *kv_copies]:
        copy.wait_send()
    for copy in stores[1:]:
        copy.wait()
    for item in (spread, cot_gather, wo_line, *wq_lines):
        item.finish()


def project(tokens, cotangent, w_qkv, gain_one, gain_two, w_in, w_down, w_out, lengths):
    R, W = tokens.shape
    H, B = lax.axis_size("head"), lax.axis_size("blk")
    A = B // 2
    hw = W // H
    D = w_qkv.shape[0]
    F = w_down.shape[1] // H
    f32, bf16 = jnp.float32, jnp.bfloat16
    shape = jax.ShapeDtypeStruct
    buffer = lambda *sizes: pltpu.VMEM(sizes, bf16)
    return pl.pallas_call(
        partial(project_kernel, H, A),
        in_specs=[*[anywhere()] * 3, *[in_vmem()] * 2, *[anywhere()] * 3, in_smem()],
        out_specs=[*[anywhere()] * 7, in_vmem(), *[anywhere()] * 2],
        out_shape=[
            shape((H, B, R, 128), bf16),
            shape((A, H // 2, R, 128), bf16),
            shape((H, R, W), bf16),
            shape((H, R, W), bf16),
            shape((H, B, D, 3 * hw), bf16),
            shape((H, D, 3 * F), bf16),
            shape((H, A, 2, D, W), bf16),
            shape((8, W), f32),
            shape((H, R, 128), f32),
            shape((H, R, 128), f32),
        ],
        scratch_shapes=[
            buffer(R, W),
            buffer(*w_in.shape),
            buffer(*w_down.shape),
            buffer(*w_out.shape),
            buffer(H, R, W),
            buffer(H, B, D, 3 * hw),
            pltpu.VMEM((H, R, 128), f32),
            pltpu.VMEM((H, R, 128), f32),
            buffer(H, D, 3 * hw),
            buffer(H, D, 3 * F),
            buffer(A, H, R, 128),
            buffer(A, H // 2, R, 128),
            pltpu.VMEM((H, R, hw), f32),
            pltpu.VMEM((H, R, W), f32),
            pltpu.VMEM((8, 128), f32),
            pltpu.VMEM((H - 1, 8, 128), f32),
            pltpu.VMEM((8, 128), f32),
            pltpu.VMEM((B, 8, 128), f32),
            dma(8),
            dma(4),
            dma(3),
            dma(H),
            dma(H // 2),
            *[dma(H - 1)] * 8,
            *[dma(B - 1)] * 2,
            *[dma(4)] * 2,
            *[dma(H - 1)] * 2,
            *[dma(4)] * 2,
            *[dma(A - 1)] * 4,
            *[dma(A)] * 2,
            *line_sems(A) * 3,
        ],
        compiler_params=params(0),
        cost_estimate=pl.CostEstimate(flops=10**9, bytes_accessed=10**7, transcendentals=10**6),
        name="project",
    )(tokens, cotangent, w_qkv, gain_one, gain_two, w_in, w_down, w_out, lengths)


class Reduce:
    def __init__(self, term, core_in, line_out, line_in, here, sems):
        self.term, self.core_in, self.line_out, self.line_in = term, core_in, line_out, line_in
        self.here, self.parts = here, here.parts
        self.core_s, self.core_r, self.line_s, self.line_r = sems

    def _core(self):
        return remote(
            self.term.at[:, 1 - self.here.share],
            self.core_in,
            self.core_s.at[0],
            self.core_r.at[0],
            self.here.beside,
        )

    def _line(self, i):
        return remote(
            self.line_out[i],
            self.line_in.at[i],
            self.line_s.at[i],
            self.line_r.at[i],
            self.here.along[i],
        )

    def _sum(self, there):
        own = self.term[there, self.here.share].astype(jnp.float32)
        return own + self.core_in[there].astype(jnp.float32)

    def start(self):
        self._core().start()

    def core_sums(self):
        self._core().wait_recv()
        return self._sum

    def middle(self):
        self._core().wait_recv()
        for i, there in enumerate(self.here.there):
            self.line_out[i][...] = self._sum(there).astype(jnp.bfloat16)
            self._line(i).start()

    def close(self):
        total = self._sum(self.here.part)
        for i in range(self.parts - 1):
            self._line(i).wait_recv()
            total += self.line_in[i].astype(jnp.float32)
        return total

    def core_finish(self):
        self._core().wait_send()

    def finish(self):
        self.core_finish()
        for i in range(self.parts - 1):
            self._line(i).wait_send()


def reduce_scratch(parts, shape):
    return [
        pltpu.VMEM((parts, 2, *shape), jnp.bfloat16),
        pltpu.VMEM((parts, *shape), jnp.bfloat16),
        pltpu.VMEM((parts - 1, *shape), jnp.bfloat16),
        pltpu.VMEM((parts - 1, *shape), jnp.bfloat16),
        dma(1),
        dma(1),
        dma(parts - 1),
        dma(parts - 1),
    ]


class PairReduce:
    def __init__(self, core_in, near_out, near_in, far_out, far_in, *sems, term, here):
        self.term, self.core_in, self.near_out, self.near_in = term, core_in, near_out, near_in
        self.far_out, self.far_in, self.sems, self.here = far_out, far_in, sems, here

    def _copy(self, step):
        here = self.here
        source, target, peer = (
            (self.term.at[:, 1 - here.share], self.core_in, here.beside),
            (self.near_out, self.near_in, (here.h, here.near * 2 + here.share)),
            (self.far_out, self.far_in, (here.h, here.far * 2 + here.share)),
        )[step]
        return remote(source, target, self.sems[2 * step].at[0], self.sems[2 * step + 1].at[0], peer)

    def _sum(self, there):
        own = self.term[there, self.here.share].astype(jnp.float32)
        return own + self.core_in[there].astype(jnp.float32)

    def start(self):
        self._copy(0).start()

    def pair(self):
        self._copy(0).wait_recv()
        self.near_out[0] = self._sum(self.here.near).astype(jnp.bfloat16)
        self.near_out[1] = self._sum(self.here.over).astype(jnp.bfloat16)
        self._copy(1).start()

    def cross(self):
        self._copy(1).wait_recv()
        self.far_out[...] = (
            self._sum(self.here.far) + self.near_in[1].astype(jnp.float32)
        ).astype(jnp.bfloat16)
        self._copy(2).start()

    def close(self):
        self._copy(2).wait_recv()
        total = self._sum(self.here.part) + self.near_in[0].astype(jnp.float32)
        return total + self.far_in[...].astype(jnp.float32)

    def finish(self):
        for step in range(3):
            self._copy(step).wait_send()


def pair_scratch(parts, shape):
    return [
        pltpu.VMEM((parts, *shape), jnp.bfloat16),
        *[pltpu.VMEM((2, *shape), jnp.bfloat16)] * 2,
        *[pltpu.VMEM(shape, jnp.bfloat16)] * 2,
        *[dma(1)] * 6,
    ]


def reducer(scratch, here):
    term, core_in, line_out, line_in, *sems = scratch
    outs = [line_out.at[i] for i in range(here.parts - 1)]
    return (term, Reduce(term, core_in, outs, line_in, here, sems))


class Swap:
    def __init__(self, out, landed, send_s, recv_s, here):
        self.out, self.landed, self.here = out, landed, here
        self.send_s, self.recv_s = send_s, recv_s

    def start(self):
        here = self.here
        self.copies = [
            send(self.out.at[peer[0]], self.landed.at[here.h], self.send_s.at[i], self.recv_s.at[i], peer)
            for i, peer in enumerate(here.across)
        ]
        self.landed[here.h] = self.out[here.h]

    def arrive(self):
        for copy in self.copies:
            copy.wait_recv()

    def finish(self):
        for copy in self.copies:
            copy.wait_send()


def swap_scratch(heads, shape):
    return [
        pltpu.VMEM((heads, *shape), jnp.bfloat16),
        pltpu.VMEM((heads, *shape), jnp.bfloat16),
        dma(heads - 1),
        dma(heads - 1),
    ]


def run_of(here, i):
    x, y = lax.rem(here.h, 2), here.h // 2
    x = x + (1 - i // 2) * (1 - 2 * x)
    y = y + (1 - i % 2) * (1 - 2 * y)
    return y * 2 + x


def load(pairs, sems):
    copies = [pltpu.make_async_copy(*pair, sems.at[i]) for i, pair in enumerate(pairs)]
    for copy in copies:
        copy.start()
    return copies


def feed_kernel(
    H, A, op, tok_in, cot_in, wo_in, wm_own, wm_before, wm_after, gain_rows,
    out_base, out_parts, grad_middle, go, kept, up_far, near_out, over_out, far_out, mixed_own, gain_part, *rest,
):
    (
        tok_all, cot_all, wo, mx_in, mixed_all, wm_all, middle, normed, act, lift,
        g2_send, g2_in, g2_own, gm_send, in_term, in_core, in_core_s, in_core_r, down_send, down_in, pair_s, pair_r,
        load_s, mx_s, mx_r, ma_s, ma_r, g2_s, g2_r, gm_s, gm_r, *more,
    ) = rest
    f32, bf16 = jnp.float32, jnp.bfloat16
    R, W = tok_all.shape[1:]
    B = 2 * A
    hw = W // H
    D = wm_own.shape[1]
    F = wm_own.shape[2] // 3
    here = Place(A)
    h, b, part, share = here.h, here.b, here.part, here.share
    across, along = here.across, here.along
    line, (down_term, down_core, *down_sems) = more[:5], more[5:9]
    down_sum = Reduce(down_term, down_core, None, None, here, [*down_sems, None, None])
    in_sum = Reduce(in_term, in_core, None, None, here, [in_core_s, in_core_r, None, None])
    near, over, far = here.near, here.over, here.far
    slot = lambda block: wm_all.at[:, block * 2 + share]
    own_loads = load(
        [(wm_own, slot(part)), (tok_in, tok_all), (wo_in, wo), (cot_in, cot_all)], load_s
    )
    near_loads = [
        pltpu.make_async_copy(wm_before, slot(part - 1), load_s.at[4]),
        pltpu.make_async_copy(wm_after, slot(part + 1), load_s.at[5]),
    ]

    @pl.when(part > 0)
    def _():
        near_loads[0].start()

    @pl.when(part < A - 1)
    def _():
        near_loads[1].start()

    others = [
        (run_of(here, i), lax.rem(part + j, A) * 2 + share)
        for i in range(H)
        for j in range(A)
        if i < H - 1 or j
    ]
    meet([*others, here.beside])

    mx_copies = [
        send(op.at[here.there[i]], mx_in.at[part], mx_s.at[i], mx_r.at[i], peer)
        for i, peer in enumerate(along)
    ]
    gather = LineGather(lambda block, side: wm_all.at[:, block * 2 + side], wm_own, here, line)
    gather.start_from({1: wm_before, -1: wm_after})
    mx_in[part] = op[part]
    for copy in own_loads[:3]:
        copy.wait()
    for copy in mx_copies:
        copy.wait_recv()
    for run in range(H):
        side, at = run // (H // 2), run % (H // 2)
        for slab in range(hw // 128):
            left, right = mx_in[2 * slab, at].astype(f32), mx_in[2 * slab + 1, at].astype(f32)
            mixed_own[run, :, slab * 128 : (slab + 1) * 128] = join(left, side, right, side).astype(bf16)
    ma_copies = [
        send(mixed_own, mixed_all.at[h], ma_s.at[i], ma_r.at[i], peer) for i, peer in enumerate(across)
    ]
    mixed_all[h] = mixed_own[...]

    def project_out(source, first):
        def one(run, carried):
            before = tok_all[run].astype(f32) if first else middle[run]
            middle[run] = before + mm(mixed_all[source, run], wo[source])
            return carried

        lax.fori_loop(0, H, one, 0)

    project_out(h, True)
    gather.step(2)
    for i in (1, 2, 0):
        ma_copies[i].wait_recv()
        project_out(here.places[i], False)

    def norm_run(run, carried):
        hat, unused = standardize(middle[run])
        normed[run] = (hat * gain_rows[1:2, :]).astype(bf16)
        return carried

    lax.fori_loop(0, H, norm_run, 0)
    own_loads[3].wait()

    @pl.when(part > 0)
    def _():
        near_loads[0].wait()

    @pl.when(part < A - 1)
    def _():
        near_loads[1].wait()

    gather.step(3)
    gather.arrive()

    def block(chunk):
        return wm_all[chunk].reshape(B * D, 3 * F)

    def part_of(run, i):
        return remote(g2_send.at[i], g2_in.at[i], g2_s.at[i], g2_r.at[i], (run, b))

    def feed_run(i, carried):
        run = run_of(here, i)
        lifted = jnp.zeros((R, 2 * F), f32)
        grad_act = jnp.zeros((R, F), f32)
        for chunk in range(H):
            lanes = slice(chunk * hw, (chunk + 1) * hw)
            weights = block(chunk)
            lifted += mm(normed[run, :, lanes], weights[:, : 2 * F])
            grad_act += mm(cot_all[run, :, lanes], weights[:, 2 * F :])
        gate, up = lifted[:, :F], lifted[:, F:]
        below = 0.5 + 0.5 * lax.erf(gate * (0.5**0.5))
        slope = below + gate * jnp.exp(-0.5 * gate * gate) * ((2.0 * np.pi) ** -0.5)
        act[run] = (gate * below * up).astype(bf16)
        lift[run, :, :F] = (grad_act * up * slope).astype(bf16)
        lift[run, :, F:] = (grad_act * gate * below).astype(bf16)

        for chunk in range(H):
            lanes = slice(chunk * hw, (chunk + 1) * hw)
            g2_own[:, lanes] = mm(lift[run], block(chunk)[:, : 2 * F], NT)

        @pl.when(i < H - 1)
        def _():
            g2_send[i] = g2_own[...].astype(bf16)
            part_of(run, i).start()

        return carried

    lax.fori_loop(0, H, feed_run, 0)

    def down_chunk(chunk, carried):
        lanes = pl.ds(pl.multiple_of(chunk * hw, hw), hw)
        left = cot_all[:, :, lanes].reshape(H * R, hw)
        grads = mm(left, act[...].reshape(H * R, F), TN).astype(bf16)
        down_term[:, :, chunk] = grads.reshape(A, 2, D, F)
        return carried

    lax.fori_loop(0, H, down_chunk, 0)
    down_sum.start()

    def in_chunk(chunk, carried):
        lanes = pl.ds(pl.multiple_of(chunk * hw, hw), hw)
        left = normed[:, :, lanes].reshape(H * R, hw)
        grads = mm(left, lift[...].reshape(H * R, 2 * F), TN).astype(bf16)
        in_term[:, :, chunk] = grads.reshape(A, 2, D, 2 * F)
        return carried

    lax.fori_loop(0, H, in_chunk, 0)
    in_sum.start()
    down_of = down_sum.core_sums()
    for n, there in enumerate((near, over)):
        down_send[n] = down_of(there).astype(bf16)
    pair_copy = send(down_send, down_in, pair_s.at[0], pair_r.at[0], (h, near * 2 + share))

    hat, scale = standardize(middle[h])
    grad = g2_own[...]
    for i in (1, 2, 0):
        part_of(here.places[i], i).wait_recv()
        grad += g2_in[i].astype(f32)
    gain_part[...] = jnp.broadcast_to(jnp.sum(grad * hat, axis=0, keepdims=True), gain_part.shape)
    total = cot_all[h].astype(f32) + norm_back(grad, hat, scale, gain_rows[1:2, :])
    grad_middle[...] = total
    branch = total.astype(bf16)
    gm_copies = []
    for i in range(H):
        place = run_of(here, i)
        mixed_grad = mm(branch, wo[place], NT)
        for a in range(A):
            slab = mixed_grad[:, a // 2 * 128 : a // 2 * 128 + 128]
            gm_send[i, a] = join(slab[: R // 2], a % 2, slab[R // 2 :], a % 2).astype(bf16)
        for j in range(A):
            there = lax.rem(part + j, A)
            if i < H - 1 or j:
                n = i * A + j
                gm_copies.append(
                    send(gm_send.at[i, there], go.at[part, h], gm_s.at[n], gm_r.at[n], (place, there * 2 + share))
                )
            else:
                go[part, h] = gm_send[i, part]

    in_of = in_sum.core_sums()
    near_out[0] = in_of(near)[:, :, :F].astype(bf16)
    near_out[1] = in_of(near)[:, :, F:].astype(bf16)
    near_out[2] = in_of(over)[:, :, F:].astype(bf16)
    over_out[...] = in_of(over)[:, :, :F].astype(bf16)
    far_out[0] = in_of(far)[:, :, :F].astype(bf16)
    up_far[...] = in_of(far)[:, :, F:].astype(bf16)
    kept[0] = in_of(part)[:, :, :F]
    kept[1] = in_of(part)[:, :, F:]
    pair_copy.wait_recv()
    kept[2] = down_of(part) + down_in[0].astype(f32)
    far_out[1] = (down_of(far) + down_in[1].astype(f32)).astype(bf16)

    def out_run(i, carried):
        run = run_of(here, i)
        for chunk in range(H):
            lanes = slice(chunk * hw, (chunk + 1) * hw)
            out_base[:, lanes] = mm(act[run], block(chunk)[:, 2 * F :], NT)

        @pl.when(i < H - 1)
        def _():
            out_parts[i] = out_base[...].astype(bf16)

        return carried

    lax.fori_loop(0, H, out_run, 0)
    out_base[...] += middle[h]
    for copy in gm_copies:
        copy.wait_recv()
    for copy in [*mx_copies, *ma_copies, *gm_copies, pair_copy]:
        copy.wait_send()
    for i in range(H - 1):
        part_of(here.places[i], i).wait_send()
    gather.finish()
    in_sum.core_finish()
    down_sum.core_finish()


def feed(op, tok_all, cot_all, wo, wm_own, wm_before, wm_after, gain_rows):
    A, half, R, lanes = op.shape
    H = 2 * half
    W = tok_all.shape[-1]
    B = 2 * A
    hw = W // H
    D = wm_own.shape[1]
    F = wm_own.shape[2] // 3
    f32, bf16 = jnp.float32, jnp.bfloat16
    shape = jax.ShapeDtypeStruct
    return pl.pallas_call(
        partial(feed_kernel, H, A),
        in_specs=[in_vmem(), *[anywhere()] * 6, in_vmem()],
        out_specs=[in_vmem()] * 11,
        out_shape=[
            shape((R, W), f32),
            shape((H - 1, R, W), bf16),
            shape((R, W), f32),
            shape((A, H, R // 2, 128), bf16),
            shape((3, H, D, F), f32),
            shape((H, D, F), bf16),
            shape((3, H, D, F), bf16),
            shape((H, D, F), bf16),
            shape((2, H, D, F), bf16),
            shape((H, R, hw), bf16),
            shape((8, W), f32),
        ],
        scratch_shapes=[
            pltpu.VMEM((H, R, W), bf16),
            pltpu.VMEM((H, R, W), bf16),
            pltpu.VMEM((H, hw, W), bf16),
            pltpu.VMEM((A, half, R, 128), bf16),
            pltpu.VMEM((H, H, R, hw), bf16),
            pltpu.VMEM((H, B, D, 3 * F), bf16),
            pltpu.VMEM((H, R, W), f32),
            pltpu.VMEM((H, R, W), bf16),
            pltpu.VMEM((H, R, F), bf16),
            pltpu.VMEM((H, R, 2 * F), bf16),
            *[pltpu.VMEM((H - 1, R, W), bf16)] * 2,
            pltpu.VMEM((R, W), f32),
            pltpu.VMEM((H, A, R // 2, 128), bf16),
            pltpu.VMEM((A, 2, H, D, 2 * F), bf16),
            pltpu.VMEM((A, H, D, 2 * F), bf16),
            *[dma(1)] * 2,
            *[pltpu.VMEM((2, H, D, F), bf16)] * 2,
            *[dma(1)] * 2,
            dma(6),
            *[dma(A - 1)] * 2,
            *[dma(H - 1)] * 4,
            *[dma(H * A)] * 2,
            *line_sems(A),
            pltpu.VMEM((A, 2, H, D, F), bf16),
            pltpu.VMEM((A, H, D, F), bf16),
            *[dma(1)] * 2,
        ],
        compiler_params=params(1),
        cost_estimate=pl.CostEstimate(flops=6 * 10**9, bytes_accessed=10**7, transcendentals=10**6),
        name="feed",
    )(op, tok_all, cot_all, wo, wm_own, wm_before, wm_after, gain_rows)


def finish_kernel(
    H, A, dqp, dkv, tok_in, wq_in, cos_in, sin_in, gain_rows, mixed_in, middle_in, gain_part, base_in, out_parts, kept_in, up_in, near_in, over_in, far_in,
    output, input_grad, qkv_grad, out_grad, in_grad, down_grad, gain_one, gain_two,
    dkv_own, tok_all, wq_all, cos_all, sin_all, mixed_own, grad_middle, out_base, o_in, kept, up_far, from_near, from_over, from_far, up_send, up_last,
    dk_in, dkv_send, dkv_in, dq_in, branch, branch_all, gp, normed, g1_send, g1_in, g1_own,
    load_s, up_s, up_r, o_s, o_r, dk_s, dk_r, dz_s, dz_r, dq_s, dq_r, br_s, br_r, g1_s, g1_r, *rest,
):
    f32, bf16 = jnp.float32, jnp.bfloat16
    R, W = tok_all.shape[1:]
    B = 2 * A
    hw = W // H
    D, F = kept_in.shape[2:]
    here = Place(A)
    h, b, part, share = here.h, here.b, here.part, here.share
    across, along, beside = here.across, here.along, here.beside
    term_gain, gain_sum = reducer(rest[:8], here)
    in_swap, qkv_swap, gain_swap = (Swap(*rest[8 + 4 * n : 12 + 4 * n], here) for n in range(3))
    term_out, *term_qkv = rest[20:23]
    out_sum, *qkv_sums = (
        PairReduce(*rest[23 + 11 * n : 34 + 11 * n], term=term, here=here)
        for n, term in enumerate((term_out, *term_qkv))
    )
    loads = load(
        [
            (dkv, dkv_own), (middle_in, grad_middle), (tok_in, tok_all), (mixed_in, mixed_own), (cos_in, cos_all),
            (sin_in, sin_all), (wq_in, wq_all), (kept_in, kept), (up_in, up_far), (near_in, from_near),
            (far_in, from_far), (base_in, out_base),
        ],
        load_s,
    )
    meet([*across, *along, beside])

    order = [*here.there, part]
    dk_copies = [
        send(dkv.at[:, there * 2 + 1 - share], dk_in.at[i], dk_s.at[i], dk_r.at[i], beside)
        for i, there in enumerate(order)
    ]
    dq_copies = [
        send(dqp.at[here.there[i]], dq_in.at[part], dq_s.at[i], dq_r.at[i], peer)
        for i, peer in enumerate(along)
    ]
    loads[0].wait()
    dz_copies = []
    for i, there in enumerate(order):
        dk_copies[i].wait_recv()
        summed = dkv_own[:, there * 2 + share].astype(f32) + dk_in[i].astype(f32)
        if i < A - 1:
            dkv_send[i] = summed.astype(bf16)
            dz_copies.append(
                send(dkv_send.at[i], dkv_in.at[part], dz_s.at[i], dz_r.at[i], along[i])
            )
        else:
            dkv_in[part] = summed.astype(bf16)
    dq_in[part] = dqp[part]
    loads[1].wait()
    branch[...] = grad_middle[...].astype(bf16)
    br_copies = [
        send(branch, branch_all.at[h], br_s.at[i], br_r.at[i], peer) for i, peer in enumerate(across)
    ]
    branch_all[h] = branch[...]
    o_copies = [
        send(out_parts.at[i], o_in.at[i], o_s.at[i], o_r.at[i], peer) for i, peer in enumerate(across)
    ]
    for copy in loads[2:]:
        copy.wait()

    def norm_run(run, carried):
        hat, unused = standardize(tok_all[run].astype(f32))
        normed[run] = (hat * gain_rows[0:1, :]).astype(bf16)
        return carried

    lax.fori_loop(0, H, norm_run, 0)
    for copy in br_copies:
        copy.wait_recv()

    def out_tile(n, carried):
        lanes = pl.ds(pl.multiple_of(n * hw, hw), hw)
        grads = mm(mixed_own[...].reshape(H * R, hw), branch_all[:, :, lanes].reshape(H * R, hw), TN)
        term_out[:, :, :, lanes] = grads.astype(bf16).reshape(A, 2, D, hw)
        return carried

    lax.fori_loop(0, W // hw, out_tile, 0)
    out_sum.start()
    up_send[...] = (up_far[...].astype(f32) + from_near[2].astype(f32)).astype(bf16)
    for copy in [*dq_copies, *dz_copies]:
        copy.wait_recv()
    out_sum.pair()
    up_copy = send(up_send, up_last, up_s.at[0], up_r.at[0], (h, here.far * 2 + share))
    over_copy = send(over_in, from_over, up_s.at[1], up_r.at[1], (h, here.over * 2 + share))
    for run in range(H):
        side, at = run // (H // 2), run % (H // 2)
        cosine, sine = cos_all[run], sin_all[run]
        for slab in range(hw // 128):
            lanes = slab * 128
            left, right = dq_in[2 * slab, at].astype(f32), dq_in[2 * slab + 1, at].astype(f32)
            gp[run, :, lanes : lanes + 128] = turn(
                join(left, side, right, side), cosine, sine, True
            ).astype(bf16)
            left, right = dkv_in[2 * slab, run].astype(f32), dkv_in[2 * slab + 1, run].astype(f32)
            gp[run, :, hw + lanes : hw + lanes + 128] = turn(
                join(left, 0, right, 0), cosine, sine, True
            ).astype(bf16)
            gp[run, :, 2 * hw + lanes : 2 * hw + lanes + 128] = join(left, 1, right, 1).astype(bf16)

    def block(chunk):
        return wq_all[chunk].reshape(B * D, 3 * hw)

    for half, (term, item) in enumerate(zip(term_qkv, qkv_sums)):

        def term_chunk(n, carried, half=half, term=term):
            lanes = pl.ds(pl.multiple_of((half * (H // 2) + n) * hw, hw), hw)
            left = normed[:, :, lanes].reshape(H * R, hw)
            grads = mm(left, gp[...].reshape(H * R, 3 * hw), TN).astype(bf16)
            term[:, :, n] = grads.reshape(A, 2, D, 3 * hw)
            return carried

        lax.fori_loop(0, H // 2, term_chunk, 0)
        item.start()
        if half:
            qkv_sums[0].pair()

    def part_of(run, i):
        return remote(g1_send.at[i], g1_in.at[i], g1_s.at[i], g1_r.at[i], (run, b))

    def one_run(i, carried):
        run = run_of(here, i)
        for chunk in range(H):
            lanes = slice(chunk * hw, (chunk + 1) * hw)
            g1_own[:, lanes] = mm(gp[run], block(chunk), NT)

        @pl.when(i < H - 1)
        def _():
            g1_send[i] = g1_own[...].astype(bf16)
            part_of(run, i).start()

        return carried

    lax.fori_loop(0, 1, one_run, 0)
    qkv_sums[1].pair()
    out_sum.cross()
    lax.fori_loop(1, H, one_run, 0)
    qkv_sums[0].cross()
    over_copy.wait_recv()
    gate = kept[0] + from_near[0].astype(f32) + from_over[...].astype(f32) + from_far[0].astype(f32)
    in_swap.out[:, :, :F] = gate.astype(bf16)
    in_swap.out[:, :, 2 * F :] = (kept[2] + from_far[1].astype(f32)).astype(bf16)
    up_copy.wait_recv()
    up = kept[1] + from_near[1].astype(f32) + up_last[...].astype(f32)
    in_swap.out[:, :, F : 2 * F] = up.astype(bf16)
    in_swap.start()
    qkv_sums[1].cross()

    grad = g1_own[...]
    hat, scale = standardize(tok_all[h].astype(f32))
    for i in (1, 2, 0):
        part_of(here.places[i], i).wait_recv()
        grad += g1_in[i].astype(f32)
    row = lax.broadcasted_iota(jnp.int32, (8, W), 0)
    rows = jnp.where(
        row == 0,
        jnp.sum(grad * hat, axis=0, keepdims=True),
        jnp.where(row == 1, gain_part[...], 0.0),
    )
    pick = (
        lax.broadcasted_iota(jnp.int32, (8, 128), 0) == lax.broadcasted_iota(jnp.int32, (8, 128), 1)
    ).astype(bf16)
    for chunk in range(H):
        gain_columns = mm(rows[:, chunk * hw : (chunk + 1) * hw].astype(bf16), pick, TN)
        term_gain[:, :, chunk] = gain_columns.astype(bf16).reshape(A, 2, D, 128)
    gain_sum.start()
    input_grad[...] = grad_middle[...] + norm_back(grad, hat, scale, gain_rows[0:1, :])
    gain_sum.middle()
    result = out_base[...]
    for i, copy in enumerate(o_copies):
        copy.wait_recv()
        result += o_in[i].astype(f32)
    output[...] = result.astype(bf16)
    in_swap.arrive()
    for place in range(H):
        in_grad[:, place * F : (place + 1) * F] = in_swap.landed[place, :, :F].astype(f32)
        in_grad[:, (H + place) * F : (H + place + 1) * F] = in_swap.landed[
            place, :, F : 2 * F
        ].astype(f32)
        down_grad[:, place * F : (place + 1) * F] = in_swap.landed[place, :, 2 * F :].astype(f32)
    for half, item in enumerate(qkv_sums):
        qkv_swap.out[half * (H // 2) : (half + 1) * (H // 2)] = item.close().astype(bf16)
    qkv_swap.start()
    gain_swap.out[...] = gain_sum.close().astype(bf16)
    gain_swap.start()
    out_grad[...] = out_sum.close()
    qkv_swap.arrive()
    for place in range(H):
        for j in range(3):
            qkv_grad[:, j * W + place * hw : j * W + (place + 1) * hw] = qkv_swap.landed[
                place, :, j * hw : (j + 1) * hw
            ].astype(f32)
    gain_swap.arrive()
    total = gain_swap.landed[0].astype(f32)
    for place in range(1, H):
        total += gain_swap.landed[place].astype(f32)
    rows = total.T
    gain_one[...] = rows[0:1, :]
    gain_two[...] = rows[1:2, :]
    for copy in [*dk_copies, *dq_copies, *br_copies, *dz_copies, *o_copies, up_copy, over_copy]:
        copy.wait_send()
    for i in range(H - 1):
        part_of(here.places[i], i).wait_send()
    for item in (out_sum, *qkv_sums, gain_sum, in_swap, qkv_swap, gain_swap):
        item.finish()


def finish(dqp, dkv, tok_all, wq_all, cos_all, sin_all, gain_rows, mixed, grad_middle, gain_part, out_base, out_parts, kept, *terms):
    A, half, R, lanes = dqp.shape
    H = 2 * half
    W = tok_all.shape[-1]
    B = 2 * A
    hw = W // H
    D, F = kept.shape[2:]
    f32, bf16 = jnp.float32, jnp.bfloat16
    shape = jax.ShapeDtypeStruct
    buffer = lambda *sizes: pltpu.VMEM(sizes, bf16)
    arrays = [
        dqp, dkv, tok_all, wq_all, cos_all, sin_all, gain_rows, mixed, grad_middle, gain_part, out_base, out_parts,
        kept, *terms,
    ]
    return pl.pallas_call(
        partial(finish_kernel, H, A),
        in_specs=[in_vmem() if n in (0, 6, 9) else anywhere() for n in range(len(arrays))],
        out_specs=[in_vmem()] * 8,
        out_shape=[
            shape((R, W), bf16),
            shape((R, W), f32),
            shape((D, 3 * W), f32),
            shape((D, W), f32),
            shape((D, 2 * H * F), f32),
            shape((D, H * F), f32),
            shape((1, D), f32),
            shape((1, D), f32),
        ],
        scratch_shapes=[
            buffer(*dkv.shape),
            buffer(*tok_all.shape),
            buffer(*wq_all.shape),
            pltpu.VMEM(cos_all.shape, f32),
            pltpu.VMEM(sin_all.shape, f32),
            buffer(*mixed.shape),
            pltpu.VMEM(grad_middle.shape, f32),
            pltpu.VMEM(out_base.shape, f32),
            buffer(*out_parts.shape),
            pltpu.VMEM(kept.shape, f32),
            *[buffer(*term.shape) for term in terms],
            *[buffer(H, D, F)] * 2,
            buffer(A, H, R, 128),
            buffer(A - 1, H, R, 128),
            buffer(A, H, R, 128),
            buffer(A, half, R, 128),
            buffer(R, W),
            buffer(H, R, W),
            buffer(H, R, 3 * hw),
            buffer(H, R, W),
            buffer(H - 1, R, W),
            buffer(H - 1, R, W),
            pltpu.VMEM((R, W), f32),
            dma(12),
            *[dma(2)] * 2,
            *[dma(H - 1)] * 2,
            *[dma(A)] * 2,
            *[dma(A - 1)] * 4,
            *[dma(H - 1)] * 4,
            *reduce_scratch(A, (H, D, 128)),
            *swap_scratch(H, (D, 3 * F)),
            *swap_scratch(H, (D, 3 * hw)),
            *swap_scratch(H, (D, 128)),
            buffer(A, 2, D, W),
            *[buffer(A, 2, H // 2, D, 3 * hw)] * 2,
            *pair_scratch(A, (D, W)),
            *pair_scratch(A, (H // 2, D, 3 * hw)),
            *pair_scratch(A, (H // 2, D, 3 * hw)),
        ],
        compiler_params=params(2),
        cost_estimate=pl.CostEstimate(flops=2 * 10**9, bytes_accessed=10**7, transcendentals=10**5),
        name="finish",
    )(*arrays)


def per_device_split(
    tokens, attn_gain, w_qkv, w_attn_out, mlp_gain, w_in, w_mlp_out, doc_lengths, cotangent
):
    R, W = tokens.shape
    H, B = lax.axis_size("head"), lax.axis_size("blk")
    A = B // 2
    hw = W // H
    T = H * B * R
    kv, qp, tok_all, cot_all, wq, wm, wo, gain_rows, cos_all, sin_all = project(
        tokens, cotangent, w_qkv, attn_gain[None], mlp_gain[None], w_in, w_mlp_out.T, w_attn_out, doc_lengths
    )
    kv = kv.reshape(T, 2 * HEAD_DIM)
    wm_before = lax.ppermute(wm, "blk", [(i, i + 2) for i in range(B - 2)])
    wm_after = lax.ppermute(wm, "blk", [(i + 2, i) for i in range(B - 2)])
    op, lse = attend(doc_lengths, qp, kv)
    out_base, out_parts, grad_middle, gp, kept, up_far, *out_terms, mixed, gain_part = feed(
        op, tok_all, cot_all, wo.reshape(H, hw, W), wm, wm_before, wm_after, gain_rows
    )
    near, over, far = out_terms
    flipped = lambda flip: [(p, (p // 2 ^ flip) * 2 + p % 2) for p in range(B)]
    near, far = lax.ppermute(near, "blk", flipped(1)), lax.ppermute(far, "blk", flipped(3))
    dqp, dkv = attend_back(doc_lengths, qp, gp, op, lse, kv)
    output, input_grad, qkv_grad, out_grad, in_grad, down_grad, gain_one, gain_two = deliver(
        *finish(
            dqp, dkv.reshape(H, B, R, 128), tok_all, wq, cos_all, sin_all, gain_rows, mixed, grad_middle, gain_part,
            out_base, out_parts, kept, up_far, near, over, far,
        )
    )
    return (
        output,
        input_grad,
        gain_one[0],
        qkv_grad,
        out_grad,
        gain_two[0],
        in_grad,
        down_grad.T,
    )


def per_device(tokens, attn_gain, w_qkv, *rest):
    heads, blocks = lax.axis_size("head"), lax.axis_size("blk")
    fits = (
        heads == 4
        and blocks == 2 * (tokens.shape[1] // HEAD_DIM // heads) == 8
        and w_qkv.shape[0] * heads == 128
        and tokens.shape[0] == 128
    )
    chosen = per_device_split if fits else per_device_general
    return chosen(tokens, attn_gain, w_qkv, *rest)


def solution(mesh):
    placed = (
        P(("head", "blk"), None),
        P(("head", "blk")),
        P(("head", "blk"), None),
        P(("head", "blk"), None),
        P(("head", "blk")),
        P(("head", "blk"), None),
        P(None, ("head", "blk")),
        P(),
        P(("head", "blk"), None),
    )
    return jax.shard_map(
        per_device,
        mesh=mesh,
        in_specs=placed,
        out_specs=(
            P(("head", "blk"), None),
            P(("head", "blk"), None),
            P(("head", "blk")),
            P(("head", "blk"), None),
            P(("head", "blk"), None),
            P(("head", "blk")),
            P(("head", "blk"), None),
            P(None, ("head", "blk")),
        ),
        check_vma=False,
    )
```

```python
from functools import partial

import jax
import jax.numpy as jnp
import numpy as np
from jax import lax
from jax.experimental import pallas as pl
from jax.experimental.pallas import tpu as pltpu
from jax.sharding import PartitionSpec as P

HEAD_DIM = 64


norm_eps = 1e-05
rope_base = 160000.0
neg_large = -1e30


def from_behind(value, axis, by):
    devices = lax.axis_size(axis)
    return lax.ppermute(value, axis, [(i, (i + by) % devices) for i in range(devices)])


def layer_norm(values, gain):
    center = values - jnp.mean(values, axis=-1, keepdims=True)
    spread = jnp.mean(center * center, axis=-1, keepdims=True)
    return center * lax.rsqrt(spread + norm_eps) * gain


def rope_tables(places, head_size):
    half = head_size // 2
    freqs = rope_base ** (-(jnp.arange(half, dtype=jnp.float32) * 2.0) / head_size)
    angles = places.astype(jnp.float32)[:, None] * freqs[None, :]
    angles = jnp.concatenate([angles, angles], axis=1)
    return (jnp.cos(angles), jnp.sin(angles))


def rotate(values, cosine, sine):
    count = values.shape[0]
    head_size = cosine.shape[1]
    half = head_size // 2
    split = values.reshape(count, -1, head_size)
    turned = jnp.concatenate([-split[..., half:], split[..., :half]], axis=-1)
    return (split * cosine[:, None, :] + turned * sine[:, None, :]).reshape(count, -1)


def rotate_pair(query, keys, cosine, sine):
    return (rotate(query, cosine, sine), rotate(keys, cosine, sine))


def doc_numbers(places, ends, lengths):
    passed = places[:, None] >= ends[None, :]
    numbers = jnp.sum(passed.astype(jnp.int32), axis=1)
    offset = jnp.sum(jnp.where(passed, lengths[None, :], 0), axis=1)
    return (numbers, places - offset)


def gelu_gate(lifted):
    half = lifted.shape[1] // 2
    return jax.nn.gelu(lifted[:, :half], approximate=False) * lifted[:, half:]


def tile_scores(query, keys):
    heads = query.shape[1] // HEAD_DIM
    query_split = query.reshape(query.shape[0], heads, HEAD_DIM)
    key_split = keys.reshape(keys.shape[0], heads, HEAD_DIM)
    return jnp.einsum(
        "qhd,khd->hqk", query_split, key_split, preferred_element_type=jnp.float32
    ) * HEAD_DIM ** (-0.5)


def unchanged(state):
    return state


def forward_tile(state, query, keys, values, mask):
    top, total, running = state
    count = query.shape[0]
    heads = top.shape[0]
    scores = tile_scores(query, keys)
    filled = jnp.where(mask[None], scores, neg_large)
    new_top = jnp.maximum(top, jnp.max(filled, axis=-1))
    weights = jnp.where(mask[None], jnp.exp(scores - new_top[:, :, None]), 0.0)
    factor = jnp.exp(top - new_top)
    new_total = total * factor + jnp.sum(weights, axis=-1)
    mixed = jnp.einsum(
        "hqk,khd->qhd",
        weights.astype(jnp.bfloat16),
        values.reshape(-1, heads, HEAD_DIM),
        preferred_element_type=jnp.float32,
    )
    new_running = running.reshape(count, heads, HEAD_DIM) * factor.T[:, :, None] + mixed
    return (new_top, new_total, new_running.reshape(count, heads * HEAD_DIM))


def backward_tile(carry, query, keys, values, mask, norm_log, grad_out, delta):
    query_grad, run_grads = carry
    count = query.shape[0]
    columns = keys.shape[0]
    heads = norm_log.shape[0]
    scores = tile_scores(query, keys)
    probs = jnp.where(mask[None], jnp.exp(scores - norm_log[:, :, None]), 0.0)
    grad_split = grad_out.reshape(count, heads, HEAD_DIM)
    value_split = values.reshape(columns, heads, HEAD_DIM)
    grad_values = jnp.einsum(
        "hqk,qhd->khd", probs.astype(jnp.bfloat16), grad_split, preferred_element_type=jnp.float32
    )
    grad_probs = jnp.einsum(
        "qhd,khd->hqk", grad_split, value_split, preferred_element_type=jnp.float32
    )
    grad_scores = (probs * (grad_probs - delta[:, :, None])).astype(jnp.bfloat16)
    grad_query = jnp.einsum(
        "hqk,khd->qhd",
        grad_scores,
        keys.reshape(columns, heads, HEAD_DIM),
        preferred_element_type=jnp.float32,
    ) * HEAD_DIM ** (-0.5)
    grad_keys = jnp.einsum(
        "hqk,qhd->khd",
        grad_scores,
        query.reshape(count, heads, HEAD_DIM),
        preferred_element_type=jnp.float32,
    ) * HEAD_DIM ** (-0.5)
    added = jnp.stack([grad_keys.reshape(columns, -1), grad_values.reshape(columns, -1)])
    return (query_grad + grad_query.reshape(count, -1), run_grads + added)


def per_device_general(
    tokens, attn_gain, w_qkv, w_attn_out, mlp_gain, w_in, w_mlp_out, doc_lengths, cotangent
):
    own_rows = tokens.shape[0]
    width = tokens.shape[1]
    head_count = lax.axis_size("head")
    cycle_count = lax.axis_size("blk")
    head_place = lax.axis_index("head")
    cycle_place = lax.axis_index("blk")
    group_rows = head_count * own_rows
    block_runs = min(head_count, max(1, 512 // own_rows))
    block_count = head_count // block_runs
    block_rows = block_runs * own_rows
    doc_ends = jnp.cumsum(doc_lengths)
    counter = jnp.arange(own_rows, dtype=jnp.int32)
    own_places = (head_place * cycle_count + cycle_place) * own_rows + counter
    unused_docs, own_positions = doc_numbers(own_places, doc_ends, doc_lengths)
    cosine, sine = rope_tables(own_positions, HEAD_DIM)
    run_numbers = jnp.arange(head_count, dtype=jnp.int32)
    query_places = (
        (run_numbers[:, None] * cycle_count + cycle_place) * own_rows + counter[None, :]
    ).reshape(group_rows)
    query_docs, unused_positions = doc_numbers(query_places, doc_ends, doc_lengths)
    params = (
        lax.all_gather(attn_gain, ("head", "blk"), axis=0, tiled=True),
        lax.all_gather(w_qkv, ("head", "blk"), axis=0, tiled=True),
        lax.all_gather(w_attn_out, ("head", "blk"), axis=0, tiled=True),
        lax.all_gather(mlp_gain, ("head", "blk"), axis=0, tiled=True),
        lax.all_gather(w_in, ("head", "blk"), axis=0, tiled=True),
        lax.all_gather(w_mlp_out, ("head", "blk"), axis=1, tiled=True),
    )
    gain_one, full_qkv, full_attn_out, gain_two, full_in, full_mlp_out = params
    inputs = tokens.astype(jnp.float32)
    normed_one, norm_one_pull = jax.vjp(layer_norm, inputs, gain_one.astype(jnp.float32))
    normed_low = normed_one.astype(jnp.bfloat16)
    projected = jnp.dot(normed_low, full_qkv, preferred_element_type=jnp.float32)
    turned, rope_pull = jax.vjp(
        partial(rotate_pair, cosine=cosine, sine=sine),
        projected[:, :width],
        projected[:, width : 2 * width],
    )
    stacked = jnp.stack(
        [
            turned[0].astype(jnp.bfloat16),
            turned[1].astype(jnp.bfloat16),
            projected[:, 2 * width :].astype(jnp.bfloat16),
        ]
    )
    regrouped = lax.all_to_all(stacked, "head", split_axis=2, concat_axis=1, tiled=True)
    query_heads = regrouped[0]
    key_heads = regrouped[1]
    value_heads = regrouped[2]
    head_width = query_heads.shape[1]
    heads_here = head_width // HEAD_DIM

    def key_docs_at(first):
        places = (
            first % group_rows // own_rows * cycle_count + first // group_rows
        ) * own_rows + counter
        found, unused = doc_numbers(places, doc_ends, doc_lengths)
        return found

    def block_live(block, key_docs):
        block_docs = query_docs[block * block_rows : (block + 1) * block_rows]
        live = jnp.maximum(jnp.min(block_docs), jnp.min(key_docs)) <= jnp.minimum(
            jnp.max(block_docs), jnp.max(key_docs)
        )
        return (block_docs[:, None] == key_docs[None, :], live)

    def fold_forward(state, piece):
        key_part, value_part = piece

        def fold_one_run(number, carried):
            first = number * own_rows
            key_docs = key_docs_at(first)
            keys = lax.dynamic_slice_in_dim(key_part, number * own_rows, own_rows, 0)
            values = lax.dynamic_slice_in_dim(value_part, number * own_rows, own_rows, 0)
            updated = []
            for block in range(block_count):
                mask, live = block_live(block, key_docs)
                query = query_heads[block * block_rows : (block + 1) * block_rows]
                advance = partial(forward_tile, query=query, keys=keys, values=values, mask=mask)
                updated.append(lax.cond(live, advance, unchanged, carried[block]))
            return tuple(updated)

        return lax.fori_loop(0, key_part.shape[0] // own_rows, fold_one_run, state)

    def fresh_state():
        return tuple(
            (
                (
                    jnp.full((heads_here, block_rows), neg_large, jnp.float32),
                    jnp.zeros((heads_here, block_rows), jnp.float32),
                    jnp.zeros((block_rows, head_width), jnp.float32),
                )
                for block in range(block_count)
            )
        )

    def finish(state):
        outputs = []
        logs = []
        for top, total, running in state:
            scaled = running.reshape(block_rows, heads_here, HEAD_DIM) / total.T[:, :, None]
            outputs.append(scaled.reshape(block_rows, head_width))
            logs.append(top + jnp.log(total))
        return (
            jnp.concatenate(outputs, axis=0).astype(jnp.bfloat16),
            jnp.concatenate(logs, axis=1),
        )

    state = fold_forward(
        fresh_state(),
        (
            lax.all_gather(key_heads, "blk", axis=0, tiled=True),
            lax.all_gather(value_heads, "blk", axis=0, tiled=True),
        ),
    )
    out_heads, norm_log = finish(state)
    out_tokens = lax.all_to_all(out_heads, "head", split_axis=0, concat_axis=1, tiled=True)
    middle = inputs + jnp.dot(out_tokens, full_attn_out, preferred_element_type=jnp.float32)
    normed_two, norm_two_pull = jax.vjp(layer_norm, middle, gain_two.astype(jnp.float32))
    normed_two_low = normed_two.astype(jnp.bfloat16)
    lifted = jnp.dot(normed_two_low, full_in, preferred_element_type=jnp.float32)
    activated, geglu_pull = jax.vjp(gelu_gate, lifted)
    activated_low = activated.astype(jnp.bfloat16)
    output = (
        middle + jnp.dot(activated_low, full_mlp_out, preferred_element_type=jnp.float32)
    ).astype(jnp.bfloat16)
    params = (
        lax.all_gather(attn_gain, ("head", "blk"), axis=0, tiled=True),
        lax.all_gather(w_qkv, ("head", "blk"), axis=0, tiled=True),
        lax.all_gather(w_attn_out, ("head", "blk"), axis=0, tiled=True),
        lax.all_gather(mlp_gain, ("head", "blk"), axis=0, tiled=True),
        lax.all_gather(w_in, ("head", "blk"), axis=0, tiled=True),
        lax.all_gather(w_mlp_out, ("head", "blk"), axis=1, tiled=True),
    )
    gain_one, full_qkv, full_attn_out, gain_two, full_in, full_mlp_out = params
    grad_act = jnp.einsum("td,fd->tf", cotangent, full_mlp_out, preferred_element_type=jnp.float32)
    grad_lifted = geglu_pull(grad_act)[0].astype(jnp.bfloat16)
    grad_normed_two = jnp.einsum(
        "tf,df->td", grad_lifted, full_in, preferred_element_type=jnp.float32
    )
    grad_middle_part, grad_gain_two = norm_two_pull(grad_normed_two)
    grad_middle = cotangent.astype(jnp.float32) + grad_middle_part
    grad_branch = grad_middle.astype(jnp.bfloat16)
    grad_mixed = jnp.einsum(
        "te,de->td", grad_branch, full_attn_out, preferred_element_type=jnp.float32
    ).astype(jnp.bfloat16)
    grad_heads = lax.all_to_all(grad_mixed, "head", split_axis=1, concat_axis=0, tiled=True)
    state = fold_forward(
        fresh_state(),
        (
            lax.all_gather(key_heads, "blk", axis=0, tiled=True),
            lax.all_gather(value_heads, "blk", axis=0, tiled=True),
        ),
    )
    out_heads, norm_log = finish(state)
    delta = jnp.einsum(
        "qhd,qhd->hq",
        grad_heads.reshape(group_rows, heads_here, HEAD_DIM).astype(jnp.float32),
        out_heads.reshape(group_rows, heads_here, HEAD_DIM).astype(jnp.float32),
    )

    def piece_backward(query_grads, key_part, value_part, start):
        piece_rows = key_part.shape[0]

        def piece_one_run(number, carried):
            query_now, piece_grads = carried
            first = start + number * own_rows
            key_docs = key_docs_at(first)
            keys = lax.dynamic_slice_in_dim(key_part, number * own_rows, own_rows, 0)
            values = lax.dynamic_slice_in_dim(value_part, number * own_rows, own_rows, 0)
            run_grads = jnp.zeros((2, own_rows, head_width), jnp.float32)
            updated = []
            for block in range(block_count):
                mask, live = block_live(block, key_docs)
                lower = block * block_rows
                upper = (block + 1) * block_rows
                advance = partial(
                    backward_tile,
                    query=query_heads[lower:upper],
                    keys=keys,
                    values=values,
                    mask=mask,
                    norm_log=norm_log[:, lower:upper],
                    grad_out=grad_heads[lower:upper],
                    delta=delta[:, lower:upper],
                )
                new_query, run_grads = lax.cond(
                    live, advance, unchanged, (query_now[block], run_grads)
                )
                updated.append(new_query)
            piece_grads = lax.dynamic_update_slice_in_dim(
                piece_grads, run_grads, number * own_rows, 1
            )
            return (tuple(updated), piece_grads)

        return lax.fori_loop(
            0,
            piece_rows // own_rows,
            piece_one_run,
            (query_grads, jnp.zeros((2, piece_rows, head_width), jnp.float32)),
        )

    start_query = tuple(
        (jnp.zeros((block_rows, head_width), jnp.float32) for block in range(block_count))
    )

    def cycle_step(step, carried):
        query_now, blocks, travelling = carried
        owner = (cycle_place - step) % cycle_count
        query_now, piece_grads = piece_backward(query_now, blocks[0], blocks[1], owner * group_rows)
        travelling = travelling + piece_grads
        blocks = from_behind(blocks, "blk", 1)
        travelling = from_behind(travelling.astype(jnp.bfloat16), "blk", 1).astype(travelling.dtype)
        return (query_now, blocks, travelling)

    start_cycle = (
        start_query,
        jnp.stack([key_heads, value_heads]),
        jnp.zeros((2, group_rows, head_width), jnp.float32),
    )
    query_grads, unused_blocks, own_grads = lax.fori_loop(0, cycle_count, cycle_step, start_cycle)
    grad_stack = jnp.stack(
        [
            jnp.concatenate(query_grads, axis=0).astype(jnp.bfloat16),
            own_grads[0].astype(jnp.bfloat16),
            own_grads[1].astype(jnp.bfloat16),
        ]
    )
    back_tokens = lax.all_to_all(grad_stack, "head", split_axis=1, concat_axis=2, tiled=True)
    grad_query, grad_keys = rope_pull(
        (back_tokens[0].astype(jnp.float32), back_tokens[1].astype(jnp.float32))
    )
    grad_projected = jnp.concatenate(
        [grad_query, grad_keys, back_tokens[2].astype(jnp.float32)], axis=1
    ).astype(jnp.bfloat16)
    grad_normed_one = jnp.einsum(
        "te,de->td", grad_projected, full_qkv, preferred_element_type=jnp.float32
    )
    grad_input_part, grad_gain_one = norm_one_pull(grad_normed_one)
    input_grad = grad_middle + grad_input_part

    def columns(source):
        return source

    term_qkv = jnp.einsum(
        "td,te->de", columns(normed_low), grad_projected, preferred_element_type=jnp.float32
    )
    term_out = jnp.einsum(
        "td,te->de", columns(out_tokens), grad_branch, preferred_element_type=jnp.float32
    )
    term_in = jnp.einsum(
        "td,tf->df", columns(normed_two_low), grad_lifted, preferred_element_type=jnp.float32
    )
    term_down = jnp.einsum(
        "td,tf->df", columns(cotangent), activated_low, preferred_element_type=jnp.float32
    )
    sums = lax.psum_scatter(
        jnp.concatenate([term_qkv, term_out, term_in, term_down], axis=1),
        ("head", "blk"),
        scatter_dimension=0,
        tiled=True,
    )
    ff_width = full_mlp_out.shape[0]
    qkv_grad = sums[:, : 3 * width]
    attn_out_grad = sums[:, 3 * width : 4 * width]
    in_grad = sums[:, 4 * width : 4 * width + 2 * ff_width]
    down_grad = sums[:, 4 * width + 2 * ff_width :].T
    gain_sums = lax.psum_scatter(
        jnp.stack([grad_gain_one, grad_gain_two]), ("head", "blk"), scatter_dimension=1, tiled=True
    )
    return (
        output,
        input_grad,
        gain_sums[0],
        qkv_grad,
        attn_out_grad,
        gain_sums[1],
        in_grad,
        down_grad,
    )


VMEM = 62 * 2**20
MESH = pl.DeviceIdType.MESH
KEY_STEP = 512
KEY_ALIGN = 256
NN = (((1,), (0,)), ((), ()))
NT = (((1,), (1,)), ((), ()))
TN = (((0,), (0,)), ((), ()))


def mm(left, right, dims=NN):
    return lax.dot_general(left, right, dims, preferred_element_type=jnp.float32)


def params(collective_id=None):
    if collective_id is None:
        return pltpu.CompilerParams(vmem_limit_bytes=VMEM)
    return pltpu.CompilerParams(
        collective_id=collective_id, has_side_effects=True, vmem_limit_bytes=VMEM
    )


def in_vmem():
    return pl.BlockSpec(memory_space=pltpu.VMEM)


def anywhere():
    return pl.BlockSpec(memory_space=pl.ANY)


def in_smem():
    return pl.BlockSpec(memory_space=pltpu.SMEM)


def dma(*counts):
    return pltpu.SemaphoreType.DMA(counts)


def halves(packed, side):
    wide = packed.astype(jnp.float32)
    if side:
        wide = pltpu.roll(wide, HEAD_DIM, 1)
    lane = lax.broadcasted_iota(jnp.int32, wide.shape, 1)
    return jnp.where(lane < HEAD_DIM, wide, 0.0)


def tile_span(lengths, side, R, T):
    hh, u = pl.program_id(0), pl.program_id(1)
    runs, parts = 2 * pl.num_programs(0), 2 * pl.num_programs(1)
    share = lax.rem(lax.axis_index("blk"), 2)
    first = (((hh + side * (runs // 2)) * parts + 2 * u) * 2 + share) * R
    last = first + 3 * R - 1
    lane = lax.broadcasted_iota(jnp.int32, (1, 2 * R), 1)
    place = first + lane + jnp.where(lane < R, 0, R)

    def one(d, carried):
        low, begin, stop, start, end = carried
        high = low + lengths[d]
        inside = (place >= low) & (place < high)
        return (
            high,
            jnp.where(inside, low, begin),
            jnp.where(inside, high, stop),
            jnp.where((first >= low) & (first < high), low, start),
            jnp.where((last >= low) & (last < high), high, end),
        )

    zero = jnp.int32(0)
    unused, begin, stop, start, end = lax.fori_loop(
        0,
        lengths.shape[0],
        one,
        (zero, jnp.zeros_like(place), jnp.zeros_like(place), zero, zero),
        unroll=True,
    )
    start = start // KEY_ALIGN
    steps = (end - start * KEY_ALIGN + KEY_STEP - 1) // KEY_STEP
    start = jnp.minimum(start, T // KEY_ALIGN - steps * (KEY_STEP // KEY_ALIGN))
    return (begin, stop, start, steps)


def attend_kernel(lengths, qp, kv, op, lse, s_scr):
    pairs = qp.shape[0] * qp.shape[2]
    T = kv.shape[0]
    half_runs = pl.num_programs(0)
    hh, u = pl.program_id(0), pl.program_id(1)
    at = lax.broadcasted_iota(jnp.int32, (KEY_STEP, pairs), 0)
    results = []
    for side in (0, 1):
        tile = (hh + side * half_runs) * pl.num_programs(1) + u
        begin, stop, start, steps = tile_span(lengths, side, pairs // 2, T)
        query = (halves(qp[...].reshape(pairs, 2 * HEAD_DIM), side) * HEAD_DIM**-0.5).astype(
            jnp.bfloat16
        )

        def keys_at(n):
            first = pl.multiple_of(start * KEY_ALIGN + n * KEY_STEP, KEY_ALIGN)
            return (first, kv[pl.ds(first, KEY_STEP), :])

        def score(n, top):
            first, keys = keys_at(n)
            same = (at >= begin - first) & (at < stop - first)
            scores = jnp.where(same, mm(keys, query, NT), neg_large)
            s_scr[n] = scores
            return jnp.maximum(top, jnp.max(scores, axis=0, keepdims=True))

        top = lax.fori_loop(0, steps, score, jnp.full((1, pairs), neg_large, jnp.float32))

        def mix(n, carried):
            total, acc = carried
            unused, keys = keys_at(n)
            weights = jnp.exp(s_scr[n] - top)
            total = total + jnp.sum(weights, axis=0, keepdims=True)
            return (total, acc + mm(keys, weights.astype(jnp.bfloat16), TN))

        total, acc = lax.fori_loop(
            0,
            steps,
            mix,
            (jnp.zeros((1, pairs), jnp.float32), jnp.zeros((2 * HEAD_DIM, pairs), jnp.float32)),
        )
        lse[tile] = top + jnp.log(total)
        results.append(acc[HEAD_DIM:] / total)
    both = jnp.concatenate(results, axis=0).T
    op[...] = both.astype(jnp.bfloat16).reshape(op.shape)


def attend(lengths, qp, kv):
    parts, half_runs, rows, lanes = qp.shape
    tiles = half_runs * parts
    piece = pl.BlockSpec((2, 1, rows, lanes), lambda i, j, s: (j, i, 0, 0))
    return pl.pallas_call(
        attend_kernel,
        grid_spec=pltpu.PrefetchScalarGridSpec(
            num_scalar_prefetch=1,
            grid=(half_runs, parts // 2),
            in_specs=[piece, in_vmem()],
            out_specs=[piece, in_vmem()],
            scratch_shapes=[pltpu.VMEM((kv.shape[0] // KEY_STEP, KEY_STEP, 2 * rows), jnp.float32)],
        ),
        out_shape=[
            jax.ShapeDtypeStruct(qp.shape, jnp.bfloat16),
            jax.ShapeDtypeStruct((tiles, 1, 2 * rows), jnp.float32),
        ],
        compiler_params=params(),
        cost_estimate=pl.CostEstimate(
            flops=10**9, bytes_accessed=50 * 10**6, transcendentals=10**6
        ),
        name="attend",
    )(lengths, qp, kv)


def attend_back_kernel(
    lengths, qp, gp, op, lse, kv, dqp, dkv, acc_scr
):
    pairs = qp.shape[0] * qp.shape[2]
    T = kv.shape[0]
    half_runs = pl.num_programs(0)
    hh, u = pl.program_id(0), pl.program_id(1)
    begins = (hh == 0) & (u == 0)
    ends = (hh == half_runs - 1) & (u == pl.num_programs(1) - 1)
    @pl.when(begins)
    def _():
        acc_scr[...] = jnp.zeros_like(acc_scr)

    at = lax.broadcasted_iota(jnp.int32, (KEY_STEP, pairs), 0)
    lane = lax.broadcasted_iota(jnp.int32, (pairs, 2 * HEAD_DIM), 1)
    flat = (pairs, 2 * HEAD_DIM)
    results = []
    for side in (0, 1):
        tile = (hh + side * half_runs) * pl.num_programs(1) + u
        begin, stop, start, steps = tile_span(lengths, side, pairs // 2, T)
        query = (halves(qp[...].reshape(flat), side) * HEAD_DIM**-0.5).astype(jnp.bfloat16)
        pieces = []
        for n in range(2):
            piece = gp[n, hh + side * half_runs].astype(jnp.float32)
            pieces += [pltpu.roll(piece, HEAD_DIM, 1), piece]
        grad = jnp.where(lane < HEAD_DIM, 0.0, jnp.concatenate(pieces, axis=0))
        mixed = op[...].reshape(flat).astype(jnp.float32)
        if not side:
            mixed = pltpu.roll(mixed, HEAD_DIM, 1)
        delta = jnp.sum((grad * mixed).T, axis=0, keepdims=True)
        both = jnp.concatenate([query, grad.astype(jnp.bfloat16)], axis=0)
        logs = lse[tile]

        def step(n, dq):
            first = pl.multiple_of(start * KEY_ALIGN + n * KEY_STEP, KEY_ALIGN)
            rows = pl.ds(first, KEY_STEP)
            keys = kv[rows, :]
            same = (at >= begin - first) & (at < stop - first)
            products = mm(keys, both, NT)
            probs = jnp.where(same, jnp.exp(products[:, :pairs] - logs), 0.0)
            grad_scores = (probs * (products[:, pairs:] - delta)).astype(jnp.bfloat16)
            left = jnp.concatenate([grad_scores, probs.astype(jnp.bfloat16)], axis=1)
            acc_scr[rows, :] += mm(left, both)
            return dq + mm(keys, grad_scores, TN)

        dq = lax.fori_loop(0, steps, step, jnp.zeros((2 * HEAD_DIM, pairs), jnp.float32))
        results.append(dq[:HEAD_DIM] * HEAD_DIM**-0.5)
    dqp[...] = jnp.concatenate(results, axis=0).T.astype(jnp.bfloat16).reshape(dqp.shape)

    @pl.when(ends)
    def _():
        dkv[...] = acc_scr[...].astype(dkv.dtype)


def attend_back(lengths, qp, gp, op, lse, kv):
    parts, half_runs, rows, lanes = qp.shape
    piece = pl.BlockSpec((2, 1, rows, lanes), lambda i, j, s: (j, i, 0, 0))
    grads = pl.BlockSpec((2, 2 * half_runs, rows // 2, lanes), lambda i, j, s: (j, 0, 0, 0))
    return pl.pallas_call(
        attend_back_kernel,
        grid_spec=pltpu.PrefetchScalarGridSpec(
            num_scalar_prefetch=1,
            grid=(half_runs, parts // 2),
            in_specs=[piece, grads, piece, *[in_vmem()] * 2],
            out_specs=[piece, in_vmem()],
            scratch_shapes=[pltpu.VMEM(kv.shape, jnp.float32)],
        ),
        out_shape=[
            jax.ShapeDtypeStruct(qp.shape, jnp.bfloat16),
            jax.ShapeDtypeStruct(kv.shape, jnp.bfloat16),
        ],
        compiler_params=params(),
        cost_estimate=pl.CostEstimate(
            flops=3 * 10**9, bytes_accessed=60 * 10**6, transcendentals=10**6
        ),
        name="attend_back",
    )(lengths, qp, gp, op, lse, kv)


def deliver_kernel(*refs):
    count = len(refs) // 2
    for source, target in zip(refs[:count], refs[count:]):
        target[...] = source[...]


def deliver(*arrays):
    return pl.pallas_call(
        deliver_kernel,
        in_specs=[in_vmem()] * len(arrays),
        out_specs=[in_vmem()] * len(arrays),
        out_shape=[jax.ShapeDtypeStruct(a.shape, a.dtype) for a in arrays],
        compiler_params=params(),
        name="deliver",
    )(*arrays)


def meet(peers):
    barrier = pltpu.get_barrier_semaphore()
    for peer in peers:
        pl.semaphore_signal(barrier, inc=1, device_id=peer, device_id_type=MESH)
    pl.semaphore_wait(barrier, len(peers))


def remote(source, target, send_sem, recv_sem, peer):
    return pltpu.make_async_remote_copy(
        src_ref=source,
        dst_ref=target,
        send_sem=send_sem,
        recv_sem=recv_sem,
        device_id=peer,
        device_id_type=MESH,
    )


def send(source, target, send_sem, recv_sem, peer):
    copy = remote(source, target, send_sem, recv_sem, peer)
    copy.start()
    return copy


class Place:
    def __init__(self, parts):
        h, b = lax.axis_index("head"), lax.axis_index("blk")
        self.h, self.b, self.parts = h, b, parts
        self.part, self.share = b // 2, lax.rem(b, 2)
        x, y = lax.rem(h, 2), h // 2
        self.places = [(1 - y) * 2 + 1 - x, y * 2 + 1 - x, (1 - y) * 2 + x]
        self.across = [(place, b) for place in self.places]
        self.there = [lax.rem(self.part + i, parts) for i in range(1, parts)]
        self.back = [lax.rem(self.part + parts - i, parts) for i in range(1, parts)]
        self.along = [(h, part * 2 + self.share) for part in self.there]
        self.beside = (h, self.part * 2 + 1 - self.share)
        self.near = self.part + 1 - 2 * lax.rem(self.part, 2)
        self.over = lax.rem(self.part + 2, 4)
        self.far = 3 - self.part
        self.askew = [(h, part * 2 + 1 - self.share) for part in self.there]


class LineGather:
    def __init__(self, view, own, here, sems):
        self.view, self.own, self.here, self.parts = view, own, here, here.parts
        self.right_s, self.left_s, self.line_r, self.core_s, self.core_r = sems
        self.first = 0

    def _copy(self, source, block, side):
        here = self.here
        if side == 0:
            sems, peer = (self.core_s, self.core_r), here.beside
        else:
            sems = (self.right_s if side > 0 else self.left_s, self.line_r)
            peer = (here.h, (here.part + side) * 2 + here.share)
        return remote(
            source, self.view(block, here.share), sems[0].at[block], sems[1].at[block], peer
        )

    def _can(self, side):
        return self.here.part < self.parts - 1 if side > 0 else self.here.part > 0

    def start(self):
        for side in (1, -1):

            @pl.when(self._can(side))
            def _():
                self._copy(self.own, self.here.part, side).start()

        self._copy(self.own, self.here.part, 0).start()

    def start_from(self, near):
        self.first = 1
        for side in (1, -1):
            block = self.here.part - side

            @pl.when((block >= 0) & (block < self.parts) & self._can(side))
            def _():
                self._copy(near[side], block, side).start()

        self._copy(self.own, self.here.part, 0).start()
        for side in (1, -1):
            block = self.here.part - side

            @pl.when((block >= 0) & (block < self.parts))
            def _():
                self._copy(near[side], block, 0).start()

    def step(self, k):
        for side in (1, -1):
            block = self.here.part - side * k

            @pl.when((block >= 0) & (block < self.parts))
            def _():
                there = self.view(block, self.here.share)
                self._copy(there, block, side).wait_recv()

                @pl.when(self._can(side))
                def _():
                    self._copy(there, block, side).start()

                self._copy(there, block, 0).start()

    def arrive(self):
        for block in range(self.parts):
            self._copy(self.own, block, 0).wait_recv()

    def finish(self):
        for side in (1, -1):
            for block in range(self.parts):
                first = self.here.part - side * self.first
                sent = block <= first if side > 0 else block >= first

                @pl.when(sent & self._can(side))
                def _():
                    self._copy(self.own, block, side).wait_send()

        for block in range(self.parts):
            self._copy(self.own, block, 0).wait_send()


class CornerGather:
    def __init__(self, whole, half, own, here, sems):
        self.whole, self.half, self.own, self.here = whole, half, own, here
        self.send_s, self.recv_s = sems

    def _copy(self, n):
        h, (corner, x, y) = self.here.h, self.here.across
        if n < 2:
            source, target, peer = self.own, self.whole(h), (x, y)[n]
        else:
            block = (y, x)[n - 2][0]
            source = target = self.half(block, n - 2)
            peer = (x, y)[n - 2]
        return remote(source, target, self.send_s.at[n], self.recv_s.at[n], peer)

    def start(self):
        for n in range(2):
            self._copy(n).start()

    def forward(self):
        for n in range(2):
            self._copy(n).wait_recv()
        for n in range(2, 4):
            self._copy(n).start()

    def arrive(self):
        for n in range(2, 4):
            self._copy(n).wait_recv()

    def finish(self):
        for n in range(4):
            self._copy(n).wait_send()


def local(source, target, sem):
    copy = pltpu.make_async_copy(source, target, sem)
    copy.start()
    return copy


def line_sems(parts):
    return [dma(parts)] * 5


def standardize(values):
    center = values - jnp.mean(values, axis=-1, keepdims=True)
    spread = jnp.mean(center * center, axis=-1, keepdims=True)
    scale = lax.rsqrt(spread + norm_eps)
    return (center * scale, scale)


def norm_back(grad, hat, scale, gain):
    inner = grad * gain
    return scale * (
        inner
        - jnp.mean(inner, axis=-1, keepdims=True)
        - hat * jnp.mean(inner * hat, axis=-1, keepdims=True)
    )


def turn(values, cosine, sine, back=False):
    lane = lax.broadcasted_iota(jnp.int32, values.shape, 1)
    first = lax.rem(lane, HEAD_DIM) < HEAD_DIM // 2
    source = values * sine if back else values
    ahead = pltpu.roll(source, 128 - HEAD_DIM // 2, 1)
    behind = pltpu.roll(source, HEAD_DIM // 2, 1)
    if back:
        return values * cosine + jnp.where(first, ahead, -behind)
    return values * cosine + jnp.where(first, -ahead, behind) * sine


def join(left, left_side, right, right_side):
    lane = lax.broadcasted_iota(jnp.int32, left.shape, 1)
    left = pltpu.roll(left, HEAD_DIM, 1) if left_side else left
    right = right if right_side else pltpu.roll(right, HEAD_DIM, 1)
    return jnp.where(lane < HEAD_DIM, left, right)


class Reduce:
    def __init__(self, term, core_in, line_out, line_in, here, sems):
        self.term, self.core_in, self.line_out, self.line_in = term, core_in, line_out, line_in
        self.here, self.parts = here, here.parts
        self.core_s, self.core_r, self.line_s, self.line_r = sems

    def _core(self):
        return remote(
            self.term.at[:, 1 - self.here.share],
            self.core_in,
            self.core_s.at[0],
            self.core_r.at[0],
            self.here.beside,
        )

    def _line(self, i):
        return remote(
            self.line_out[i],
            self.line_in.at[i],
            self.line_s.at[i],
            self.line_r.at[i],
            self.here.along[i],
        )

    def _sum(self, there):
        own = self.term[there, self.here.share].astype(jnp.float32)
        return own + self.core_in[there].astype(jnp.float32)

    def start(self):
        self._core().start()

    def core_sums(self):
        self._core().wait_recv()
        return self._sum

    def middle(self):
        self._core().wait_recv()
        for i, there in enumerate(self.here.there):
            self.line_out[i][...] = self._sum(there).astype(jnp.bfloat16)
            self._line(i).start()

    def close(self):
        total = self._sum(self.here.part)
        for i in range(self.parts - 1):
            self._line(i).wait_recv()
            total += self.line_in[i].astype(jnp.float32)
        return total

    def core_finish(self):
        self._core().wait_send()

    def finish(self):
        self.core_finish()
        for i in range(self.parts - 1):
            self._line(i).wait_send()


def reduce_scratch(parts, shape):
    return [
        pltpu.VMEM((parts, 2, *shape), jnp.bfloat16),
        pltpu.VMEM((parts, *shape), jnp.bfloat16),
        pltpu.VMEM((parts - 1, *shape), jnp.bfloat16),
        pltpu.VMEM((parts - 1, *shape), jnp.bfloat16),
        dma(1),
        dma(1),
        dma(parts - 1),
        dma(parts - 1),
    ]


class PairReduce:
    def __init__(self, core_in, near_out, near_in, far_out, far_in, *sems, term, here):
        self.term, self.core_in, self.near_out, self.near_in = term, core_in, near_out, near_in
        self.far_out, self.far_in, self.sems, self.here = far_out, far_in, sems, here

    def _copy(self, step):
        here = self.here
        source, target, peer = (
            (self.term.at[:, 1 - here.share], self.core_in, here.beside),
            (self.near_out, self.near_in, (here.h, here.near * 2 + here.share)),
            (self.far_out, self.far_in, (here.h, here.far * 2 + here.share)),
        )[step]
        return remote(source, target, self.sems[2 * step].at[0], self.sems[2 * step + 1].at[0], peer)

    def _sum(self, there):
        own = self.term[there, self.here.share].astype(jnp.float32)
        return own + self.core_in[there].astype(jnp.float32)

    def start(self):
        self._copy(0).start()

    def pair(self):
        self._copy(0).wait_recv()
        self.near_out[0] = self._sum(self.here.near).astype(jnp.bfloat16)
        self.near_out[1] = self._sum(self.here.over).astype(jnp.bfloat16)
        self._copy(1).start()

    def cross(self):
        self._copy(1).wait_recv()
        self.far_out[...] = (
            self._sum(self.here.far) + self.near_in[1].astype(jnp.float32)
        ).astype(jnp.bfloat16)
        self._copy(2).start()

    def close(self):
        self._copy(2).wait_recv()
        total = self._sum(self.here.part) + self.near_in[0].astype(jnp.float32)
        return total + self.far_in[...].astype(jnp.float32)

    def finish(self):
        for step in range(3):
            self._copy(step).wait_send()


def pair_scratch(parts, shape):
    return [
        pltpu.VMEM((parts, *shape), jnp.bfloat16),
        *[pltpu.VMEM((2, *shape), jnp.bfloat16)] * 2,
        *[pltpu.VMEM(shape, jnp.bfloat16)] * 2,
        *[dma(1)] * 6,
    ]


def reducer(scratch, here):
    term, core_in, line_out, line_in, *sems = scratch
    outs = [line_out.at[i] for i in range(here.parts - 1)]
    return (term, Reduce(term, core_in, outs, line_in, here, sems))


class Swap:
    def __init__(self, out, landed, send_s, recv_s, here):
        self.out, self.landed, self.here = out, landed, here
        self.send_s, self.recv_s = send_s, recv_s

    def start(self):
        here = self.here
        self.copies = [
            send(self.out.at[peer[0]], self.landed.at[here.h], self.send_s.at[i], self.recv_s.at[i], peer)
            for i, peer in enumerate(here.across)
        ]
        self.landed[here.h] = self.out[here.h]

    def arrive(self):
        for copy in self.copies:
            copy.wait_recv()

    def finish(self):
        for copy in self.copies:
            copy.wait_send()


def swap_scratch(heads, shape):
    return [
        pltpu.VMEM((heads, *shape), jnp.bfloat16),
        pltpu.VMEM((heads, *shape), jnp.bfloat16),
        dma(heads - 1),
        dma(heads - 1),
    ]


def run_of(here, i):
    x, y = lax.rem(here.h, 2), here.h // 2
    x = x + (1 - i // 2) * (1 - 2 * x)
    y = y + (1 - i % 2) * (1 - 2 * y)
    return y * 2 + x


def load(pairs, sems):
    copies = [pltpu.make_async_copy(*pair, sems.at[i]) for i, pair in enumerate(pairs)]
    for copy in copies:
        copy.start()
    return copies


def forward_kernel(
    H, A, tok_in, cot_in, wq_in, gain_one, gain_two, w_in_in, w_down_in, w_out_in, lengths,
    kv_out, q_out, op_out, lse, go, tok_out, wq_out, cos_out, sin_out, gain_rows, gain_part, mixed_out, middle_out,
    base_out, parts_out, kept_out, up_out, near_to, over_to, far_to,
    cot, w_in, w_down, w_out, tok_all, cot_all, wq_all, cos_all, sin_all,
    wq_st, wm_src, wm_own, wo_all, kv, kv_send, q_all, q_send, q_runs, hats, gain_src, gain_st, gain_tile, gain_all,
    bounds, s_scr, op, mx_in, mixed_own, mixed_early, mixed_late, wm_all, middle, normed, act, lift,
    g2_send, g2_in, g2_own, gm_send, in_term, in_core, down_term, down_core, down_send, down_in,
    out_base, out_parts, grad_middle, kept, up_far, near_out, over_out, far_out,
    load_s, store_s, own_s, o_s,
    tok_s, tok_r, wq_s, wq_r, wm_s, wm_r, ga_s, ga_r, gb_s, gb_r, wx_s, wx_r, wf_s, wf_r, cot_s, cot_r,
    q_s, q_r, kv_s, kv_r, kc_s, kc_r, mx_s, mx_r, ma_s, ma_r, g2_s, g2_r, gm_s, gm_r,
    in_core_s, in_core_r, down_core_s, down_core_r, pair_s, pair_r, *line,
):
    f32, bf16 = jnp.float32, jnp.bfloat16
    R, W = tok_all.shape[1:]
    B = 2 * A
    hw = W // H
    D = wq_in.shape[0]
    F = w_in.shape[1] // 2 // H
    here = Place(A)
    h, b, part, share = here.h, here.b, here.part, here.share
    across, along, beside = here.across, here.along, here.beside

    def slices(source, target, place):
        return [
            (
                source.at[:, pl.ds(pl.multiple_of(j * W + place * hw, hw), hw)],
                target.at[h, :, j * hw : (j + 1) * hw],
            )
            for j in range(3)
        ]

    loads = [
        local(source, target, load_s.at[n])
        for n, (source, target) in enumerate(
            [
                (w_out_in, w_out), (w_in_in, w_in), (w_down_in, w_down), (cot_in, cot), (tok_in, tok_all.at[h]),
                *slices(wq_in, wq_st, h),
            ]
        )
    ]
    row = lax.broadcasted_iota(jnp.int32, (8, 128), 0)
    lane = lax.broadcasted_iota(jnp.int32, (8, 128), 1)
    gain_src[...] = jnp.zeros((8, 128), f32)
    gain_src[0:1, :D] = gain_one[...].astype(f32)
    gain_src[1:2, :D] = gain_two[...].astype(f32)
    gain_src[...] = pltpu.roll(gain_src[...], h * D, 1)
    others = [
        (run_of(here, i), lax.rem(part + j, A) * 2 + share)
        for i in range(H)
        for j in range(A)
        if i < H - 1 or j
    ]
    meet([*others, *here.askew, beside])

    for i, peer in enumerate(across):
        for source, target in slices(wq_in, wq_st, peer[0]):
            send(source, target, wq_s.at[i], wq_r.at[i], peer)
    wq_copies = [
        remote(wq_st.at[peer[0]], wq_st.at[h], wq_s.at[i], wq_r.at[i], peer)
        for i, peer in enumerate(across)
    ]
    gain_copies = [
        send(gain_src, gain_st.at[i], ga_s.at[i], ga_r.at[i], peer) for i, peer in enumerate(across)
    ]
    wo_line = LineGather(lambda block, side: wo_all.at[h, block, side], w_out, here, line[:5])
    loads[0].wait()
    wo_line.start()
    stores = [local(w_out, wo_all.at[h, part, share], own_s.at[0])]
    for copy in loads[1:]:
        copy.wait()
    for place in range(H):
        wm_src[place, :, :F] = w_in[:, place * F : (place + 1) * F]
        wm_src[place, :, F : 2 * F] = w_in[:, (H + place) * F : (H + place + 1) * F]
        wm_src[place, :, 2 * F :] = w_down[:, place * F : (place + 1) * F]
    wm_own[h] = wm_src[h]
    cot_all[h] = cot[...]

    wide = lax.broadcasted_iota(jnp.int32, (R, 128), 1)
    freqs = jnp.exp(
        lax.rem(wide, HEAD_DIM // 2).astype(f32) * (-2.0 / HEAD_DIM * float(np.log(rope_base)))
    )

    def tables(run):
        place = (run * B + b) * R + lax.broadcasted_iota(jnp.int32, (R, 128), 0)

        def one(d, carried):
            low, begin = carried
            return (low + lengths[d], jnp.where(place >= low, low, begin))

        unused, begin = lax.fori_loop(
            0, lengths.shape[0], one, (jnp.int32(0), jnp.zeros((R, 128), jnp.int32))
        )
        angles = (place - begin).astype(f32) * freqs
        cos_all[run] = jnp.cos(angles)
        sin_all[run] = jnp.sin(angles)

    tables(0)
    tables(1)
    wo_line.step(1)
    for copy in wq_copies:
        copy.wait_recv()
    wq_lines = []
    for half in range(2):
        rows = pl.ds(half * (H // 2), H // 2)
        wq_lines.append(
            LineGather(
                lambda block, side, rows=rows: wq_all.at[rows, block * 2 + side],
                wq_st.at[rows],
                here,
                line[5 * half + 5 : 5 * half + 10],
            )
        )
        wq_lines[half].start()
    tok_copies = [
        send(tok_in, tok_all.at[h], tok_s.at[i], tok_r.at[i], peer) for i, peer in enumerate(across)
    ]
    tile = gain_src[...]
    for i, copy in enumerate(gain_copies):
        copy.wait_recv()
        tile += gain_st[i]
    gain_tile[...] = tile
    gain_all[b] = tile
    gain_copies += [
        send(gain_tile, gain_all.at[b], gb_s.at[i], gb_r.at[i], peer)
        for i, peer in enumerate([*along, *here.askew, beside])
    ]
    wo_line.step(2)
    wq_all[:, b] = wq_st[...]
    tables(2)
    wq_lines[0].step(1)
    wo_line.step(3)
    wq_lines[1].step(1)
    wo_line.arrive()
    spread = CornerGather(
        lambda place: wo_all.at[place, :, share],
        lambda place, half: wo_all.at[place, half * (A // 2) : (half + 1) * (A // 2), share],
        wo_all.at[h, :, share],
        here,
        (wx_s, wx_r),
    )
    for copy in stores[:1]:
        copy.wait()
    spread.start()
    wm_copies = [
        send(wm_src.at[peer[0]], wm_own.at[h], wm_s.at[i], wm_r.at[i], peer)
        for i, peer in enumerate(across)
    ]
    cot_gather = CornerGather(
        lambda place: cot_all.at[place],
        lambda place, half: cot_all.at[place, half * (R // 2) : (half + 1) * (R // 2)],
        cot,
        here,
        (cot_s, cot_r),
    )
    cot_gather.start()
    tables(3)
    stores += [local(cos_all, cos_out, store_s.at[0]), local(sin_all, sin_out, store_s.at[1])]
    for copy in tok_copies:
        copy.wait_recv()
    stores.append(local(tok_all, tok_out, store_s.at[2]))

    def norm_run(run, carried):
        hat, unused = standardize(tok_all[run].astype(f32))
        hats[run] = hat
        return carried

    wq_lines[0].step(2)
    lax.fori_loop(0, H // 2, norm_run, 0)
    wq_lines[1].step(2)
    lax.fori_loop(H // 2, H, norm_run, 0)
    for copy in gain_copies[len(across) :]:
        copy.wait_recv()
    for slab in range(W // 128):
        place, first = slab // (hw // 128), slab % (hw // 128) * (128 // D)
        piece = jnp.zeros((8, 128), f32)
        for j in range(128 // D):
            moved = gain_all[first + j]
            if j != place:
                moved = pltpu.roll(moved, (j - place) * D % 128, 1)
            piece = jnp.where(lane // D == j, moved, piece)
        gain_rows[:, slab * 128 : (slab + 1) * 128] = piece
    wq_lines[0].step(3)
    wq_lines[1].step(3)
    wq_lines[0].arrive()
    wq_lines[1].arrive()
    stores.append(local(wq_all, wq_out, store_s.at[3]))

    for run in [run for low in range(H // 2) for run in (low, low + H // 2)]:
        rounded = (hats[run] * gain_rows[0:1, :]).astype(bf16)
        projected = jnp.zeros((R, 3 * hw), f32)
        for chunk in range(H):
            block = wq_all[chunk].reshape(B * D, 3 * hw)
            projected += mm(rounded[:, chunk * hw : (chunk + 1) * hw], block)
        cosine, sine = cos_all[run], sin_all[run]
        for slab in range(hw // 128):
            at = slab * 128
            q_runs[run, :, at : at + 128] = turn(projected[:, at : at + 128], cosine, sine)
            key = turn(projected[:, hw + at : hw + at + 128], cosine, sine)
            value = projected[:, 2 * hw + at : 2 * hw + at + 128]
            kv_send[2 * slab, run] = join(key, 0, value, 0).astype(bf16)
            kv_send[2 * slab + 1, run] = join(key, 1, value, 1).astype(bf16)
        for i, peer in enumerate(along):
            send(kv_send.at[here.there[i], run], kv.at[run, b], kv_s.at[i], kv_r.at[i], peer)
        send(kv_send.at[part, run], kv.at[run, b], kc_s.at[0], kc_r.at[0], beside)
        kv[run, b] = kv_send[part, run]
        if run >= H // 2:
            low = run - H // 2
            for a in range(A):
                at = a // 2 * 128
                q_send[a, low] = join(
                    q_runs[low, :, at : at + 128], a % 2, q_runs[run, :, at : at + 128], a % 2
                ).astype(bf16)
            for i, peer in enumerate(along):
                send(q_send.at[here.there[i], low], q_all.at[part, low], q_s.at[i], q_r.at[i], peer)
            q_all[part, low] = q_send[part, low]

    kv_copies = [
        remote(kv_send.at[here.there[i]], kv.at[:, b], kv_s.at[i], kv_r.at[i], peer)
        for i, peer in enumerate(along)
    ]
    kc_copies = [remote(kv_send.at[part], kv.at[:, b], kc_s.at[0], kc_r.at[0], beside)]
    q_copies = [
        remote(q_send.at[here.there[i]], q_all.at[part], q_s.at[i], q_r.at[i], peer)
        for i, peer in enumerate(along)
    ]
    spread.forward()
    cot_gather.forward()

    tiles = H * A // 2
    spot = lax.broadcasted_iota(jnp.int32, (1, 2 * R), 1)
    spot = spot + jnp.where(spot < R, 0, R) + share * R
    for tile in range(tiles):
        place = spot + tile * 4 * R

        def one(d, carried, place=place):
            low, begin, stop = carried
            high = low + lengths[d]
            inside = (place >= low) & (place < high)
            return (high, jnp.where(inside, low, begin), jnp.where(inside, high, stop))

        unused, bounds[tile, 0:1], bounds[tile, 1:2] = lax.fori_loop(
            0, lengths.shape[0], one, (jnp.int32(0), jnp.zeros_like(place), jnp.zeros_like(place))
        )

    def pass_on(i):
        there = wo_all.at[here.places[i], :, share]
        kc_copies.append(send(there, there, wf_s.at[i], wf_r.at[i], beside))

    pass_on(1)
    pass_on(2)
    for i, copy in enumerate(kv_copies):
        copy.wait_recv()
        there = kv.at[:, here.back[i] * 2 + share]
        kc_copies.append(send(there, there, kc_s.at[i + 1], kc_r.at[i + 1], beside))
    wm_lines = []
    for copy in wm_copies:
        copy.wait_recv()
    for half in range(2):
        rows = pl.ds(half * (H // 2), H // 2)
        wm_lines.append(
            LineGather(
                lambda block, side, rows=rows: wm_all.at[rows, block * 2 + side],
                wm_own.at[rows],
                here,
                line[5 * half + 15 : 5 * half + 20],
            )
        )
        wm_lines[half].start()
    wm_all[:, b] = wm_own[...]
    for copy in [*kc_copies, *q_copies]:
        copy.wait_recv()
    stores += [local(kv, kv_out, store_s.at[4]), local(q_all, q_out, store_s.at[5])]
    spread.arrive()
    last = len(kc_copies)
    pass_on(0)

    steps = H * B * R // KEY_STEP
    at = lax.broadcasted_iota(jnp.int32, (KEY_STEP, 2 * R), 0)
    spans = KEY_STEP // R

    def attend_pair(hh, u):
        results = []
        for side in (0, 1):
            tile = (hh + side * (H // 2)) * (A // 2) + u
            low, high = max(tile - 2, 0), min(tile + 3, steps)
            begin, stop = bounds[tile, 0:1], bounds[tile, 1:2]
            pair = q_all[2 * u : 2 * u + 2, hh].reshape(2 * R, 128)
            query = (halves(pair, side) * HEAD_DIM**-0.5).astype(bf16)

            def keys_at(n):
                return kv[n * spans // B, pl.ds(lax.rem(n * spans, B), spans)].reshape(KEY_STEP, 128)

            def score(n, top, low=low, begin=begin, stop=stop, query=query):
                same = (at >= begin - n * KEY_STEP) & (at < stop - n * KEY_STEP)
                scores = jnp.where(same, mm(keys_at(n), query, NT), neg_large)
                s_scr[n - low] = scores
                return jnp.maximum(top, jnp.max(scores, axis=0, keepdims=True))

            top = lax.fori_loop(low, high, score, jnp.full((1, 2 * R), neg_large, f32))

            def mix(n, carried, low=low, top=top):
                total, acc = carried
                weights = jnp.exp(s_scr[n - low] - top)
                total = total + jnp.sum(weights, axis=0, keepdims=True)
                return (total, acc + mm(keys_at(n), weights.astype(bf16), TN))

            total, acc = lax.fori_loop(
                low, high, mix, (jnp.zeros((1, 2 * R), f32), jnp.zeros((128, 2 * R), f32))
            )
            lse[tile] = top + jnp.log(total)
            results.append(acc[HEAD_DIM:] / total)
        both = jnp.concatenate(results, axis=0).T.astype(bf16)
        op[hh, 2 * u : 2 * u + 2] = both.reshape(2, R, 128)

    def mixed_out_copies(hh):
        mx_in[hh, part] = op[hh, part]
        return [
            send(op.at[hh, here.there[i]], mx_in.at[hh, part], mx_s.at[n], mx_r.at[n], peer)
            for i, peer in enumerate(along)
            for n in [hh * (A - 1) + i]
        ]

    ma_copies, mixed_all = {}, (mixed_early, mixed_late)

    def assemble(hh, copies):
        for copy in copies:
            copy.wait_recv()
        for side in (0, 1):
            run = hh + side * (H // 2)
            slabs = []
            for slab in range(hw // 128):
                left, right = mx_in[hh, 2 * slab].astype(f32), mx_in[hh, 2 * slab + 1].astype(f32)
                slabs.append(join(left, side, right, side))
            mixed = jnp.concatenate(slabs, axis=1).astype(bf16)
            mixed_own[run] = mixed
            for i, peer in enumerate(across):
                ma_copies[i, run] = send(
                    mixed_own.at[run], mixed_all[hh].at[h, side], ma_s.at[i * H + run], ma_r.at[i * H + run], peer
                )

    def project_own(runs):
        for run in runs:
            middle[run] = tok_all[run].astype(f32) + mm(mixed_own[run], wo_rows(h))

    def project_others(runs):
        for i in range(H - 1):
            for run in runs:
                ma_copies[i, run].wait_recv()
        for source in here.places:
            for run in runs:
                mixed = mixed_all[run % (H // 2)][source, run // (H // 2)]
                middle[run] += mm(mixed, wo_rows(source))

    def wo_rows(source):
        return wo_all[source].reshape(hw, W)

    attend_pair(0, 0)
    attend_pair(0, 1)
    mx_copies = mixed_out_copies(0)
    wm_lines[0].step(1)
    attend_pair(1, 0)
    wm_lines[1].step(1)
    assemble(0, mx_copies)
    attend_pair(1, 1)
    mx_late = mixed_out_copies(1)
    stores += [local(op.at[hh], op_out.at[:, hh], o_s.at[hh]) for hh in range(H // 2)]
    wm_lines[0].step(2)
    cot_gather.arrive()
    kc_copies[last].wait_recv()
    early, late = (0, H // 2), (1, H // 2 + 1)
    project_own(early)
    assemble(1, mx_late)
    stores.append(local(mixed_own, mixed_out, store_s.at[7]))
    project_own(late)
    wm_lines[1].step(2)
    project_others(early)
    wm_lines[0].step(3)
    project_others(late)

    def norm_two(run, carried):
        hat, unused = standardize(middle[run])
        normed[run] = (hat * gain_rows[1:2, :]).astype(bf16)
        return carried

    lax.fori_loop(0, H, norm_two, 0)
    wm_lines[1].step(3)
    for item in wm_lines:
        item.arrive()
    down_sum = Reduce(down_term, down_core, None, None, here, [down_core_s, down_core_r, None, None])
    in_sum = Reduce(in_term, in_core, None, None, here, [in_core_s, in_core_r, None, None])
    near, over, far = here.near, here.over, here.far

    def block(chunk):
        return wm_all[chunk].reshape(B * D, 3 * F)

    def part_of(run, i):
        return remote(g2_send.at[i], g2_in.at[i], g2_s.at[i], g2_r.at[i], (run, b))

    def feed_run(i, carried):
        run = run_of(here, i)
        lifted = jnp.zeros((R, 2 * F), f32)
        grad_act = jnp.zeros((R, F), f32)
        for chunk in range(H):
            lanes = slice(chunk * hw, (chunk + 1) * hw)
            weights = block(chunk)
            lifted += mm(normed[run, :, lanes], weights[:, : 2 * F])
            grad_act += mm(cot_all[run, :, lanes], weights[:, 2 * F :])
        gate, up = lifted[:, :F], lifted[:, F:]
        below = 0.5 + 0.5 * lax.erf(gate * (0.5**0.5))
        slope = below + gate * jnp.exp(-0.5 * gate * gate) * ((2.0 * np.pi) ** -0.5)
        act[run] = (gate * below * up).astype(bf16)
        lift[run, :, :F] = (grad_act * up * slope).astype(bf16)
        lift[run, :, F:] = (grad_act * gate * below).astype(bf16)

        for chunk in range(H):
            lanes = slice(chunk * hw, (chunk + 1) * hw)
            g2_own[:, lanes] = mm(lift[run], block(chunk)[:, : 2 * F], NT)

        @pl.when(i < H - 1)
        def _():
            g2_send[i] = g2_own[...].astype(bf16)
            part_of(run, i).start()

        return carried

    lax.fori_loop(0, H, feed_run, 0)

    def down_chunk(chunk, carried):
        lanes = pl.ds(pl.multiple_of(chunk * hw, hw), hw)
        left = cot_all[:, :, lanes].reshape(H * R, hw)
        grads = mm(left, act[...].reshape(H * R, F), TN).astype(bf16)
        down_term[:, :, chunk] = grads.reshape(A, 2, D, F)
        return carried

    lax.fori_loop(0, H, down_chunk, 0)
    down_sum.start()

    def in_chunk(chunk, carried):
        lanes = pl.ds(pl.multiple_of(chunk * hw, hw), hw)
        left = normed[:, :, lanes].reshape(H * R, hw)
        grads = mm(left, lift[...].reshape(H * R, 2 * F), TN).astype(bf16)
        in_term[:, :, chunk] = grads.reshape(A, 2, D, 2 * F)
        return carried

    lax.fori_loop(0, H, in_chunk, 0)
    in_sum.start()
    down_of = down_sum.core_sums()
    for n, there in enumerate((near, over)):
        down_send[n] = down_of(there).astype(bf16)
    pair_copy = send(down_send, down_in, pair_s.at[0], pair_r.at[0], (h, near * 2 + share))

    hat, scale = standardize(middle[h])
    grad = g2_own[...]
    for i in (1, 2, 0):
        part_of(here.places[i], i).wait_recv()
        grad += g2_in[i].astype(f32)
    gain_part[...] = jnp.broadcast_to(jnp.sum(grad * hat, axis=0, keepdims=True), gain_part.shape)
    total = cot_all[h].astype(f32) + norm_back(grad, hat, scale, gain_rows[1:2, :])
    grad_middle[...] = total
    stores.append(local(grad_middle, middle_out, store_s.at[8]))
    branch = total.astype(bf16)
    gm_copies = []
    for i in range(H):
        place = run_of(here, i)
        mixed_grad = mm(branch, wo_rows(place), NT)
        for a in range(A):
            slab = mixed_grad[:, a // 2 * 128 : a // 2 * 128 + 128]
            gm_send[i, a] = join(slab[: R // 2], a % 2, slab[R // 2 :], a % 2).astype(bf16)
        for j in range(A):
            there = lax.rem(part + j, A)
            if i < H - 1 or j:
                n = i * A + j
                gm_copies.append(
                    send(gm_send.at[i, there], go.at[part, h], gm_s.at[n], gm_r.at[n], (place, there * 2 + share))
                )
            else:
                stores.append(local(gm_send.at[i, part], go.at[part, h], own_s.at[1]))

    in_of = in_sum.core_sums()
    near_out[0] = in_of(near)[:, :, :F].astype(bf16)
    near_out[1] = in_of(near)[:, :, F:].astype(bf16)
    near_out[2] = in_of(over)[:, :, F:].astype(bf16)
    over_out[...] = in_of(over)[:, :, :F].astype(bf16)
    far_out[0] = in_of(far)[:, :, :F].astype(bf16)
    up_far[...] = in_of(far)[:, :, F:].astype(bf16)
    kept[0] = in_of(part)[:, :, :F]
    kept[1] = in_of(part)[:, :, F:]
    stores += [
        local(near_out, near_to, store_s.at[9]),
        local(over_out, over_to, store_s.at[10]),
        local(up_far, up_out, store_s.at[11]),
    ]
    pair_copy.wait_recv()
    kept[2] = down_of(part) + down_in[0].astype(f32)
    far_out[1] = (down_of(far) + down_in[1].astype(f32)).astype(bf16)
    stores += [local(far_out, far_to, store_s.at[12]), local(kept, kept_out, store_s.at[13])]

    def out_run(i, carried):
        run = run_of(here, i)
        for chunk in range(H):
            lanes = slice(chunk * hw, (chunk + 1) * hw)
            out_base[:, lanes] = mm(act[run], block(chunk)[:, 2 * F :], NT)

        @pl.when(i < H - 1)
        def _():
            out_parts[i] = out_base[...].astype(bf16)

        return carried

    lax.fori_loop(0, H, out_run, 0)
    out_base[...] += middle[h]
    stores += [local(out_parts, parts_out, store_s.at[14]), local(out_base, base_out, store_s.at[15])]
    for copy in gm_copies:
        copy.wait_recv()
    for copy in [
        *kc_copies, *q_copies, *wm_copies, *wq_copies, *gain_copies, *tok_copies, *kv_copies,
        *mx_copies, *mx_late, *ma_copies.values(), *gm_copies, pair_copy,
    ]:
        copy.wait_send()
    for i in range(H - 1):
        part_of(here.places[i], i).wait_send()
    for copy in stores[1:]:
        copy.wait()
    for item in (spread, cot_gather, wo_line, *wq_lines, *wm_lines):
        item.finish()
    in_sum.core_finish()
    down_sum.core_finish()


def forward(tokens, cotangent, w_qkv, gain_one, gain_two, w_in, w_down, w_out, lengths):
    R, W = tokens.shape
    H, B = lax.axis_size("head"), lax.axis_size("blk")
    A = B // 2
    hw = W // H
    D = w_qkv.shape[0]
    F = w_down.shape[1] // H
    f32, bf16 = jnp.float32, jnp.bfloat16
    shape = jax.ShapeDtypeStruct
    buffer = lambda *sizes: pltpu.VMEM(sizes, bf16)
    wide = lambda *sizes: pltpu.VMEM(sizes, f32)
    outs = [
        shape((H, B, R, 128), bf16),
        shape((A, H // 2, R, 128), bf16),
        shape((A, H // 2, R, 128), bf16),
        shape((H * A // 2, 1, 2 * R), f32),
        shape((A, H, R // 2, 128), bf16),
        shape((H, R, W), bf16),
        shape((H, B, D, 3 * hw), bf16),
        shape((H, R, 128), f32),
        shape((H, R, 128), f32),
        shape((8, W), f32),
        shape((8, W), f32),
        shape((H, R, hw), bf16),
        shape((R, W), f32),
        shape((R, W), f32),
        shape((H - 1, R, W), bf16),
        shape((3, H, D, F), f32),
        shape((H, D, F), bf16),
        shape((3, H, D, F), bf16),
        shape((H, D, F), bf16),
        shape((2, H, D, F), bf16),
    ]
    return pl.pallas_call(
        partial(forward_kernel, H, A),
        in_specs=[*[anywhere()] * 3, *[in_vmem()] * 2, *[anywhere()] * 3, in_smem()],
        out_specs=[in_vmem() if n in (3, 9, 10) else anywhere() for n in range(len(outs))],
        out_shape=outs,
        scratch_shapes=[
            buffer(R, W),
            buffer(*w_in.shape),
            buffer(*w_down.shape),
            buffer(*w_out.shape),
            buffer(H, R, W),
            buffer(H, R, W),
            buffer(H, B, D, 3 * hw),
            wide(H, R, 128),
            wide(H, R, 128),
            buffer(H, D, 3 * hw),
            buffer(H, D, 3 * F),
            buffer(H, D, 3 * F),
            buffer(H, A, 2, D, W),
            buffer(H, B, R, 128),
            buffer(A, H, R, 128),
            buffer(A, H // 2, R, 128),
            buffer(A, H // 2, R, 128),
            wide(H, R, hw),
            wide(H, R, W),
            wide(8, 128),
            wide(H - 1, 8, 128),
            wide(8, 128),
            wide(B, 8, 128),
            pltpu.VMEM((H * A // 2, 8, 2 * R), jnp.int32),
            wide(5, KEY_STEP, 2 * R),
            buffer(H // 2, A, R, 128),
            buffer(H // 2, A, R, 128),
            buffer(H, R, hw),
            *[buffer(H, 2, R, hw)] * 2,
            buffer(H, B, D, 3 * F),
            wide(H, R, W),
            buffer(H, R, W),
            buffer(H, R, F),
            buffer(H, R, 2 * F),
            buffer(H - 1, R, W),
            buffer(H - 1, R, W),
            wide(R, W),
            buffer(H, A, R // 2, 128),
            buffer(A, 2, H, D, 2 * F),
            buffer(A, H, D, 2 * F),
            buffer(A, 2, H, D, F),
            buffer(A, H, D, F),
            buffer(2, H, D, F),
            buffer(2, H, D, F),
            wide(R, W),
            buffer(H - 1, R, W),
            wide(R, W),
            wide(3, H, D, F),
            buffer(H, D, F),
            buffer(3, H, D, F),
            buffer(H, D, F),
            buffer(2, H, D, F),
            dma(8),
            dma(16),
            dma(2),
            dma(H // 2),
            *[dma(H - 1)] * 8,
            *[dma(B - 1)] * 2,
            *[dma(4)] * 2,
            *[dma(H - 1)] * 2,
            *[dma(4)] * 2,
            *[dma(A - 1)] * 4,
            *[dma(A)] * 2,
            *[dma((A - 1) * (H // 2))] * 2,
            *[dma((H - 1) * H)] * 2,
            *[dma(H - 1)] * 2,
            *[dma(H * A)] * 2,
            *[dma(1)] * 6,
            *line_sems(A) * 5,
        ],
        compiler_params=params(0),
        cost_estimate=pl.CostEstimate(flops=10**10, bytes_accessed=10**7, transcendentals=10**6),
        name="forward",
    )(tokens, cotangent, w_qkv, gain_one, gain_two, w_in, w_down, w_out, lengths)


def finish_kernel(
    H, A, dqp, dkv, tok_in, wq_in, cos_in, sin_in, gain_rows, mixed_in, middle_in, gain_part, base_in, out_parts, kept_in, up_in, near_in, over_in, far_in,
    output, input_grad, qkv_grad, out_grad, in_grad, down_grad, gain_one, gain_two,
    dkv_own, tok_all, wq_all, cos_all, sin_all, mixed_own, grad_middle, out_base, o_in, kept, up_far, from_near, from_over, from_far, up_send, up_last,
    dk_in, dkv_send, dkv_in, dq_in, branch, branch_all, gp, normed, g1_send, g1_in, g1_own,
    load_s, up_s, up_r, o_s, o_r, dk_s, dk_r, dz_s, dz_r, dq_s, dq_r, br_s, br_r, g1_s, g1_r, *rest,
):
    f32, bf16 = jnp.float32, jnp.bfloat16
    R, W = tok_all.shape[1:]
    B = 2 * A
    hw = W // H
    D, F = kept_in.shape[2:]
    here = Place(A)
    h, b, part, share = here.h, here.b, here.part, here.share
    across, along, beside = here.across, here.along, here.beside
    term_gain, gain_sum = reducer(rest[:8], here)
    in_swap, qkv_swap, gain_swap = (Swap(*rest[8 + 4 * n : 12 + 4 * n], here) for n in range(3))
    term_out, *term_qkv = rest[20:23]
    out_sum, *qkv_sums = (
        PairReduce(*rest[23 + 11 * n : 34 + 11 * n], term=term, here=here)
        for n, term in enumerate((term_out, *term_qkv))
    )
    loads = load(
        [
            (dkv, dkv_own), (middle_in, grad_middle), (tok_in, tok_all), (mixed_in, mixed_own), (cos_in, cos_all),
            (sin_in, sin_all), (wq_in, wq_all), (kept_in, kept), (up_in, up_far), (near_in, from_near),
            (far_in, from_far), (base_in, out_base),
        ],
        load_s,
    )
    meet([*across, *along, beside])

    order = [*here.there, part]
    dk_copies = [
        send(dkv.at[:, there * 2 + 1 - share], dk_in.at[i], dk_s.at[i], dk_r.at[i], beside)
        for i, there in enumerate(order)
    ]
    dq_copies = [
        send(dqp.at[here.there[i]], dq_in.at[part], dq_s.at[i], dq_r.at[i], peer)
        for i, peer in enumerate(along)
    ]
    loads[0].wait()
    dz_copies = []
    for i, there in enumerate(order):
        dk_copies[i].wait_recv()
        summed = dkv_own[:, there * 2 + share].astype(f32) + dk_in[i].astype(f32)
        if i < A - 1:
            dkv_send[i] = summed.astype(bf16)
            dz_copies.append(
                send(dkv_send.at[i], dkv_in.at[part], dz_s.at[i], dz_r.at[i], along[i])
            )
        else:
            dkv_in[part] = summed.astype(bf16)
    dq_in[part] = dqp[part]
    loads[1].wait()
    branch[...] = grad_middle[...].astype(bf16)
    br_copies = [
        send(branch, branch_all.at[h], br_s.at[i], br_r.at[i], peer) for i, peer in enumerate(across)
    ]
    branch_all[h] = branch[...]
    for copy in loads[2:]:
        copy.wait()

    def norm_run(run, carried):
        hat, unused = standardize(tok_all[run].astype(f32))
        normed[run] = (hat * gain_rows[0:1, :]).astype(bf16)
        return carried

    lax.fori_loop(0, H, norm_run, 0)
    for copy in br_copies:
        copy.wait_recv()
    o_copies = [
        send(out_parts.at[i], o_in.at[i], o_s.at[i], o_r.at[i], peer) for i, peer in enumerate(across)
    ]

    def out_tile(n, carried):
        lanes = pl.ds(pl.multiple_of(n * hw, hw), hw)
        grads = mm(mixed_own[...].reshape(H * R, hw), branch_all[:, :, lanes].reshape(H * R, hw), TN)
        term_out[:, :, :, lanes] = grads.astype(bf16).reshape(A, 2, D, hw)
        return carried

    lax.fori_loop(0, W // hw, out_tile, 0)
    out_sum.start()
    up_send[...] = (up_far[...].astype(f32) + from_near[2].astype(f32)).astype(bf16)
    for copy in [*dq_copies, *dz_copies]:
        copy.wait_recv()
    out_sum.pair()
    up_copy = send(up_send, up_last, up_s.at[0], up_r.at[0], (h, here.far * 2 + share))
    over_copy = send(over_in, from_over, up_s.at[1], up_r.at[1], (h, here.over * 2 + share))
    for run in range(H):
        side, at = run // (H // 2), run % (H // 2)
        cosine, sine = cos_all[run], sin_all[run]
        for slab in range(hw // 128):
            lanes = slab * 128
            left, right = dq_in[2 * slab, at].astype(f32), dq_in[2 * slab + 1, at].astype(f32)
            gp[run, :, lanes : lanes + 128] = turn(
                join(left, side, right, side), cosine, sine, True
            ).astype(bf16)
            left, right = dkv_in[2 * slab, run].astype(f32), dkv_in[2 * slab + 1, run].astype(f32)
            gp[run, :, hw + lanes : hw + lanes + 128] = turn(
                join(left, 0, right, 0), cosine, sine, True
            ).astype(bf16)
            gp[run, :, 2 * hw + lanes : 2 * hw + lanes + 128] = join(left, 1, right, 1).astype(bf16)

    def block(chunk):
        return wq_all[chunk].reshape(B * D, 3 * hw)

    for half, (term, item) in enumerate(zip(term_qkv, qkv_sums)):

        def term_chunk(n, carried, half=half, term=term):
            lanes = pl.ds(pl.multiple_of((half * (H // 2) + n) * hw, hw), hw)
            left = normed[:, :, lanes].reshape(H * R, hw)
            grads = mm(left, gp[...].reshape(H * R, 3 * hw), TN).astype(bf16)
            term[:, :, n] = grads.reshape(A, 2, D, 3 * hw)
            return carried

        lax.fori_loop(0, H // 2, term_chunk, 0)
        item.start()
        if half:
            qkv_sums[0].pair()

    def part_of(run, i):
        return remote(g1_send.at[i], g1_in.at[i], g1_s.at[i], g1_r.at[i], (run, b))

    def one_run(i, carried):
        run = run_of(here, i)
        for chunk in range(H):
            lanes = slice(chunk * hw, (chunk + 1) * hw)
            g1_own[:, lanes] = mm(gp[run], block(chunk), NT)

        @pl.when(i < H - 1)
        def _():
            g1_send[i] = g1_own[...].astype(bf16)
            part_of(run, i).start()

        return carried

    lax.fori_loop(0, 1, one_run, 0)
    qkv_sums[1].pair()
    out_sum.cross()
    lax.fori_loop(1, H, one_run, 0)
    qkv_sums[0].cross()
    over_copy.wait_recv()
    gate = kept[0] + from_near[0].astype(f32) + from_over[...].astype(f32) + from_far[0].astype(f32)
    in_swap.out[:, :, :F] = gate.astype(bf16)
    in_swap.out[:, :, 2 * F :] = (kept[2] + from_far[1].astype(f32)).astype(bf16)
    up_copy.wait_recv()
    up = kept[1] + from_near[1].astype(f32) + up_last[...].astype(f32)
    in_swap.out[:, :, F : 2 * F] = up.astype(bf16)
    in_swap.start()
    qkv_sums[1].cross()

    grad = g1_own[...]
    hat, scale = standardize(tok_all[h].astype(f32))
    for i in (1, 2, 0):
        part_of(here.places[i], i).wait_recv()
        grad += g1_in[i].astype(f32)
    row = lax.broadcasted_iota(jnp.int32, (8, W), 0)
    rows = jnp.where(
        row == 0,
        jnp.sum(grad * hat, axis=0, keepdims=True),
        jnp.where(row == 1, gain_part[...], 0.0),
    )
    pick = (
        lax.broadcasted_iota(jnp.int32, (8, 128), 0) == lax.broadcasted_iota(jnp.int32, (8, 128), 1)
    ).astype(bf16)
    for chunk in range(H):
        gain_columns = mm(rows[:, chunk * hw : (chunk + 1) * hw].astype(bf16), pick, TN)
        term_gain[:, :, chunk] = gain_columns.astype(bf16).reshape(A, 2, D, 128)
    gain_sum.start()
    input_grad[...] = grad_middle[...] + norm_back(grad, hat, scale, gain_rows[0:1, :])
    gain_sum.middle()
    result = out_base[...]
    for i, copy in enumerate(o_copies):
        copy.wait_recv()
        result += o_in[i].astype(f32)
    output[...] = result.astype(bf16)
    in_swap.arrive()
    for place in range(H):
        in_grad[:, place * F : (place + 1) * F] = in_swap.landed[place, :, :F].astype(f32)
        in_grad[:, (H + place) * F : (H + place + 1) * F] = in_swap.landed[
            place, :, F : 2 * F
        ].astype(f32)
        down_grad[:, place * F : (place + 1) * F] = in_swap.landed[place, :, 2 * F :].astype(f32)
    for half, item in enumerate(qkv_sums):
        qkv_swap.out[half * (H // 2) : (half + 1) * (H // 2)] = item.close().astype(bf16)
    qkv_swap.start()
    gain_swap.out[...] = gain_sum.close().astype(bf16)
    gain_swap.start()
    out_grad[...] = out_sum.close()
    qkv_swap.arrive()
    for place in range(H):
        for j in range(3):
            qkv_grad[:, j * W + place * hw : j * W + (place + 1) * hw] = qkv_swap.landed[
                place, :, j * hw : (j + 1) * hw
            ].astype(f32)
    gain_swap.arrive()
    total = gain_swap.landed[0].astype(f32)
    for place in range(1, H):
        total += gain_swap.landed[place].astype(f32)
    rows = total.T
    gain_one[...] = rows[0:1, :]
    gain_two[...] = rows[1:2, :]
    for copy in [*dk_copies, *dq_copies, *br_copies, *dz_copies, *o_copies, up_copy, over_copy]:
        copy.wait_send()
    for i in range(H - 1):
        part_of(here.places[i], i).wait_send()
    for item in (out_sum, *qkv_sums, gain_sum, in_swap, qkv_swap, gain_swap):
        item.finish()


def finish(dqp, dkv, tok_all, wq_all, cos_all, sin_all, gain_rows, mixed, grad_middle, gain_part, out_base, out_parts, kept, *terms):
    A, half, R, lanes = dqp.shape
    H = 2 * half
    W = tok_all.shape[-1]
    B = 2 * A
    hw = W // H
    D, F = kept.shape[2:]
    f32, bf16 = jnp.float32, jnp.bfloat16
    shape = jax.ShapeDtypeStruct
    buffer = lambda *sizes: pltpu.VMEM(sizes, bf16)
    arrays = [
        dqp, dkv, tok_all, wq_all, cos_all, sin_all, gain_rows, mixed, grad_middle, gain_part, out_base, out_parts,
        kept, *terms,
    ]
    return pl.pallas_call(
        partial(finish_kernel, H, A),
        in_specs=[in_vmem() if n in (0, 6, 9) else anywhere() for n in range(len(arrays))],
        out_specs=[in_vmem()] * 8,
        out_shape=[
            shape((R, W), bf16),
            shape((R, W), f32),
            shape((D, 3 * W), f32),
            shape((D, W), f32),
            shape((D, 2 * H * F), f32),
            shape((D, H * F), f32),
            shape((1, D), f32),
            shape((1, D), f32),
        ],
        scratch_shapes=[
            buffer(*dkv.shape),
            buffer(*tok_all.shape),
            buffer(*wq_all.shape),
            pltpu.VMEM(cos_all.shape, f32),
            pltpu.VMEM(sin_all.shape, f32),
            buffer(*mixed.shape),
            pltpu.VMEM(grad_middle.shape, f32),
            pltpu.VMEM(out_base.shape, f32),
            buffer(*out_parts.shape),
            pltpu.VMEM(kept.shape, f32),
            *[buffer(*term.shape) for term in terms],
            *[buffer(H, D, F)] * 2,
            buffer(A, H, R, 128),
            buffer(A - 1, H, R, 128),
            buffer(A, H, R, 128),
            buffer(A, half, R, 128),
            buffer(R, W),
            buffer(H, R, W),
            buffer(H, R, 3 * hw),
            buffer(H, R, W),
            buffer(H - 1, R, W),
            buffer(H - 1, R, W),
            pltpu.VMEM((R, W), f32),
            dma(12),
            *[dma(2)] * 2,
            *[dma(H - 1)] * 2,
            *[dma(A)] * 2,
            *[dma(A - 1)] * 4,
            *[dma(H - 1)] * 4,
            *reduce_scratch(A, (H, D, 128)),
            *swap_scratch(H, (D, 3 * F)),
            *swap_scratch(H, (D, 3 * hw)),
            *swap_scratch(H, (D, 128)),
            buffer(A, 2, D, W),
            *[buffer(A, 2, H // 2, D, 3 * hw)] * 2,
            *pair_scratch(A, (D, W)),
            *pair_scratch(A, (H // 2, D, 3 * hw)),
            *pair_scratch(A, (H // 2, D, 3 * hw)),
        ],
        compiler_params=params(2),
        cost_estimate=pl.CostEstimate(flops=2 * 10**9, bytes_accessed=10**7, transcendentals=10**5),
        name="finish",
    )(*arrays)


def per_device_split(
    tokens, attn_gain, w_qkv, w_attn_out, mlp_gain, w_in, w_mlp_out, doc_lengths, cotangent
):
    R, W = tokens.shape
    H, B = lax.axis_size("head"), lax.axis_size("blk")
    A = B // 2
    hw = W // H
    T = H * B * R
    (
        kv, qp, op, lse, gp, tok_all, wq, cos_all, sin_all, gain_rows, gain_part, mixed, grad_middle,
        out_base, out_parts, kept, up_far, near, over, far,
    ) = forward(
        tokens, cotangent, w_qkv, attn_gain[None], mlp_gain[None], w_in, w_mlp_out.T, w_attn_out, doc_lengths
    )
    kv = kv.reshape(T, 2 * HEAD_DIM)
    flipped = lambda flip: [(p, (p // 2 ^ flip) * 2 + p % 2) for p in range(B)]
    near, far = lax.ppermute(near, "blk", flipped(1)), lax.ppermute(far, "blk", flipped(3))
    dqp, dkv = attend_back(doc_lengths, qp, gp, op, lse, kv)
    output, input_grad, qkv_grad, out_grad, in_grad, down_grad, gain_one, gain_two = deliver(
        *finish(
            dqp, dkv.reshape(H, B, R, 128), tok_all, wq, cos_all, sin_all, gain_rows, mixed, grad_middle, gain_part,
            out_base, out_parts, kept, up_far, near, over, far,
        )
    )
    return (
        output,
        input_grad,
        gain_one[0],
        qkv_grad,
        out_grad,
        gain_two[0],
        in_grad,
        down_grad.T,
    )


def per_device(tokens, attn_gain, w_qkv, *rest):
    heads, blocks = lax.axis_size("head"), lax.axis_size("blk")
    fits = (
        heads == 4
        and blocks == 2 * (tokens.shape[1] // HEAD_DIM // heads) == 8
        and w_qkv.shape[0] * heads == 128
        and tokens.shape[0] == 128
    )
    chosen = per_device_split if fits else per_device_general
    return chosen(tokens, attn_gain, w_qkv, *rest)


def solution(mesh):
    placed = (
        P(("head", "blk"), None),
        P(("head", "blk")),
        P(("head", "blk"), None),
        P(("head", "blk"), None),
        P(("head", "blk")),
        P(("head", "blk"), None),
        P(None, ("head", "blk")),
        P(),
        P(("head", "blk"), None),
    )
    return jax.shard_map(
        per_device,
        mesh=mesh,
        in_specs=placed,
        out_specs=(
            P(("head", "blk"), None),
            P(("head", "blk"), None),
            P(("head", "blk")),
            P(("head", "blk"), None),
            P(("head", "blk"), None),
            P(("head", "blk")),
            P(("head", "blk"), None),
            P(None, ("head", "blk")),
        ),
        check_vma=False,
    )
```

```python
from functools import partial

import jax
import jax.numpy as jnp
import numpy as np
from jax import lax
from jax.experimental import pallas as pl
from jax.experimental.pallas import tpu as pltpu
from jax.sharding import PartitionSpec as P

HEAD_DIM = 64


norm_eps = 1e-05
rope_base = 160000.0
neg_large = -1e30


def from_behind(value, axis, by):
    devices = lax.axis_size(axis)
    return lax.ppermute(value, axis, [(i, (i + by) % devices) for i in range(devices)])


def layer_norm(values, gain):
    center = values - jnp.mean(values, axis=-1, keepdims=True)
    spread = jnp.mean(center * center, axis=-1, keepdims=True)
    return center * lax.rsqrt(spread + norm_eps) * gain


def rope_tables(places, head_size):
    half = head_size // 2
    freqs = rope_base ** (-(jnp.arange(half, dtype=jnp.float32) * 2.0) / head_size)
    angles = places.astype(jnp.float32)[:, None] * freqs[None, :]
    angles = jnp.concatenate([angles, angles], axis=1)
    return (jnp.cos(angles), jnp.sin(angles))


def rotate(values, cosine, sine):
    count = values.shape[0]
    head_size = cosine.shape[1]
    half = head_size // 2
    split = values.reshape(count, -1, head_size)
    turned = jnp.concatenate([-split[..., half:], split[..., :half]], axis=-1)
    return (split * cosine[:, None, :] + turned * sine[:, None, :]).reshape(count, -1)


def rotate_pair(query, keys, cosine, sine):
    return (rotate(query, cosine, sine), rotate(keys, cosine, sine))


def doc_numbers(places, ends, lengths):
    passed = places[:, None] >= ends[None, :]
    numbers = jnp.sum(passed.astype(jnp.int32), axis=1)
    offset = jnp.sum(jnp.where(passed, lengths[None, :], 0), axis=1)
    return (numbers, places - offset)


def gelu_gate(lifted):
    half = lifted.shape[1] // 2
    return jax.nn.gelu(lifted[:, :half], approximate=False) * lifted[:, half:]


def tile_scores(query, keys):
    heads = query.shape[1] // HEAD_DIM
    query_split = query.reshape(query.shape[0], heads, HEAD_DIM)
    key_split = keys.reshape(keys.shape[0], heads, HEAD_DIM)
    return jnp.einsum(
        "qhd,khd->hqk", query_split, key_split, preferred_element_type=jnp.float32
    ) * HEAD_DIM ** (-0.5)


def unchanged(state):
    return state


def forward_tile(state, query, keys, values, mask):
    top, total, running = state
    count = query.shape[0]
    heads = top.shape[0]
    scores = tile_scores(query, keys)
    filled = jnp.where(mask[None], scores, neg_large)
    new_top = jnp.maximum(top, jnp.max(filled, axis=-1))
    weights = jnp.where(mask[None], jnp.exp(scores - new_top[:, :, None]), 0.0)
    factor = jnp.exp(top - new_top)
    new_total = total * factor + jnp.sum(weights, axis=-1)
    mixed = jnp.einsum(
        "hqk,khd->qhd",
        weights.astype(jnp.bfloat16),
        values.reshape(-1, heads, HEAD_DIM),
        preferred_element_type=jnp.float32,
    )
    new_running = running.reshape(count, heads, HEAD_DIM) * factor.T[:, :, None] + mixed
    return (new_top, new_total, new_running.reshape(count, heads * HEAD_DIM))


def backward_tile(carry, query, keys, values, mask, norm_log, grad_out, delta):
    query_grad, run_grads = carry
    count = query.shape[0]
    columns = keys.shape[0]
    heads = norm_log.shape[0]
    scores = tile_scores(query, keys)
    probs = jnp.where(mask[None], jnp.exp(scores - norm_log[:, :, None]), 0.0)
    grad_split = grad_out.reshape(count, heads, HEAD_DIM)
    value_split = values.reshape(columns, heads, HEAD_DIM)
    grad_values = jnp.einsum(
        "hqk,qhd->khd", probs.astype(jnp.bfloat16), grad_split, preferred_element_type=jnp.float32
    )
    grad_probs = jnp.einsum(
        "qhd,khd->hqk", grad_split, value_split, preferred_element_type=jnp.float32
    )
    grad_scores = (probs * (grad_probs - delta[:, :, None])).astype(jnp.bfloat16)
    grad_query = jnp.einsum(
        "hqk,khd->qhd",
        grad_scores,
        keys.reshape(columns, heads, HEAD_DIM),
        preferred_element_type=jnp.float32,
    ) * HEAD_DIM ** (-0.5)
    grad_keys = jnp.einsum(
        "hqk,qhd->khd",
        grad_scores,
        query.reshape(count, heads, HEAD_DIM),
        preferred_element_type=jnp.float32,
    ) * HEAD_DIM ** (-0.5)
    added = jnp.stack([grad_keys.reshape(columns, -1), grad_values.reshape(columns, -1)])
    return (query_grad + grad_query.reshape(count, -1), run_grads + added)


def per_device_general(
    tokens, attn_gain, w_qkv, w_attn_out, mlp_gain, w_in, w_mlp_out, doc_lengths, cotangent
):
    own_rows = tokens.shape[0]
    width = tokens.shape[1]
    head_count = lax.axis_size("head")
    cycle_count = lax.axis_size("blk")
    head_place = lax.axis_index("head")
    cycle_place = lax.axis_index("blk")
    group_rows = head_count * own_rows
    block_runs = min(head_count, max(1, 512 // own_rows))
    block_count = head_count // block_runs
    block_rows = block_runs * own_rows
    doc_ends = jnp.cumsum(doc_lengths)
    counter = jnp.arange(own_rows, dtype=jnp.int32)
    own_places = (head_place * cycle_count + cycle_place) * own_rows + counter
    unused_docs, own_positions = doc_numbers(own_places, doc_ends, doc_lengths)
    cosine, sine = rope_tables(own_positions, HEAD_DIM)
    run_numbers = jnp.arange(head_count, dtype=jnp.int32)
    query_places = (
        (run_numbers[:, None] * cycle_count + cycle_place) * own_rows + counter[None, :]
    ).reshape(group_rows)
    query_docs, unused_positions = doc_numbers(query_places, doc_ends, doc_lengths)
    params = (
        lax.all_gather(attn_gain, ("head", "blk"), axis=0, tiled=True),
        lax.all_gather(w_qkv, ("head", "blk"), axis=0, tiled=True),
        lax.all_gather(w_attn_out, ("head", "blk"), axis=0, tiled=True),
        lax.all_gather(mlp_gain, ("head", "blk"), axis=0, tiled=True),
        lax.all_gather(w_in, ("head", "blk"), axis=0, tiled=True),
        lax.all_gather(w_mlp_out, ("head", "blk"), axis=1, tiled=True),
    )
    gain_one, full_qkv, full_attn_out, gain_two, full_in, full_mlp_out = params
    inputs = tokens.astype(jnp.float32)
    normed_one, norm_one_pull = jax.vjp(layer_norm, inputs, gain_one.astype(jnp.float32))
    normed_low = normed_one.astype(jnp.bfloat16)
    projected = jnp.dot(normed_low, full_qkv, preferred_element_type=jnp.float32)
    turned, rope_pull = jax.vjp(
        partial(rotate_pair, cosine=cosine, sine=sine),
        projected[:, :width],
        projected[:, width : 2 * width],
    )
    stacked = jnp.stack(
        [
            turned[0].astype(jnp.bfloat16),
            turned[1].astype(jnp.bfloat16),
            projected[:, 2 * width :].astype(jnp.bfloat16),
        ]
    )
    regrouped = lax.all_to_all(stacked, "head", split_axis=2, concat_axis=1, tiled=True)
    query_heads = regrouped[0]
    key_heads = regrouped[1]
    value_heads = regrouped[2]
    head_width = query_heads.shape[1]
    heads_here = head_width // HEAD_DIM

    def key_docs_at(first):
        places = (
            first % group_rows // own_rows * cycle_count + first // group_rows
        ) * own_rows + counter
        found, unused = doc_numbers(places, doc_ends, doc_lengths)
        return found

    def block_live(block, key_docs):
        block_docs = query_docs[block * block_rows : (block + 1) * block_rows]
        live = jnp.maximum(jnp.min(block_docs), jnp.min(key_docs)) <= jnp.minimum(
            jnp.max(block_docs), jnp.max(key_docs)
        )
        return (block_docs[:, None] == key_docs[None, :], live)

    def fold_forward(state, piece):
        key_part, value_part = piece

        def fold_one_run(number, carried):
            first = number * own_rows
            key_docs = key_docs_at(first)
            keys = lax.dynamic_slice_in_dim(key_part, number * own_rows, own_rows, 0)
            values = lax.dynamic_slice_in_dim(value_part, number * own_rows, own_rows, 0)
            updated = []
            for block in range(block_count):
                mask, live = block_live(block, key_docs)
                query = query_heads[block * block_rows : (block + 1) * block_rows]
                advance = partial(forward_tile, query=query, keys=keys, values=values, mask=mask)
                updated.append(lax.cond(live, advance, unchanged, carried[block]))
            return tuple(updated)

        return lax.fori_loop(0, key_part.shape[0] // own_rows, fold_one_run, state)

    def fresh_state():
        return tuple(
            (
                (
                    jnp.full((heads_here, block_rows), neg_large, jnp.float32),
                    jnp.zeros((heads_here, block_rows), jnp.float32),
                    jnp.zeros((block_rows, head_width), jnp.float32),
                )
                for block in range(block_count)
            )
        )

    def finish(state):
        outputs = []
        logs = []
        for top, total, running in state:
            scaled = running.reshape(block_rows, heads_here, HEAD_DIM) / total.T[:, :, None]
            outputs.append(scaled.reshape(block_rows, head_width))
            logs.append(top + jnp.log(total))
        return (
            jnp.concatenate(outputs, axis=0).astype(jnp.bfloat16),
            jnp.concatenate(logs, axis=1),
        )

    state = fold_forward(
        fresh_state(),
        (
            lax.all_gather(key_heads, "blk", axis=0, tiled=True),
            lax.all_gather(value_heads, "blk", axis=0, tiled=True),
        ),
    )
    out_heads, norm_log = finish(state)
    out_tokens = lax.all_to_all(out_heads, "head", split_axis=0, concat_axis=1, tiled=True)
    middle = inputs + jnp.dot(out_tokens, full_attn_out, preferred_element_type=jnp.float32)
    normed_two, norm_two_pull = jax.vjp(layer_norm, middle, gain_two.astype(jnp.float32))
    normed_two_low = normed_two.astype(jnp.bfloat16)
    lifted = jnp.dot(normed_two_low, full_in, preferred_element_type=jnp.float32)
    activated, geglu_pull = jax.vjp(gelu_gate, lifted)
    activated_low = activated.astype(jnp.bfloat16)
    output = (
        middle + jnp.dot(activated_low, full_mlp_out, preferred_element_type=jnp.float32)
    ).astype(jnp.bfloat16)
    params = (
        lax.all_gather(attn_gain, ("head", "blk"), axis=0, tiled=True),
        lax.all_gather(w_qkv, ("head", "blk"), axis=0, tiled=True),
        lax.all_gather(w_attn_out, ("head", "blk"), axis=0, tiled=True),
        lax.all_gather(mlp_gain, ("head", "blk"), axis=0, tiled=True),
        lax.all_gather(w_in, ("head", "blk"), axis=0, tiled=True),
        lax.all_gather(w_mlp_out, ("head", "blk"), axis=1, tiled=True),
    )
    gain_one, full_qkv, full_attn_out, gain_two, full_in, full_mlp_out = params
    grad_act = jnp.einsum("td,fd->tf", cotangent, full_mlp_out, preferred_element_type=jnp.float32)
    grad_lifted = geglu_pull(grad_act)[0].astype(jnp.bfloat16)
    grad_normed_two = jnp.einsum(
        "tf,df->td", grad_lifted, full_in, preferred_element_type=jnp.float32
    )
    grad_middle_part, grad_gain_two = norm_two_pull(grad_normed_two)
    grad_middle = cotangent.astype(jnp.float32) + grad_middle_part
    grad_branch = grad_middle.astype(jnp.bfloat16)
    grad_mixed = jnp.einsum(
        "te,de->td", grad_branch, full_attn_out, preferred_element_type=jnp.float32
    ).astype(jnp.bfloat16)
    grad_heads = lax.all_to_all(grad_mixed, "head", split_axis=1, concat_axis=0, tiled=True)
    state = fold_forward(
        fresh_state(),
        (
            lax.all_gather(key_heads, "blk", axis=0, tiled=True),
            lax.all_gather(value_heads, "blk", axis=0, tiled=True),
        ),
    )
    out_heads, norm_log = finish(state)
    delta = jnp.einsum(
        "qhd,qhd->hq",
        grad_heads.reshape(group_rows, heads_here, HEAD_DIM).astype(jnp.float32),
        out_heads.reshape(group_rows, heads_here, HEAD_DIM).astype(jnp.float32),
    )

    def piece_backward(query_grads, key_part, value_part, start):
        piece_rows = key_part.shape[0]

        def piece_one_run(number, carried):
            query_now, piece_grads = carried
            first = start + number * own_rows
            key_docs = key_docs_at(first)
            keys = lax.dynamic_slice_in_dim(key_part, number * own_rows, own_rows, 0)
            values = lax.dynamic_slice_in_dim(value_part, number * own_rows, own_rows, 0)
            run_grads = jnp.zeros((2, own_rows, head_width), jnp.float32)
            updated = []
            for block in range(block_count):
                mask, live = block_live(block, key_docs)
                lower = block * block_rows
                upper = (block + 1) * block_rows
                advance = partial(
                    backward_tile,
                    query=query_heads[lower:upper],
                    keys=keys,
                    values=values,
                    mask=mask,
                    norm_log=norm_log[:, lower:upper],
                    grad_out=grad_heads[lower:upper],
                    delta=delta[:, lower:upper],
                )
                new_query, run_grads = lax.cond(
                    live, advance, unchanged, (query_now[block], run_grads)
                )
                updated.append(new_query)
            piece_grads = lax.dynamic_update_slice_in_dim(
                piece_grads, run_grads, number * own_rows, 1
            )
            return (tuple(updated), piece_grads)

        return lax.fori_loop(
            0,
            piece_rows // own_rows,
            piece_one_run,
            (query_grads, jnp.zeros((2, piece_rows, head_width), jnp.float32)),
        )

    start_query = tuple(
        (jnp.zeros((block_rows, head_width), jnp.float32) for block in range(block_count))
    )

    def cycle_step(step, carried):
        query_now, blocks, travelling = carried
        owner = (cycle_place - step) % cycle_count
        query_now, piece_grads = piece_backward(query_now, blocks[0], blocks[1], owner * group_rows)
        travelling = travelling + piece_grads
        blocks = from_behind(blocks, "blk", 1)
        travelling = from_behind(travelling.astype(jnp.bfloat16), "blk", 1).astype(travelling.dtype)
        return (query_now, blocks, travelling)

    start_cycle = (
        start_query,
        jnp.stack([key_heads, value_heads]),
        jnp.zeros((2, group_rows, head_width), jnp.float32),
    )
    query_grads, unused_blocks, own_grads = lax.fori_loop(0, cycle_count, cycle_step, start_cycle)
    grad_stack = jnp.stack(
        [
            jnp.concatenate(query_grads, axis=0).astype(jnp.bfloat16),
            own_grads[0].astype(jnp.bfloat16),
            own_grads[1].astype(jnp.bfloat16),
        ]
    )
    back_tokens = lax.all_to_all(grad_stack, "head", split_axis=1, concat_axis=2, tiled=True)
    grad_query, grad_keys = rope_pull(
        (back_tokens[0].astype(jnp.float32), back_tokens[1].astype(jnp.float32))
    )
    grad_projected = jnp.concatenate(
        [grad_query, grad_keys, back_tokens[2].astype(jnp.float32)], axis=1
    ).astype(jnp.bfloat16)
    grad_normed_one = jnp.einsum(
        "te,de->td", grad_projected, full_qkv, preferred_element_type=jnp.float32
    )
    grad_input_part, grad_gain_one = norm_one_pull(grad_normed_one)
    input_grad = grad_middle + grad_input_part

    def columns(source):
        return source

    term_qkv = jnp.einsum(
        "td,te->de", columns(normed_low), grad_projected, preferred_element_type=jnp.float32
    )
    term_out = jnp.einsum(
        "td,te->de", columns(out_tokens), grad_branch, preferred_element_type=jnp.float32
    )
    term_in = jnp.einsum(
        "td,tf->df", columns(normed_two_low), grad_lifted, preferred_element_type=jnp.float32
    )
    term_down = jnp.einsum(
        "td,tf->df", columns(cotangent), activated_low, preferred_element_type=jnp.float32
    )
    sums = lax.psum_scatter(
        jnp.concatenate([term_qkv, term_out, term_in, term_down], axis=1),
        ("head", "blk"),
        scatter_dimension=0,
        tiled=True,
    )
    ff_width = full_mlp_out.shape[0]
    qkv_grad = sums[:, : 3 * width]
    attn_out_grad = sums[:, 3 * width : 4 * width]
    in_grad = sums[:, 4 * width : 4 * width + 2 * ff_width]
    down_grad = sums[:, 4 * width + 2 * ff_width :].T
    gain_sums = lax.psum_scatter(
        jnp.stack([grad_gain_one, grad_gain_two]), ("head", "blk"), scatter_dimension=1, tiled=True
    )
    return (
        output,
        input_grad,
        gain_sums[0],
        qkv_grad,
        attn_out_grad,
        gain_sums[1],
        in_grad,
        down_grad,
    )


VMEM = 62 * 2**20
MESH = pl.DeviceIdType.MESH
KEY_STEP = 512
KEY_ALIGN = 256
NN = (((1,), (0,)), ((), ()))
NT = (((1,), (1,)), ((), ()))
TN = (((0,), (0,)), ((), ()))


def mm(left, right, dims=NN):
    return lax.dot_general(left, right, dims, preferred_element_type=jnp.float32)


def params(collective_id=None):
    if collective_id is None:
        return pltpu.CompilerParams(vmem_limit_bytes=VMEM)
    return pltpu.CompilerParams(
        collective_id=collective_id, has_side_effects=True, vmem_limit_bytes=VMEM
    )


def in_vmem():
    return pl.BlockSpec(memory_space=pltpu.VMEM)


def anywhere():
    return pl.BlockSpec(memory_space=pl.ANY)


def in_smem():
    return pl.BlockSpec(memory_space=pltpu.SMEM)


def dma(*counts):
    return pltpu.SemaphoreType.DMA(counts)


def halves(packed, side):
    wide = packed.astype(jnp.float32)
    if side:
        wide = pltpu.roll(wide, HEAD_DIM, 1)
    lane = lax.broadcasted_iota(jnp.int32, wide.shape, 1)
    return jnp.where(lane < HEAD_DIM, wide, 0.0)


def tile_span(lengths, side, R, T):
    hh, u = pl.program_id(0), pl.program_id(1)
    runs, parts = 2 * pl.num_programs(0), 2 * pl.num_programs(1)
    share = lax.rem(lax.axis_index("blk"), 2)
    first = (((hh + side * (runs // 2)) * parts + 2 * u) * 2 + share) * R
    last = first + 3 * R - 1
    lane = lax.broadcasted_iota(jnp.int32, (1, 2 * R), 1)
    place = first + lane + jnp.where(lane < R, 0, R)

    def one(d, carried):
        low, begin, stop, start, end = carried
        high = low + lengths[d]
        inside = (place >= low) & (place < high)
        return (
            high,
            jnp.where(inside, low, begin),
            jnp.where(inside, high, stop),
            jnp.where((first >= low) & (first < high), low, start),
            jnp.where((last >= low) & (last < high), high, end),
        )

    zero = jnp.int32(0)
    unused, begin, stop, start, end = lax.fori_loop(
        0,
        lengths.shape[0],
        one,
        (zero, jnp.zeros_like(place), jnp.zeros_like(place), zero, zero),
        unroll=True,
    )
    start = start // KEY_ALIGN
    steps = (end - start * KEY_ALIGN + KEY_STEP - 1) // KEY_STEP
    start = jnp.minimum(start, T // KEY_ALIGN - steps * (KEY_STEP // KEY_ALIGN))
    return (begin, stop, start, steps)


def attend_kernel(lengths, qp, kv, op, lse, s_scr):
    pairs = qp.shape[0] * qp.shape[2]
    T = kv.shape[0]
    half_runs = pl.num_programs(0)
    hh, u = pl.program_id(0), pl.program_id(1)
    at = lax.broadcasted_iota(jnp.int32, (KEY_STEP, pairs), 0)
    results = []
    for side in (0, 1):
        tile = (hh + side * half_runs) * pl.num_programs(1) + u
        begin, stop, start, steps = tile_span(lengths, side, pairs // 2, T)
        query = (halves(qp[...].reshape(pairs, 2 * HEAD_DIM), side) * HEAD_DIM**-0.5).astype(
            jnp.bfloat16
        )

        def keys_at(n):
            first = pl.multiple_of(start * KEY_ALIGN + n * KEY_STEP, KEY_ALIGN)
            return (first, kv[pl.ds(first, KEY_STEP), :])

        def score(n, top):
            first, keys = keys_at(n)
            same = (at >= begin - first) & (at < stop - first)
            scores = jnp.where(same, mm(keys, query, NT), neg_large)
            s_scr[n] = scores
            return jnp.maximum(top, jnp.max(scores, axis=0, keepdims=True))

        top = lax.fori_loop(0, steps, score, jnp.full((1, pairs), neg_large, jnp.float32))

        def mix(n, carried):
            total, acc = carried
            unused, keys = keys_at(n)
            weights = jnp.exp(s_scr[n] - top)
            total = total + jnp.sum(weights, axis=0, keepdims=True)
            return (total, acc + mm(keys, weights.astype(jnp.bfloat16), TN))

        total, acc = lax.fori_loop(
            0,
            steps,
            mix,
            (jnp.zeros((1, pairs), jnp.float32), jnp.zeros((2 * HEAD_DIM, pairs), jnp.float32)),
        )
        lse[tile] = top + jnp.log(total)
        results.append(acc[HEAD_DIM:] / total)
    both = jnp.concatenate(results, axis=0).T
    op[...] = both.astype(jnp.bfloat16).reshape(op.shape)


def attend(lengths, qp, kv):
    parts, half_runs, rows, lanes = qp.shape
    tiles = half_runs * parts
    piece = pl.BlockSpec((2, 1, rows, lanes), lambda i, j, s: (j, i, 0, 0))
    return pl.pallas_call(
        attend_kernel,
        grid_spec=pltpu.PrefetchScalarGridSpec(
            num_scalar_prefetch=1,
            grid=(half_runs, parts // 2),
            in_specs=[piece, in_vmem()],
            out_specs=[piece, in_vmem()],
            scratch_shapes=[pltpu.VMEM((kv.shape[0] // KEY_STEP, KEY_STEP, 2 * rows), jnp.float32)],
        ),
        out_shape=[
            jax.ShapeDtypeStruct(qp.shape, jnp.bfloat16),
            jax.ShapeDtypeStruct((tiles, 1, 2 * rows), jnp.float32),
        ],
        compiler_params=params(),
        cost_estimate=pl.CostEstimate(
            flops=10**9, bytes_accessed=50 * 10**6, transcendentals=10**6
        ),
        name="attend",
    )(lengths, qp, kv)


def attend_back_kernel(
    lengths, qp, gp, op, lse, kv, dqp, dkv, acc_scr
):
    pairs = qp.shape[0] * qp.shape[2]
    T = kv.shape[0]
    half_runs = pl.num_programs(0)
    hh, u = pl.program_id(0), pl.program_id(1)
    begins = (hh == 0) & (u == 0)
    ends = (hh == half_runs - 1) & (u == pl.num_programs(1) - 1)
    @pl.when(begins)
    def _():
        acc_scr[...] = jnp.zeros_like(acc_scr)

    at = lax.broadcasted_iota(jnp.int32, (KEY_STEP, pairs), 0)
    lane = lax.broadcasted_iota(jnp.int32, (pairs, 2 * HEAD_DIM), 1)
    flat = (pairs, 2 * HEAD_DIM)
    results = []
    for side in (0, 1):
        tile = (hh + side * half_runs) * pl.num_programs(1) + u
        begin, stop, start, steps = tile_span(lengths, side, pairs // 2, T)
        query = (halves(qp[...].reshape(flat), side) * HEAD_DIM**-0.5).astype(jnp.bfloat16)
        pieces = []
        for n in range(2):
            piece = gp[n, hh + side * half_runs].astype(jnp.float32)
            pieces += [pltpu.roll(piece, HEAD_DIM, 1), piece]
        grad = jnp.where(lane < HEAD_DIM, 0.0, jnp.concatenate(pieces, axis=0))
        mixed = op[...].reshape(flat).astype(jnp.float32)
        if not side:
            mixed = pltpu.roll(mixed, HEAD_DIM, 1)
        delta = jnp.sum((grad * mixed).T, axis=0, keepdims=True)
        both = jnp.concatenate([query, grad.astype(jnp.bfloat16)], axis=0)
        logs = lse[tile]

        def step(n, dq):
            first = pl.multiple_of(start * KEY_ALIGN + n * KEY_STEP, KEY_ALIGN)
            rows = pl.ds(first, KEY_STEP)
            keys = kv[rows, :]
            same = (at >= begin - first) & (at < stop - first)
            products = mm(keys, both, NT)
            probs = jnp.where(same, jnp.exp(products[:, :pairs] - logs), 0.0)
            grad_scores = (probs * (products[:, pairs:] - delta)).astype(jnp.bfloat16)
            left = jnp.concatenate([grad_scores, probs.astype(jnp.bfloat16)], axis=1)
            acc_scr[rows, :] += mm(left, both)
            return dq + mm(keys, grad_scores, TN)

        dq = lax.fori_loop(0, steps, step, jnp.zeros((2 * HEAD_DIM, pairs), jnp.float32))
        results.append(dq[:HEAD_DIM] * HEAD_DIM**-0.5)
    dqp[...] = jnp.concatenate(results, axis=0).T.astype(jnp.bfloat16).reshape(dqp.shape)

    @pl.when(ends)
    def _():
        dkv[...] = acc_scr[...].astype(dkv.dtype)


def attend_back(lengths, qp, gp, op, lse, kv):
    parts, half_runs, rows, lanes = qp.shape
    piece = pl.BlockSpec((2, 1, rows, lanes), lambda i, j, s: (j, i, 0, 0))
    grads = pl.BlockSpec((2, 2 * half_runs, rows // 2, lanes), lambda i, j, s: (j, 0, 0, 0))
    return pl.pallas_call(
        attend_back_kernel,
        grid_spec=pltpu.PrefetchScalarGridSpec(
            num_scalar_prefetch=1,
            grid=(half_runs, parts // 2),
            in_specs=[piece, grads, piece, *[in_vmem()] * 2],
            out_specs=[piece, in_vmem()],
            scratch_shapes=[pltpu.VMEM(kv.shape, jnp.float32)],
        ),
        out_shape=[
            jax.ShapeDtypeStruct(qp.shape, jnp.bfloat16),
            jax.ShapeDtypeStruct(kv.shape, jnp.bfloat16),
        ],
        compiler_params=params(),
        cost_estimate=pl.CostEstimate(
            flops=3 * 10**9, bytes_accessed=60 * 10**6, transcendentals=10**6
        ),
        name="attend_back",
    )(lengths, qp, gp, op, lse, kv)


def deliver_kernel(*refs):
    count = len(refs) // 2
    for source, target in zip(refs[:count], refs[count:]):
        target[...] = source[...]


def deliver(*arrays):
    return pl.pallas_call(
        deliver_kernel,
        in_specs=[in_vmem()] * len(arrays),
        out_specs=[in_vmem()] * len(arrays),
        out_shape=[jax.ShapeDtypeStruct(a.shape, a.dtype) for a in arrays],
        compiler_params=params(),
        name="deliver",
    )(*arrays)


def meet(peers):
    barrier = pltpu.get_barrier_semaphore()
    for peer in peers:
        pl.semaphore_signal(barrier, inc=1, device_id=peer, device_id_type=MESH)
    pl.semaphore_wait(barrier, len(peers))


def remote(source, target, send_sem, recv_sem, peer):
    return pltpu.make_async_remote_copy(
        src_ref=source,
        dst_ref=target,
        send_sem=send_sem,
        recv_sem=recv_sem,
        device_id=peer,
        device_id_type=MESH,
    )


def send(source, target, send_sem, recv_sem, peer):
    copy = remote(source, target, send_sem, recv_sem, peer)
    copy.start()
    return copy


class Place:
    def __init__(self, parts):
        h, b = lax.axis_index("head"), lax.axis_index("blk")
        self.h, self.b, self.parts = h, b, parts
        self.part, self.share = b // 2, lax.rem(b, 2)
        x, y = lax.rem(h, 2), h // 2
        self.places = [(1 - y) * 2 + 1 - x, y * 2 + 1 - x, (1 - y) * 2 + x]
        self.across = [(place, b) for place in self.places]
        self.there = [lax.rem(self.part + i, parts) for i in range(1, parts)]
        self.back = [lax.rem(self.part + parts - i, parts) for i in range(1, parts)]
        self.along = [(h, part * 2 + self.share) for part in self.there]
        self.beside = (h, self.part * 2 + 1 - self.share)
        self.near = self.part + 1 - 2 * lax.rem(self.part, 2)
        self.over = lax.rem(self.part + 2, 4)
        self.far = 3 - self.part
        self.askew = [(h, part * 2 + 1 - self.share) for part in self.there]


class LineGather:
    def __init__(self, view, own, here, sems):
        self.view, self.own, self.here, self.parts = view, own, here, here.parts
        self.right_s, self.left_s, self.line_r, self.core_s, self.core_r = sems
        self.first = 0

    def _copy(self, source, block, side):
        here = self.here
        if side == 0:
            sems, peer = (self.core_s, self.core_r), here.beside
        else:
            sems = (self.right_s if side > 0 else self.left_s, self.line_r)
            peer = (here.h, (here.part + side) * 2 + here.share)
        return remote(
            source, self.view(block, here.share), sems[0].at[block], sems[1].at[block], peer
        )

    def _can(self, side):
        return self.here.part < self.parts - 1 if side > 0 else self.here.part > 0

    def start(self):
        for side in (1, -1):

            @pl.when(self._can(side))
            def _():
                self._copy(self.own, self.here.part, side).start()

        self._copy(self.own, self.here.part, 0).start()

    def start_from(self, near):
        self.first = 1
        for side in (1, -1):
            block = self.here.part - side

            @pl.when((block >= 0) & (block < self.parts) & self._can(side))
            def _():
                self._copy(near[side], block, side).start()

        self._copy(self.own, self.here.part, 0).start()
        for side in (1, -1):
            block = self.here.part - side

            @pl.when((block >= 0) & (block < self.parts))
            def _():
                self._copy(near[side], block, 0).start()

    def step(self, k):
        for side in (1, -1):
            block = self.here.part - side * k

            @pl.when((block >= 0) & (block < self.parts))
            def _():
                there = self.view(block, self.here.share)
                self._copy(there, block, side).wait_recv()

                @pl.when(self._can(side))
                def _():
                    self._copy(there, block, side).start()

                self._copy(there, block, 0).start()

    def arrive(self):
        for block in range(self.parts):
            self._copy(self.own, block, 0).wait_recv()

    def finish(self):
        for side in (1, -1):
            for block in range(self.parts):
                first = self.here.part - side * self.first
                sent = block <= first if side > 0 else block >= first

                @pl.when(sent & self._can(side))
                def _():
                    self._copy(self.own, block, side).wait_send()

        for block in range(self.parts):
            self._copy(self.own, block, 0).wait_send()


class CornerGather:
    def __init__(self, whole, half, own, here, sems):
        self.whole, self.half, self.own, self.here = whole, half, own, here
        self.send_s, self.recv_s = sems

    def _copy(self, n):
        h, (corner, x, y) = self.here.h, self.here.across
        if n < 2:
            source, target, peer = self.own, self.whole(h), (x, y)[n]
        else:
            block = (y, x)[n - 2][0]
            source = target = self.half(block, n - 2)
            peer = (x, y)[n - 2]
        return remote(source, target, self.send_s.at[n], self.recv_s.at[n], peer)

    def start(self):
        for n in range(2):
            self._copy(n).start()

    def forward(self):
        for n in range(2):
            self._copy(n).wait_recv()
        for n in range(2, 4):
            self._copy(n).start()

    def arrive(self):
        for n in range(2, 4):
            self._copy(n).wait_recv()

    def finish(self):
        for n in range(4):
            self._copy(n).wait_send()


def local(source, target, sem):
    copy = pltpu.make_async_copy(source, target, sem)
    copy.start()
    return copy


def line_sems(parts):
    return [dma(parts)] * 5


def standardize(values):
    center = values - jnp.mean(values, axis=-1, keepdims=True)
    spread = jnp.mean(center * center, axis=-1, keepdims=True)
    scale = lax.rsqrt(spread + norm_eps)
    return (center * scale, scale)


def norm_back(grad, hat, scale, gain):
    inner = grad * gain
    return scale * (
        inner
        - jnp.mean(inner, axis=-1, keepdims=True)
        - hat * jnp.mean(inner * hat, axis=-1, keepdims=True)
    )


def turn(values, cosine, sine, back=False):
    lane = lax.broadcasted_iota(jnp.int32, values.shape, 1)
    first = lax.rem(lane, HEAD_DIM) < HEAD_DIM // 2
    source = values * sine if back else values
    ahead = pltpu.roll(source, 128 - HEAD_DIM // 2, 1)
    behind = pltpu.roll(source, HEAD_DIM // 2, 1)
    if back:
        return values * cosine + jnp.where(first, ahead, -behind)
    return values * cosine + jnp.where(first, -ahead, behind) * sine


def join(left, left_side, right, right_side):
    lane = lax.broadcasted_iota(jnp.int32, left.shape, 1)
    left = pltpu.roll(left, HEAD_DIM, 1) if left_side else left
    right = right if right_side else pltpu.roll(right, HEAD_DIM, 1)
    return jnp.where(lane < HEAD_DIM, left, right)


class Reduce:
    def __init__(self, term, core_in, line_out, line_in, here, sems):
        self.term, self.core_in, self.line_out, self.line_in = term, core_in, line_out, line_in
        self.here, self.parts = here, here.parts
        self.core_s, self.core_r, self.line_s, self.line_r = sems

    def _core(self):
        return remote(
            self.term.at[:, 1 - self.here.share],
            self.core_in,
            self.core_s.at[0],
            self.core_r.at[0],
            self.here.beside,
        )

    def _line(self, i):
        return remote(
            self.line_out[i],
            self.line_in.at[i],
            self.line_s.at[i],
            self.line_r.at[i],
            self.here.along[i],
        )

    def _sum(self, there):
        own = self.term[there, self.here.share].astype(jnp.float32)
        return own + self.core_in[there].astype(jnp.float32)

    def start(self):
        self._core().start()

    def core_sums(self):
        self._core().wait_recv()
        return self._sum

    def middle(self):
        self._core().wait_recv()
        for i, there in enumerate(self.here.there):
            self.line_out[i][...] = self._sum(there).astype(jnp.bfloat16)
            self._line(i).start()

    def close(self):
        total = self._sum(self.here.part)
        for i in range(self.parts - 1):
            self._line(i).wait_recv()
            total += self.line_in[i].astype(jnp.float32)
        return total

    def core_finish(self):
        self._core().wait_send()

    def finish(self):
        self.core_finish()
        for i in range(self.parts - 1):
            self._line(i).wait_send()


def reduce_scratch(parts, shape):
    return [
        pltpu.VMEM((parts, 2, *shape), jnp.bfloat16),
        pltpu.VMEM((parts, *shape), jnp.bfloat16),
        pltpu.VMEM((parts - 1, *shape), jnp.bfloat16),
        pltpu.VMEM((parts - 1, *shape), jnp.bfloat16),
        dma(1),
        dma(1),
        dma(parts - 1),
        dma(parts - 1),
    ]


class PairReduce:
    def __init__(self, core_in, near_out, near_in, far_out, far_in, *sems, term, here):
        self.term, self.core_in, self.near_out, self.near_in = term, core_in, near_out, near_in
        self.far_out, self.far_in, self.sems, self.here = far_out, far_in, sems, here

    def _copy(self, step):
        here = self.here
        source, target, peer = (
            (self.term.at[:, 1 - here.share], self.core_in, here.beside),
            (self.near_out, self.near_in, (here.h, here.near * 2 + here.share)),
            (self.far_out, self.far_in, (here.h, here.far * 2 + here.share)),
        )[step]
        return remote(source, target, self.sems[2 * step].at[0], self.sems[2 * step + 1].at[0], peer)

    def _sum(self, there):
        own = self.term[there, self.here.share].astype(jnp.float32)
        return own + self.core_in[there].astype(jnp.float32)

    def start(self):
        self._copy(0).start()

    def pair(self):
        self._copy(0).wait_recv()
        self.near_out[0] = self._sum(self.here.near).astype(jnp.bfloat16)
        self.near_out[1] = self._sum(self.here.over).astype(jnp.bfloat16)
        self._copy(1).start()

    def cross(self):
        self._copy(1).wait_recv()
        self.far_out[...] = (
            self._sum(self.here.far) + self.near_in[1].astype(jnp.float32)
        ).astype(jnp.bfloat16)
        self._copy(2).start()

    def close(self):
        self._copy(2).wait_recv()
        total = self._sum(self.here.part) + self.near_in[0].astype(jnp.float32)
        return total + self.far_in[...].astype(jnp.float32)

    def finish(self):
        for step in range(3):
            self._copy(step).wait_send()


def pair_scratch(parts, shape):
    return [
        pltpu.VMEM((parts, *shape), jnp.bfloat16),
        *[pltpu.VMEM((2, *shape), jnp.bfloat16)] * 2,
        *[pltpu.VMEM(shape, jnp.bfloat16)] * 2,
        *[dma(1)] * 6,
    ]


def reducer(scratch, here):
    term, core_in, line_out, line_in, *sems = scratch
    outs = [line_out.at[i] for i in range(here.parts - 1)]
    return (term, Reduce(term, core_in, outs, line_in, here, sems))


class Swap:
    def __init__(self, out, landed, send_s, recv_s, here):
        self.out, self.landed, self.here = out, landed, here
        self.send_s, self.recv_s = send_s, recv_s

    def start(self):
        here = self.here
        self.copies = [
            send(self.out.at[peer[0]], self.landed.at[here.h], self.send_s.at[i], self.recv_s.at[i], peer)
            for i, peer in enumerate(here.across)
        ]
        self.landed[here.h] = self.out[here.h]

    def arrive(self):
        for copy in self.copies:
            copy.wait_recv()

    def finish(self):
        for copy in self.copies:
            copy.wait_send()


def swap_scratch(heads, shape):
    return [
        pltpu.VMEM((heads, *shape), jnp.bfloat16),
        pltpu.VMEM((heads, *shape), jnp.bfloat16),
        dma(heads - 1),
        dma(heads - 1),
    ]


def run_of(here, i):
    x, y = lax.rem(here.h, 2), here.h // 2
    x = x + (1 - i // 2) * (1 - 2 * x)
    y = y + (1 - i % 2) * (1 - 2 * y)
    return y * 2 + x


def load(pairs, sems):
    copies = [pltpu.make_async_copy(*pair, sems.at[i]) for i, pair in enumerate(pairs)]
    for copy in copies:
        copy.start()
    return copies


def layer_kernel(
    H, A, tok_in, cot_in, wq_in, gain_one_in, gain_two_in, w_in_in, w_down_in, w_out_in, lengths,
    output, input_grad, qkv_grad, out_grad, in_grad, down_grad, gain_one, gain_two,
    cot, w_in, w_down, w_out, tok_all, cot_all, wq_all, cos_all, sin_all,
    wq_st, wm_src, wm_own, wo_all, kv, kv_send, q_all, q_send, q_runs, hats, gain_src, gain_st, gain_tile, gain_all,
    bounds, s_scr, op, mx_in, mixed_own, mixed_early, mixed_late, wm_all, middle, normed, act, lift,
    g2_send, g2_in, g2_own, gm_send, in_term, in_core, down_term, down_core, down_send, down_in,
    out_base, out_parts, grad_middle, near_out, far_out,
    lse, go, gain_rows, gain_part, branch_own, branch_all, o_in, from_near, from_far, in_send, in_last,
    dkv_sum, dq_send, dq_in, dk_send, dk_in, dkv_send, dkv_in, gp, g1_send, g1_in, g1_own,
    term_out, term_qkv_low, term_qkv_high,
    load_s, own_s,
    tok_s, tok_r, wq_s, wq_r, wm_s, wm_r, ga_s, ga_r, gb_s, gb_r, wx_s, wx_r, wf_s, wf_r, cot_s, cot_r,
    q_s, q_r, kv_s, kv_r, kc_s, kc_r, mx_s, mx_r, ma_s, ma_r, g2_s, g2_r, gm_s, gm_r,
    in_core_s, in_core_r, down_core_s, down_core_r, pair_s, pair_r,
    br_s, br_r, o_s, o_r, g1_s, g1_r, nr_s, nr_r, dq_s, dq_r, dz_s, dz_r, dk_s, dk_r, *more,
):
    line, more = more[:25], more[25:]
    term_qkv = (term_qkv_low, term_qkv_high)
    f32, bf16 = jnp.float32, jnp.bfloat16
    R, W = tok_all.shape[1:]
    B = 2 * A
    hw = W // H
    D = wq_in.shape[0]
    F = w_in.shape[1] // 2 // H
    here = Place(A)
    h, b, part, share = here.h, here.b, here.part, here.share
    across, along, beside = here.across, here.along, here.beside

    def slices(source, target, place):
        return [
            (
                source.at[:, pl.ds(pl.multiple_of(j * W + place * hw, hw), hw)],
                target.at[h, :, j * hw : (j + 1) * hw],
            )
            for j in range(3)
        ]

    loads = [
        local(source, target, load_s.at[n])
        for n, (source, target) in enumerate(
            [
                (w_out_in, w_out), (w_in_in, w_in), (w_down_in, w_down), (cot_in, cot), (tok_in, tok_all.at[h]),
                *slices(wq_in, wq_st, h),
            ]
        )
    ]
    row = lax.broadcasted_iota(jnp.int32, (8, 128), 0)
    lane = lax.broadcasted_iota(jnp.int32, (8, 128), 1)
    gain_src[...] = jnp.zeros((8, 128), f32)
    gain_src[0:1, :D] = gain_one_in[...].astype(f32)
    gain_src[1:2, :D] = gain_two_in[...].astype(f32)
    gain_src[...] = pltpu.roll(gain_src[...], h * D, 1)
    others = [
        (run_of(here, i), lax.rem(part + j, A) * 2 + share)
        for i in range(H)
        for j in range(A)
        if i < H - 1 or j
    ]
    meet([*others, *here.askew, beside])

    for i, peer in enumerate(across):
        for source, target in slices(wq_in, wq_st, peer[0]):
            send(source, target, wq_s.at[i], wq_r.at[i], peer)
    wq_copies = [
        remote(wq_st.at[peer[0]], wq_st.at[h], wq_s.at[i], wq_r.at[i], peer)
        for i, peer in enumerate(across)
    ]
    gain_copies = [
        send(gain_src, gain_st.at[i], ga_s.at[i], ga_r.at[i], peer) for i, peer in enumerate(across)
    ]
    wo_line = LineGather(lambda block, side: wo_all.at[h, block, side], w_out, here, line[:5])
    loads[0].wait()
    wo_line.start()
    own_copy = local(w_out, wo_all.at[h, part, share], own_s.at[0])
    for copy in loads[1:]:
        copy.wait()
    for place in range(H):
        wm_src[place, :, :F] = w_in[:, place * F : (place + 1) * F]
        wm_src[place, :, F : 2 * F] = w_in[:, (H + place) * F : (H + place + 1) * F]
        wm_src[place, :, 2 * F :] = w_down[:, place * F : (place + 1) * F]
    wm_own[h] = wm_src[h]
    cot_all[h] = cot[...]

    wide = lax.broadcasted_iota(jnp.int32, (R, 128), 1)
    freqs = jnp.exp(
        lax.rem(wide, HEAD_DIM // 2).astype(f32) * (-2.0 / HEAD_DIM * float(np.log(rope_base)))
    )

    def tables(run):
        place = (run * B + b) * R + lax.broadcasted_iota(jnp.int32, (R, 128), 0)

        def one(d, carried):
            low, begin = carried
            return (low + lengths[d], jnp.where(place >= low, low, begin))

        unused, begin = lax.fori_loop(
            0, lengths.shape[0], one, (jnp.int32(0), jnp.zeros((R, 128), jnp.int32))
        )
        angles = (place - begin).astype(f32) * freqs
        cos_all[run] = jnp.cos(angles)
        sin_all[run] = jnp.sin(angles)

    tables(0)
    tables(1)
    wo_line.step(1)
    for copy in wq_copies:
        copy.wait_recv()
    wq_lines = []
    for half in range(2):
        rows = pl.ds(half * (H // 2), H // 2)
        wq_lines.append(
            LineGather(
                lambda block, side, rows=rows: wq_all.at[rows, block * 2 + side],
                wq_st.at[rows],
                here,
                line[5 * half + 5 : 5 * half + 10],
            )
        )
        wq_lines[half].start()
    tok_copies = [
        send(tok_in, tok_all.at[h], tok_s.at[i], tok_r.at[i], peer) for i, peer in enumerate(across)
    ]
    tile = gain_src[...]
    for i, copy in enumerate(gain_copies):
        copy.wait_recv()
        tile += gain_st[i]
    gain_tile[...] = tile
    gain_all[b] = tile
    gain_copies += [
        send(gain_tile, gain_all.at[b], gb_s.at[i], gb_r.at[i], peer)
        for i, peer in enumerate([*along, *here.askew, beside])
    ]
    wo_line.step(2)
    wq_all[:, b] = wq_st[...]
    tables(2)
    wq_lines[0].step(1)
    wo_line.step(3)
    wq_lines[1].step(1)
    wo_line.arrive()
    spread = CornerGather(
        lambda place: wo_all.at[place, :, share],
        lambda place, half: wo_all.at[place, half * (A // 2) : (half + 1) * (A // 2), share],
        wo_all.at[h, :, share],
        here,
        (wx_s, wx_r),
    )
    own_copy.wait()
    spread.start()
    wm_copies = [
        send(wm_src.at[peer[0]], wm_own.at[h], wm_s.at[i], wm_r.at[i], peer)
        for i, peer in enumerate(across)
    ]
    cot_gather = CornerGather(
        lambda place: cot_all.at[place],
        lambda place, half: cot_all.at[place, half * (R // 2) : (half + 1) * (R // 2)],
        cot,
        here,
        (cot_s, cot_r),
    )
    cot_gather.start()
    tables(3)
    for copy in tok_copies:
        copy.wait_recv()

    def norm_run(run, carried):
        hat, unused = standardize(tok_all[run].astype(f32))
        hats[run] = hat
        return carried

    wq_lines[0].step(2)
    lax.fori_loop(0, H // 2, norm_run, 0)
    wq_lines[1].step(2)
    lax.fori_loop(H // 2, H, norm_run, 0)
    for copy in gain_copies[len(across) :]:
        copy.wait_recv()
    for slab in range(W // 128):
        place, first = slab // (hw // 128), slab % (hw // 128) * (128 // D)
        piece = jnp.zeros((8, 128), f32)
        for j in range(128 // D):
            moved = gain_all[first + j]
            if j != place:
                moved = pltpu.roll(moved, (j - place) * D % 128, 1)
            piece = jnp.where(lane // D == j, moved, piece)
        gain_rows[:, slab * 128 : (slab + 1) * 128] = piece
    wq_lines[0].step(3)
    wq_lines[1].step(3)
    wq_lines[0].arrive()
    wq_lines[1].arrive()

    for run in [run for low in range(H // 2) for run in (low, low + H // 2)]:
        rounded = (hats[run] * gain_rows[0:1, :]).astype(bf16)
        projected = jnp.zeros((R, 3 * hw), f32)
        for chunk in range(H):
            block = wq_all[chunk].reshape(B * D, 3 * hw)
            projected += mm(rounded[:, chunk * hw : (chunk + 1) * hw], block)
        cosine, sine = cos_all[run], sin_all[run]
        for slab in range(hw // 128):
            at = slab * 128
            q_runs[run, :, at : at + 128] = turn(projected[:, at : at + 128], cosine, sine)
            key = turn(projected[:, hw + at : hw + at + 128], cosine, sine)
            value = projected[:, 2 * hw + at : 2 * hw + at + 128]
            kv_send[2 * slab, run] = join(key, 0, value, 0).astype(bf16)
            kv_send[2 * slab + 1, run] = join(key, 1, value, 1).astype(bf16)
        for i, peer in enumerate(along):
            send(kv_send.at[here.there[i], run], kv.at[run, b], kv_s.at[i], kv_r.at[i], peer)
        send(kv_send.at[part, run], kv.at[run, b], kc_s.at[0], kc_r.at[0], beside)
        kv[run, b] = kv_send[part, run]
        if run >= H // 2:
            low = run - H // 2
            for a in range(A):
                at = a // 2 * 128
                q_send[a, low] = join(
                    q_runs[low, :, at : at + 128], a % 2, q_runs[run, :, at : at + 128], a % 2
                ).astype(bf16)
            for i, peer in enumerate(along):
                send(q_send.at[here.there[i], low], q_all.at[part, low], q_s.at[i], q_r.at[i], peer)
            q_all[part, low] = q_send[part, low]

    kv_copies = [
        remote(kv_send.at[here.there[i]], kv.at[:, b], kv_s.at[i], kv_r.at[i], peer)
        for i, peer in enumerate(along)
    ]
    kc_copies = [remote(kv_send.at[part], kv.at[:, b], kc_s.at[0], kc_r.at[0], beside)]
    q_copies = [
        remote(q_send.at[here.there[i]], q_all.at[part], q_s.at[i], q_r.at[i], peer)
        for i, peer in enumerate(along)
    ]
    spread.forward()
    cot_gather.forward()

    tiles = H * A // 2
    spot = lax.broadcasted_iota(jnp.int32, (1, 2 * R), 1)
    spot = spot + jnp.where(spot < R, 0, R) + share * R
    for tile in range(tiles):
        place = spot + tile * 4 * R

        def one(d, carried, place=place):
            low, begin, stop = carried
            high = low + lengths[d]
            inside = (place >= low) & (place < high)
            return (high, jnp.where(inside, low, begin), jnp.where(inside, high, stop))

        unused, bounds[tile, 0:1], bounds[tile, 1:2] = lax.fori_loop(
            0, lengths.shape[0], one, (jnp.int32(0), jnp.zeros_like(place), jnp.zeros_like(place))
        )

    def pass_on(i):
        there = wo_all.at[here.places[i], :, share]
        kc_copies.append(send(there, there, wf_s.at[i], wf_r.at[i], beside))

    pass_on(1)
    pass_on(2)
    for i, copy in enumerate(kv_copies):
        copy.wait_recv()
        there = kv.at[:, here.back[i] * 2 + share]
        kc_copies.append(send(there, there, kc_s.at[i + 1], kc_r.at[i + 1], beside))
    wm_lines = []
    for copy in wm_copies:
        copy.wait_recv()
    for half in range(2):
        rows = pl.ds(half * (H // 2), H // 2)
        wm_lines.append(
            LineGather(
                lambda block, side, rows=rows: wm_all.at[rows, block * 2 + side],
                wm_own.at[rows],
                here,
                line[5 * half + 15 : 5 * half + 20],
            )
        )
        wm_lines[half].start()
    wm_all[:, b] = wm_own[...]
    for copy in [*kc_copies, *q_copies]:
        copy.wait_recv()
    spread.arrive()
    last = len(kc_copies)
    pass_on(0)

    steps = H * B * R // KEY_STEP
    at = lax.broadcasted_iota(jnp.int32, (KEY_STEP, 2 * R), 0)
    spans = KEY_STEP // R

    def attend_pair(hh, u):
        results = []
        for side in (0, 1):
            tile = (hh + side * (H // 2)) * (A // 2) + u
            low, high = max(tile - 2, 0), min(tile + 3, steps)
            begin, stop = bounds[tile, 0:1], bounds[tile, 1:2]
            pair = q_all[2 * u : 2 * u + 2, hh].reshape(2 * R, 128)
            query = (halves(pair, side) * HEAD_DIM**-0.5).astype(bf16)

            def keys_at(n):
                return kv[n * spans // B, pl.ds(lax.rem(n * spans, B), spans)].reshape(KEY_STEP, 128)

            def score(n, top, low=low, begin=begin, stop=stop, query=query):
                same = (at >= begin - n * KEY_STEP) & (at < stop - n * KEY_STEP)
                scores = jnp.where(same, mm(keys_at(n), query, NT), neg_large)
                s_scr[n - low] = scores
                return jnp.maximum(top, jnp.max(scores, axis=0, keepdims=True))

            top = lax.fori_loop(low, high, score, jnp.full((1, 2 * R), neg_large, f32))

            def mix(n, carried, low=low, top=top):
                total, acc = carried
                weights = jnp.exp(s_scr[n - low] - top)
                total = total + jnp.sum(weights, axis=0, keepdims=True)
                return (total, acc + mm(keys_at(n), weights.astype(bf16), TN))

            total, acc = lax.fori_loop(
                low, high, mix, (jnp.zeros((1, 2 * R), f32), jnp.zeros((128, 2 * R), f32))
            )
            lse[tile] = top + jnp.log(total)
            results.append(acc[HEAD_DIM:] / total)
        both = jnp.concatenate(results, axis=0).T.astype(bf16)
        op[hh, 2 * u : 2 * u + 2] = both.reshape(2, R, 128)

    def mixed_out_copies(hh):
        mx_in[hh, part] = op[hh, part]
        return [
            send(op.at[hh, here.there[i]], mx_in.at[hh, part], mx_s.at[n], mx_r.at[n], peer)
            for i, peer in enumerate(along)
            for n in [hh * (A - 1) + i]
        ]

    ma_copies, mixed_all = {}, (mixed_early, mixed_late)

    def assemble(hh, copies):
        for copy in copies:
            copy.wait_recv()
        for side in (0, 1):
            run = hh + side * (H // 2)
            slabs = []
            for slab in range(hw // 128):
                left, right = mx_in[hh, 2 * slab].astype(f32), mx_in[hh, 2 * slab + 1].astype(f32)
                slabs.append(join(left, side, right, side))
            mixed = jnp.concatenate(slabs, axis=1).astype(bf16)
            mixed_own[run] = mixed
            for i, peer in enumerate(across):
                ma_copies[i, run] = send(
                    mixed_own.at[run], mixed_all[hh].at[h, side], ma_s.at[i * H + run], ma_r.at[i * H + run], peer
                )

    def project_own(runs):
        for run in runs:
            middle[run] = tok_all[run].astype(f32) + mm(mixed_own[run], wo_rows(h))

    def project_others(runs):
        for i in range(H - 1):
            for run in runs:
                ma_copies[i, run].wait_recv()
        for source in here.places:
            for run in runs:
                mixed = mixed_all[run % (H // 2)][source, run // (H // 2)]
                middle[run] += mm(mixed, wo_rows(source))

    def wo_rows(source):
        return wo_all[source].reshape(hw, W)

    attend_pair(0, 0)
    attend_pair(0, 1)
    mx_copies = mixed_out_copies(0)
    wm_lines[0].step(1)
    attend_pair(1, 0)
    wm_lines[1].step(1)
    assemble(0, mx_copies)
    attend_pair(1, 1)
    mx_late = mixed_out_copies(1)
    wm_lines[0].step(2)
    cot_gather.arrive()
    kc_copies[last].wait_recv()
    early, late = (0, H // 2), (1, H // 2 + 1)
    project_own(early)
    assemble(1, mx_late)
    project_own(late)
    wm_lines[1].step(2)
    project_others(early)
    wm_lines[0].step(3)
    project_others(late)

    def norm_two(run, carried):
        hat, unused = standardize(middle[run])
        normed[run] = (hat * gain_rows[1:2, :]).astype(bf16)
        return carried

    lax.fori_loop(0, H, norm_two, 0)
    wm_lines[1].step(3)
    for item in wm_lines:
        item.arrive()
    down_sum = Reduce(down_term, down_core, None, None, here, [down_core_s, down_core_r, None, None])
    in_sum = Reduce(in_term, in_core, None, None, here, [in_core_s, in_core_r, None, None])
    near, over, far = here.near, here.over, here.far

    def block(chunk):
        return wm_all[chunk].reshape(B * D, 3 * F)

    def part_of(run, i):
        return remote(g2_send.at[i], g2_in.at[i], g2_s.at[i], g2_r.at[i], (run, b))

    def feed_run(i, carried):
        run = run_of(here, i)
        lifted = jnp.zeros((R, 2 * F), f32)
        grad_act = jnp.zeros((R, F), f32)
        for chunk in range(H):
            lanes = slice(chunk * hw, (chunk + 1) * hw)
            weights = block(chunk)
            lifted += mm(normed[run, :, lanes], weights[:, : 2 * F])
            grad_act += mm(cot_all[run, :, lanes], weights[:, 2 * F :])
        gate, up = lifted[:, :F], lifted[:, F:]
        below = 0.5 + 0.5 * lax.erf(gate * (0.5**0.5))
        slope = below + gate * jnp.exp(-0.5 * gate * gate) * ((2.0 * np.pi) ** -0.5)
        act[run] = (gate * below * up).astype(bf16)
        lift[run, :, :F] = (grad_act * up * slope).astype(bf16)
        lift[run, :, F:] = (grad_act * gate * below).astype(bf16)

        for chunk in range(H):
            lanes = slice(chunk * hw, (chunk + 1) * hw)
            g2_own[:, lanes] = mm(lift[run], block(chunk)[:, : 2 * F], NT)

        @pl.when(i < H - 1)
        def _():
            g2_send[i] = g2_own[...].astype(bf16)
            part_of(run, i).start()

        return carried

    lax.fori_loop(0, H, feed_run, 0)

    def down_chunk(chunk, carried):
        lanes = pl.ds(pl.multiple_of(chunk * hw, hw), hw)
        left = cot_all[:, :, lanes].reshape(H * R, hw)
        grads = mm(left, act[...].reshape(H * R, F), TN).astype(bf16)
        down_term[:, :, chunk] = grads.reshape(A, 2, D, F)
        return carried

    lax.fori_loop(0, H, down_chunk, 0)
    down_sum.start()

    def in_chunk(chunk, carried):
        lanes = pl.ds(pl.multiple_of(chunk * hw, hw), hw)
        left = normed[:, :, lanes].reshape(H * R, hw)
        grads = mm(left, lift[...].reshape(H * R, 2 * F), TN).astype(bf16)
        in_term[:, :, chunk] = grads.reshape(A, 2, D, 2 * F)
        return carried

    lax.fori_loop(0, H, in_chunk, 0)
    in_sum.start()
    down_of = down_sum.core_sums()
    for n, there in enumerate((near, over)):
        down_send[n] = down_of(there).astype(bf16)
    pair_copy = send(down_send, down_in, pair_s.at[0], pair_r.at[0], (h, near * 2 + share))

    hat, scale = standardize(middle[h])
    grad = g2_own[...]
    for i in (1, 2, 0):
        part_of(here.places[i], i).wait_recv()
        grad += g2_in[i].astype(f32)
    gain_part[...] = jnp.broadcast_to(jnp.sum(grad * hat, axis=0, keepdims=True), gain_part.shape)
    total = cot_all[h].astype(f32) + norm_back(grad, hat, scale, gain_rows[1:2, :])
    grad_middle[...] = total
    branch = total.astype(bf16)
    branch_own[...] = branch
    gm_copies = []
    for i in range(H):
        place = run_of(here, i)
        mixed_grad = mm(branch, wo_rows(place), NT)
        for a in range(A):
            slab = mixed_grad[:, a // 2 * 128 : a // 2 * 128 + 128]
            gm_send[i, a] = join(slab[: R // 2], a % 2, slab[R // 2 :], a % 2).astype(bf16)
        for j in range(A):
            there = lax.rem(part + j, A)
            if i < H - 1 or j:
                n = i * A + j
                gm_copies.append(
                    send(gm_send.at[i, there], go.at[part, h], gm_s.at[n], gm_r.at[n], (place, there * 2 + share))
                )
            else:
                go[part, h] = gm_send[i, part]

    br_copies = [
        send(branch_own, branch_all.at[h], br_s.at[i], br_r.at[i], peer) for i, peer in enumerate(across)
    ]
    branch_all[h] = branch
    in_of = in_sum.core_sums()
    near_out[0] = in_of(near).astype(bf16)
    near_out[1] = in_of(over).astype(bf16)
    near_copy = send(near_out, from_near, nr_s.at[0], nr_r.at[0], (h, near * 2 + share))
    pair_copy.wait_recv()
    far_out[...] = (down_of(far) + down_in[1].astype(f32)).astype(bf16)

    def out_run(i, carried):
        run = run_of(here, i)
        for chunk in range(H):
            lanes = slice(chunk * hw, (chunk + 1) * hw)
            out_base[:, lanes] = mm(act[run], block(chunk)[:, 2 * F :], NT)

        @pl.when(i < H - 1)
        def _():
            out_parts[i] = out_base[...].astype(bf16)

        return carried

    lax.fori_loop(0, H, out_run, 0)
    out_base[...] += middle[h]
    o_copies = [
        send(out_parts.at[i], o_in.at[i], o_s.at[i], o_r.at[i], peer) for i, peer in enumerate(across)
    ]
    dkv_sum[...] = jnp.zeros_like(dkv_sum)
    for copy in gm_copies:
        copy.wait_recv()
    far_copy = send(far_out, from_far, nr_s.at[1], nr_r.at[1], (h, far * 2 + share))

    wide_lane = lax.broadcasted_iota(jnp.int32, (2 * R, 128), 1)

    def attend_back_tile(tile):
        run, u = tile // (A // 2), tile % (A // 2)
        side, hh = run // (H // 2), run % (H // 2)
        low, high = max(tile - 2, 0), min(tile + 3, steps)
        begin, stop = bounds[tile, 0:1], bounds[tile, 1:2]
        pair = q_all[2 * u : 2 * u + 2, hh].reshape(2 * R, 128)
        query = (halves(pair, side) * HEAD_DIM**-0.5).astype(bf16)
        pieces = []
        for a in (2 * u, 2 * u + 1):
            piece = go[a, run].astype(f32)
            pieces += [pltpu.roll(piece, HEAD_DIM, 1), piece]
        grad = jnp.where(wide_lane < HEAD_DIM, 0.0, jnp.concatenate(pieces, axis=0))
        mixed = op[hh, 2 * u : 2 * u + 2].reshape(2 * R, 128).astype(f32)
        if not side:
            mixed = pltpu.roll(mixed, HEAD_DIM, 1)
        delta = jnp.sum((grad * mixed).T, axis=0, keepdims=True)
        both = jnp.concatenate([query, grad.astype(bf16)], axis=0)
        logs = lse[tile]

        def step(n, dq):
            keys = kv[n * spans // B, pl.ds(lax.rem(n * spans, B), spans)].reshape(KEY_STEP, 128)
            same = (at >= begin - n * KEY_STEP) & (at < stop - n * KEY_STEP)
            products = mm(keys, both, NT)
            probs = jnp.where(same, jnp.exp(products[:, : 2 * R] - logs), 0.0)
            grad_scores = (probs * (products[:, 2 * R :] - delta)).astype(bf16)
            left = jnp.concatenate([grad_scores, probs.astype(bf16)], axis=1)
            dkv_sum[n] += mm(left, both)
            return dq + mm(keys, grad_scores, TN)

        dq = lax.fori_loop(low, high, step, jnp.zeros((128, 2 * R), f32))
        dq = (dq * HEAD_DIM**-0.5).T
        for k, a in enumerate((2 * u, 2 * u + 1)):
            rows = dq[k * R : (k + 1) * R]
            dq_send[a, run] = join(rows[: R // 2], 0, rows[R // 2 :], 0).astype(bf16)

            @pl.when(part == a)
            def _(a=a):
                dq_in[a, run] = dq_send[a, run]

            @pl.when(part != a)
            def _(a=a):
                n = part * H + run
                remote(
                    dq_send.at[a, run], dq_in.at[part, run], dq_s.at[a * H + run], dq_r.at[n], (h, a * 2 + share)
                ).start()

    def dk_copy(k):
        return remote(dk_send.at[k], dk_in.at[k], dk_s.at[k], dk_r.at[k], beside)

    def keys_done(k):
        for n in range(2):
            first = pl.multiple_of((2 * n + 1 - share) * R, R)
            dk_send[k, n] = dkv_sum[k, pl.ds(first, R), :].astype(bf16)
        dk_copy(k).start()

    def keys_sum(k):
        dk_copy(k).wait_recv()
        run = k * spans // B
        for n in range(2):
            a = k * spans % B // 2 + n
            first = pl.multiple_of((2 * n + share) * R, R)
            summed = dkv_sum[k, pl.ds(first, R), :] + dk_in[k, n].astype(f32)
            dkv_send[a, run] = summed.astype(bf16)

            @pl.when(part == a)
            def _(a=a):
                dkv_in[a, run] = dkv_send[a, run]

            @pl.when(part != a)
            def _(a=a):
                n = part * H + run
                remote(
                    dkv_send.at[a, run], dkv_in.at[part, run], dz_s.at[a * H + run], dz_r.at[n], (h, a * 2 + share)
                ).start()

    out_sum, *qkv_sums = (
        PairReduce(*more[11 * n : 11 * n + 11], term=term, here=here)
        for n, term in enumerate((term_out, *term_qkv))
    )
    gain_scratch, swaps = more[33:41], more[41:]
    term_gain, gain_sum = reducer(gain_scratch, here)
    in_swap, qkv_swap, gain_swap = (Swap(*swaps[4 * n : 4 * n + 4], here) for n in range(3))

    def out_tile(n, carried):
        lanes = pl.ds(pl.multiple_of(n * hw, hw), hw)
        grads = mm(mixed_own[...].reshape(H * R, hw), branch_all[:, :, lanes].reshape(H * R, hw), TN)
        term_out[:, :, :, lanes] = grads.astype(bf16).reshape(A, 2, D, hw)
        return carried

    for tile in range(tiles):
        attend_back_tile(tile)
        if tile >= 2:
            keys_done(tile - 2)
        if tile >= 3:
            keys_sum(tile - 3)
        if tile == 3:
            for copy in br_copies:
                copy.wait_recv()
            lax.fori_loop(0, W // hw, out_tile, 0)
            out_sum.start()
        if tile == 4:
            out_sum.pair()
        if tile == 6:
            near_copy.wait_recv()
            in_send[...] = (in_of(far) + from_near[1].astype(f32)).astype(bf16)
    for k in (tiles - 2, tiles - 1):
        keys_done(k)
    for k in (tiles - 3, tiles - 2, tiles - 1):
        keys_sum(k)
    out_sum.cross()
    last_copy = send(in_send, in_last, nr_s.at[2], nr_r.at[2], (h, far * 2 + share))
    for source in here.back:
        for run in range(H):
            n = source * H + run
            remote(dq_send.at[0, 0], dq_in.at[0, 0], dq_s.at[n], dq_r.at[n], beside).wait_recv()
            remote(dkv_send.at[0, 0], dkv_in.at[0, 0], dz_s.at[n], dz_r.at[n], beside).wait_recv()
    for run in range(H):
        cosine, sine = cos_all[run], sin_all[run]
        for slab in range(hw // 128):
            lanes = slab * 128
            left, right = dq_in[2 * slab, run].astype(f32), dq_in[2 * slab + 1, run].astype(f32)
            both = jnp.concatenate([join(left, 0, right, 0), join(left, 1, right, 1)], axis=0)
            gp[run, :, lanes : lanes + 128] = turn(both, cosine, sine, True).astype(bf16)
            left, right = dkv_in[2 * slab, run].astype(f32), dkv_in[2 * slab + 1, run].astype(f32)
            gp[run, :, hw + lanes : hw + lanes + 128] = turn(
                join(left, 0, right, 0), cosine, sine, True
            ).astype(bf16)
            gp[run, :, 2 * hw + lanes : 2 * hw + lanes + 128] = join(left, 1, right, 1).astype(bf16)

    def qkv_block(chunk):
        return wq_all[chunk].reshape(B * D, 3 * hw)

    for half, (term, item) in enumerate(zip(term_qkv, qkv_sums)):

        def term_chunk(n, carried, half=half, term=term):
            lanes = pl.ds(pl.multiple_of((half * (H // 2) + n) * hw, hw), hw)
            left = (hats[:, :, lanes] * gain_rows[0:1, lanes]).astype(bf16).reshape(H * R, hw)
            grads = mm(left, gp[...].reshape(H * R, 3 * hw), TN).astype(bf16)
            term[:, :, n] = grads.reshape(A, 2, D, 3 * hw)
            return carried

        lax.fori_loop(0, H // 2, term_chunk, 0)
        item.start()
        if half:
            qkv_sums[0].pair()

    def part_one(run, i):
        return remote(g1_send.at[i], g1_in.at[i], g1_s.at[i], g1_r.at[i], (run, b))

    def one_run(i, carried):
        run = run_of(here, i)
        for chunk in range(H):
            lanes = slice(chunk * hw, (chunk + 1) * hw)
            g1_own[:, lanes] = mm(gp[run], qkv_block(chunk), NT)

        @pl.when(i < H - 1)
        def _():
            g1_send[i] = g1_own[...].astype(bf16)
            part_one(run, i).start()

        return carried

    lax.fori_loop(0, 1, one_run, 0)
    qkv_sums[1].pair()
    lax.fori_loop(1, H, one_run, 0)
    qkv_sums[0].cross()
    far_copy.wait_recv()
    down = down_of(part) + down_in[0].astype(f32) + from_far[...].astype(f32)
    in_swap.out[:, :, 2 * F :] = down.astype(bf16)
    last_copy.wait_recv()
    total = in_of(part) + from_near[0].astype(f32) + in_last[...].astype(f32)
    in_swap.out[:, :, : 2 * F] = total.astype(bf16)
    in_swap.start()
    qkv_sums[1].cross()

    grad = g1_own[...]
    hat, scale = standardize(tok_all[h].astype(f32))
    for i in (1, 2, 0):
        part_one(here.places[i], i).wait_recv()
        grad += g1_in[i].astype(f32)
    row = lax.broadcasted_iota(jnp.int32, (8, W), 0)
    rows = jnp.where(
        row == 0,
        jnp.sum(grad * hat, axis=0, keepdims=True),
        jnp.where(row == 1, gain_part[...], 0.0),
    )
    pick = (
        lax.broadcasted_iota(jnp.int32, (8, 128), 0) == lax.broadcasted_iota(jnp.int32, (8, 128), 1)
    ).astype(bf16)
    for chunk in range(H):
        gain_columns = mm(rows[:, chunk * hw : (chunk + 1) * hw].astype(bf16), pick, TN)
        term_gain[:, :, chunk] = gain_columns.astype(bf16).reshape(A, 2, D, 128)
    gain_sum.start()
    input_grad[...] = grad_middle[...] + norm_back(grad, hat, scale, gain_rows[0:1, :])
    gain_sum.middle()
    result = out_base[...]
    for i, copy in enumerate(o_copies):
        copy.wait_recv()
        result += o_in[i].astype(f32)
    output[...] = result.astype(bf16)
    in_swap.arrive()
    for place in range(H):
        in_grad[:, place * F : (place + 1) * F] = in_swap.landed[place, :, :F].astype(f32)
        in_grad[:, (H + place) * F : (H + place + 1) * F] = in_swap.landed[
            place, :, F : 2 * F
        ].astype(f32)
        down_grad[:, place * F : (place + 1) * F] = in_swap.landed[place, :, 2 * F :].astype(f32)
    for half, item in enumerate(qkv_sums):
        qkv_swap.out[half * (H // 2) : (half + 1) * (H // 2)] = item.close().astype(bf16)
    qkv_swap.start()
    gain_swap.out[...] = gain_sum.close().astype(bf16)
    gain_swap.start()
    out_grad[...] = out_sum.close()
    qkv_swap.arrive()
    for place in range(H):
        for j in range(3):
            qkv_grad[:, j * W + place * hw : j * W + (place + 1) * hw] = qkv_swap.landed[
                place, :, j * hw : (j + 1) * hw
            ].astype(f32)
    gain_swap.arrive()
    total = gain_swap.landed[0].astype(f32)
    for place in range(1, H):
        total += gain_swap.landed[place].astype(f32)
    rows = total.T
    gain_one[...] = rows[0:1, :]
    gain_two[...] = rows[1:2, :]
    for copy in [
        *kc_copies, *q_copies, *wm_copies, *wq_copies, *gain_copies, *tok_copies, *kv_copies,
        *mx_copies, *mx_late, *ma_copies.values(), *gm_copies, pair_copy,
        *br_copies, *o_copies, near_copy, far_copy, last_copy,
    ]:
        copy.wait_send()
    for k in range(tiles):
        dk_copy(k).wait_send()
    for there in here.there:
        for run in range(H):
            n = there * H + run
            remote(dq_send.at[0, 0], dq_in.at[0, 0], dq_s.at[n], dq_r.at[n], beside).wait_send()
            remote(dkv_send.at[0, 0], dkv_in.at[0, 0], dz_s.at[n], dz_r.at[n], beside).wait_send()
    for i in range(H - 1):
        part_of(here.places[i], i).wait_send()
        part_one(here.places[i], i).wait_send()
    for item in (spread, cot_gather, wo_line, *wq_lines, *wm_lines):
        item.finish()
    in_sum.core_finish()
    down_sum.core_finish()
    for item in (out_sum, *qkv_sums, gain_sum, in_swap, qkv_swap, gain_swap):
        item.finish()


def layer(tokens, cotangent, w_qkv, gain_one, gain_two, w_in, w_down, w_out, lengths):
    R, W = tokens.shape
    H, B = lax.axis_size("head"), lax.axis_size("blk")
    A = B // 2
    hw = W // H
    D = w_qkv.shape[0]
    F = w_down.shape[1] // H
    f32, bf16 = jnp.float32, jnp.bfloat16
    shape = jax.ShapeDtypeStruct
    buffer = lambda *sizes: pltpu.VMEM(sizes, bf16)
    wide = lambda *sizes: pltpu.VMEM(sizes, f32)
    outs = [
        shape((R, W), bf16),
        shape((R, W), f32),
        shape((D, 3 * W), f32),
        shape((D, W), f32),
        shape((D, 2 * H * F), f32),
        shape((D, H * F), f32),
        shape((1, D), f32),
        shape((1, D), f32),
    ]
    return pl.pallas_call(
        partial(layer_kernel, H, A),
        in_specs=[*[anywhere()] * 3, *[in_vmem()] * 2, *[anywhere()] * 3, in_smem()],
        out_specs=[in_vmem()] * len(outs),
        out_shape=outs,
        scratch_shapes=[
            buffer(R, W),
            buffer(*w_in.shape),
            buffer(*w_down.shape),
            buffer(*w_out.shape),
            buffer(H, R, W),
            buffer(H, R, W),
            buffer(H, B, D, 3 * hw),
            wide(H, R, 128),
            wide(H, R, 128),
            buffer(H, D, 3 * hw),
            buffer(H, D, 3 * F),
            buffer(H, D, 3 * F),
            buffer(H, A, 2, D, W),
            buffer(H, B, R, 128),
            buffer(A, H, R, 128),
            buffer(A, H // 2, R, 128),
            buffer(A, H // 2, R, 128),
            wide(H, R, hw),
            wide(H, R, W),
            wide(8, 128),
            wide(H - 1, 8, 128),
            wide(8, 128),
            wide(B, 8, 128),
            pltpu.VMEM((H * A // 2, 8, 2 * R), jnp.int32),
            wide(5, KEY_STEP, 2 * R),
            buffer(H // 2, A, R, 128),
            buffer(H // 2, A, R, 128),
            buffer(H, R, hw),
            *[buffer(H, 2, R, hw)] * 2,
            buffer(H, B, D, 3 * F),
            wide(H, R, W),
            buffer(H, R, W),
            buffer(H, R, F),
            buffer(H, R, 2 * F),
            buffer(H - 1, R, W),
            buffer(H - 1, R, W),
            wide(R, W),
            buffer(H, A, R // 2, 128),
            buffer(A, 2, H, D, 2 * F),
            buffer(A, H, D, 2 * F),
            buffer(A, 2, H, D, F),
            buffer(A, H, D, F),
            buffer(2, H, D, F),
            buffer(2, H, D, F),
            wide(R, W),
            buffer(H - 1, R, W),
            wide(R, W),
            buffer(2, H, D, 2 * F),
            buffer(H, D, F),
            wide(H * A // 2, 1, 2 * R),
            buffer(A, H, R // 2, 128),
            wide(8, W),
            wide(8, W),
            buffer(R, W),
            buffer(H, R, W),
            buffer(H - 1, R, W),
            buffer(2, H, D, 2 * F),
            buffer(H, D, F),
            *[buffer(H, D, 2 * F)] * 2,
            wide(H * B * R // KEY_STEP, KEY_STEP, 128),
            *[buffer(A, H, R // 2, 128)] * 2,
            *[buffer(H * B * R // KEY_STEP, 2, R, 128)] * 2,
            *[buffer(A, H, R, 128)] * 2,
            buffer(H, R, 3 * hw),
            *[buffer(H - 1, R, W)] * 2,
            wide(R, W),
            buffer(A, 2, D, W),
            *[buffer(A, 2, H // 2, D, 3 * hw)] * 2,
            dma(8),
            dma(1),
            *[dma(H - 1)] * 8,
            *[dma(B - 1)] * 2,
            *[dma(4)] * 2,
            *[dma(H - 1)] * 2,
            *[dma(4)] * 2,
            *[dma(A - 1)] * 4,
            *[dma(A)] * 2,
            *[dma((A - 1) * (H // 2))] * 2,
            *[dma((H - 1) * H)] * 2,
            *[dma(H - 1)] * 2,
            *[dma(H * A)] * 2,
            *[dma(1)] * 6,
            *[dma(H - 1)] * 6,
            *[dma(4)] * 2,
            *[dma(A * H)] * 4,
            *[dma(H * B * R // KEY_STEP)] * 2,
            *line_sems(A) * 5,
            *pair_scratch(A, (D, W)),
            *pair_scratch(A, (H // 2, D, 3 * hw)),
            *pair_scratch(A, (H // 2, D, 3 * hw)),
            *reduce_scratch(A, (H, D, 128)),
            *swap_scratch(H, (D, 3 * F)),
            *swap_scratch(H, (D, 3 * hw)),
            *swap_scratch(H, (D, 128)),
        ],
        compiler_params=params(0),
        cost_estimate=pl.CostEstimate(flops=10**10, bytes_accessed=10**7, transcendentals=10**6),
        name="layer",
    )(tokens, cotangent, w_qkv, gain_one, gain_two, w_in, w_down, w_out, lengths)


def per_device_split(
    tokens, attn_gain, w_qkv, w_attn_out, mlp_gain, w_in, w_mlp_out, doc_lengths, cotangent
):
    output, input_grad, qkv_grad, out_grad, in_grad, down_grad, gain_one, gain_two = deliver(
        *layer(
            tokens, cotangent, w_qkv, attn_gain[None], mlp_gain[None], w_in, w_mlp_out.T, w_attn_out, doc_lengths
        )
    )
    return (
        output,
        input_grad,
        gain_one[0],
        qkv_grad,
        out_grad,
        gain_two[0],
        in_grad,
        down_grad.T,
    )


def per_device(tokens, attn_gain, w_qkv, *rest):
    heads, blocks = lax.axis_size("head"), lax.axis_size("blk")
    fits = (
        heads == 4
        and blocks == 2 * (tokens.shape[1] // HEAD_DIM // heads) == 8
        and w_qkv.shape[0] * heads == 128
        and tokens.shape[0] == 128
    )
    chosen = per_device_split if fits else per_device_general
    return chosen(tokens, attn_gain, w_qkv, *rest)


def solution(mesh):
    placed = (
        P(("head", "blk"), None),
        P(("head", "blk")),
        P(("head", "blk"), None),
        P(("head", "blk"), None),
        P(("head", "blk")),
        P(("head", "blk"), None),
        P(None, ("head", "blk")),
        P(),
        P(("head", "blk"), None),
    )
    return jax.shard_map(
        per_device,
        mesh=mesh,
        in_specs=placed,
        out_specs=(
            P(("head", "blk"), None),
            P(("head", "blk"), None),
            P(("head", "blk")),
            P(("head", "blk"), None),
            P(("head", "blk"), None),
            P(("head", "blk")),
            P(("head", "blk"), None),
            P(None, ("head", "blk")),
        ),
        check_vma=False,
    )
```

```python
from functools import partial

import jax
import jax.numpy as jnp
import numpy as np
from jax import lax
from jax.experimental import pallas as pl
from jax.experimental.pallas import tpu as pltpu
from jax.sharding import PartitionSpec as P

HEAD_DIM = 64


norm_eps = 1e-05
rope_base = 160000.0
neg_large = -1e30


def from_behind(value, axis, by):
    devices = lax.axis_size(axis)
    return lax.ppermute(value, axis, [(i, (i + by) % devices) for i in range(devices)])


def layer_norm(values, gain):
    center = values - jnp.mean(values, axis=-1, keepdims=True)
    spread = jnp.mean(center * center, axis=-1, keepdims=True)
    return center * lax.rsqrt(spread + norm_eps) * gain


def rope_tables(places, head_size):
    half = head_size // 2
    freqs = rope_base ** (-(jnp.arange(half, dtype=jnp.float32) * 2.0) / head_size)
    angles = places.astype(jnp.float32)[:, None] * freqs[None, :]
    angles = jnp.concatenate([angles, angles], axis=1)
    return (jnp.cos(angles), jnp.sin(angles))


def rotate(values, cosine, sine):
    count = values.shape[0]
    head_size = cosine.shape[1]
    half = head_size // 2
    split = values.reshape(count, -1, head_size)
    turned = jnp.concatenate([-split[..., half:], split[..., :half]], axis=-1)
    return (split * cosine[:, None, :] + turned * sine[:, None, :]).reshape(count, -1)


def rotate_pair(query, keys, cosine, sine):
    return (rotate(query, cosine, sine), rotate(keys, cosine, sine))


def doc_numbers(places, ends, lengths):
    passed = places[:, None] >= ends[None, :]
    numbers = jnp.sum(passed.astype(jnp.int32), axis=1)
    offset = jnp.sum(jnp.where(passed, lengths[None, :], 0), axis=1)
    return (numbers, places - offset)


def gelu_gate(lifted):
    half = lifted.shape[1] // 2
    return jax.nn.gelu(lifted[:, :half], approximate=False) * lifted[:, half:]


def tile_scores(query, keys):
    heads = query.shape[1] // HEAD_DIM
    query_split = query.reshape(query.shape[0], heads, HEAD_DIM)
    key_split = keys.reshape(keys.shape[0], heads, HEAD_DIM)
    return jnp.einsum(
        "qhd,khd->hqk", query_split, key_split, preferred_element_type=jnp.float32
    ) * HEAD_DIM ** (-0.5)


def unchanged(state):
    return state


def forward_tile(state, query, keys, values, mask):
    top, total, running = state
    count = query.shape[0]
    heads = top.shape[0]
    scores = tile_scores(query, keys)
    filled = jnp.where(mask[None], scores, neg_large)
    new_top = jnp.maximum(top, jnp.max(filled, axis=-1))
    weights = jnp.where(mask[None], jnp.exp(scores - new_top[:, :, None]), 0.0)
    factor = jnp.exp(top - new_top)
    new_total = total * factor + jnp.sum(weights, axis=-1)
    mixed = jnp.einsum(
        "hqk,khd->qhd",
        weights.astype(jnp.bfloat16),
        values.reshape(-1, heads, HEAD_DIM),
        preferred_element_type=jnp.float32,
    )
    new_running = running.reshape(count, heads, HEAD_DIM) * factor.T[:, :, None] + mixed
    return (new_top, new_total, new_running.reshape(count, heads * HEAD_DIM))


def backward_tile(carry, query, keys, values, mask, norm_log, grad_out, delta):
    query_grad, run_grads = carry
    count = query.shape[0]
    columns = keys.shape[0]
    heads = norm_log.shape[0]
    scores = tile_scores(query, keys)
    probs = jnp.where(mask[None], jnp.exp(scores - norm_log[:, :, None]), 0.0)
    grad_split = grad_out.reshape(count, heads, HEAD_DIM)
    value_split = values.reshape(columns, heads, HEAD_DIM)
    grad_values = jnp.einsum(
        "hqk,qhd->khd", probs.astype(jnp.bfloat16), grad_split, preferred_element_type=jnp.float32
    )
    grad_probs = jnp.einsum(
        "qhd,khd->hqk", grad_split, value_split, preferred_element_type=jnp.float32
    )
    grad_scores = (probs * (grad_probs - delta[:, :, None])).astype(jnp.bfloat16)
    grad_query = jnp.einsum(
        "hqk,khd->qhd",
        grad_scores,
        keys.reshape(columns, heads, HEAD_DIM),
        preferred_element_type=jnp.float32,
    ) * HEAD_DIM ** (-0.5)
    grad_keys = jnp.einsum(
        "hqk,qhd->khd",
        grad_scores,
        query.reshape(count, heads, HEAD_DIM),
        preferred_element_type=jnp.float32,
    ) * HEAD_DIM ** (-0.5)
    added = jnp.stack([grad_keys.reshape(columns, -1), grad_values.reshape(columns, -1)])
    return (query_grad + grad_query.reshape(count, -1), run_grads + added)


def per_device_general(
    tokens, attn_gain, w_qkv, w_attn_out, mlp_gain, w_in, w_mlp_out, doc_lengths, cotangent
):
    own_rows = tokens.shape[0]
    width = tokens.shape[1]
    head_count = lax.axis_size("head")
    cycle_count = lax.axis_size("blk")
    head_place = lax.axis_index("head")
    cycle_place = lax.axis_index("blk")
    group_rows = head_count * own_rows
    block_runs = min(head_count, max(1, 512 // own_rows))
    block_count = head_count // block_runs
    block_rows = block_runs * own_rows
    doc_ends = jnp.cumsum(doc_lengths)
    counter = jnp.arange(own_rows, dtype=jnp.int32)
    own_places = (head_place * cycle_count + cycle_place) * own_rows + counter
    unused_docs, own_positions = doc_numbers(own_places, doc_ends, doc_lengths)
    cosine, sine = rope_tables(own_positions, HEAD_DIM)
    run_numbers = jnp.arange(head_count, dtype=jnp.int32)
    query_places = (
        (run_numbers[:, None] * cycle_count + cycle_place) * own_rows + counter[None, :]
    ).reshape(group_rows)
    query_docs, unused_positions = doc_numbers(query_places, doc_ends, doc_lengths)
    params = (
        lax.all_gather(attn_gain, ("head", "blk"), axis=0, tiled=True),
        lax.all_gather(w_qkv, ("head", "blk"), axis=0, tiled=True),
        lax.all_gather(w_attn_out, ("head", "blk"), axis=0, tiled=True),
        lax.all_gather(mlp_gain, ("head", "blk"), axis=0, tiled=True),
        lax.all_gather(w_in, ("head", "blk"), axis=0, tiled=True),
        lax.all_gather(w_mlp_out, ("head", "blk"), axis=1, tiled=True),
    )
    gain_one, full_qkv, full_attn_out, gain_two, full_in, full_mlp_out = params
    inputs = tokens.astype(jnp.float32)
    normed_one, norm_one_pull = jax.vjp(layer_norm, inputs, gain_one.astype(jnp.float32))
    normed_low = normed_one.astype(jnp.bfloat16)
    projected = jnp.dot(normed_low, full_qkv, preferred_element_type=jnp.float32)
    turned, rope_pull = jax.vjp(
        partial(rotate_pair, cosine=cosine, sine=sine),
        projected[:, :width],
        projected[:, width : 2 * width],
    )
    stacked = jnp.stack(
        [
            turned[0].astype(jnp.bfloat16),
            turned[1].astype(jnp.bfloat16),
            projected[:, 2 * width :].astype(jnp.bfloat16),
        ]
    )
    regrouped = lax.all_to_all(stacked, "head", split_axis=2, concat_axis=1, tiled=True)
    query_heads = regrouped[0]
    key_heads = regrouped[1]
    value_heads = regrouped[2]
    head_width = query_heads.shape[1]
    heads_here = head_width // HEAD_DIM

    def key_docs_at(first):
        places = (
            first % group_rows // own_rows * cycle_count + first // group_rows
        ) * own_rows + counter
        found, unused = doc_numbers(places, doc_ends, doc_lengths)
        return found

    def block_live(block, key_docs):
        block_docs = query_docs[block * block_rows : (block + 1) * block_rows]
        live = jnp.maximum(jnp.min(block_docs), jnp.min(key_docs)) <= jnp.minimum(
            jnp.max(block_docs), jnp.max(key_docs)
        )
        return (block_docs[:, None] == key_docs[None, :], live)

    def fold_forward(state, piece):
        key_part, value_part = piece

        def fold_one_run(number, carried):
            first = number * own_rows
            key_docs = key_docs_at(first)
            keys = lax.dynamic_slice_in_dim(key_part, number * own_rows, own_rows, 0)
            values = lax.dynamic_slice_in_dim(value_part, number * own_rows, own_rows, 0)
            updated = []
            for block in range(block_count):
                mask, live = block_live(block, key_docs)
                query = query_heads[block * block_rows : (block + 1) * block_rows]
                advance = partial(forward_tile, query=query, keys=keys, values=values, mask=mask)
                updated.append(lax.cond(live, advance, unchanged, carried[block]))
            return tuple(updated)

        return lax.fori_loop(0, key_part.shape[0] // own_rows, fold_one_run, state)

    def fresh_state():
        return tuple(
            (
                (
                    jnp.full((heads_here, block_rows), neg_large, jnp.float32),
                    jnp.zeros((heads_here, block_rows), jnp.float32),
                    jnp.zeros((block_rows, head_width), jnp.float32),
                )
                for block in range(block_count)
            )
        )

    def finish(state):
        outputs = []
        logs = []
        for top, total, running in state:
            scaled = running.reshape(block_rows, heads_here, HEAD_DIM) / total.T[:, :, None]
            outputs.append(scaled.reshape(block_rows, head_width))
            logs.append(top + jnp.log(total))
        return (
            jnp.concatenate(outputs, axis=0).astype(jnp.bfloat16),
            jnp.concatenate(logs, axis=1),
        )

    state = fold_forward(
        fresh_state(),
        (
            lax.all_gather(key_heads, "blk", axis=0, tiled=True),
            lax.all_gather(value_heads, "blk", axis=0, tiled=True),
        ),
    )
    out_heads, norm_log = finish(state)
    out_tokens = lax.all_to_all(out_heads, "head", split_axis=0, concat_axis=1, tiled=True)
    middle = inputs + jnp.dot(out_tokens, full_attn_out, preferred_element_type=jnp.float32)
    normed_two, norm_two_pull = jax.vjp(layer_norm, middle, gain_two.astype(jnp.float32))
    normed_two_low = normed_two.astype(jnp.bfloat16)
    lifted = jnp.dot(normed_two_low, full_in, preferred_element_type=jnp.float32)
    activated, geglu_pull = jax.vjp(gelu_gate, lifted)
    activated_low = activated.astype(jnp.bfloat16)
    output = (
        middle + jnp.dot(activated_low, full_mlp_out, preferred_element_type=jnp.float32)
    ).astype(jnp.bfloat16)
    params = (
        lax.all_gather(attn_gain, ("head", "blk"), axis=0, tiled=True),
        lax.all_gather(w_qkv, ("head", "blk"), axis=0, tiled=True),
        lax.all_gather(w_attn_out, ("head", "blk"), axis=0, tiled=True),
        lax.all_gather(mlp_gain, ("head", "blk"), axis=0, tiled=True),
        lax.all_gather(w_in, ("head", "blk"), axis=0, tiled=True),
        lax.all_gather(w_mlp_out, ("head", "blk"), axis=1, tiled=True),
    )
    gain_one, full_qkv, full_attn_out, gain_two, full_in, full_mlp_out = params
    grad_act = jnp.einsum("td,fd->tf", cotangent, full_mlp_out, preferred_element_type=jnp.float32)
    grad_lifted = geglu_pull(grad_act)[0].astype(jnp.bfloat16)
    grad_normed_two = jnp.einsum(
        "tf,df->td", grad_lifted, full_in, preferred_element_type=jnp.float32
    )
    grad_middle_part, grad_gain_two = norm_two_pull(grad_normed_two)
    grad_middle = cotangent.astype(jnp.float32) + grad_middle_part
    grad_branch = grad_middle.astype(jnp.bfloat16)
    grad_mixed = jnp.einsum(
        "te,de->td", grad_branch, full_attn_out, preferred_element_type=jnp.float32
    ).astype(jnp.bfloat16)
    grad_heads = lax.all_to_all(grad_mixed, "head", split_axis=1, concat_axis=0, tiled=True)
    state = fold_forward(
        fresh_state(),
        (
            lax.all_gather(key_heads, "blk", axis=0, tiled=True),
            lax.all_gather(value_heads, "blk", axis=0, tiled=True),
        ),
    )
    out_heads, norm_log = finish(state)
    delta = jnp.einsum(
        "qhd,qhd->hq",
        grad_heads.reshape(group_rows, heads_here, HEAD_DIM).astype(jnp.float32),
        out_heads.reshape(group_rows, heads_here, HEAD_DIM).astype(jnp.float32),
    )

    def piece_backward(query_grads, key_part, value_part, start):
        piece_rows = key_part.shape[0]

        def piece_one_run(number, carried):
            query_now, piece_grads = carried
            first = start + number * own_rows
            key_docs = key_docs_at(first)
            keys = lax.dynamic_slice_in_dim(key_part, number * own_rows, own_rows, 0)
            values = lax.dynamic_slice_in_dim(value_part, number * own_rows, own_rows, 0)
            run_grads = jnp.zeros((2, own_rows, head_width), jnp.float32)
            updated = []
            for block in range(block_count):
                mask, live = block_live(block, key_docs)
                lower = block * block_rows
                upper = (block + 1) * block_rows
                advance = partial(
                    backward_tile,
                    query=query_heads[lower:upper],
                    keys=keys,
                    values=values,
                    mask=mask,
                    norm_log=norm_log[:, lower:upper],
                    grad_out=grad_heads[lower:upper],
                    delta=delta[:, lower:upper],
                )
                new_query, run_grads = lax.cond(
                    live, advance, unchanged, (query_now[block], run_grads)
                )
                updated.append(new_query)
            piece_grads = lax.dynamic_update_slice_in_dim(
                piece_grads, run_grads, number * own_rows, 1
            )
            return (tuple(updated), piece_grads)

        return lax.fori_loop(
            0,
            piece_rows // own_rows,
            piece_one_run,
            (query_grads, jnp.zeros((2, piece_rows, head_width), jnp.float32)),
        )

    start_query = tuple(
        (jnp.zeros((block_rows, head_width), jnp.float32) for block in range(block_count))
    )

    def cycle_step(step, carried):
        query_now, blocks, travelling = carried
        owner = (cycle_place - step) % cycle_count
        query_now, piece_grads = piece_backward(query_now, blocks[0], blocks[1], owner * group_rows)
        travelling = travelling + piece_grads
        blocks = from_behind(blocks, "blk", 1)
        travelling = from_behind(travelling.astype(jnp.bfloat16), "blk", 1).astype(travelling.dtype)
        return (query_now, blocks, travelling)

    start_cycle = (
        start_query,
        jnp.stack([key_heads, value_heads]),
        jnp.zeros((2, group_rows, head_width), jnp.float32),
    )
    query_grads, unused_blocks, own_grads = lax.fori_loop(0, cycle_count, cycle_step, start_cycle)
    grad_stack = jnp.stack(
        [
            jnp.concatenate(query_grads, axis=0).astype(jnp.bfloat16),
            own_grads[0].astype(jnp.bfloat16),
            own_grads[1].astype(jnp.bfloat16),
        ]
    )
    back_tokens = lax.all_to_all(grad_stack, "head", split_axis=1, concat_axis=2, tiled=True)
    grad_query, grad_keys = rope_pull(
        (back_tokens[0].astype(jnp.float32), back_tokens[1].astype(jnp.float32))
    )
    grad_projected = jnp.concatenate(
        [grad_query, grad_keys, back_tokens[2].astype(jnp.float32)], axis=1
    ).astype(jnp.bfloat16)
    grad_normed_one = jnp.einsum(
        "te,de->td", grad_projected, full_qkv, preferred_element_type=jnp.float32
    )
    grad_input_part, grad_gain_one = norm_one_pull(grad_normed_one)
    input_grad = grad_middle + grad_input_part

    def columns(source):
        return source

    term_qkv = jnp.einsum(
        "td,te->de", columns(normed_low), grad_projected, preferred_element_type=jnp.float32
    )
    term_out = jnp.einsum(
        "td,te->de", columns(out_tokens), grad_branch, preferred_element_type=jnp.float32
    )
    term_in = jnp.einsum(
        "td,tf->df", columns(normed_two_low), grad_lifted, preferred_element_type=jnp.float32
    )
    term_down = jnp.einsum(
        "td,tf->df", columns(cotangent), activated_low, preferred_element_type=jnp.float32
    )
    sums = lax.psum_scatter(
        jnp.concatenate([term_qkv, term_out, term_in, term_down], axis=1),
        ("head", "blk"),
        scatter_dimension=0,
        tiled=True,
    )
    ff_width = full_mlp_out.shape[0]
    qkv_grad = sums[:, : 3 * width]
    attn_out_grad = sums[:, 3 * width : 4 * width]
    in_grad = sums[:, 4 * width : 4 * width + 2 * ff_width]
    down_grad = sums[:, 4 * width + 2 * ff_width :].T
    gain_sums = lax.psum_scatter(
        jnp.stack([grad_gain_one, grad_gain_two]), ("head", "blk"), scatter_dimension=1, tiled=True
    )
    return (
        output,
        input_grad,
        gain_sums[0],
        qkv_grad,
        attn_out_grad,
        gain_sums[1],
        in_grad,
        down_grad,
    )


VMEM = 62 * 2**20
MESH = pl.DeviceIdType.MESH
KEY_STEP = 512
KEY_ALIGN = 256
NN = (((1,), (0,)), ((), ()))
NT = (((1,), (1,)), ((), ()))
TN = (((0,), (0,)), ((), ()))


def mm(left, right, dims=NN):
    return lax.dot_general(left, right, dims, preferred_element_type=jnp.float32)


def params(collective_id=None):
    if collective_id is None:
        return pltpu.CompilerParams(vmem_limit_bytes=VMEM)
    return pltpu.CompilerParams(
        collective_id=collective_id, has_side_effects=True, vmem_limit_bytes=VMEM
    )


def in_vmem():
    return pl.BlockSpec(memory_space=pltpu.VMEM)


def anywhere():
    return pl.BlockSpec(memory_space=pl.ANY)


def in_smem():
    return pl.BlockSpec(memory_space=pltpu.SMEM)


def dma(*counts):
    return pltpu.SemaphoreType.DMA(counts)


def halves(packed, side):
    wide = packed.astype(jnp.float32)
    if side:
        wide = pltpu.roll(wide, HEAD_DIM, 1)
    lane = lax.broadcasted_iota(jnp.int32, wide.shape, 1)
    return jnp.where(lane < HEAD_DIM, wide, 0.0)


def tile_span(lengths, side, R, T):
    hh, u = pl.program_id(0), pl.program_id(1)
    runs, parts = 2 * pl.num_programs(0), 2 * pl.num_programs(1)
    share = lax.rem(lax.axis_index("blk"), 2)
    first = (((hh + side * (runs // 2)) * parts + 2 * u) * 2 + share) * R
    last = first + 3 * R - 1
    lane = lax.broadcasted_iota(jnp.int32, (1, 2 * R), 1)
    place = first + lane + jnp.where(lane < R, 0, R)

    def one(d, carried):
        low, begin, stop, start, end = carried
        high = low + lengths[d]
        inside = (place >= low) & (place < high)
        return (
            high,
            jnp.where(inside, low, begin),
            jnp.where(inside, high, stop),
            jnp.where((first >= low) & (first < high), low, start),
            jnp.where((last >= low) & (last < high), high, end),
        )

    zero = jnp.int32(0)
    unused, begin, stop, start, end = lax.fori_loop(
        0,
        lengths.shape[0],
        one,
        (zero, jnp.zeros_like(place), jnp.zeros_like(place), zero, zero),
        unroll=True,
    )
    start = start // KEY_ALIGN
    steps = (end - start * KEY_ALIGN + KEY_STEP - 1) // KEY_STEP
    start = jnp.minimum(start, T // KEY_ALIGN - steps * (KEY_STEP // KEY_ALIGN))
    return (begin, stop, start, steps)


def attend_kernel(lengths, qp, kv, op, lse, s_scr):
    pairs = qp.shape[0] * qp.shape[2]
    T = kv.shape[0]
    half_runs = pl.num_programs(0)
    hh, u = pl.program_id(0), pl.program_id(1)
    at = lax.broadcasted_iota(jnp.int32, (KEY_STEP, pairs), 0)
    results = []
    for side in (0, 1):
        tile = (hh + side * half_runs) * pl.num_programs(1) + u
        begin, stop, start, steps = tile_span(lengths, side, pairs // 2, T)
        query = (halves(qp[...].reshape(pairs, 2 * HEAD_DIM), side) * HEAD_DIM**-0.5).astype(
            jnp.bfloat16
        )

        def keys_at(n):
            first = pl.multiple_of(start * KEY_ALIGN + n * KEY_STEP, KEY_ALIGN)
            return (first, kv[pl.ds(first, KEY_STEP), :])

        def score(n, top):
            first, keys = keys_at(n)
            same = (at >= begin - first) & (at < stop - first)
            scores = jnp.where(same, mm(keys, query, NT), neg_large)
            s_scr[n] = scores
            return jnp.maximum(top, jnp.max(scores, axis=0, keepdims=True))

        top = lax.fori_loop(0, steps, score, jnp.full((1, pairs), neg_large, jnp.float32))

        def mix(n, carried):
            total, acc = carried
            unused, keys = keys_at(n)
            weights = jnp.exp(s_scr[n] - top)
            total = total + jnp.sum(weights, axis=0, keepdims=True)
            return (total, acc + mm(keys, weights.astype(jnp.bfloat16), TN))

        total, acc = lax.fori_loop(
            0,
            steps,
            mix,
            (jnp.zeros((1, pairs), jnp.float32), jnp.zeros((2 * HEAD_DIM, pairs), jnp.float32)),
        )
        lse[tile] = top + jnp.log(total)
        results.append(acc[HEAD_DIM:] / total)
    both = jnp.concatenate(results, axis=0).T
    op[...] = both.astype(jnp.bfloat16).reshape(op.shape)


def attend(lengths, qp, kv):
    parts, half_runs, rows, lanes = qp.shape
    tiles = half_runs * parts
    piece = pl.BlockSpec((2, 1, rows, lanes), lambda i, j, s: (j, i, 0, 0))
    return pl.pallas_call(
        attend_kernel,
        grid_spec=pltpu.PrefetchScalarGridSpec(
            num_scalar_prefetch=1,
            grid=(half_runs, parts // 2),
            in_specs=[piece, in_vmem()],
            out_specs=[piece, in_vmem()],
            scratch_shapes=[pltpu.VMEM((kv.shape[0] // KEY_STEP, KEY_STEP, 2 * rows), jnp.float32)],
        ),
        out_shape=[
            jax.ShapeDtypeStruct(qp.shape, jnp.bfloat16),
            jax.ShapeDtypeStruct((tiles, 1, 2 * rows), jnp.float32),
        ],
        compiler_params=params(),
        cost_estimate=pl.CostEstimate(
            flops=10**9, bytes_accessed=50 * 10**6, transcendentals=10**6
        ),
        name="attend",
    )(lengths, qp, kv)


def attend_back_kernel(
    lengths, qp, gp, op, lse, kv, dqp, dkv, acc_scr
):
    pairs = qp.shape[0] * qp.shape[2]
    T = kv.shape[0]
    half_runs = pl.num_programs(0)
    hh, u = pl.program_id(0), pl.program_id(1)
    begins = (hh == 0) & (u == 0)
    ends = (hh == half_runs - 1) & (u == pl.num_programs(1) - 1)
    @pl.when(begins)
    def _():
        acc_scr[...] = jnp.zeros_like(acc_scr)

    at = lax.broadcasted_iota(jnp.int32, (KEY_STEP, pairs), 0)
    lane = lax.broadcasted_iota(jnp.int32, (pairs, 2 * HEAD_DIM), 1)
    flat = (pairs, 2 * HEAD_DIM)
    results = []
    for side in (0, 1):
        tile = (hh + side * half_runs) * pl.num_programs(1) + u
        begin, stop, start, steps = tile_span(lengths, side, pairs // 2, T)
        query = (halves(qp[...].reshape(flat), side) * HEAD_DIM**-0.5).astype(jnp.bfloat16)
        pieces = []
        for n in range(2):
            piece = gp[n, hh + side * half_runs].astype(jnp.float32)
            pieces += [pltpu.roll(piece, HEAD_DIM, 1), piece]
        grad = jnp.where(lane < HEAD_DIM, 0.0, jnp.concatenate(pieces, axis=0))
        mixed = op[...].reshape(flat).astype(jnp.float32)
        if not side:
            mixed = pltpu.roll(mixed, HEAD_DIM, 1)
        delta = jnp.sum((grad * mixed).T, axis=0, keepdims=True)
        both = jnp.concatenate([query, grad.astype(jnp.bfloat16)], axis=0)
        logs = lse[tile]

        def step(n, dq):
            first = pl.multiple_of(start * KEY_ALIGN + n * KEY_STEP, KEY_ALIGN)
            rows = pl.ds(first, KEY_STEP)
            keys = kv[rows, :]
            same = (at >= begin - first) & (at < stop - first)
            products = mm(keys, both, NT)
            probs = jnp.where(same, jnp.exp(products[:, :pairs] - logs), 0.0)
            grad_scores = (probs * (products[:, pairs:] - delta)).astype(jnp.bfloat16)
            left = jnp.concatenate([grad_scores, probs.astype(jnp.bfloat16)], axis=1)
            acc_scr[rows, :] += mm(left, both)
            return dq + mm(keys, grad_scores, TN)

        dq = lax.fori_loop(0, steps, step, jnp.zeros((2 * HEAD_DIM, pairs), jnp.float32))
        results.append(dq[:HEAD_DIM] * HEAD_DIM**-0.5)
    dqp[...] = jnp.concatenate(results, axis=0).T.astype(jnp.bfloat16).reshape(dqp.shape)

    @pl.when(ends)
    def _():
        dkv[...] = acc_scr[...].astype(dkv.dtype)


def attend_back(lengths, qp, gp, op, lse, kv):
    parts, half_runs, rows, lanes = qp.shape
    piece = pl.BlockSpec((2, 1, rows, lanes), lambda i, j, s: (j, i, 0, 0))
    grads = pl.BlockSpec((2, 2 * half_runs, rows // 2, lanes), lambda i, j, s: (j, 0, 0, 0))
    return pl.pallas_call(
        attend_back_kernel,
        grid_spec=pltpu.PrefetchScalarGridSpec(
            num_scalar_prefetch=1,
            grid=(half_runs, parts // 2),
            in_specs=[piece, grads, piece, *[in_vmem()] * 2],
            out_specs=[piece, in_vmem()],
            scratch_shapes=[pltpu.VMEM(kv.shape, jnp.float32)],
        ),
        out_shape=[
            jax.ShapeDtypeStruct(qp.shape, jnp.bfloat16),
            jax.ShapeDtypeStruct(kv.shape, jnp.bfloat16),
        ],
        compiler_params=params(),
        cost_estimate=pl.CostEstimate(
            flops=3 * 10**9, bytes_accessed=60 * 10**6, transcendentals=10**6
        ),
        name="attend_back",
    )(lengths, qp, gp, op, lse, kv)


def deliver_kernel(*refs):
    count = len(refs) // 2
    for source, target in zip(refs[:count], refs[count:]):
        target[...] = source[...]


def deliver(*arrays):
    return pl.pallas_call(
        deliver_kernel,
        in_specs=[in_vmem()] * len(arrays),
        out_specs=[in_vmem()] * len(arrays),
        out_shape=[jax.ShapeDtypeStruct(a.shape, a.dtype) for a in arrays],
        compiler_params=params(),
        name="deliver",
    )(*arrays)


def meet(peers):
    barrier = pltpu.get_barrier_semaphore()
    for peer in peers:
        pl.semaphore_signal(barrier, inc=1, device_id=peer, device_id_type=MESH)
    pl.semaphore_wait(barrier, len(peers))


def remote(source, target, send_sem, recv_sem, peer):
    return pltpu.make_async_remote_copy(
        src_ref=source,
        dst_ref=target,
        send_sem=send_sem,
        recv_sem=recv_sem,
        device_id=peer,
        device_id_type=MESH,
    )


def send(source, target, send_sem, recv_sem, peer):
    copy = remote(source, target, send_sem, recv_sem, peer)
    copy.start()
    return copy


class Place:
    def __init__(self, parts):
        h, b = lax.axis_index("head"), lax.axis_index("blk")
        self.h, self.b, self.parts = h, b, parts
        self.part, self.share = b // 2, lax.rem(b, 2)
        x, y = lax.rem(h, 2), h // 2
        self.places = [(1 - y) * 2 + 1 - x, y * 2 + 1 - x, (1 - y) * 2 + x]
        self.across = [(place, b) for place in self.places]
        self.there = [lax.rem(self.part + i, parts) for i in range(1, parts)]
        self.back = [lax.rem(self.part + parts - i, parts) for i in range(1, parts)]
        self.along = [(h, part * 2 + self.share) for part in self.there]
        self.beside = (h, self.part * 2 + 1 - self.share)
        self.near = self.part + 1 - 2 * lax.rem(self.part, 2)
        self.over = lax.rem(self.part + 2, 4)
        self.far = 3 - self.part
        self.askew = [(h, part * 2 + 1 - self.share) for part in self.there]


class LineGather:
    def __init__(self, view, own, here, sems):
        self.view, self.own, self.here, self.parts = view, own, here, here.parts
        self.right_s, self.left_s, self.line_r, self.core_s, self.core_r = sems
        self.first = 0

    def _copy(self, source, block, side):
        here = self.here
        if side == 0:
            sems, peer = (self.core_s, self.core_r), here.beside
        else:
            sems = (self.right_s if side > 0 else self.left_s, self.line_r)
            peer = (here.h, (here.part + side) * 2 + here.share)
        return remote(
            source, self.view(block, here.share), sems[0].at[block], sems[1].at[block], peer
        )

    def _can(self, side):
        return self.here.part < self.parts - 1 if side > 0 else self.here.part > 0

    def start(self):
        for side in (1, -1):

            @pl.when(self._can(side))
            def _():
                self._copy(self.own, self.here.part, side).start()

        self._copy(self.own, self.here.part, 0).start()

    def start_from(self, near):
        self.first = 1
        for side in (1, -1):
            block = self.here.part - side

            @pl.when((block >= 0) & (block < self.parts) & self._can(side))
            def _():
                self._copy(near[side], block, side).start()

        self._copy(self.own, self.here.part, 0).start()
        for side in (1, -1):
            block = self.here.part - side

            @pl.when((block >= 0) & (block < self.parts))
            def _():
                self._copy(near[side], block, 0).start()

    def step(self, k):
        for side in (1, -1):
            block = self.here.part - side * k

            @pl.when((block >= 0) & (block < self.parts))
            def _():
                there = self.view(block, self.here.share)
                self._copy(there, block, side).wait_recv()

                @pl.when(self._can(side))
                def _():
                    self._copy(there, block, side).start()

                self._copy(there, block, 0).start()

    def arrive(self):
        for block in range(self.parts):
            self._copy(self.own, block, 0).wait_recv()

    def finish(self):
        for side in (1, -1):
            for block in range(self.parts):
                first = self.here.part - side * self.first
                sent = block <= first if side > 0 else block >= first

                @pl.when(sent & self._can(side))
                def _():
                    self._copy(self.own, block, side).wait_send()

        for block in range(self.parts):
            self._copy(self.own, block, 0).wait_send()


class CornerGather:
    def __init__(self, whole, half, own, here, sems):
        self.whole, self.half, self.own, self.here = whole, half, own, here
        self.send_s, self.recv_s = sems

    def _copy(self, n):
        h, (corner, x, y) = self.here.h, self.here.across
        if n < 2:
            source, target, peer = self.own, self.whole(h), (x, y)[n]
        else:
            block = (y, x)[n - 2][0]
            source = target = self.half(block, n - 2)
            peer = (x, y)[n - 2]
        return remote(source, target, self.send_s.at[n], self.recv_s.at[n], peer)

    def start(self):
        for n in range(2):
            self._copy(n).start()

    def forward(self):
        for n in range(2):
            self._copy(n).wait_recv()
        for n in range(2, 4):
            self._copy(n).start()

    def arrive(self):
        for n in range(2, 4):
            self._copy(n).wait_recv()

    def finish(self):
        for n in range(4):
            self._copy(n).wait_send()


def local(source, target, sem):
    copy = pltpu.make_async_copy(source, target, sem)
    copy.start()
    return copy


def line_sems(parts):
    return [dma(parts)] * 5


def standardize(values):
    center = values - jnp.mean(values, axis=-1, keepdims=True)
    spread = jnp.mean(center * center, axis=-1, keepdims=True)
    scale = lax.rsqrt(spread + norm_eps)
    return (center * scale, scale)


def norm_back(grad, hat, scale, gain):
    inner = grad * gain
    return scale * (
        inner
        - jnp.mean(inner, axis=-1, keepdims=True)
        - hat * jnp.mean(inner * hat, axis=-1, keepdims=True)
    )


def turn(values, cosine, sine, back=False):
    lane = lax.broadcasted_iota(jnp.int32, values.shape, 1)
    first = lax.rem(lane, HEAD_DIM) < HEAD_DIM // 2
    source = values * sine if back else values
    ahead = pltpu.roll(source, 128 - HEAD_DIM // 2, 1)
    behind = pltpu.roll(source, HEAD_DIM // 2, 1)
    if back:
        return values * cosine + jnp.where(first, ahead, -behind)
    return values * cosine + jnp.where(first, -ahead, behind) * sine


def join(left, left_side, right, right_side):
    lane = lax.broadcasted_iota(jnp.int32, left.shape, 1)
    left = pltpu.roll(left, HEAD_DIM, 1) if left_side else left
    right = right if right_side else pltpu.roll(right, HEAD_DIM, 1)
    return jnp.where(lane < HEAD_DIM, left, right)


class Reduce:
    def __init__(self, term, core_in, line_out, line_in, here, sems):
        self.term, self.core_in, self.line_out, self.line_in = term, core_in, line_out, line_in
        self.here, self.parts = here, here.parts
        self.core_s, self.core_r, self.line_s, self.line_r = sems

    def _core(self):
        return remote(
            self.term.at[:, 1 - self.here.share],
            self.core_in,
            self.core_s.at[0],
            self.core_r.at[0],
            self.here.beside,
        )

    def _line(self, i):
        return remote(
            self.line_out[i],
            self.line_in.at[i],
            self.line_s.at[i],
            self.line_r.at[i],
            self.here.along[i],
        )

    def _sum(self, there):
        own = self.term[there, self.here.share].astype(jnp.float32)
        return own + self.core_in[there].astype(jnp.float32)

    def start(self):
        self._core().start()

    def core_sums(self):
        self._core().wait_recv()
        return self._sum

    def middle(self):
        self._core().wait_recv()
        for i, there in enumerate(self.here.there):
            self.line_out[i][...] = self._sum(there).astype(jnp.bfloat16)
            self._line(i).start()

    def close(self):
        total = self._sum(self.here.part)
        for i in range(self.parts - 1):
            self._line(i).wait_recv()
            total += self.line_in[i].astype(jnp.float32)
        return total

    def core_finish(self):
        self._core().wait_send()

    def finish(self):
        self.core_finish()
        for i in range(self.parts - 1):
            self._line(i).wait_send()


def reduce_scratch(parts, shape):
    return [
        pltpu.VMEM((parts, 2, *shape), jnp.bfloat16),
        pltpu.VMEM((parts, *shape), jnp.bfloat16),
        pltpu.VMEM((parts - 1, *shape), jnp.bfloat16),
        pltpu.VMEM((parts - 1, *shape), jnp.bfloat16),
        dma(1),
        dma(1),
        dma(parts - 1),
        dma(parts - 1),
    ]


class PairReduce:
    def __init__(self, core_in, near_out, near_in, far_out, far_in, *sems, term, here):
        self.term, self.core_in, self.near_out, self.near_in = term, core_in, near_out, near_in
        self.far_out, self.far_in, self.sems, self.here = far_out, far_in, sems, here

    def _copy(self, step):
        here = self.here
        source, target, peer = (
            (self.term.at[:, 1 - here.share], self.core_in, here.beside),
            (self.near_out, self.near_in, (here.h, here.near * 2 + here.share)),
            (self.far_out, self.far_in, (here.h, here.far * 2 + here.share)),
        )[step]
        return remote(source, target, self.sems[2 * step].at[0], self.sems[2 * step + 1].at[0], peer)

    def _sum(self, there):
        own = self.term[there, self.here.share].astype(jnp.float32)
        return own + self.core_in[there].astype(jnp.float32)

    def start(self):
        self._copy(0).start()

    def pair(self):
        self._copy(0).wait_recv()
        self.near_out[0] = self._sum(self.here.near).astype(jnp.bfloat16)
        self.near_out[1] = self._sum(self.here.over).astype(jnp.bfloat16)
        self._copy(1).start()

    def cross(self):
        self._copy(1).wait_recv()
        self.far_out[...] = (
            self._sum(self.here.far) + self.near_in[1].astype(jnp.float32)
        ).astype(jnp.bfloat16)
        self._copy(2).start()

    def close(self):
        self._copy(2).wait_recv()
        total = self._sum(self.here.part) + self.near_in[0].astype(jnp.float32)
        return total + self.far_in[...].astype(jnp.float32)

    def finish(self):
        for step in range(3):
            self._copy(step).wait_send()


def pair_scratch(parts, shape):
    return [
        pltpu.VMEM((parts, *shape), jnp.bfloat16),
        *[pltpu.VMEM((2, *shape), jnp.bfloat16)] * 2,
        *[pltpu.VMEM(shape, jnp.bfloat16)] * 2,
        *[dma(1)] * 6,
    ]


def reducer(scratch, here):
    term, core_in, line_out, line_in, *sems = scratch
    outs = [line_out.at[i] for i in range(here.parts - 1)]
    return (term, Reduce(term, core_in, outs, line_in, here, sems))


class Swap:
    def __init__(self, out, landed, send_s, recv_s, here):
        self.out, self.landed, self.here = out, landed, here
        self.send_s, self.recv_s = send_s, recv_s

    def start(self):
        here = self.here
        self.copies = [
            send(self.out.at[peer[0]], self.landed.at[here.h], self.send_s.at[i], self.recv_s.at[i], peer)
            for i, peer in enumerate(here.across)
        ]
        self.landed[here.h] = self.out[here.h]

    def arrive(self):
        for copy in self.copies:
            copy.wait_recv()

    def finish(self):
        for copy in self.copies:
            copy.wait_send()


def swap_scratch(heads, shape):
    return [
        pltpu.VMEM((heads, *shape), jnp.bfloat16),
        pltpu.VMEM((heads, *shape), jnp.bfloat16),
        dma(heads - 1),
        dma(heads - 1),
    ]


def run_of(here, i):
    x, y = lax.rem(here.h, 2), here.h // 2
    x = x + (1 - i // 2) * (1 - 2 * x)
    y = y + (1 - i % 2) * (1 - 2 * y)
    return y * 2 + x


def load(pairs, sems):
    copies = [pltpu.make_async_copy(*pair, sems.at[i]) for i, pair in enumerate(pairs)]
    for copy in copies:
        copy.start()
    return copies


def layer_kernel(
    H, A, tok_in, cot_in, wq_in, gain_one_in, gain_two_in, w_in_in, w_down_in, w_out_in, lengths,
    output, input_grad, qkv_grad, out_grad, in_grad, down_grad, gain_one, gain_two,
    cot, w_in, w_down, w_out, tok_all, cot_all, wq_all, cos_all, sin_all,
    wq_st, wm_src, wm_own, wo_all, kv, kv_send, q_all, q_send, q_runs, hats, gain_src, gain_st, gain_tile, gain_all,
    bounds, s_scr, op, mx_in, mixed_own, mixed_early, mixed_late, wm_all, middle, normed, act, lift,
    g2_send, g2_in, g2_own, gm_send, in_term, in_core, down_term, down_core, down_send, down_in,
    out_base, out_parts, grad_middle, near_out, far_out,
    lse, go, gain_rows, gain_part, branch_own, branch_all, o_in, from_near, from_far, in_send, in_last,
    dkv_sum, dq_send, dq_in, dk_send, dk_in, dkv_send, dkv_in, gp, g1_send, g1_in, g1_own,
    term_out, term_qkv_low, term_qkv_high,
    load_s, own_s,
    tok_s, tok_r, wq_s, wq_r, wm_s, wm_r, ga_s, ga_r, gb_s, gb_r, wx_s, wx_r, wf_s, wf_r, cot_s, cot_r,
    q_s, q_r, kv_s, kv_r, kc_s, kc_r, mx_s, mx_r, ma_s, ma_r, g2_s, g2_r, gm_s, gm_r,
    in_core_s, in_core_r, down_core_s, down_core_r, pair_s, pair_r,
    br_s, br_r, o_s, o_r, g1_s, g1_r, nr_s, nr_r, dq_s, dq_r, dz_s, dz_r, dk_s, dk_r, *more,
):
    line, more = more[:25], more[25:]
    term_qkv = (term_qkv_low, term_qkv_high)
    f32, bf16 = jnp.float32, jnp.bfloat16
    R, W = tok_all.shape[1:]
    B = 2 * A
    hw = W // H
    D = wq_in.shape[0]
    F = w_in.shape[1] // 2 // H
    here = Place(A)
    h, b, part, share = here.h, here.b, here.part, here.share
    across, along, beside = here.across, here.along, here.beside

    def slices(source, target, place):
        return [
            (
                source.at[:, pl.ds(pl.multiple_of(j * W + place * hw, hw), hw)],
                target.at[h, :, j * hw : (j + 1) * hw],
            )
            for j in range(3)
        ]

    loads = [
        local(source, target, load_s.at[n])
        for n, (source, target) in enumerate(
            [
                (w_out_in, w_out), (w_in_in, w_in), (w_down_in, w_down), (cot_in, cot), (tok_in, tok_all.at[h]),
                *slices(wq_in, wq_st, h),
            ]
        )
    ]
    row = lax.broadcasted_iota(jnp.int32, (8, 128), 0)
    lane = lax.broadcasted_iota(jnp.int32, (8, 128), 1)
    gain_src[...] = jnp.zeros((8, 128), f32)
    gain_src[0:1, :D] = gain_one_in[...].astype(f32)
    gain_src[1:2, :D] = gain_two_in[...].astype(f32)
    gain_src[...] = pltpu.roll(gain_src[...], h * D, 1)
    others = [
        (run_of(here, i), lax.rem(part + j, A) * 2 + share)
        for i in range(H)
        for j in range(A)
        if i < H - 1 or j
    ]
    meet([*others, *here.askew, beside])

    for i, peer in enumerate(across):
        for source, target in slices(wq_in, wq_st, peer[0]):
            send(source, target, wq_s.at[i], wq_r.at[i], peer)
    wq_copies = [
        remote(wq_st.at[peer[0]], wq_st.at[h], wq_s.at[i], wq_r.at[i], peer)
        for i, peer in enumerate(across)
    ]
    gain_copies = [
        send(gain_src, gain_st.at[i], ga_s.at[i], ga_r.at[i], peer) for i, peer in enumerate(across)
    ]
    wo_line = LineGather(lambda block, side: wo_all.at[h, block, side], w_out, here, line[:5])
    loads[0].wait()
    wo_line.start()
    own_copy = local(w_out, wo_all.at[h, part, share], own_s.at[0])
    for copy in loads[1:]:
        copy.wait()
    for place in range(H):
        wm_src[place, :, :F] = w_in[:, place * F : (place + 1) * F]
        wm_src[place, :, F : 2 * F] = w_in[:, (H + place) * F : (H + place + 1) * F]
        wm_src[place, :, 2 * F :] = w_down[:, place * F : (place + 1) * F]
    wm_own[h] = wm_src[h]
    cot_all[h] = cot[...]

    wide = lax.broadcasted_iota(jnp.int32, (R, 128), 1)
    freqs = jnp.exp(
        lax.rem(wide, HEAD_DIM // 2).astype(f32) * (-2.0 / HEAD_DIM * float(np.log(rope_base)))
    )

    def tables(run):
        place = (run * B + b) * R + lax.broadcasted_iota(jnp.int32, (R, 128), 0)

        def one(d, carried):
            low, begin = carried
            return (low + lengths[d], jnp.where(place >= low, low, begin))

        unused, begin = lax.fori_loop(
            0, lengths.shape[0], one, (jnp.int32(0), jnp.zeros((R, 128), jnp.int32))
        )
        angles = (place - begin).astype(f32) * freqs
        cos_all[run] = jnp.cos(angles)
        sin_all[run] = jnp.sin(angles)

    tables(0)
    tables(1)
    wo_line.step(1)
    for copy in wq_copies:
        copy.wait_recv()
    wq_lines = []
    for half in range(2):
        rows = pl.ds(half * (H // 2), H // 2)
        wq_lines.append(
            LineGather(
                lambda block, side, rows=rows: wq_all.at[rows, block * 2 + side],
                wq_st.at[rows],
                here,
                line[5 * half + 5 : 5 * half + 10],
            )
        )
        wq_lines[half].start()
    tok_copies = [
        send(tok_in, tok_all.at[h], tok_s.at[i], tok_r.at[i], peer) for i, peer in enumerate(across)
    ]
    tile = gain_src[...]
    for i, copy in enumerate(gain_copies):
        copy.wait_recv()
        tile += gain_st[i]
    gain_tile[...] = tile
    gain_all[b] = tile
    gain_copies += [
        send(gain_tile, gain_all.at[b], gb_s.at[i], gb_r.at[i], peer)
        for i, peer in enumerate([*along, *here.askew, beside])
    ]
    wo_line.step(2)
    wq_all[:, b] = wq_st[...]
    tables(2)
    wq_lines[0].step(1)
    wo_line.step(3)
    wq_lines[1].step(1)
    wo_line.arrive()
    spread = CornerGather(
        lambda place: wo_all.at[place, :, share],
        lambda place, half: wo_all.at[place, half * (A // 2) : (half + 1) * (A // 2), share],
        wo_all.at[h, :, share],
        here,
        (wx_s, wx_r),
    )
    own_copy.wait()
    spread.start()
    wm_copies = [
        send(wm_src.at[peer[0]], wm_own.at[h], wm_s.at[i], wm_r.at[i], peer)
        for i, peer in enumerate(across)
    ]
    cot_gather = CornerGather(
        lambda place: cot_all.at[place],
        lambda place, half: cot_all.at[place, half * (R // 2) : (half + 1) * (R // 2)],
        cot,
        here,
        (cot_s, cot_r),
    )
    cot_gather.start()
    tables(3)
    for copy in tok_copies:
        copy.wait_recv()

    def norm_run(run, carried):
        hat, unused = standardize(tok_all[run].astype(f32))
        hats[run] = hat
        return carried

    wq_lines[0].step(2)
    lax.fori_loop(0, H // 2, norm_run, 0)
    wq_lines[1].step(2)
    lax.fori_loop(H // 2, H, norm_run, 0)
    for copy in gain_copies[len(across) :]:
        copy.wait_recv()
    for slab in range(W // 128):
        place, first = slab // (hw // 128), slab % (hw // 128) * (128 // D)
        piece = jnp.zeros((8, 128), f32)
        for j in range(128 // D):
            moved = gain_all[first + j]
            if j != place:
                moved = pltpu.roll(moved, (j - place) * D % 128, 1)
            piece = jnp.where(lane // D == j, moved, piece)
        gain_rows[:, slab * 128 : (slab + 1) * 128] = piece
    wq_lines[0].step(3)
    wq_lines[1].step(3)
    wq_lines[0].arrive()
    wq_lines[1].arrive()

    for run in [run for low in range(H // 2) for run in (low, low + H // 2)]:
        rounded = (hats[run] * gain_rows[0:1, :]).astype(bf16)
        projected = jnp.zeros((R, 3 * hw), f32)
        for chunk in range(H):
            block = wq_all[chunk].reshape(B * D, 3 * hw)
            projected += mm(rounded[:, chunk * hw : (chunk + 1) * hw], block)
        cosine, sine = cos_all[run], sin_all[run]
        for slab in range(hw // 128):
            at = slab * 128
            q_runs[run, :, at : at + 128] = turn(projected[:, at : at + 128], cosine, sine)
            key = turn(projected[:, hw + at : hw + at + 128], cosine, sine)
            value = projected[:, 2 * hw + at : 2 * hw + at + 128]
            kv_send[2 * slab, run] = join(key, 0, value, 0).astype(bf16)
            kv_send[2 * slab + 1, run] = join(key, 1, value, 1).astype(bf16)
        for i, peer in enumerate(along):
            send(kv_send.at[here.there[i], run], kv.at[run, b], kv_s.at[i], kv_r.at[i], peer)
        send(kv_send.at[part, run], kv.at[run, b], kc_s.at[0], kc_r.at[0], beside)
        kv[run, b] = kv_send[part, run]
        if run >= H // 2:
            low = run - H // 2
            for a in range(A):
                at = a // 2 * 128
                q_send[a, low] = join(
                    q_runs[low, :, at : at + 128], a % 2, q_runs[run, :, at : at + 128], a % 2
                ).astype(bf16)
            for i, peer in enumerate(along):
                send(q_send.at[here.there[i], low], q_all.at[part, low], q_s.at[i], q_r.at[i], peer)
            q_all[part, low] = q_send[part, low]

    kv_copies = [
        remote(kv_send.at[here.there[i]], kv.at[:, b], kv_s.at[i], kv_r.at[i], peer)
        for i, peer in enumerate(along)
    ]
    kc_copies = [remote(kv_send.at[part], kv.at[:, b], kc_s.at[0], kc_r.at[0], beside)]
    q_copies = [
        remote(q_send.at[here.there[i]], q_all.at[part], q_s.at[i], q_r.at[i], peer)
        for i, peer in enumerate(along)
    ]
    spread.forward()
    cot_gather.forward()

    tiles = H * A // 2
    spot = lax.broadcasted_iota(jnp.int32, (1, 2 * R), 1)
    spot = spot + jnp.where(spot < R, 0, R) + share * R
    for tile in range(tiles):
        place = spot + tile * 4 * R

        def one(d, carried, place=place):
            low, begin, stop = carried
            high = low + lengths[d]
            inside = (place >= low) & (place < high)
            return (high, jnp.where(inside, low, begin), jnp.where(inside, high, stop))

        unused, bounds[tile, 0:1], bounds[tile, 1:2] = lax.fori_loop(
            0, lengths.shape[0], one, (jnp.int32(0), jnp.zeros_like(place), jnp.zeros_like(place))
        )

    def pass_on(i):
        there = wo_all.at[here.places[i], :, share]
        kc_copies.append(send(there, there, wf_s.at[i], wf_r.at[i], beside))

    pass_on(1)
    pass_on(2)
    for i, copy in enumerate(kv_copies):
        copy.wait_recv()
        there = kv.at[:, here.back[i] * 2 + share]
        kc_copies.append(send(there, there, kc_s.at[i + 1], kc_r.at[i + 1], beside))
    wm_lines = []
    for copy in wm_copies:
        copy.wait_recv()
    for half in range(2):
        rows = pl.ds(half * (H // 2), H // 2)
        wm_lines.append(
            LineGather(
                lambda block, side, rows=rows: wm_all.at[rows, block * 2 + side],
                wm_own.at[rows],
                here,
                line[5 * half + 15 : 5 * half + 20],
            )
        )
        wm_lines[half].start()
    wm_all[:, b] = wm_own[...]
    for copy in [*kc_copies, *q_copies]:
        copy.wait_recv()
    spread.arrive()
    last = len(kc_copies)
    pass_on(0)

    steps = H * B * R // KEY_STEP
    at = lax.broadcasted_iota(jnp.int32, (KEY_STEP, 2 * R), 0)
    spans = KEY_STEP // R

    def attend_pair(hh, u):
        results = []
        for side in (0, 1):
            tile = (hh + side * (H // 2)) * (A // 2) + u
            low, high = max(tile - 2, 0), min(tile + 3, steps)
            begin, stop = bounds[tile, 0:1], bounds[tile, 1:2]
            pair = q_all[2 * u : 2 * u + 2, hh].reshape(2 * R, 128)
            query = (halves(pair, side) * HEAD_DIM**-0.5).astype(bf16)

            def keys_at(n):
                return kv[n * spans // B, pl.ds(lax.rem(n * spans, B), spans)].reshape(KEY_STEP, 128)

            def score(n, top, low=low, begin=begin, stop=stop, query=query):
                same = (at >= begin - n * KEY_STEP) & (at < stop - n * KEY_STEP)
                scores = jnp.where(same, mm(keys_at(n), query, NT), neg_large)
                s_scr[n - low] = scores
                return jnp.maximum(top, jnp.max(scores, axis=0, keepdims=True))

            top = lax.fori_loop(low, high, score, jnp.full((1, 2 * R), neg_large, f32))

            def mix(n, carried, low=low, top=top):
                total, acc = carried
                weights = jnp.exp(s_scr[n - low] - top)
                total = total + jnp.sum(weights, axis=0, keepdims=True)
                return (total, acc + mm(keys_at(n), weights.astype(bf16), TN))

            total, acc = lax.fori_loop(
                low, high, mix, (jnp.zeros((1, 2 * R), f32), jnp.zeros((128, 2 * R), f32))
            )
            lse[tile] = top + jnp.log(total)
            results.append(acc[HEAD_DIM:] / total)
        both = jnp.concatenate(results, axis=0).T.astype(bf16)
        op[hh, 2 * u : 2 * u + 2] = both.reshape(2, R, 128)

    def mixed_out_copies(hh):
        mx_in[hh, part] = op[hh, part]
        return [
            send(op.at[hh, here.there[i]], mx_in.at[hh, part], mx_s.at[n], mx_r.at[n], peer)
            for i, peer in enumerate(along)
            for n in [hh * (A - 1) + i]
        ]

    ma_copies, mixed_all = {}, (mixed_early, mixed_late)

    def assemble(hh, copies):
        for copy in copies:
            copy.wait_recv()
        for side in (0, 1):
            run = hh + side * (H // 2)
            slabs = []
            for slab in range(hw // 128):
                left, right = mx_in[hh, 2 * slab].astype(f32), mx_in[hh, 2 * slab + 1].astype(f32)
                slabs.append(join(left, side, right, side))
            mixed = jnp.concatenate(slabs, axis=1).astype(bf16)
            mixed_own[run] = mixed
            for i, peer in enumerate(across):
                ma_copies[i, run] = send(
                    mixed_own.at[run], mixed_all[hh].at[h, side], ma_s.at[i * H + run], ma_r.at[i * H + run], peer
                )

    def project_own(runs):
        for run in runs:
            middle[run] = tok_all[run].astype(f32) + mm(mixed_own[run], wo_rows(h))

    def project_others(runs):
        for i in range(H - 1):
            for run in runs:
                ma_copies[i, run].wait_recv()
        for source in here.places:
            for run in runs:
                mixed = mixed_all[run % (H // 2)][source, run // (H // 2)]
                middle[run] += mm(mixed, wo_rows(source))

    def wo_rows(source):
        return wo_all[source].reshape(hw, W)

    attend_pair(0, 0)
    attend_pair(0, 1)
    mx_copies = mixed_out_copies(0)
    wm_lines[0].step(1)
    attend_pair(1, 0)
    wm_lines[1].step(1)
    assemble(0, mx_copies)
    attend_pair(1, 1)
    mx_late = mixed_out_copies(1)
    wm_lines[0].step(2)
    cot_gather.arrive()
    kc_copies[last].wait_recv()
    early, late = (0, H // 2), (1, H // 2 + 1)
    project_own(early)
    assemble(1, mx_late)
    project_own(late)
    wm_lines[1].step(2)
    project_others(early)
    wm_lines[0].step(3)
    project_others(late)

    def norm_two(run, carried):
        hat, unused = standardize(middle[run])
        normed[run] = (hat * gain_rows[1:2, :]).astype(bf16)
        return carried

    lax.fori_loop(0, H, norm_two, 0)
    wm_lines[1].step(3)
    for item in wm_lines:
        item.arrive()
    down_sum = Reduce(down_term, down_core, None, None, here, [down_core_s, down_core_r, None, None])
    in_sum = Reduce(in_term, in_core, None, None, here, [in_core_s, in_core_r, None, None])
    near, over, far = here.near, here.over, here.far

    def block(chunk):
        return wm_all[chunk].reshape(B * D, 3 * F)

    def part_of(run, i):
        return remote(g2_send.at[i], g2_in.at[i], g2_s.at[i], g2_r.at[i], (run, b))

    def feed_run(i, carried):
        run = run_of(here, i)
        lifted = jnp.zeros((R, 2 * F), f32)
        grad_act = jnp.zeros((R, F), f32)
        for chunk in range(H):
            lanes = slice(chunk * hw, (chunk + 1) * hw)
            weights = block(chunk)
            lifted += mm(normed[run, :, lanes], weights[:, : 2 * F])
            grad_act += mm(cot_all[run, :, lanes], weights[:, 2 * F :])
        gate, up = lifted[:, :F], lifted[:, F:]
        below = 0.5 + 0.5 * lax.erf(gate * (0.5**0.5))
        slope = below + gate * jnp.exp(-0.5 * gate * gate) * ((2.0 * np.pi) ** -0.5)
        act[run] = (gate * below * up).astype(bf16)
        lift[run, :, :F] = (grad_act * up * slope).astype(bf16)
        lift[run, :, F:] = (grad_act * gate * below).astype(bf16)

        for chunk in range(H):
            lanes = slice(chunk * hw, (chunk + 1) * hw)
            g2_own[:, lanes] = mm(lift[run], block(chunk)[:, : 2 * F], NT)

        @pl.when(i < H - 1)
        def _():
            g2_send[i] = g2_own[...].astype(bf16)
            part_of(run, i).start()

        return carried

    lax.fori_loop(0, H, feed_run, 0)

    def down_chunk(chunk, carried):
        lanes = pl.ds(pl.multiple_of(chunk * hw, hw), hw)
        left = cot_all[:, :, lanes].reshape(H * R, hw)
        grads = mm(left, act[...].reshape(H * R, F), TN).astype(bf16)
        down_term[:, :, chunk] = grads.reshape(A, 2, D, F)
        return carried

    lax.fori_loop(0, H, down_chunk, 0)
    down_sum.start()

    def in_chunk(chunk, carried):
        lanes = pl.ds(pl.multiple_of(chunk * hw, hw), hw)
        left = normed[:, :, lanes].reshape(H * R, hw)
        grads = mm(left, lift[...].reshape(H * R, 2 * F), TN).astype(bf16)
        in_term[:, :, chunk] = grads.reshape(A, 2, D, 2 * F)
        return carried

    lax.fori_loop(0, H, in_chunk, 0)
    in_sum.start()
    down_of = down_sum.core_sums()
    for n, there in enumerate((near, over)):
        down_send[n] = down_of(there).astype(bf16)
    pair_copy = send(down_send, down_in, pair_s.at[0], pair_r.at[0], (h, near * 2 + share))

    hat, scale = standardize(middle[h])
    grad = g2_own[...]
    for i in (1, 2, 0):
        part_of(here.places[i], i).wait_recv()
        grad += g2_in[i].astype(f32)
    gain_part[...] = jnp.broadcast_to(jnp.sum(grad * hat, axis=0, keepdims=True), gain_part.shape)
    total = cot_all[h].astype(f32) + norm_back(grad, hat, scale, gain_rows[1:2, :])
    grad_middle[...] = total
    branch = total.astype(bf16)
    branch_own[...] = branch
    gm_copies = []
    for i in range(H):
        place = run_of(here, i)
        mixed_grad = mm(branch, wo_rows(place), NT)
        for a in range(A):
            slab = mixed_grad[:, a // 2 * 128 : a // 2 * 128 + 128]
            gm_send[i, a] = join(slab[: R // 2], a % 2, slab[R // 2 :], a % 2).astype(bf16)
        for j in range(A):
            there = lax.rem(part + j, A)
            if i < H - 1 or j:
                n = i * A + j
                gm_copies.append(
                    send(gm_send.at[i, there], go.at[part, h], gm_s.at[n], gm_r.at[n], (place, there * 2 + share))
                )
            else:
                go[part, h] = gm_send[i, part]

    br_copies = [
        send(branch_own, branch_all.at[h], br_s.at[i], br_r.at[i], peer) for i, peer in enumerate(across)
    ]
    branch_all[h] = branch
    in_of = in_sum.core_sums()
    near_out[0] = in_of(near).astype(bf16)
    near_out[1] = in_of(over).astype(bf16)
    near_copy = send(near_out, from_near, nr_s.at[0], nr_r.at[0], (h, near * 2 + share))
    pair_copy.wait_recv()
    far_out[...] = (down_of(far) + down_in[1].astype(f32)).astype(bf16)

    def out_run(i, carried):
        run = run_of(here, i)
        for chunk in range(H):
            lanes = slice(chunk * hw, (chunk + 1) * hw)
            out_base[:, lanes] = mm(act[run], block(chunk)[:, 2 * F :], NT)

        @pl.when(i < H - 1)
        def _():
            out_parts[i] = out_base[...].astype(bf16)

        return carried

    lax.fori_loop(0, H, out_run, 0)
    out_base[...] += middle[h]
    dkv_sum[...] = jnp.zeros_like(dkv_sum)
    for copy in gm_copies:
        copy.wait_recv()
    far_copy = send(far_out, from_far, nr_s.at[1], nr_r.at[1], (h, far * 2 + share))

    wide_lane = lax.broadcasted_iota(jnp.int32, (2 * R, 128), 1)

    def attend_back_tile(tile):
        run, u = tile // (A // 2), tile % (A // 2)
        side, hh = run // (H // 2), run % (H // 2)
        low, high = max(tile - 2, 0), min(tile + 3, steps)
        begin, stop = bounds[tile, 0:1], bounds[tile, 1:2]
        pair = q_all[2 * u : 2 * u + 2, hh].reshape(2 * R, 128)
        query = (halves(pair, side) * HEAD_DIM**-0.5).astype(bf16)
        pieces = []
        for a in (2 * u, 2 * u + 1):
            piece = go[a, run].astype(f32)
            pieces += [pltpu.roll(piece, HEAD_DIM, 1), piece]
        grad = jnp.where(wide_lane < HEAD_DIM, 0.0, jnp.concatenate(pieces, axis=0))
        mixed = op[hh, 2 * u : 2 * u + 2].reshape(2 * R, 128).astype(f32)
        if not side:
            mixed = pltpu.roll(mixed, HEAD_DIM, 1)
        delta = jnp.sum((grad * mixed).T, axis=0, keepdims=True)
        both = jnp.concatenate([query, grad.astype(bf16)], axis=0)
        logs = lse[tile]

        def step(n, dq):
            keys = kv[n * spans // B, pl.ds(lax.rem(n * spans, B), spans)].reshape(KEY_STEP, 128)
            same = (at >= begin - n * KEY_STEP) & (at < stop - n * KEY_STEP)
            products = mm(keys, both, NT)
            probs = jnp.where(same, jnp.exp(products[:, : 2 * R] - logs), 0.0)
            grad_scores = (probs * (products[:, 2 * R :] - delta)).astype(bf16)
            left = jnp.concatenate([grad_scores, probs.astype(bf16)], axis=1)
            dkv_sum[n] += mm(left, both)
            return dq + mm(keys, grad_scores, TN)

        dq = lax.fori_loop(low, high, step, jnp.zeros((128, 2 * R), f32))
        dq = (dq * HEAD_DIM**-0.5).T
        for k, a in enumerate((2 * u, 2 * u + 1)):
            rows = dq[k * R : (k + 1) * R]
            dq_send[a, run] = join(rows[: R // 2], 0, rows[R // 2 :], 0).astype(bf16)

            @pl.when(part == a)
            def _(a=a):
                dq_in[a, run] = dq_send[a, run]

            @pl.when(part != a)
            def _(a=a):
                n = part * H + run
                remote(
                    dq_send.at[a, run], dq_in.at[part, run], dq_s.at[a * H + run], dq_r.at[n], (h, a * 2 + share)
                ).start()

    def dk_copy(k):
        return remote(dk_send.at[k], dk_in.at[k], dk_s.at[k], dk_r.at[k], beside)

    def keys_done(k):
        for n in range(2):
            first = pl.multiple_of((2 * n + 1 - share) * R, R)
            dk_send[k, n] = dkv_sum[k, pl.ds(first, R), :].astype(bf16)
        dk_copy(k).start()

    def keys_sum(k):
        dk_copy(k).wait_recv()
        run = k * spans // B
        for n in range(2):
            a = k * spans % B // 2 + n
            first = pl.multiple_of((2 * n + share) * R, R)
            summed = dkv_sum[k, pl.ds(first, R), :] + dk_in[k, n].astype(f32)
            dkv_send[a, run] = summed.astype(bf16)

            @pl.when(part == a)
            def _(a=a):
                dkv_in[a, run] = dkv_send[a, run]

            @pl.when(part != a)
            def _(a=a):
                n = part * H + run
                remote(
                    dkv_send.at[a, run], dkv_in.at[part, run], dz_s.at[a * H + run], dz_r.at[n], (h, a * 2 + share)
                ).start()

    out_sum, *qkv_sums = (
        PairReduce(*more[11 * n : 11 * n + 11], term=term, here=here)
        for n, term in enumerate((term_out, *term_qkv))
    )
    gain_scratch, swaps = more[33:41], more[41:]
    term_gain, gain_sum = reducer(gain_scratch, here)
    in_swap, qkv_swap, gain_swap = (Swap(*swaps[4 * n : 4 * n + 4], here) for n in range(3))

    def out_tile(n, carried):
        lanes = pl.ds(pl.multiple_of(n * hw, hw), hw)
        grads = mm(mixed_own[...].reshape(H * R, hw), branch_all[:, :, lanes].reshape(H * R, hw), TN)
        term_out[:, :, :, lanes] = grads.astype(bf16).reshape(A, 2, D, hw)
        return carried

    for tile in range(tiles):
        attend_back_tile(tile)
        if tile >= 2:
            keys_done(tile - 2)
        if tile >= 3:
            keys_sum(tile - 3)
        if tile == 5:
            for copy in br_copies:
                copy.wait_recv()
            o_copies = [
                send(out_parts.at[i], o_in.at[i], o_s.at[i], o_r.at[i], peer)
                for i, peer in enumerate(across)
            ]
            lax.fori_loop(0, W // hw, out_tile, 0)
            out_sum.start()
        if tile == 6:
            near_copy.wait_recv()
            in_send[...] = (in_of(far) + from_near[1].astype(f32)).astype(bf16)
    for k in (tiles - 2, tiles - 1):
        keys_done(k)
    for k in (tiles - 3, tiles - 2, tiles - 1):
        keys_sum(k)
    out_sum.pair()
    last_copy = send(in_send, in_last, nr_s.at[2], nr_r.at[2], (h, far * 2 + share))
    for source in here.back:
        for run in range(H):
            n = source * H + run
            remote(dq_send.at[0, 0], dq_in.at[0, 0], dq_s.at[n], dq_r.at[n], beside).wait_recv()
            remote(dkv_send.at[0, 0], dkv_in.at[0, 0], dz_s.at[n], dz_r.at[n], beside).wait_recv()
    for run in range(H):
        cosine, sine = cos_all[run], sin_all[run]
        for slab in range(hw // 128):
            lanes = slab * 128
            left, right = dq_in[2 * slab, run].astype(f32), dq_in[2 * slab + 1, run].astype(f32)
            both = jnp.concatenate([join(left, 0, right, 0), join(left, 1, right, 1)], axis=0)
            gp[run, :, lanes : lanes + 128] = turn(both, cosine, sine, True).astype(bf16)
            left, right = dkv_in[2 * slab, run].astype(f32), dkv_in[2 * slab + 1, run].astype(f32)
            gp[run, :, hw + lanes : hw + lanes + 128] = turn(
                join(left, 0, right, 0), cosine, sine, True
            ).astype(bf16)
            gp[run, :, 2 * hw + lanes : 2 * hw + lanes + 128] = join(left, 1, right, 1).astype(bf16)

    out_sum.cross()

    def qkv_block(chunk):
        return wq_all[chunk].reshape(B * D, 3 * hw)

    for half, (term, item) in enumerate(zip(term_qkv, qkv_sums)):

        def term_chunk(n, carried, half=half, term=term):
            lanes = pl.ds(pl.multiple_of((half * (H // 2) + n) * hw, hw), hw)
            left = (hats[:, :, lanes] * gain_rows[0:1, lanes]).astype(bf16).reshape(H * R, hw)
            grads = mm(left, gp[...].reshape(H * R, 3 * hw), TN).astype(bf16)
            term[:, :, n] = grads.reshape(A, 2, D, 3 * hw)
            return carried

        lax.fori_loop(0, H // 2, term_chunk, 0)
        item.start()
        if half:
            qkv_sums[0].pair()

    def part_one(run, i):
        return remote(g1_send.at[i], g1_in.at[i], g1_s.at[i], g1_r.at[i], (run, b))

    def one_run(i, carried):
        run = run_of(here, i)
        for chunk in range(H):
            lanes = slice(chunk * hw, (chunk + 1) * hw)
            g1_own[:, lanes] = mm(gp[run], qkv_block(chunk), NT)

        @pl.when(i < H - 1)
        def _():
            g1_send[i] = g1_own[...].astype(bf16)
            part_one(run, i).start()

        return carried

    lax.fori_loop(0, 1, one_run, 0)
    qkv_sums[1].pair()
    lax.fori_loop(1, H, one_run, 0)
    qkv_sums[0].cross()
    far_copy.wait_recv()
    down = down_of(part) + down_in[0].astype(f32) + from_far[...].astype(f32)
    in_swap.out[:, :, 2 * F :] = down.astype(bf16)
    last_copy.wait_recv()
    total = in_of(part) + from_near[0].astype(f32) + in_last[...].astype(f32)
    in_swap.out[:, :, : 2 * F] = total.astype(bf16)
    in_swap.start()
    qkv_sums[1].cross()

    grad = g1_own[...]
    hat, scale = standardize(tok_all[h].astype(f32))
    for i in (1, 2, 0):
        part_one(here.places[i], i).wait_recv()
        grad += g1_in[i].astype(f32)
    row = lax.broadcasted_iota(jnp.int32, (8, W), 0)
    rows = jnp.where(
        row == 0,
        jnp.sum(grad * hat, axis=0, keepdims=True),
        jnp.where(row == 1, gain_part[...], 0.0),
    )
    pick = (
        lax.broadcasted_iota(jnp.int32, (8, 128), 0) == lax.broadcasted_iota(jnp.int32, (8, 128), 1)
    ).astype(bf16)
    for chunk in range(H):
        gain_columns = mm(rows[:, chunk * hw : (chunk + 1) * hw].astype(bf16), pick, TN)
        term_gain[:, :, chunk] = gain_columns.astype(bf16).reshape(A, 2, D, 128)
    gain_sum.start()
    input_grad[...] = grad_middle[...] + norm_back(grad, hat, scale, gain_rows[0:1, :])
    gain_sum.middle()
    result = out_base[...]
    for i, copy in enumerate(o_copies):
        copy.wait_recv()
        result += o_in[i].astype(f32)
    output[...] = result.astype(bf16)
    in_swap.arrive()
    for place in range(H):
        in_grad[:, place * F : (place + 1) * F] = in_swap.landed[place, :, :F].astype(f32)
        in_grad[:, (H + place) * F : (H + place + 1) * F] = in_swap.landed[
            place, :, F : 2 * F
        ].astype(f32)
        down_grad[:, place * F : (place + 1) * F] = in_swap.landed[place, :, 2 * F :].astype(f32)
    for half, item in enumerate(qkv_sums):
        qkv_swap.out[half * (H // 2) : (half + 1) * (H // 2)] = item.close().astype(bf16)
    qkv_swap.start()
    gain_swap.out[...] = gain_sum.close().astype(bf16)
    gain_swap.start()
    out_grad[...] = out_sum.close()
    qkv_swap.arrive()
    for place in range(H):
        for j in range(3):
            qkv_grad[:, j * W + place * hw : j * W + (place + 1) * hw] = qkv_swap.landed[
                place, :, j * hw : (j + 1) * hw
            ].astype(f32)
    gain_swap.arrive()
    total = gain_swap.landed[0].astype(f32)
    for place in range(1, H):
        total += gain_swap.landed[place].astype(f32)
    rows = total.T
    gain_one[...] = rows[0:1, :]
    gain_two[...] = rows[1:2, :]
    for copy in [
        *kc_copies, *q_copies, *wm_copies, *wq_copies, *gain_copies, *tok_copies, *kv_copies,
        *mx_copies, *mx_late, *ma_copies.values(), *gm_copies, pair_copy,
        *br_copies, *o_copies, near_copy, far_copy, last_copy,
    ]:
        copy.wait_send()
    for k in range(tiles):
        dk_copy(k).wait_send()
    for there in here.there:
        for run in range(H):
            n = there * H + run
            remote(dq_send.at[0, 0], dq_in.at[0, 0], dq_s.at[n], dq_r.at[n], beside).wait_send()
            remote(dkv_send.at[0, 0], dkv_in.at[0, 0], dz_s.at[n], dz_r.at[n], beside).wait_send()
    for i in range(H - 1):
        part_of(here.places[i], i).wait_send()
        part_one(here.places[i], i).wait_send()
    for item in (spread, cot_gather, wo_line, *wq_lines, *wm_lines):
        item.finish()
    in_sum.core_finish()
    down_sum.core_finish()
    for item in (out_sum, *qkv_sums, gain_sum, in_swap, qkv_swap, gain_swap):
        item.finish()


def layer(tokens, cotangent, w_qkv, gain_one, gain_two, w_in, w_down, w_out, lengths):
    R, W = tokens.shape
    H, B = lax.axis_size("head"), lax.axis_size("blk")
    A = B // 2
    hw = W // H
    D = w_qkv.shape[0]
    F = w_down.shape[1] // H
    f32, bf16 = jnp.float32, jnp.bfloat16
    shape = jax.ShapeDtypeStruct
    buffer = lambda *sizes: pltpu.VMEM(sizes, bf16)
    wide = lambda *sizes: pltpu.VMEM(sizes, f32)
    outs = [
        shape((R, W), bf16),
        shape((R, W), f32),
        shape((D, 3 * W), f32),
        shape((D, W), f32),
        shape((D, 2 * H * F), f32),
        shape((D, H * F), f32),
        shape((1, D), f32),
        shape((1, D), f32),
    ]
    return pl.pallas_call(
        partial(layer_kernel, H, A),
        in_specs=[*[anywhere()] * 3, *[in_vmem()] * 2, *[anywhere()] * 3, in_smem()],
        out_specs=[in_vmem()] * len(outs),
        out_shape=outs,
        scratch_shapes=[
            buffer(R, W),
            buffer(*w_in.shape),
            buffer(*w_down.shape),
            buffer(*w_out.shape),
            buffer(H, R, W),
            buffer(H, R, W),
            buffer(H, B, D, 3 * hw),
            wide(H, R, 128),
            wide(H, R, 128),
            buffer(H, D, 3 * hw),
            buffer(H, D, 3 * F),
            buffer(H, D, 3 * F),
            buffer(H, A, 2, D, W),
            buffer(H, B, R, 128),
            buffer(A, H, R, 128),
            buffer(A, H // 2, R, 128),
            buffer(A, H // 2, R, 128),
            wide(H, R, hw),
            wide(H, R, W),
            wide(8, 128),
            wide(H - 1, 8, 128),
            wide(8, 128),
            wide(B, 8, 128),
            pltpu.VMEM((H * A // 2, 8, 2 * R), jnp.int32),
            wide(5, KEY_STEP, 2 * R),
            buffer(H // 2, A, R, 128),
            buffer(H // 2, A, R, 128),
            buffer(H, R, hw),
            *[buffer(H, 2, R, hw)] * 2,
            buffer(H, B, D, 3 * F),
            wide(H, R, W),
            buffer(H, R, W),
            buffer(H, R, F),
            buffer(H, R, 2 * F),
            buffer(H - 1, R, W),
            buffer(H - 1, R, W),
            wide(R, W),
            buffer(H, A, R // 2, 128),
            buffer(A, 2, H, D, 2 * F),
            buffer(A, H, D, 2 * F),
            buffer(A, 2, H, D, F),
            buffer(A, H, D, F),
            buffer(2, H, D, F),
            buffer(2, H, D, F),
            wide(R, W),
            buffer(H - 1, R, W),
            wide(R, W),
            buffer(2, H, D, 2 * F),
            buffer(H, D, F),
            wide(H * A // 2, 1, 2 * R),
            buffer(A, H, R // 2, 128),
            wide(8, W),
            wide(8, W),
            buffer(R, W),
            buffer(H, R, W),
            buffer(H - 1, R, W),
            buffer(2, H, D, 2 * F),
            buffer(H, D, F),
            *[buffer(H, D, 2 * F)] * 2,
            wide(H * B * R // KEY_STEP, KEY_STEP, 128),
            *[buffer(A, H, R // 2, 128)] * 2,
            *[buffer(H * B * R // KEY_STEP, 2, R, 128)] * 2,
            *[buffer(A, H, R, 128)] * 2,
            buffer(H, R, 3 * hw),
            *[buffer(H - 1, R, W)] * 2,
            wide(R, W),
            buffer(A, 2, D, W),
            *[buffer(A, 2, H // 2, D, 3 * hw)] * 2,
            dma(8),
            dma(1),
            *[dma(H - 1)] * 8,
            *[dma(B - 1)] * 2,
            *[dma(4)] * 2,
            *[dma(H - 1)] * 2,
            *[dma(4)] * 2,
            *[dma(A - 1)] * 4,
            *[dma(A)] * 2,
            *[dma((A - 1) * (H // 2))] * 2,
            *[dma((H - 1) * H)] * 2,
            *[dma(H - 1)] * 2,
            *[dma(H * A)] * 2,
            *[dma(1)] * 6,
            *[dma(H - 1)] * 6,
            *[dma(4)] * 2,
            *[dma(A * H)] * 4,
            *[dma(H * B * R // KEY_STEP)] * 2,
            *line_sems(A) * 5,
            *pair_scratch(A, (D, W)),
            *pair_scratch(A, (H // 2, D, 3 * hw)),
            *pair_scratch(A, (H // 2, D, 3 * hw)),
            *reduce_scratch(A, (H, D, 128)),
            *swap_scratch(H, (D, 3 * F)),
            *swap_scratch(H, (D, 3 * hw)),
            *swap_scratch(H, (D, 128)),
        ],
        compiler_params=params(0),
        cost_estimate=pl.CostEstimate(flops=10**10, bytes_accessed=10**7, transcendentals=10**6),
        name="layer",
    )(tokens, cotangent, w_qkv, gain_one, gain_two, w_in, w_down, w_out, lengths)


def per_device_split(
    tokens, attn_gain, w_qkv, w_attn_out, mlp_gain, w_in, w_mlp_out, doc_lengths, cotangent
):
    output, input_grad, qkv_grad, out_grad, in_grad, down_grad, gain_one, gain_two = deliver(
        *layer(
            tokens, cotangent, w_qkv, attn_gain[None], mlp_gain[None], w_in, w_mlp_out.T, w_attn_out, doc_lengths
        )
    )
    return (
        output,
        input_grad,
        gain_one[0],
        qkv_grad,
        out_grad,
        gain_two[0],
        in_grad,
        down_grad.T,
    )


def per_device(tokens, attn_gain, w_qkv, *rest):
    heads, blocks = lax.axis_size("head"), lax.axis_size("blk")
    fits = (
        heads == 4
        and blocks == 2 * (tokens.shape[1] // HEAD_DIM // heads) == 8
        and w_qkv.shape[0] * heads == 128
        and tokens.shape[0] == 128
    )
    chosen = per_device_split if fits else per_device_general
    return chosen(tokens, attn_gain, w_qkv, *rest)


def solution(mesh):
    placed = (
        P(("head", "blk"), None),
        P(("head", "blk")),
        P(("head", "blk"), None),
        P(("head", "blk"), None),
        P(("head", "blk")),
        P(("head", "blk"), None),
        P(None, ("head", "blk")),
        P(),
        P(("head", "blk"), None),
    )
    return jax.shard_map(
        per_device,
        mesh=mesh,
        in_specs=placed,
        out_specs=(
            P(("head", "blk"), None),
            P(("head", "blk"), None),
            P(("head", "blk")),
            P(("head", "blk"), None),
            P(("head", "blk"), None),
            P(("head", "blk")),
            P(("head", "blk"), None),
            P(None, ("head", "blk")),
        ),
        check_vma=False,
    )
```

```python
from functools import partial

import jax
import jax.numpy as jnp
import numpy as np
from jax import lax
from jax.experimental import pallas as pl
from jax.experimental.pallas import tpu as pltpu
from jax.sharding import PartitionSpec as P

HEAD_DIM = 64


norm_eps = 1e-05
rope_base = 160000.0
neg_large = -1e30


def from_behind(value, axis, by):
    devices = lax.axis_size(axis)
    return lax.ppermute(value, axis, [(i, (i + by) % devices) for i in range(devices)])


def layer_norm(values, gain):
    center = values - jnp.mean(values, axis=-1, keepdims=True)
    spread = jnp.mean(center * center, axis=-1, keepdims=True)
    return center * lax.rsqrt(spread + norm_eps) * gain


def rope_tables(places, head_size):
    half = head_size // 2
    freqs = rope_base ** (-(jnp.arange(half, dtype=jnp.float32) * 2.0) / head_size)
    angles = places.astype(jnp.float32)[:, None] * freqs[None, :]
    angles = jnp.concatenate([angles, angles], axis=1)
    return (jnp.cos(angles), jnp.sin(angles))


def rotate(values, cosine, sine):
    count = values.shape[0]
    head_size = cosine.shape[1]
    half = head_size // 2
    split = values.reshape(count, -1, head_size)
    turned = jnp.concatenate([-split[..., half:], split[..., :half]], axis=-1)
    return (split * cosine[:, None, :] + turned * sine[:, None, :]).reshape(count, -1)


def rotate_pair(query, keys, cosine, sine):
    return (rotate(query, cosine, sine), rotate(keys, cosine, sine))


def doc_numbers(places, ends, lengths):
    passed = places[:, None] >= ends[None, :]
    numbers = jnp.sum(passed.astype(jnp.int32), axis=1)
    offset = jnp.sum(jnp.where(passed, lengths[None, :], 0), axis=1)
    return (numbers, places - offset)


def gelu_gate(lifted):
    half = lifted.shape[1] // 2
    return jax.nn.gelu(lifted[:, :half], approximate=False) * lifted[:, half:]


def tile_scores(query, keys):
    heads = query.shape[1] // HEAD_DIM
    query_split = query.reshape(query.shape[0], heads, HEAD_DIM)
    key_split = keys.reshape(keys.shape[0], heads, HEAD_DIM)
    return jnp.einsum(
        "qhd,khd->hqk", query_split, key_split, preferred_element_type=jnp.float32
    ) * HEAD_DIM ** (-0.5)


def unchanged(state):
    return state


def forward_tile(state, query, keys, values, mask):
    top, total, running = state
    count = query.shape[0]
    heads = top.shape[0]
    scores = tile_scores(query, keys)
    filled = jnp.where(mask[None], scores, neg_large)
    new_top = jnp.maximum(top, jnp.max(filled, axis=-1))
    weights = jnp.where(mask[None], jnp.exp(scores - new_top[:, :, None]), 0.0)
    factor = jnp.exp(top - new_top)
    new_total = total * factor + jnp.sum(weights, axis=-1)
    mixed = jnp.einsum(
        "hqk,khd->qhd",
        weights.astype(jnp.bfloat16),
        values.reshape(-1, heads, HEAD_DIM),
        preferred_element_type=jnp.float32,
    )
    new_running = running.reshape(count, heads, HEAD_DIM) * factor.T[:, :, None] + mixed
    return (new_top, new_total, new_running.reshape(count, heads * HEAD_DIM))


def backward_tile(carry, query, keys, values, mask, norm_log, grad_out, delta):
    query_grad, run_grads = carry
    count = query.shape[0]
    columns = keys.shape[0]
    heads = norm_log.shape[0]
    scores = tile_scores(query, keys)
    probs = jnp.where(mask[None], jnp.exp(scores - norm_log[:, :, None]), 0.0)
    grad_split = grad_out.reshape(count, heads, HEAD_DIM)
    value_split = values.reshape(columns, heads, HEAD_DIM)
    grad_values = jnp.einsum(
        "hqk,qhd->khd", probs.astype(jnp.bfloat16), grad_split, preferred_element_type=jnp.float32
    )
    grad_probs = jnp.einsum(
        "qhd,khd->hqk", grad_split, value_split, preferred_element_type=jnp.float32
    )
    grad_scores = (probs * (grad_probs - delta[:, :, None])).astype(jnp.bfloat16)
    grad_query = jnp.einsum(
        "hqk,khd->qhd",
        grad_scores,
        keys.reshape(columns, heads, HEAD_DIM),
        preferred_element_type=jnp.float32,
    ) * HEAD_DIM ** (-0.5)
    grad_keys = jnp.einsum(
        "hqk,qhd->khd",
        grad_scores,
        query.reshape(count, heads, HEAD_DIM),
        preferred_element_type=jnp.float32,
    ) * HEAD_DIM ** (-0.5)
    added = jnp.stack([grad_keys.reshape(columns, -1), grad_values.reshape(columns, -1)])
    return (query_grad + grad_query.reshape(count, -1), run_grads + added)


def per_device_general(
    tokens, attn_gain, w_qkv, w_attn_out, mlp_gain, w_in, w_mlp_out, doc_lengths, cotangent
):
    own_rows = tokens.shape[0]
    width = tokens.shape[1]
    head_count = lax.axis_size("head")
    cycle_count = lax.axis_size("blk")
    head_place = lax.axis_index("head")
    cycle_place = lax.axis_index("blk")
    group_rows = head_count * own_rows
    block_runs = min(head_count, max(1, 512 // own_rows))
    block_count = head_count // block_runs
    block_rows = block_runs * own_rows
    doc_ends = jnp.cumsum(doc_lengths)
    counter = jnp.arange(own_rows, dtype=jnp.int32)
    own_places = (head_place * cycle_count + cycle_place) * own_rows + counter
    unused_docs, own_positions = doc_numbers(own_places, doc_ends, doc_lengths)
    cosine, sine = rope_tables(own_positions, HEAD_DIM)
    run_numbers = jnp.arange(head_count, dtype=jnp.int32)
    query_places = (
        (run_numbers[:, None] * cycle_count + cycle_place) * own_rows + counter[None, :]
    ).reshape(group_rows)
    query_docs, unused_positions = doc_numbers(query_places, doc_ends, doc_lengths)
    params = (
        lax.all_gather(attn_gain, ("head", "blk"), axis=0, tiled=True),
        lax.all_gather(w_qkv, ("head", "blk"), axis=0, tiled=True),
        lax.all_gather(w_attn_out, ("head", "blk"), axis=0, tiled=True),
        lax.all_gather(mlp_gain, ("head", "blk"), axis=0, tiled=True),
        lax.all_gather(w_in, ("head", "blk"), axis=0, tiled=True),
        lax.all_gather(w_mlp_out, ("head", "blk"), axis=1, tiled=True),
    )
    gain_one, full_qkv, full_attn_out, gain_two, full_in, full_mlp_out = params
    inputs = tokens.astype(jnp.float32)
    normed_one, norm_one_pull = jax.vjp(layer_norm, inputs, gain_one.astype(jnp.float32))
    normed_low = normed_one.astype(jnp.bfloat16)
    projected = jnp.dot(normed_low, full_qkv, preferred_element_type=jnp.float32)
    turned, rope_pull = jax.vjp(
        partial(rotate_pair, cosine=cosine, sine=sine),
        projected[:, :width],
        projected[:, width : 2 * width],
    )
    stacked = jnp.stack(
        [
            turned[0].astype(jnp.bfloat16),
            turned[1].astype(jnp.bfloat16),
            projected[:, 2 * width :].astype(jnp.bfloat16),
        ]
    )
    regrouped = lax.all_to_all(stacked, "head", split_axis=2, concat_axis=1, tiled=True)
    query_heads = regrouped[0]
    key_heads = regrouped[1]
    value_heads = regrouped[2]
    head_width = query_heads.shape[1]
    heads_here = head_width // HEAD_DIM

    def key_docs_at(first):
        places = (
            first % group_rows // own_rows * cycle_count + first // group_rows
        ) * own_rows + counter
        found, unused = doc_numbers(places, doc_ends, doc_lengths)
        return found

    def block_live(block, key_docs):
        block_docs = query_docs[block * block_rows : (block + 1) * block_rows]
        live = jnp.maximum(jnp.min(block_docs), jnp.min(key_docs)) <= jnp.minimum(
            jnp.max(block_docs), jnp.max(key_docs)
        )
        return (block_docs[:, None] == key_docs[None, :], live)

    def fold_forward(state, piece):
        key_part, value_part = piece

        def fold_one_run(number, carried):
            first = number * own_rows
            key_docs = key_docs_at(first)
            keys = lax.dynamic_slice_in_dim(key_part, number * own_rows, own_rows, 0)
            values = lax.dynamic_slice_in_dim(value_part, number * own_rows, own_rows, 0)
            updated = []
            for block in range(block_count):
                mask, live = block_live(block, key_docs)
                query = query_heads[block * block_rows : (block + 1) * block_rows]
                advance = partial(forward_tile, query=query, keys=keys, values=values, mask=mask)
                updated.append(lax.cond(live, advance, unchanged, carried[block]))
            return tuple(updated)

        return lax.fori_loop(0, key_part.shape[0] // own_rows, fold_one_run, state)

    def fresh_state():
        return tuple(
            (
                (
                    jnp.full((heads_here, block_rows), neg_large, jnp.float32),
                    jnp.zeros((heads_here, block_rows), jnp.float32),
                    jnp.zeros((block_rows, head_width), jnp.float32),
                )
                for block in range(block_count)
            )
        )

    def finish(state):
        outputs = []
        logs = []
        for top, total, running in state:
            scaled = running.reshape(block_rows, heads_here, HEAD_DIM) / total.T[:, :, None]
            outputs.append(scaled.reshape(block_rows, head_width))
            logs.append(top + jnp.log(total))
        return (
            jnp.concatenate(outputs, axis=0).astype(jnp.bfloat16),
            jnp.concatenate(logs, axis=1),
        )

    state = fold_forward(
        fresh_state(),
        (
            lax.all_gather(key_heads, "blk", axis=0, tiled=True),
            lax.all_gather(value_heads, "blk", axis=0, tiled=True),
        ),
    )
    out_heads, norm_log = finish(state)
    out_tokens = lax.all_to_all(out_heads, "head", split_axis=0, concat_axis=1, tiled=True)
    middle = inputs + jnp.dot(out_tokens, full_attn_out, preferred_element_type=jnp.float32)
    normed_two, norm_two_pull = jax.vjp(layer_norm, middle, gain_two.astype(jnp.float32))
    normed_two_low = normed_two.astype(jnp.bfloat16)
    lifted = jnp.dot(normed_two_low, full_in, preferred_element_type=jnp.float32)
    activated, geglu_pull = jax.vjp(gelu_gate, lifted)
    activated_low = activated.astype(jnp.bfloat16)
    output = (
        middle + jnp.dot(activated_low, full_mlp_out, preferred_element_type=jnp.float32)
    ).astype(jnp.bfloat16)
    params = (
        lax.all_gather(attn_gain, ("head", "blk"), axis=0, tiled=True),
        lax.all_gather(w_qkv, ("head", "blk"), axis=0, tiled=True),
        lax.all_gather(w_attn_out, ("head", "blk"), axis=0, tiled=True),
        lax.all_gather(mlp_gain, ("head", "blk"), axis=0, tiled=True),
        lax.all_gather(w_in, ("head", "blk"), axis=0, tiled=True),
        lax.all_gather(w_mlp_out, ("head", "blk"), axis=1, tiled=True),
    )
    gain_one, full_qkv, full_attn_out, gain_two, full_in, full_mlp_out = params
    grad_act = jnp.einsum("td,fd->tf", cotangent, full_mlp_out, preferred_element_type=jnp.float32)
    grad_lifted = geglu_pull(grad_act)[0].astype(jnp.bfloat16)
    grad_normed_two = jnp.einsum(
        "tf,df->td", grad_lifted, full_in, preferred_element_type=jnp.float32
    )
    grad_middle_part, grad_gain_two = norm_two_pull(grad_normed_two)
    grad_middle = cotangent.astype(jnp.float32) + grad_middle_part
    grad_branch = grad_middle.astype(jnp.bfloat16)
    grad_mixed = jnp.einsum(
        "te,de->td", grad_branch, full_attn_out, preferred_element_type=jnp.float32
    ).astype(jnp.bfloat16)
    grad_heads = lax.all_to_all(grad_mixed, "head", split_axis=1, concat_axis=0, tiled=True)
    state = fold_forward(
        fresh_state(),
        (
            lax.all_gather(key_heads, "blk", axis=0, tiled=True),
            lax.all_gather(value_heads, "blk", axis=0, tiled=True),
        ),
    )
    out_heads, norm_log = finish(state)
    delta = jnp.einsum(
        "qhd,qhd->hq",
        grad_heads.reshape(group_rows, heads_here, HEAD_DIM).astype(jnp.float32),
        out_heads.reshape(group_rows, heads_here, HEAD_DIM).astype(jnp.float32),
    )

    def piece_backward(query_grads, key_part, value_part, start):
        piece_rows = key_part.shape[0]

        def piece_one_run(number, carried):
            query_now, piece_grads = carried
            first = start + number * own_rows
            key_docs = key_docs_at(first)
            keys = lax.dynamic_slice_in_dim(key_part, number * own_rows, own_rows, 0)
            values = lax.dynamic_slice_in_dim(value_part, number * own_rows, own_rows, 0)
            run_grads = jnp.zeros((2, own_rows, head_width), jnp.float32)
            updated = []
            for block in range(block_count):
                mask, live = block_live(block, key_docs)
                lower = block * block_rows
                upper = (block + 1) * block_rows
                advance = partial(
                    backward_tile,
                    query=query_heads[lower:upper],
                    keys=keys,
                    values=values,
                    mask=mask,
                    norm_log=norm_log[:, lower:upper],
                    grad_out=grad_heads[lower:upper],
                    delta=delta[:, lower:upper],
                )
                new_query, run_grads = lax.cond(
                    live, advance, unchanged, (query_now[block], run_grads)
                )
                updated.append(new_query)
            piece_grads = lax.dynamic_update_slice_in_dim(
                piece_grads, run_grads, number * own_rows, 1
            )
            return (tuple(updated), piece_grads)

        return lax.fori_loop(
            0,
            piece_rows // own_rows,
            piece_one_run,
            (query_grads, jnp.zeros((2, piece_rows, head_width), jnp.float32)),
        )

    start_query = tuple(
        (jnp.zeros((block_rows, head_width), jnp.float32) for block in range(block_count))
    )

    def cycle_step(step, carried):
        query_now, blocks, travelling = carried
        owner = (cycle_place - step) % cycle_count
        query_now, piece_grads = piece_backward(query_now, blocks[0], blocks[1], owner * group_rows)
        travelling = travelling + piece_grads
        blocks = from_behind(blocks, "blk", 1)
        travelling = from_behind(travelling.astype(jnp.bfloat16), "blk", 1).astype(travelling.dtype)
        return (query_now, blocks, travelling)

    start_cycle = (
        start_query,
        jnp.stack([key_heads, value_heads]),
        jnp.zeros((2, group_rows, head_width), jnp.float32),
    )
    query_grads, unused_blocks, own_grads = lax.fori_loop(0, cycle_count, cycle_step, start_cycle)
    grad_stack = jnp.stack(
        [
            jnp.concatenate(query_grads, axis=0).astype(jnp.bfloat16),
            own_grads[0].astype(jnp.bfloat16),
            own_grads[1].astype(jnp.bfloat16),
        ]
    )
    back_tokens = lax.all_to_all(grad_stack, "head", split_axis=1, concat_axis=2, tiled=True)
    grad_query, grad_keys = rope_pull(
        (back_tokens[0].astype(jnp.float32), back_tokens[1].astype(jnp.float32))
    )
    grad_projected = jnp.concatenate(
        [grad_query, grad_keys, back_tokens[2].astype(jnp.float32)], axis=1
    ).astype(jnp.bfloat16)
    grad_normed_one = jnp.einsum(
        "te,de->td", grad_projected, full_qkv, preferred_element_type=jnp.float32
    )
    grad_input_part, grad_gain_one = norm_one_pull(grad_normed_one)
    input_grad = grad_middle + grad_input_part

    def columns(source):
        return source

    term_qkv = jnp.einsum(
        "td,te->de", columns(normed_low), grad_projected, preferred_element_type=jnp.float32
    )
    term_out = jnp.einsum(
        "td,te->de", columns(out_tokens), grad_branch, preferred_element_type=jnp.float32
    )
    term_in = jnp.einsum(
        "td,tf->df", columns(normed_two_low), grad_lifted, preferred_element_type=jnp.float32
    )
    term_down = jnp.einsum(
        "td,tf->df", columns(cotangent), activated_low, preferred_element_type=jnp.float32
    )
    sums = lax.psum_scatter(
        jnp.concatenate([term_qkv, term_out, term_in, term_down], axis=1),
        ("head", "blk"),
        scatter_dimension=0,
        tiled=True,
    )
    ff_width = full_mlp_out.shape[0]
    qkv_grad = sums[:, : 3 * width]
    attn_out_grad = sums[:, 3 * width : 4 * width]
    in_grad = sums[:, 4 * width : 4 * width + 2 * ff_width]
    down_grad = sums[:, 4 * width + 2 * ff_width :].T
    gain_sums = lax.psum_scatter(
        jnp.stack([grad_gain_one, grad_gain_two]), ("head", "blk"), scatter_dimension=1, tiled=True
    )
    return (
        output,
        input_grad,
        gain_sums[0],
        qkv_grad,
        attn_out_grad,
        gain_sums[1],
        in_grad,
        down_grad,
    )


VMEM = 62 * 2**20
MESH = pl.DeviceIdType.MESH
KEY_STEP = 512
KEY_ALIGN = 256
NN = (((1,), (0,)), ((), ()))
NT = (((1,), (1,)), ((), ()))
TN = (((0,), (0,)), ((), ()))


def mm(left, right, dims=NN):
    return lax.dot_general(left, right, dims, preferred_element_type=jnp.float32)


def params(collective_id=None):
    if collective_id is None:
        return pltpu.CompilerParams(vmem_limit_bytes=VMEM)
    return pltpu.CompilerParams(
        collective_id=collective_id, has_side_effects=True, vmem_limit_bytes=VMEM
    )


def in_vmem():
    return pl.BlockSpec(memory_space=pltpu.VMEM)


def anywhere():
    return pl.BlockSpec(memory_space=pl.ANY)


def in_smem():
    return pl.BlockSpec(memory_space=pltpu.SMEM)


def dma(*counts):
    return pltpu.SemaphoreType.DMA(counts)


def halves(packed, side):
    wide = packed.astype(jnp.float32)
    if side:
        wide = pltpu.roll(wide, HEAD_DIM, 1)
    lane = lax.broadcasted_iota(jnp.int32, wide.shape, 1)
    return jnp.where(lane < HEAD_DIM, wide, 0.0)


def tile_span(lengths, side, R, T):
    hh, u = pl.program_id(0), pl.program_id(1)
    runs, parts = 2 * pl.num_programs(0), 2 * pl.num_programs(1)
    share = lax.rem(lax.axis_index("blk"), 2)
    first = (((hh + side * (runs // 2)) * parts + 2 * u) * 2 + share) * R
    last = first + 3 * R - 1
    lane = lax.broadcasted_iota(jnp.int32, (1, 2 * R), 1)
    place = first + lane + jnp.where(lane < R, 0, R)

    def one(d, carried):
        low, begin, stop, start, end = carried
        high = low + lengths[d]
        inside = (place >= low) & (place < high)
        return (
            high,
            jnp.where(inside, low, begin),
            jnp.where(inside, high, stop),
            jnp.where((first >= low) & (first < high), low, start),
            jnp.where((last >= low) & (last < high), high, end),
        )

    zero = jnp.int32(0)
    unused, begin, stop, start, end = lax.fori_loop(
        0,
        lengths.shape[0],
        one,
        (zero, jnp.zeros_like(place), jnp.zeros_like(place), zero, zero),
        unroll=True,
    )
    start = start // KEY_ALIGN
    steps = (end - start * KEY_ALIGN + KEY_STEP - 1) // KEY_STEP
    start = jnp.minimum(start, T // KEY_ALIGN - steps * (KEY_STEP // KEY_ALIGN))
    return (begin, stop, start, steps)


def attend_kernel(lengths, qp, kv, op, lse, s_scr):
    pairs = qp.shape[0] * qp.shape[2]
    T = kv.shape[0]
    half_runs = pl.num_programs(0)
    hh, u = pl.program_id(0), pl.program_id(1)
    at = lax.broadcasted_iota(jnp.int32, (KEY_STEP, pairs), 0)
    results = []
    for side in (0, 1):
        tile = (hh + side * half_runs) * pl.num_programs(1) + u
        begin, stop, start, steps = tile_span(lengths, side, pairs // 2, T)
        query = (halves(qp[...].reshape(pairs, 2 * HEAD_DIM), side) * HEAD_DIM**-0.5).astype(
            jnp.bfloat16
        )

        def keys_at(n):
            first = pl.multiple_of(start * KEY_ALIGN + n * KEY_STEP, KEY_ALIGN)
            return (first, kv[pl.ds(first, KEY_STEP), :])

        def score(n, top):
            first, keys = keys_at(n)
            same = (at >= begin - first) & (at < stop - first)
            scores = jnp.where(same, mm(keys, query, NT), neg_large)
            s_scr[n] = scores
            return jnp.maximum(top, jnp.max(scores, axis=0, keepdims=True))

        top = lax.fori_loop(0, steps, score, jnp.full((1, pairs), neg_large, jnp.float32))

        def mix(n, carried):
            total, acc = carried
            unused, keys = keys_at(n)
            weights = jnp.exp(s_scr[n] - top)
            total = total + jnp.sum(weights, axis=0, keepdims=True)
            return (total, acc + mm(keys, weights.astype(jnp.bfloat16), TN))

        total, acc = lax.fori_loop(
            0,
            steps,
            mix,
            (jnp.zeros((1, pairs), jnp.float32), jnp.zeros((2 * HEAD_DIM, pairs), jnp.float32)),
        )
        lse[tile] = top + jnp.log(total)
        results.append(acc[HEAD_DIM:] / total)
    both = jnp.concatenate(results, axis=0).T
    op[...] = both.astype(jnp.bfloat16).reshape(op.shape)


def attend(lengths, qp, kv):
    parts, half_runs, rows, lanes = qp.shape
    tiles = half_runs * parts
    piece = pl.BlockSpec((2, 1, rows, lanes), lambda i, j, s: (j, i, 0, 0))
    return pl.pallas_call(
        attend_kernel,
        grid_spec=pltpu.PrefetchScalarGridSpec(
            num_scalar_prefetch=1,
            grid=(half_runs, parts // 2),
            in_specs=[piece, in_vmem()],
            out_specs=[piece, in_vmem()],
            scratch_shapes=[pltpu.VMEM((kv.shape[0] // KEY_STEP, KEY_STEP, 2 * rows), jnp.float32)],
        ),
        out_shape=[
            jax.ShapeDtypeStruct(qp.shape, jnp.bfloat16),
            jax.ShapeDtypeStruct((tiles, 1, 2 * rows), jnp.float32),
        ],
        compiler_params=params(),
        cost_estimate=pl.CostEstimate(
            flops=10**9, bytes_accessed=50 * 10**6, transcendentals=10**6
        ),
        name="attend",
    )(lengths, qp, kv)


def attend_back_kernel(
    lengths, qp, gp, op, lse, kv, dqp, dkv, acc_scr
):
    pairs = qp.shape[0] * qp.shape[2]
    T = kv.shape[0]
    half_runs = pl.num_programs(0)
    hh, u = pl.program_id(0), pl.program_id(1)
    begins = (hh == 0) & (u == 0)
    ends = (hh == half_runs - 1) & (u == pl.num_programs(1) - 1)
    @pl.when(begins)
    def _():
        acc_scr[...] = jnp.zeros_like(acc_scr)

    at = lax.broadcasted_iota(jnp.int32, (KEY_STEP, pairs), 0)
    lane = lax.broadcasted_iota(jnp.int32, (pairs, 2 * HEAD_DIM), 1)
    flat = (pairs, 2 * HEAD_DIM)
    results = []
    for side in (0, 1):
        tile = (hh + side * half_runs) * pl.num_programs(1) + u
        begin, stop, start, steps = tile_span(lengths, side, pairs // 2, T)
        query = (halves(qp[...].reshape(flat), side) * HEAD_DIM**-0.5).astype(jnp.bfloat16)
        pieces = []
        for n in range(2):
            piece = gp[n, hh + side * half_runs].astype(jnp.float32)
            pieces += [pltpu.roll(piece, HEAD_DIM, 1), piece]
        grad = jnp.where(lane < HEAD_DIM, 0.0, jnp.concatenate(pieces, axis=0))
        mixed = op[...].reshape(flat).astype(jnp.float32)
        if not side:
            mixed = pltpu.roll(mixed, HEAD_DIM, 1)
        delta = jnp.sum((grad * mixed).T, axis=0, keepdims=True)
        both = jnp.concatenate([query, grad.astype(jnp.bfloat16)], axis=0)
        logs = lse[tile]

        def step(n, dq):
            first = pl.multiple_of(start * KEY_ALIGN + n * KEY_STEP, KEY_ALIGN)
            rows = pl.ds(first, KEY_STEP)
            keys = kv[rows, :]
            same = (at >= begin - first) & (at < stop - first)
            products = mm(keys, both, NT)
            probs = jnp.where(same, jnp.exp(products[:, :pairs] - logs), 0.0)
            grad_scores = (probs * (products[:, pairs:] - delta)).astype(jnp.bfloat16)
            left = jnp.concatenate([grad_scores, probs.astype(jnp.bfloat16)], axis=1)
            acc_scr[rows, :] += mm(left, both)
            return dq + mm(keys, grad_scores, TN)

        dq = lax.fori_loop(0, steps, step, jnp.zeros((2 * HEAD_DIM, pairs), jnp.float32))
        results.append(dq[:HEAD_DIM] * HEAD_DIM**-0.5)
    dqp[...] = jnp.concatenate(results, axis=0).T.astype(jnp.bfloat16).reshape(dqp.shape)

    @pl.when(ends)
    def _():
        dkv[...] = acc_scr[...].astype(dkv.dtype)


def attend_back(lengths, qp, gp, op, lse, kv):
    parts, half_runs, rows, lanes = qp.shape
    piece = pl.BlockSpec((2, 1, rows, lanes), lambda i, j, s: (j, i, 0, 0))
    grads = pl.BlockSpec((2, 2 * half_runs, rows // 2, lanes), lambda i, j, s: (j, 0, 0, 0))
    return pl.pallas_call(
        attend_back_kernel,
        grid_spec=pltpu.PrefetchScalarGridSpec(
            num_scalar_prefetch=1,
            grid=(half_runs, parts // 2),
            in_specs=[piece, grads, piece, *[in_vmem()] * 2],
            out_specs=[piece, in_vmem()],
            scratch_shapes=[pltpu.VMEM(kv.shape, jnp.float32)],
        ),
        out_shape=[
            jax.ShapeDtypeStruct(qp.shape, jnp.bfloat16),
            jax.ShapeDtypeStruct(kv.shape, jnp.bfloat16),
        ],
        compiler_params=params(),
        cost_estimate=pl.CostEstimate(
            flops=3 * 10**9, bytes_accessed=60 * 10**6, transcendentals=10**6
        ),
        name="attend_back",
    )(lengths, qp, gp, op, lse, kv)


def deliver_kernel(count, *refs):
    sources, targets, held = refs[:count], refs[count : 2 * count], refs[2 * count : 3 * count]
    into, out = refs[3 * count :]
    first = [pltpu.make_async_copy(sources[n], held[n], into.at[n]) for n in range(count)]
    second = [pltpu.make_async_copy(held[n], targets[n], out.at[n]) for n in range(count)]
    for copy in first:
        copy.start()
    for arrived, leaving in zip(first, second):
        arrived.wait()
        leaving.start()
    for copy in second:
        copy.wait()


def deliver(*arrays):
    count = len(arrays)
    return pl.pallas_call(
        partial(deliver_kernel, count),
        in_specs=[anywhere()] * count,
        out_specs=[anywhere()] * count,
        out_shape=[jax.ShapeDtypeStruct(a.shape, a.dtype) for a in arrays],
        scratch_shapes=[*[pltpu.VMEM(a.shape, a.dtype) for a in arrays], dma(count), dma(count)],
        compiler_params=params(),
        name="deliver",
    )(*arrays)


def meet(peers):
    barrier = pltpu.get_barrier_semaphore()
    for peer in peers:
        pl.semaphore_signal(barrier, inc=1, device_id=peer, device_id_type=MESH)
    pl.semaphore_wait(barrier, len(peers))


def remote(source, target, send_sem, recv_sem, peer):
    return pltpu.make_async_remote_copy(
        src_ref=source,
        dst_ref=target,
        send_sem=send_sem,
        recv_sem=recv_sem,
        device_id=peer,
        device_id_type=MESH,
    )


def send(source, target, send_sem, recv_sem, peer):
    copy = remote(source, target, send_sem, recv_sem, peer)
    copy.start()
    return copy


class Place:
    def __init__(self, parts):
        h, b = lax.axis_index("head"), lax.axis_index("blk")
        self.h, self.b, self.parts = h, b, parts
        self.part, self.share = b // 2, lax.rem(b, 2)
        x, y = lax.rem(h, 2), h // 2
        self.places = [(1 - y) * 2 + 1 - x, y * 2 + 1 - x, (1 - y) * 2 + x]
        self.across = [(place, b) for place in self.places]
        self.there = [lax.rem(self.part + i, parts) for i in range(1, parts)]
        self.back = [lax.rem(self.part + parts - i, parts) for i in range(1, parts)]
        self.along = [(h, part * 2 + self.share) for part in self.there]
        self.beside = (h, self.part * 2 + 1 - self.share)
        self.near = self.part + 1 - 2 * lax.rem(self.part, 2)
        self.over = lax.rem(self.part + 2, 4)
        self.far = 3 - self.part
        self.askew = [(h, part * 2 + 1 - self.share) for part in self.there]


class LineGather:
    def __init__(self, view, own, here, sems):
        self.view, self.own, self.here, self.parts = view, own, here, here.parts
        self.right_s, self.left_s, self.line_r, self.core_s, self.core_r = sems
        self.first = 0

    def _copy(self, source, block, side):
        here = self.here
        if side == 0:
            sems, peer = (self.core_s, self.core_r), here.beside
        else:
            sems = (self.right_s if side > 0 else self.left_s, self.line_r)
            peer = (here.h, (here.part + side) * 2 + here.share)
        return remote(
            source, self.view(block, here.share), sems[0].at[block], sems[1].at[block], peer
        )

    def _can(self, side):
        return self.here.part < self.parts - 1 if side > 0 else self.here.part > 0

    def start(self):
        for side in (1, -1):

            @pl.when(self._can(side))
            def _():
                self._copy(self.own, self.here.part, side).start()

        self._copy(self.own, self.here.part, 0).start()

    def start_from(self, near):
        self.first = 1
        for side in (1, -1):
            block = self.here.part - side

            @pl.when((block >= 0) & (block < self.parts) & self._can(side))
            def _():
                self._copy(near[side], block, side).start()

        self._copy(self.own, self.here.part, 0).start()
        for side in (1, -1):
            block = self.here.part - side

            @pl.when((block >= 0) & (block < self.parts))
            def _():
                self._copy(near[side], block, 0).start()

    def step(self, k):
        for side in (1, -1):
            block = self.here.part - side * k

            @pl.when((block >= 0) & (block < self.parts))
            def _():
                there = self.view(block, self.here.share)
                self._copy(there, block, side).wait_recv()

                @pl.when(self._can(side))
                def _():
                    self._copy(there, block, side).start()

                self._copy(there, block, 0).start()

    def arrive(self):
        for block in range(self.parts):
            self._copy(self.own, block, 0).wait_recv()

    def finish(self):
        for side in (1, -1):
            for block in range(self.parts):
                first = self.here.part - side * self.first
                sent = block <= first if side > 0 else block >= first

                @pl.when(sent & self._can(side))
                def _():
                    self._copy(self.own, block, side).wait_send()

        for block in range(self.parts):
            self._copy(self.own, block, 0).wait_send()


class CornerGather:
    def __init__(self, whole, half, own, here, sems):
        self.whole, self.half, self.own, self.here = whole, half, own, here
        self.send_s, self.recv_s = sems

    def _copy(self, n):
        h, (corner, x, y) = self.here.h, self.here.across
        if n < 2:
            source, target, peer = self.own, self.whole(h), (x, y)[n]
        else:
            block = (y, x)[n - 2][0]
            source = target = self.half(block, n - 2)
            peer = (x, y)[n - 2]
        return remote(source, target, self.send_s.at[n], self.recv_s.at[n], peer)

    def start(self):
        for n in range(2):
            self._copy(n).start()

    def forward(self):
        for n in range(2):
            self._copy(n).wait_recv()
        for n in range(2, 4):
            self._copy(n).start()

    def arrive(self):
        for n in range(2, 4):
            self._copy(n).wait_recv()

    def finish(self):
        for n in range(4):
            self._copy(n).wait_send()


def local(source, target, sem):
    copy = pltpu.make_async_copy(source, target, sem)
    copy.start()
    return copy


def line_sems(parts):
    return [dma(parts)] * 5


def standardize(values):
    center = values - jnp.mean(values, axis=-1, keepdims=True)
    spread = jnp.mean(center * center, axis=-1, keepdims=True)
    scale = lax.rsqrt(spread + norm_eps)
    return (center * scale, scale)


def norm_back(grad, hat, scale, gain):
    inner = grad * gain
    return scale * (
        inner
        - jnp.mean(inner, axis=-1, keepdims=True)
        - hat * jnp.mean(inner * hat, axis=-1, keepdims=True)
    )


def turn(values, cosine, sine, back=False):
    lane = lax.broadcasted_iota(jnp.int32, values.shape, 1)
    first = lax.rem(lane, HEAD_DIM) < HEAD_DIM // 2
    source = values * sine if back else values
    ahead = pltpu.roll(source, 128 - HEAD_DIM // 2, 1)
    behind = pltpu.roll(source, HEAD_DIM // 2, 1)
    if back:
        return values * cosine + jnp.where(first, ahead, -behind)
    return values * cosine + jnp.where(first, -ahead, behind) * sine


def join(left, left_side, right, right_side):
    lane = lax.broadcasted_iota(jnp.int32, left.shape, 1)
    left = pltpu.roll(left, HEAD_DIM, 1) if left_side else left
    right = right if right_side else pltpu.roll(right, HEAD_DIM, 1)
    return jnp.where(lane < HEAD_DIM, left, right)


class Reduce:
    def __init__(self, term, core_in, line_out, line_in, here, sems):
        self.term, self.core_in, self.line_out, self.line_in = term, core_in, line_out, line_in
        self.here, self.parts = here, here.parts
        self.core_s, self.core_r, self.line_s, self.line_r = sems

    def _core(self):
        return remote(
            self.term.at[:, 1 - self.here.share],
            self.core_in,
            self.core_s.at[0],
            self.core_r.at[0],
            self.here.beside,
        )

    def _line(self, i):
        return remote(
            self.line_out[i],
            self.line_in.at[i],
            self.line_s.at[i],
            self.line_r.at[i],
            self.here.along[i],
        )

    def _sum(self, there):
        own = self.term[there, self.here.share].astype(jnp.float32)
        return own + self.core_in[there].astype(jnp.float32)

    def start(self):
        self._core().start()

    def core_sums(self):
        self._core().wait_recv()
        return self._sum

    def middle(self):
        self._core().wait_recv()
        for i, there in enumerate(self.here.there):
            self.line_out[i][...] = self._sum(there).astype(jnp.bfloat16)
            self._line(i).start()

    def close(self):
        total = self._sum(self.here.part)
        for i in range(self.parts - 1):
            self._line(i).wait_recv()
            total += self.line_in[i].astype(jnp.float32)
        return total

    def core_finish(self):
        self._core().wait_send()

    def finish(self):
        self.core_finish()
        for i in range(self.parts - 1):
            self._line(i).wait_send()


def reduce_scratch(parts, shape):
    return [
        pltpu.VMEM((parts, 2, *shape), jnp.bfloat16),
        pltpu.VMEM((parts, *shape), jnp.bfloat16),
        pltpu.VMEM((parts - 1, *shape), jnp.bfloat16),
        pltpu.VMEM((parts - 1, *shape), jnp.bfloat16),
        dma(1),
        dma(1),
        dma(parts - 1),
        dma(parts - 1),
    ]


class PairReduce:
    def __init__(self, core_in, near_out, near_in, far_out, far_in, *sems, term, here):
        self.term, self.core_in, self.near_out, self.near_in = term, core_in, near_out, near_in
        self.far_out, self.far_in, self.sems, self.here = far_out, far_in, sems, here

    def _copy(self, step):
        here = self.here
        source, target, peer = (
            (self.term.at[:, 1 - here.share], self.core_in, here.beside),
            (self.near_out, self.near_in, (here.h, here.near * 2 + here.share)),
            (self.far_out, self.far_in, (here.h, here.far * 2 + here.share)),
        )[step]
        return remote(source, target, self.sems[2 * step].at[0], self.sems[2 * step + 1].at[0], peer)

    def _sum(self, there):
        own = self.term[there, self.here.share].astype(jnp.float32)
        return own + self.core_in[there].astype(jnp.float32)

    def start(self):
        self._copy(0).start()

    def pair(self):
        self._copy(0).wait_recv()
        self.near_out[0] = self._sum(self.here.near).astype(jnp.bfloat16)
        self.near_out[1] = self._sum(self.here.over).astype(jnp.bfloat16)
        self._copy(1).start()

    def cross(self):
        self._copy(1).wait_recv()
        self.far_out[...] = (
            self._sum(self.here.far) + self.near_in[1].astype(jnp.float32)
        ).astype(jnp.bfloat16)
        self._copy(2).start()

    def close(self):
        self._copy(2).wait_recv()
        total = self._sum(self.here.part) + self.near_in[0].astype(jnp.float32)
        return total + self.far_in[...].astype(jnp.float32)

    def finish(self):
        for step in range(3):
            self._copy(step).wait_send()


def pair_scratch(parts, shape):
    return [
        pltpu.VMEM((parts, *shape), jnp.bfloat16),
        *[pltpu.VMEM((2, *shape), jnp.bfloat16)] * 2,
        *[pltpu.VMEM(shape, jnp.bfloat16)] * 2,
        *[dma(1)] * 6,
    ]


def reducer(scratch, here):
    term, core_in, line_out, line_in, *sems = scratch
    outs = [line_out.at[i] for i in range(here.parts - 1)]
    return (term, Reduce(term, core_in, outs, line_in, here, sems))


class Swap:
    def __init__(self, out, landed, send_s, recv_s, here):
        self.out, self.landed, self.here = out, landed, here
        self.send_s, self.recv_s = send_s, recv_s

    def start(self):
        here = self.here
        self.copies = [
            send(self.out.at[peer[0]], self.landed.at[here.h], self.send_s.at[i], self.recv_s.at[i], peer)
            for i, peer in enumerate(here.across)
        ]
        self.landed[here.h] = self.out[here.h]

    def arrive(self):
        for copy in self.copies:
            copy.wait_recv()

    def finish(self):
        for copy in self.copies:
            copy.wait_send()


def swap_scratch(heads, shape):
    return [
        pltpu.VMEM((heads, *shape), jnp.bfloat16),
        pltpu.VMEM((heads, *shape), jnp.bfloat16),
        dma(heads - 1),
        dma(heads - 1),
    ]


def run_of(here, i):
    x, y = lax.rem(here.h, 2), here.h // 2
    x = x + (1 - i // 2) * (1 - 2 * x)
    y = y + (1 - i % 2) * (1 - 2 * y)
    return y * 2 + x


def load(pairs, sems):
    copies = [pltpu.make_async_copy(*pair, sems.at[i]) for i, pair in enumerate(pairs)]
    for copy in copies:
        copy.start()
    return copies


def layer_kernel(
    H, A, tok_in, cot_in, wq_in, gain_one_in, gain_two_in, w_in_in, w_down_in, w_out_in, lengths,
    output_to, input_to, qkv_grad, out_grad, in_to, down_to, gain_one, gain_two,
    cot, w_in, w_down, w_out, tok_all, cot_all, wq_all, cos_all, sin_all,
    wq_st, wm_src, wm_own, wo_all, kv, kv_send, q_all, q_send, q_runs, hats, gain_src, gain_st, gain_tile, gain_all,
    bounds, s_scr, op, mx_in, mixed_own, mixed_early, mixed_late, wm_all, middle, normed, act, lift,
    g2_send, g2_in, g2_own, gm_send, in_term, in_core, down_term, down_core, down_send, down_in,
    out_base, out_parts, grad_middle, near_out, far_out,
    lse, go, gain_rows, gain_part, branch_own, branch_all, o_in, from_near, from_far, in_send, in_last,
    dkv_sum, dq_send, dq_in, dk_send, dk_in, dkv_send, dkv_in, gp, g1_send, g1_in, g1_own,
    term_out, term_qkv_low, term_qkv_high, output, input_grad, in_grad, down_grad,
    load_s, own_s, result_s,
    tok_s, tok_r, wq_s, wq_r, wm_s, wm_r, ga_s, ga_r, gb_s, gb_r, wx_s, wx_r, wf_s, wf_r, cot_s, cot_r,
    q_s, q_r, kv_s, kv_r, kc_s, kc_r, mx_s, mx_r, ma_s, ma_r, g2_s, g2_r, gm_s, gm_r,
    in_core_s, in_core_r, down_core_s, down_core_r, pair_s, pair_r,
    br_s, br_r, o_s, o_r, g1_s, g1_r, nr_s, nr_r, dq_s, dq_r, dz_s, dz_r, dk_s, dk_r, *more,
):
    line, more = more[:25], more[25:]
    term_qkv = (term_qkv_low, term_qkv_high)
    f32, bf16 = jnp.float32, jnp.bfloat16
    R, W = tok_all.shape[1:]
    B = 2 * A
    hw = W // H
    D = wq_in.shape[0]
    F = w_in.shape[1] // 2 // H
    here = Place(A)
    h, b, part, share = here.h, here.b, here.part, here.share
    across, along, beside = here.across, here.along, here.beside

    def slices(source, target, place):
        return [
            (
                source.at[:, pl.ds(pl.multiple_of(j * W + place * hw, hw), hw)],
                target.at[h, :, j * hw : (j + 1) * hw],
            )
            for j in range(3)
        ]

    loads = [
        local(source, target, load_s.at[n])
        for n, (source, target) in enumerate(
            [
                (w_out_in, w_out), (w_in_in, w_in), (w_down_in, w_down), (cot_in, cot), (tok_in, tok_all.at[h]),
                *slices(wq_in, wq_st, h),
            ]
        )
    ]
    row = lax.broadcasted_iota(jnp.int32, (8, 128), 0)
    lane = lax.broadcasted_iota(jnp.int32, (8, 128), 1)
    gain_src[...] = jnp.zeros((8, 128), f32)
    gain_src[0:1, :D] = gain_one_in[...].astype(f32)
    gain_src[1:2, :D] = gain_two_in[...].astype(f32)
    gain_src[...] = pltpu.roll(gain_src[...], h * D, 1)
    others = [
        (run_of(here, i), lax.rem(part + j, A) * 2 + share)
        for i in range(H)
        for j in range(A)
        if i < H - 1 or j
    ]
    meet([*others, *here.askew, beside])

    for i, peer in enumerate(across):
        for source, target in slices(wq_in, wq_st, peer[0]):
            send(source, target, wq_s.at[i], wq_r.at[i], peer)
    wq_copies = [
        remote(wq_st.at[peer[0]], wq_st.at[h], wq_s.at[i], wq_r.at[i], peer)
        for i, peer in enumerate(across)
    ]
    gain_copies = [
        send(gain_src, gain_st.at[i], ga_s.at[i], ga_r.at[i], peer) for i, peer in enumerate(across)
    ]
    wo_line = LineGather(lambda block, side: wo_all.at[h, block, side], w_out, here, line[:5])
    loads[0].wait()
    wo_line.start()
    own_copy = local(w_out, wo_all.at[h, part, share], own_s.at[0])
    for copy in loads[1:]:
        copy.wait()
    for place in range(H):
        wm_src[place, :, :F] = w_in[:, place * F : (place + 1) * F]
        wm_src[place, :, F : 2 * F] = w_in[:, (H + place) * F : (H + place + 1) * F]
        wm_src[place, :, 2 * F :] = w_down[:, place * F : (place + 1) * F]
    wm_own[h] = wm_src[h]
    cot_all[h] = cot[...]

    wide = lax.broadcasted_iota(jnp.int32, (R, 128), 1)
    freqs = jnp.exp(
        lax.rem(wide, HEAD_DIM // 2).astype(f32) * (-2.0 / HEAD_DIM * float(np.log(rope_base)))
    )

    def tables(run):
        place = (run * B + b) * R + lax.broadcasted_iota(jnp.int32, (R, 128), 0)

        def one(d, carried):
            low, begin = carried
            return (low + lengths[d], jnp.where(place >= low, low, begin))

        unused, begin = lax.fori_loop(
            0, lengths.shape[0], one, (jnp.int32(0), jnp.zeros((R, 128), jnp.int32))
        )
        angles = (place - begin).astype(f32) * freqs
        cos_all[run] = jnp.cos(angles)
        sin_all[run] = jnp.sin(angles)

    tables(0)
    tables(1)
    wo_line.step(1)
    for copy in wq_copies:
        copy.wait_recv()
    wq_lines = []
    for half in range(2):
        rows = pl.ds(half * (H // 2), H // 2)
        wq_lines.append(
            LineGather(
                lambda block, side, rows=rows: wq_all.at[rows, block * 2 + side],
                wq_st.at[rows],
                here,
                line[5 * half + 5 : 5 * half + 10],
            )
        )
        wq_lines[half].start()
    tok_copies = [
        send(tok_in, tok_all.at[h], tok_s.at[i], tok_r.at[i], peer) for i, peer in enumerate(across)
    ]
    tile = gain_src[...]
    for i, copy in enumerate(gain_copies):
        copy.wait_recv()
        tile += gain_st[i]
    gain_tile[...] = tile
    gain_all[b] = tile
    gain_copies += [
        send(gain_tile, gain_all.at[b], gb_s.at[i], gb_r.at[i], peer)
        for i, peer in enumerate([*along, *here.askew, beside])
    ]
    wo_line.step(2)
    wq_all[:, b] = wq_st[...]
    tables(2)
    wq_lines[0].step(1)
    wo_line.step(3)
    wq_lines[1].step(1)
    wo_line.arrive()
    spread = CornerGather(
        lambda place: wo_all.at[place, :, share],
        lambda place, half: wo_all.at[place, half * (A // 2) : (half + 1) * (A // 2), share],
        wo_all.at[h, :, share],
        here,
        (wx_s, wx_r),
    )
    own_copy.wait()
    spread.start()
    wm_copies = [
        send(wm_src.at[peer[0]], wm_own.at[h], wm_s.at[i], wm_r.at[i], peer)
        for i, peer in enumerate(across)
    ]
    cot_gather = CornerGather(
        lambda place: cot_all.at[place],
        lambda place, half: cot_all.at[place, half * (R // 2) : (half + 1) * (R // 2)],
        cot,
        here,
        (cot_s, cot_r),
    )
    cot_gather.start()
    tables(3)
    for copy in tok_copies:
        copy.wait_recv()

    def norm_run(run, carried):
        hat, unused = standardize(tok_all[run].astype(f32))
        hats[run] = hat
        return carried

    wq_lines[0].step(2)
    lax.fori_loop(0, H // 2, norm_run, 0)
    wq_lines[1].step(2)
    lax.fori_loop(H // 2, H, norm_run, 0)
    for copy in gain_copies[len(across) :]:
        copy.wait_recv()
    for slab in range(W // 128):
        place, first = slab // (hw // 128), slab % (hw // 128) * (128 // D)
        piece = jnp.zeros((8, 128), f32)
        for j in range(128 // D):
            moved = gain_all[first + j]
            if j != place:
                moved = pltpu.roll(moved, (j - place) * D % 128, 1)
            piece = jnp.where(lane // D == j, moved, piece)
        gain_rows[:, slab * 128 : (slab + 1) * 128] = piece
    wq_lines[0].step(3)
    wq_lines[1].step(3)
    wq_lines[0].arrive()
    wq_lines[1].arrive()

    for run in [run for low in range(H // 2) for run in (low, low + H // 2)]:
        rounded = (hats[run] * gain_rows[0:1, :]).astype(bf16)
        projected = jnp.zeros((R, 3 * hw), f32)
        for chunk in range(H):
            block = wq_all[chunk].reshape(B * D, 3 * hw)
            projected += mm(rounded[:, chunk * hw : (chunk + 1) * hw], block)
        cosine, sine = cos_all[run], sin_all[run]
        for slab in range(hw // 128):
            at = slab * 128
            q_runs[run, :, at : at + 128] = turn(projected[:, at : at + 128], cosine, sine)
            key = turn(projected[:, hw + at : hw + at + 128], cosine, sine)
            value = projected[:, 2 * hw + at : 2 * hw + at + 128]
            kv_send[2 * slab, run] = join(key, 0, value, 0).astype(bf16)
            kv_send[2 * slab + 1, run] = join(key, 1, value, 1).astype(bf16)
        for i, peer in enumerate(along):
            send(kv_send.at[here.there[i], run], kv.at[run, b], kv_s.at[i], kv_r.at[i], peer)
        send(kv_send.at[part, run], kv.at[run, b], kc_s.at[0], kc_r.at[0], beside)
        kv[run, b] = kv_send[part, run]
        if run >= H // 2:
            low = run - H // 2
            for a in range(A):
                at = a // 2 * 128
                q_send[a, low] = join(
                    q_runs[low, :, at : at + 128], a % 2, q_runs[run, :, at : at + 128], a % 2
                ).astype(bf16)
            for i, peer in enumerate(along):
                send(q_send.at[here.there[i], low], q_all.at[part, low], q_s.at[i], q_r.at[i], peer)
            q_all[part, low] = q_send[part, low]

    kv_copies = [
        remote(kv_send.at[here.there[i]], kv.at[:, b], kv_s.at[i], kv_r.at[i], peer)
        for i, peer in enumerate(along)
    ]
    kc_copies = [remote(kv_send.at[part], kv.at[:, b], kc_s.at[0], kc_r.at[0], beside)]
    q_copies = [
        remote(q_send.at[here.there[i]], q_all.at[part], q_s.at[i], q_r.at[i], peer)
        for i, peer in enumerate(along)
    ]
    spread.forward()
    cot_gather.forward()

    tiles = H * A // 2
    spot = lax.broadcasted_iota(jnp.int32, (1, 2 * R), 1)
    spot = spot + jnp.where(spot < R, 0, R) + share * R
    for tile in range(tiles):
        place = spot + tile * 4 * R

        def one(d, carried, place=place):
            low, begin, stop = carried
            high = low + lengths[d]
            inside = (place >= low) & (place < high)
            return (high, jnp.where(inside, low, begin), jnp.where(inside, high, stop))

        unused, bounds[tile, 0:1], bounds[tile, 1:2] = lax.fori_loop(
            0, lengths.shape[0], one, (jnp.int32(0), jnp.zeros_like(place), jnp.zeros_like(place))
        )

    def pass_on(i):
        there = wo_all.at[here.places[i], :, share]
        kc_copies.append(send(there, there, wf_s.at[i], wf_r.at[i], beside))

    pass_on(1)
    pass_on(2)
    for i, copy in enumerate(kv_copies):
        copy.wait_recv()
        there = kv.at[:, here.back[i] * 2 + share]
        kc_copies.append(send(there, there, kc_s.at[i + 1], kc_r.at[i + 1], beside))
    wm_lines = []
    for copy in wm_copies:
        copy.wait_recv()
    for half in range(2):
        rows = pl.ds(half * (H // 2), H // 2)
        wm_lines.append(
            LineGather(
                lambda block, side, rows=rows: wm_all.at[rows, block * 2 + side],
                wm_own.at[rows],
                here,
                line[5 * half + 15 : 5 * half + 20],
            )
        )
        wm_lines[half].start()
    wm_all[:, b] = wm_own[...]
    for copy in [*kc_copies, *q_copies]:
        copy.wait_recv()
    spread.arrive()
    last = len(kc_copies)
    pass_on(0)

    steps = H * B * R // KEY_STEP
    at = lax.broadcasted_iota(jnp.int32, (KEY_STEP, 2 * R), 0)
    spans = KEY_STEP // R

    def attend_pair(hh, u):
        results = []
        for side in (0, 1):
            tile = (hh + side * (H // 2)) * (A // 2) + u
            low, high = max(tile - 2, 0), min(tile + 3, steps)
            begin, stop = bounds[tile, 0:1], bounds[tile, 1:2]
            pair = q_all[2 * u : 2 * u + 2, hh].reshape(2 * R, 128)
            query = (halves(pair, side) * HEAD_DIM**-0.5).astype(bf16)

            def keys_at(n):
                return kv[n * spans // B, pl.ds(lax.rem(n * spans, B), spans)].reshape(KEY_STEP, 128)

            def score(n, top, low=low, begin=begin, stop=stop, query=query):
                same = (at >= begin - n * KEY_STEP) & (at < stop - n * KEY_STEP)
                scores = jnp.where(same, mm(keys_at(n), query, NT), neg_large)
                s_scr[n - low] = scores
                return jnp.maximum(top, jnp.max(scores, axis=0, keepdims=True))

            top = lax.fori_loop(low, high, score, jnp.full((1, 2 * R), neg_large, f32))

            def mix(n, carried, low=low, top=top):
                total, acc = carried
                weights = jnp.exp(s_scr[n - low] - top)
                total = total + jnp.sum(weights, axis=0, keepdims=True)
                return (total, acc + mm(keys_at(n), weights.astype(bf16), TN))

            total, acc = lax.fori_loop(
                low, high, mix, (jnp.zeros((1, 2 * R), f32), jnp.zeros((128, 2 * R), f32))
            )
            lse[tile] = top + jnp.log(total)
            results.append(acc[HEAD_DIM:] / total)
        both = jnp.concatenate(results, axis=0).T.astype(bf16)
        op[hh, 2 * u : 2 * u + 2] = both.reshape(2, R, 128)

    def mixed_out_copies(hh):
        mx_in[hh, part] = op[hh, part]
        return [
            send(op.at[hh, here.there[i]], mx_in.at[hh, part], mx_s.at[n], mx_r.at[n], peer)
            for i, peer in enumerate(along)
            for n in [hh * (A - 1) + i]
        ]

    ma_copies, mixed_all = {}, (mixed_early, mixed_late)

    def assemble(hh, copies):
        for copy in copies:
            copy.wait_recv()
        for side in (0, 1):
            run = hh + side * (H // 2)
            slabs = []
            for slab in range(hw // 128):
                left, right = mx_in[hh, 2 * slab].astype(f32), mx_in[hh, 2 * slab + 1].astype(f32)
                slabs.append(join(left, side, right, side))
            mixed = jnp.concatenate(slabs, axis=1).astype(bf16)
            mixed_own[run] = mixed
            for i, peer in enumerate(across):
                ma_copies[i, run] = send(
                    mixed_own.at[run], mixed_all[hh].at[h, side], ma_s.at[i * H + run], ma_r.at[i * H + run], peer
                )

    def project_own(runs):
        for run in runs:
            middle[run] = tok_all[run].astype(f32) + mm(mixed_own[run], wo_rows(h))

    def project_others(runs):
        for i in range(H - 1):
            for run in runs:
                ma_copies[i, run].wait_recv()
        for source in here.places:
            for run in runs:
                mixed = mixed_all[run % (H // 2)][source, run // (H // 2)]
                middle[run] += mm(mixed, wo_rows(source))

    def wo_rows(source):
        return wo_all[source].reshape(hw, W)

    attend_pair(0, 0)
    attend_pair(0, 1)
    mx_copies = mixed_out_copies(0)
    wm_lines[0].step(1)
    attend_pair(1, 0)
    wm_lines[1].step(1)
    assemble(0, mx_copies)
    attend_pair(1, 1)
    mx_late = mixed_out_copies(1)
    wm_lines[0].step(2)
    cot_gather.arrive()
    kc_copies[last].wait_recv()
    early, late = (0, H // 2), (1, H // 2 + 1)
    project_own(early)
    assemble(1, mx_late)
    project_own(late)
    wm_lines[1].step(2)
    project_others(early)
    wm_lines[0].step(3)
    project_others(late)

    def norm_two(run, carried):
        hat, unused = standardize(middle[run])
        normed[run] = (hat * gain_rows[1:2, :]).astype(bf16)
        return carried

    lax.fori_loop(0, H, norm_two, 0)
    wm_lines[1].step(3)
    for item in wm_lines:
        item.arrive()
    down_sum = Reduce(down_term, down_core, None, None, here, [down_core_s, down_core_r, None, None])
    in_sum = Reduce(in_term, in_core, None, None, here, [in_core_s, in_core_r, None, None])
    near, over, far = here.near, here.over, here.far

    def block(chunk):
        return wm_all[chunk].reshape(B * D, 3 * F)

    def part_of(run, i):
        return remote(g2_send.at[i], g2_in.at[i], g2_s.at[i], g2_r.at[i], (run, b))

    def feed_run(i, carried):
        run = run_of(here, i)
        lifted = jnp.zeros((R, 2 * F), f32)
        grad_act = jnp.zeros((R, F), f32)
        for chunk in range(H):
            lanes = slice(chunk * hw, (chunk + 1) * hw)
            weights = block(chunk)
            lifted += mm(normed[run, :, lanes], weights[:, : 2 * F])
            grad_act += mm(cot_all[run, :, lanes], weights[:, 2 * F :])
        gate, up = lifted[:, :F], lifted[:, F:]
        below = 0.5 + 0.5 * lax.erf(gate * (0.5**0.5))
        slope = below + gate * jnp.exp(-0.5 * gate * gate) * ((2.0 * np.pi) ** -0.5)
        act[run] = (gate * below * up).astype(bf16)
        lift[run, :, :F] = (grad_act * up * slope).astype(bf16)
        lift[run, :, F:] = (grad_act * gate * below).astype(bf16)

        for chunk in range(H):
            lanes = slice(chunk * hw, (chunk + 1) * hw)
            g2_own[:, lanes] = mm(lift[run], block(chunk)[:, : 2 * F], NT)

        @pl.when(i < H - 1)
        def _():
            g2_send[i] = g2_own[...].astype(bf16)
            part_of(run, i).start()

        return carried

    lax.fori_loop(0, H, feed_run, 0)

    def down_chunk(chunk, carried):
        lanes = pl.ds(pl.multiple_of(chunk * hw, hw), hw)
        left = cot_all[:, :, lanes].reshape(H * R, hw)
        grads = mm(left, act[...].reshape(H * R, F), TN).astype(bf16)
        down_term[:, :, chunk] = grads.reshape(A, 2, D, F)
        return carried

    lax.fori_loop(0, H, down_chunk, 0)
    down_sum.start()

    def in_chunk(chunk, carried):
        lanes = pl.ds(pl.multiple_of(chunk * hw, hw), hw)
        left = normed[:, :, lanes].reshape(H * R, hw)
        grads = mm(left, lift[...].reshape(H * R, 2 * F), TN).astype(bf16)
        in_term[:, :, chunk] = grads.reshape(A, 2, D, 2 * F)
        return carried

    lax.fori_loop(0, H, in_chunk, 0)
    in_sum.start()
    down_of = down_sum.core_sums()
    for n, there in enumerate((near, over)):
        down_send[n] = down_of(there).astype(bf16)
    pair_copy = send(down_send, down_in, pair_s.at[0], pair_r.at[0], (h, near * 2 + share))

    hat, scale = standardize(middle[h])
    grad = g2_own[...]
    for i in (1, 2, 0):
        part_of(here.places[i], i).wait_recv()
        grad += g2_in[i].astype(f32)
    gain_part[...] = jnp.broadcast_to(jnp.sum(grad * hat, axis=0, keepdims=True), gain_part.shape)
    total = cot_all[h].astype(f32) + norm_back(grad, hat, scale, gain_rows[1:2, :])
    grad_middle[...] = total
    branch = total.astype(bf16)
    branch_own[...] = branch
    gm_copies = []
    for i in range(H):
        place = run_of(here, i)
        mixed_grad = mm(branch, wo_rows(place), NT)
        for a in range(A):
            slab = mixed_grad[:, a // 2 * 128 : a // 2 * 128 + 128]
            gm_send[i, a] = join(slab[: R // 2], a % 2, slab[R // 2 :], a % 2).astype(bf16)
        for j in range(A):
            there = lax.rem(part + j, A)
            if i < H - 1 or j:
                n = i * A + j
                gm_copies.append(
                    send(gm_send.at[i, there], go.at[part, h], gm_s.at[n], gm_r.at[n], (place, there * 2 + share))
                )
            else:
                go[part, h] = gm_send[i, part]

    br_copies = [
        send(branch_own, branch_all.at[h], br_s.at[i], br_r.at[i], peer) for i, peer in enumerate(across)
    ]
    branch_all[h] = branch
    in_of = in_sum.core_sums()
    near_out[0] = in_of(near).astype(bf16)
    near_out[1] = in_of(over).astype(bf16)
    near_copy = send(near_out, from_near, nr_s.at[0], nr_r.at[0], (h, near * 2 + share))
    pair_copy.wait_recv()
    far_out[...] = (down_of(far) + down_in[1].astype(f32)).astype(bf16)

    def out_run(i, carried):
        run = run_of(here, i)
        for chunk in range(H):
            lanes = slice(chunk * hw, (chunk + 1) * hw)
            out_base[:, lanes] = mm(act[run], block(chunk)[:, 2 * F :], NT)

        @pl.when(i < H - 1)
        def _():
            out_parts[i] = out_base[...].astype(bf16)

        return carried

    lax.fori_loop(0, H, out_run, 0)
    out_base[...] += middle[h]
    dkv_sum[...] = jnp.zeros_like(dkv_sum)
    for copy in gm_copies:
        copy.wait_recv()
    far_copy = send(far_out, from_far, nr_s.at[1], nr_r.at[1], (h, far * 2 + share))

    wide_lane = lax.broadcasted_iota(jnp.int32, (2 * R, 128), 1)

    def attend_back_tile(tile):
        run, u = tile // (A // 2), tile % (A // 2)
        side, hh = run // (H // 2), run % (H // 2)
        low, high = max(tile - 2, 0), min(tile + 3, steps)
        begin, stop = bounds[tile, 0:1], bounds[tile, 1:2]
        pair = q_all[2 * u : 2 * u + 2, hh].reshape(2 * R, 128)
        query = (halves(pair, side) * HEAD_DIM**-0.5).astype(bf16)
        pieces = []
        for a in (2 * u, 2 * u + 1):
            piece = go[a, run].astype(f32)
            pieces += [pltpu.roll(piece, HEAD_DIM, 1), piece]
        grad = jnp.where(wide_lane < HEAD_DIM, 0.0, jnp.concatenate(pieces, axis=0))
        mixed = op[hh, 2 * u : 2 * u + 2].reshape(2 * R, 128).astype(f32)
        if not side:
            mixed = pltpu.roll(mixed, HEAD_DIM, 1)
        delta = jnp.sum((grad * mixed).T, axis=0, keepdims=True)
        both = jnp.concatenate([query, grad.astype(bf16)], axis=0)
        logs = lse[tile]

        def step(n, dq):
            keys = kv[n * spans // B, pl.ds(lax.rem(n * spans, B), spans)].reshape(KEY_STEP, 128)
            same = (at >= begin - n * KEY_STEP) & (at < stop - n * KEY_STEP)
            products = mm(keys, both, NT)
            probs = jnp.where(same, jnp.exp(products[:, : 2 * R] - logs), 0.0)
            grad_scores = (probs * (products[:, 2 * R :] - delta)).astype(bf16)
            left = jnp.concatenate([grad_scores, probs.astype(bf16)], axis=1)
            dkv_sum[n] += mm(left, both)
            return dq + mm(keys, grad_scores, TN)

        dq = lax.fori_loop(low, high, step, jnp.zeros((128, 2 * R), f32))
        dq = (dq * HEAD_DIM**-0.5).T
        for k, a in enumerate((2 * u, 2 * u + 1)):
            rows = dq[k * R : (k + 1) * R]
            dq_send[a, run] = join(rows[: R // 2], 0, rows[R // 2 :], 0).astype(bf16)

            @pl.when(part == a)
            def _(a=a):
                dq_in[a, run] = dq_send[a, run]

            @pl.when(part != a)
            def _(a=a):
                n = part * H + run
                remote(
                    dq_send.at[a, run], dq_in.at[part, run], dq_s.at[a * H + run], dq_r.at[n], (h, a * 2 + share)
                ).start()

    def dk_copy(k):
        return remote(dk_send.at[k], dk_in.at[k], dk_s.at[k], dk_r.at[k], beside)

    def keys_done(k):
        for n in range(2):
            first = pl.multiple_of((2 * n + 1 - share) * R, R)
            dk_send[k, n] = dkv_sum[k, pl.ds(first, R), :].astype(bf16)
        dk_copy(k).start()

    def keys_sum(k):
        dk_copy(k).wait_recv()
        run = k * spans // B
        for n in range(2):
            a = k * spans % B // 2 + n
            first = pl.multiple_of((2 * n + share) * R, R)
            summed = dkv_sum[k, pl.ds(first, R), :] + dk_in[k, n].astype(f32)
            dkv_send[a, run] = summed.astype(bf16)

            @pl.when(part == a)
            def _(a=a):
                dkv_in[a, run] = dkv_send[a, run]

            @pl.when(part != a)
            def _(a=a):
                n = part * H + run
                remote(
                    dkv_send.at[a, run], dkv_in.at[part, run], dz_s.at[a * H + run], dz_r.at[n], (h, a * 2 + share)
                ).start()

    out_sum, *qkv_sums = (
        PairReduce(*more[11 * n : 11 * n + 11], term=term, here=here)
        for n, term in enumerate((term_out, *term_qkv))
    )
    gain_scratch, swaps = more[33:41], more[41:]
    term_gain, gain_sum = reducer(gain_scratch, here)
    in_swap, qkv_swap, gain_swap = (Swap(*swaps[4 * n : 4 * n + 4], here) for n in range(3))

    def out_tile(n, carried):
        lanes = pl.ds(pl.multiple_of(n * hw, hw), hw)
        grads = mm(mixed_own[...].reshape(H * R, hw), branch_all[:, :, lanes].reshape(H * R, hw), TN)
        term_out[:, :, :, lanes] = grads.astype(bf16).reshape(A, 2, D, hw)
        return carried

    for tile in range(tiles):
        attend_back_tile(tile)
        if tile >= 2:
            keys_done(tile - 2)
        if tile >= 3:
            keys_sum(tile - 3)
        if tile == 5:
            for copy in br_copies:
                copy.wait_recv()
            o_copies = [
                send(out_parts.at[i], o_in.at[i], o_s.at[i], o_r.at[i], peer)
                for i, peer in enumerate(across)
            ]
            lax.fori_loop(0, W // hw, out_tile, 0)
            out_sum.start()
        if tile == 6:
            near_copy.wait_recv()
            in_send[...] = (in_of(far) + from_near[1].astype(f32)).astype(bf16)
    for k in (tiles - 2, tiles - 1):
        keys_done(k)
    for k in (tiles - 3, tiles - 2, tiles - 1):
        keys_sum(k)
    out_sum.pair()
    last_copy = send(in_send, in_last, nr_s.at[2], nr_r.at[2], (h, far * 2 + share))
    for source in here.back:
        for run in range(H):
            n = source * H + run
            remote(dq_send.at[0, 0], dq_in.at[0, 0], dq_s.at[n], dq_r.at[n], beside).wait_recv()
            remote(dkv_send.at[0, 0], dkv_in.at[0, 0], dz_s.at[n], dz_r.at[n], beside).wait_recv()
    for run in range(H):
        cosine, sine = cos_all[run], sin_all[run]
        for slab in range(hw // 128):
            lanes = slab * 128
            left, right = dq_in[2 * slab, run].astype(f32), dq_in[2 * slab + 1, run].astype(f32)
            both = jnp.concatenate([join(left, 0, right, 0), join(left, 1, right, 1)], axis=0)
            gp[run, :, lanes : lanes + 128] = turn(both, cosine, sine, True).astype(bf16)
            left, right = dkv_in[2 * slab, run].astype(f32), dkv_in[2 * slab + 1, run].astype(f32)
            gp[run, :, hw + lanes : hw + lanes + 128] = turn(
                join(left, 0, right, 0), cosine, sine, True
            ).astype(bf16)
            gp[run, :, 2 * hw + lanes : 2 * hw + lanes + 128] = join(left, 1, right, 1).astype(bf16)

    out_sum.cross()

    def qkv_block(chunk):
        return wq_all[chunk].reshape(B * D, 3 * hw)

    for half, (term, item) in enumerate(zip(term_qkv, qkv_sums)):

        def term_chunk(n, carried, half=half, term=term):
            lanes = pl.ds(pl.multiple_of((half * (H // 2) + n) * hw, hw), hw)
            left = (hats[:, :, lanes] * gain_rows[0:1, lanes]).astype(bf16).reshape(H * R, hw)
            grads = mm(left, gp[...].reshape(H * R, 3 * hw), TN).astype(bf16)
            term[:, :, n] = grads.reshape(A, 2, D, 3 * hw)
            return carried

        lax.fori_loop(0, H // 2, term_chunk, 0)
        item.start()
        if half:
            qkv_sums[0].pair()

    def part_one(run, i):
        return remote(g1_send.at[i], g1_in.at[i], g1_s.at[i], g1_r.at[i], (run, b))

    def one_run(i, carried):
        run = run_of(here, i)
        for chunk in range(H):
            lanes = slice(chunk * hw, (chunk + 1) * hw)
            g1_own[:, lanes] = mm(gp[run], qkv_block(chunk), NT)

        @pl.when(i < H - 1)
        def _():
            g1_send[i] = g1_own[...].astype(bf16)
            part_one(run, i).start()

        return carried

    lax.fori_loop(0, 1, one_run, 0)
    qkv_sums[1].pair()
    lax.fori_loop(1, H, one_run, 0)
    qkv_sums[0].cross()
    far_copy.wait_recv()
    down = down_of(part) + down_in[0].astype(f32) + from_far[...].astype(f32)
    in_swap.out[:, :, 2 * F :] = down.astype(bf16)
    last_copy.wait_recv()
    total = in_of(part) + from_near[0].astype(f32) + in_last[...].astype(f32)
    in_swap.out[:, :, : 2 * F] = total.astype(bf16)
    in_swap.start()
    qkv_sums[1].cross()

    grad = g1_own[...]
    hat, scale = standardize(tok_all[h].astype(f32))
    for i in (1, 2, 0):
        part_one(here.places[i], i).wait_recv()
        grad += g1_in[i].astype(f32)
    row = lax.broadcasted_iota(jnp.int32, (8, W), 0)
    rows = jnp.where(
        row == 0,
        jnp.sum(grad * hat, axis=0, keepdims=True),
        jnp.where(row == 1, gain_part[...], 0.0),
    )
    pick = (
        lax.broadcasted_iota(jnp.int32, (8, 128), 0) == lax.broadcasted_iota(jnp.int32, (8, 128), 1)
    ).astype(bf16)
    for chunk in range(H):
        gain_columns = mm(rows[:, chunk * hw : (chunk + 1) * hw].astype(bf16), pick, TN)
        term_gain[:, :, chunk] = gain_columns.astype(bf16).reshape(A, 2, D, 128)
    gain_sum.start()
    input_grad[...] = grad_middle[...] + norm_back(grad, hat, scale, gain_rows[0:1, :])
    gain_sum.middle()
    result = out_base[...]
    for i, copy in enumerate(o_copies):
        copy.wait_recv()
        result += o_in[i].astype(f32)
    output[...] = result.astype(bf16)
    results = [local(output, output_to, result_s.at[0]), local(input_grad, input_to, result_s.at[1])]
    in_swap.arrive()
    for place in range(H):
        in_grad[:, place * F : (place + 1) * F] = in_swap.landed[place, :, :F].astype(f32)
        in_grad[:, (H + place) * F : (H + place + 1) * F] = in_swap.landed[
            place, :, F : 2 * F
        ].astype(f32)
        down_grad[:, place * F : (place + 1) * F] = in_swap.landed[place, :, 2 * F :].astype(f32)
    results += [local(in_grad, in_to, result_s.at[2]), local(down_grad, down_to, result_s.at[3])]
    for half, item in enumerate(qkv_sums):
        qkv_swap.out[half * (H // 2) : (half + 1) * (H // 2)] = item.close().astype(bf16)
    qkv_swap.start()
    gain_swap.out[...] = gain_sum.close().astype(bf16)
    gain_swap.start()
    out_grad[...] = out_sum.close()
    qkv_swap.arrive()
    for place in range(H):
        for j in range(3):
            qkv_grad[:, j * W + place * hw : j * W + (place + 1) * hw] = qkv_swap.landed[
                place, :, j * hw : (j + 1) * hw
            ].astype(f32)
    gain_swap.arrive()
    total = gain_swap.landed[0].astype(f32)
    for place in range(1, H):
        total += gain_swap.landed[place].astype(f32)
    rows = total.T
    gain_one[...] = rows[0:1, :]
    gain_two[...] = rows[1:2, :]
    for copy in [
        *kc_copies, *q_copies, *wm_copies, *wq_copies, *gain_copies, *tok_copies, *kv_copies,
        *mx_copies, *mx_late, *ma_copies.values(), *gm_copies, pair_copy,
        *br_copies, *o_copies, near_copy, far_copy, last_copy,
    ]:
        copy.wait_send()
    for k in range(tiles):
        dk_copy(k).wait_send()
    for there in here.there:
        for run in range(H):
            n = there * H + run
            remote(dq_send.at[0, 0], dq_in.at[0, 0], dq_s.at[n], dq_r.at[n], beside).wait_send()
            remote(dkv_send.at[0, 0], dkv_in.at[0, 0], dz_s.at[n], dz_r.at[n], beside).wait_send()
    for i in range(H - 1):
        part_of(here.places[i], i).wait_send()
        part_one(here.places[i], i).wait_send()
    for item in (spread, cot_gather, wo_line, *wq_lines, *wm_lines):
        item.finish()
    in_sum.core_finish()
    down_sum.core_finish()
    for copy in results:
        copy.wait()
    for item in (out_sum, *qkv_sums, gain_sum, in_swap, qkv_swap, gain_swap):
        item.finish()


def layer(tokens, cotangent, w_qkv, gain_one, gain_two, w_in, w_down, w_out, lengths):
    R, W = tokens.shape
    H, B = lax.axis_size("head"), lax.axis_size("blk")
    A = B // 2
    hw = W // H
    D = w_qkv.shape[0]
    F = w_down.shape[1] // H
    f32, bf16 = jnp.float32, jnp.bfloat16
    shape = jax.ShapeDtypeStruct
    buffer = lambda *sizes: pltpu.VMEM(sizes, bf16)
    wide = lambda *sizes: pltpu.VMEM(sizes, f32)
    outs = [
        shape((R, W), bf16),
        shape((R, W), f32),
        shape((D, 3 * W), f32),
        shape((D, W), f32),
        shape((D, 2 * H * F), f32),
        shape((D, H * F), f32),
        shape((1, D), f32),
        shape((1, D), f32),
    ]
    return pl.pallas_call(
        partial(layer_kernel, H, A),
        in_specs=[*[anywhere()] * 3, *[in_vmem()] * 2, *[anywhere()] * 3, in_smem()],
        out_specs=[anywhere() if n in (0, 1, 4, 5) else in_vmem() for n in range(len(outs))],
        out_shape=outs,
        scratch_shapes=[
            buffer(R, W),
            buffer(*w_in.shape),
            buffer(*w_down.shape),
            buffer(*w_out.shape),
            buffer(H, R, W),
            buffer(H, R, W),
            buffer(H, B, D, 3 * hw),
            wide(H, R, 128),
            wide(H, R, 128),
            buffer(H, D, 3 * hw),
            buffer(H, D, 3 * F),
            buffer(H, D, 3 * F),
            buffer(H, A, 2, D, W),
            buffer(H, B, R, 128),
            buffer(A, H, R, 128),
            buffer(A, H // 2, R, 128),
            buffer(A, H // 2, R, 128),
            wide(H, R, hw),
            wide(H, R, W),
            wide(8, 128),
            wide(H - 1, 8, 128),
            wide(8, 128),
            wide(B, 8, 128),
            pltpu.VMEM((H * A // 2, 8, 2 * R), jnp.int32),
            wide(5, KEY_STEP, 2 * R),
            buffer(H // 2, A, R, 128),
            buffer(H // 2, A, R, 128),
            buffer(H, R, hw),
            *[buffer(H, 2, R, hw)] * 2,
            buffer(H, B, D, 3 * F),
            wide(H, R, W),
            buffer(H, R, W),
            buffer(H, R, F),
            buffer(H, R, 2 * F),
            buffer(H - 1, R, W),
            buffer(H - 1, R, W),
            wide(R, W),
            buffer(H, A, R // 2, 128),
            buffer(A, 2, H, D, 2 * F),
            buffer(A, H, D, 2 * F),
            buffer(A, 2, H, D, F),
            buffer(A, H, D, F),
            buffer(2, H, D, F),
            buffer(2, H, D, F),
            wide(R, W),
            buffer(H - 1, R, W),
            wide(R, W),
            buffer(2, H, D, 2 * F),
            buffer(H, D, F),
            wide(H * A // 2, 1, 2 * R),
            buffer(A, H, R // 2, 128),
            wide(8, W),
            wide(8, W),
            buffer(R, W),
            buffer(H, R, W),
            buffer(H - 1, R, W),
            buffer(2, H, D, 2 * F),
            buffer(H, D, F),
            *[buffer(H, D, 2 * F)] * 2,
            wide(H * B * R // KEY_STEP, KEY_STEP, 128),
            *[buffer(A, H, R // 2, 128)] * 2,
            *[buffer(H * B * R // KEY_STEP, 2, R, 128)] * 2,
            *[buffer(A, H, R, 128)] * 2,
            buffer(H, R, 3 * hw),
            *[buffer(H - 1, R, W)] * 2,
            wide(R, W),
            buffer(A, 2, D, W),
            *[buffer(A, 2, H // 2, D, 3 * hw)] * 2,
            *[pltpu.VMEM(outs[n].shape, outs[n].dtype) for n in (0, 1, 4, 5)],
            dma(8),
            dma(1),
            dma(4),
            *[dma(H - 1)] * 8,
            *[dma(B - 1)] * 2,
            *[dma(4)] * 2,
            *[dma(H - 1)] * 2,
            *[dma(4)] * 2,
            *[dma(A - 1)] * 4,
            *[dma(A)] * 2,
            *[dma((A - 1) * (H // 2))] * 2,
            *[dma((H - 1) * H)] * 2,
            *[dma(H - 1)] * 2,
            *[dma(H * A)] * 2,
            *[dma(1)] * 6,
            *[dma(H - 1)] * 6,
            *[dma(4)] * 2,
            *[dma(A * H)] * 4,
            *[dma(H * B * R // KEY_STEP)] * 2,
            *line_sems(A) * 5,
            *pair_scratch(A, (D, W)),
            *pair_scratch(A, (H // 2, D, 3 * hw)),
            *pair_scratch(A, (H // 2, D, 3 * hw)),
            *reduce_scratch(A, (H, D, 128)),
            *swap_scratch(H, (D, 3 * F)),
            *swap_scratch(H, (D, 3 * hw)),
            *swap_scratch(H, (D, 128)),
        ],
        compiler_params=params(0),
        cost_estimate=pl.CostEstimate(flops=10**10, bytes_accessed=10**7, transcendentals=10**6),
        name="layer",
    )(tokens, cotangent, w_qkv, gain_one, gain_two, w_in, w_down, w_out, lengths)


def per_device_split(
    tokens, attn_gain, w_qkv, w_attn_out, mlp_gain, w_in, w_mlp_out, doc_lengths, cotangent
):
    output, input_grad, qkv_grad, out_grad, in_grad, down_grad, gain_one, gain_two = deliver(
        *layer(
            tokens, cotangent, w_qkv, attn_gain[None], mlp_gain[None], w_in, w_mlp_out.T, w_attn_out, doc_lengths
        )
    )
    return (
        output,
        input_grad,
        gain_one[0],
        qkv_grad,
        out_grad,
        gain_two[0],
        in_grad,
        down_grad.T,
    )


def per_device(tokens, attn_gain, w_qkv, *rest):
    heads, blocks = lax.axis_size("head"), lax.axis_size("blk")
    fits = (
        heads == 4
        and blocks == 2 * (tokens.shape[1] // HEAD_DIM // heads) == 8
        and w_qkv.shape[0] * heads == 128
        and tokens.shape[0] == 128
    )
    chosen = per_device_split if fits else per_device_general
    return chosen(tokens, attn_gain, w_qkv, *rest)


def solution(mesh):
    placed = (
        P(("head", "blk"), None),
        P(("head", "blk")),
        P(("head", "blk"), None),
        P(("head", "blk"), None),
        P(("head", "blk")),
        P(("head", "blk"), None),
        P(None, ("head", "blk")),
        P(),
        P(("head", "blk"), None),
    )
    return jax.shard_map(
        per_device,
        mesh=mesh,
        in_specs=placed,
        out_specs=(
            P(("head", "blk"), None),
            P(("head", "blk"), None),
            P(("head", "blk")),
            P(("head", "blk"), None),
            P(("head", "blk"), None),
            P(("head", "blk")),
            P(("head", "blk"), None),
            P(None, ("head", "blk")),
        ),
        check_vma=False,
    )
```
